32 devices in a mesh: seq: 16 (over z, x, core), batch: 2 (over y).
Axes of the slice: x: 2, y: 2, z: 4, core: 2. Of those that a mesh axis runs over, the one named last changes fastest.
Arguments:
- inputs: bfloat16 [2, 2048, 192], P('batch', 'seq'), may hold values from -6 to 6
- targets: bfloat16 [2, 2048, 192], P('batch', 'seq'), may hold values from -22 to 22
- var_ids: int32 [2, 48], P('batch'), may hold values from 0 to 47, each once within a row
- lead_ids: int32 [2], P('batch'), may hold values from 0 to 31
- block_order: int32 [768], replicated, may hold values from 0 to 767, each once
- blocks: float32 [768, 128, 128], P(('seq', 'batch')), may hold values from -0.1875 to 0.1875
- block_momentum: float32 [768, 128, 128], P(('seq', 'batch'))
- left_stats: float32 [768, 128, 128], P(('seq', 'batch')), as said below
- right_stats: float32 [768, 128, 128], P(('seq', 'batch')), as said below
- left_roots: float32 [768, 128, 128], P(('seq', 'batch')), as said below
- right_roots: float32 [768, 128, 128], P(('seq', 'batch')), as said below
- embed_params: float32 [272, 1024], replicated, may hold values from -3 to 3
- embed_first: float32 [272, 1024], replicated
- embed_second: float32 [272, 1024], replicated
- vectors: float32 [15, 1024], replicated, may hold values from -3 to 3
- vector_first: float32 [15, 1024], replicated
- vector_second: float32 [15, 1024], replicated
- head_weight: float32 [1024, 192], replicated, may hold values from -0.1875 to 0.1875
- head_first: float32 [1024, 192], replicated
- head_second: float32 [1024, 192], replicated
Outputs:
- loss_total: float32 [], replicated
- grad_norm: float32 [], replicated
- new_blocks: float32 [768, 128, 128], P(('seq', 'batch'))
- new_momentum: float32 [768, 128, 128], P(('seq', 'batch'))
- new_left: float32 [768, 128, 128], P(('seq', 'batch'))
- new_right: float32 [768, 128, 128], P(('seq', 'batch'))
- new_embed_first: float32 [272, 1024], replicated
- new_embed_second: float32 [272, 1024], replicated
- new_embed: float32 [272, 1024], replicated
- new_vector_first: float32 [15, 1024], replicated
- new_vector_second: float32 [15, 1024], replicated
- new_vectors: float32 [15, 1024], replicated
- new_head_first: float32 [1024, 192], replicated
- new_head_second: float32 [1024, 192], replicated
- new_head: float32 [1024, 192], replicated
The draws below stay inside these ranges and needn't reach their ends.
Inputs may be any that keep to these rules, and one draw needn't show every extreme that they name: `var_ids`: each row names each of the 48 variables once. `block_order`: names each of the 768 blocks once. `left_stats`: every block is symmetric. `right_stats`: every block is symmetric. `left_roots`: every block is symmetric. `right_roots`: every block is symmetric.
All inputs are finite; a program needn't handle non-finite values.
Results may differ from the reference program's by a relative error of at most 0.004.
The reference program's roundings to bfloat16 on the way count: a program that leaves them out, or rounds other values in their place, can miss the bound.
Values may be sent and summed in bfloat16 or wider, within the bound.
A program may use at most 448 MiB of HBM per device.

```python
import math
import jax
import jax.numpy as jnp
from jax import lax

D = 1024
HEADS = 16
HD = 64
FF = 4096
VARS = 48
LEADS = 32
LAT_P = 64
KMODES = 32
BLK = 128
STEP = 10
SEQS = 2
LENGTH = 2048
NLAT = 128
NLON = 64
HOUT = 192
NVEC = 15
EROWS = 272
NBLK = 768


CLIP_NORM = 0.001


KEEP_TWO = 0.95


def grad_size():
    count = 4 * D * D + 2 * D * FF + (VARS * 5 + LEADS) * D + (11 + FF // D) * D + D * VARS * 4
    return CLIP_NORM / math.sqrt(count)


def signed(key, shape, scale):
    return scale * jax.random.truncated_normal(key, -4.0, 4.0, shape, jnp.float32)


def squared(key, shape, scale):
    base = (1.0 - KEEP_TWO) / KEEP_TWO * scale * scale
    return base * jnp.exp(jax.random.uniform(key, shape, jnp.float32, 0.0, math.log(4.0)))


def symmetric(key, low_end):
    first, second = jax.random.split(key)
    diagonal = low_end * jnp.exp(jax.random.uniform(first, (NBLK, BLK), jnp.float32, 0.0, math.log(4.0)))
    noise = jax.random.normal(second, (NBLK, BLK, BLK), jnp.float32) * (0.03 * low_end)
    eye = jnp.eye(BLK, dtype=jnp.float32)
    return (noise + jnp.swapaxes(noise, 1, 2)) * (1.0 - eye) + diagonal[:, :, None] * eye


def draw_targets(key, part):
    key = jax.random.fold_in(key, 1)
    place = jnp.arange(LENGTH, dtype=jnp.float32)[None, :, None] / LENGTH
    order = jnp.arange(SEQS, dtype=jnp.float32)[:, None, None] / max(SEQS - 1, 1)
    base = jax.random.truncated_normal(key, -4.0, 4.0, (SEQS, LENGTH, VARS * 4), jnp.float32)
    return (0.5 * base * (1.0 + 2.0 * place) * (1.0 + 2.0 * order)).astype(jnp.bfloat16)


def draw_block_momentum(key, part):
    key = jax.random.fold_in(key, 2)
    return signed(key, (NBLK, BLK, BLK), grad_size())


def draw_left_stats(key, part):
    key = jax.random.fold_in(key, 3)
    return symmetric(key, (1.0 - KEEP_TWO) / KEEP_TWO * BLK * grad_size() ** 2)


def draw_right_stats(key, part):
    key = jax.random.fold_in(key, 4)
    return symmetric(key, (1.0 - KEEP_TWO) / KEEP_TWO * BLK * grad_size() ** 2)


def draw_left_roots(key, part):
    key = jax.random.fold_in(key, 5)
    return symmetric(key, 0.5 * (0.1 * BLK * grad_size() ** 2) ** (-0.25))


def draw_right_roots(key, part):
    key = jax.random.fold_in(key, 6)
    return symmetric(key, 0.5 * (0.1 * BLK * grad_size() ** 2) ** (-0.25))


def draw_vectors(key, part):
    key = jax.random.fold_in(key, 7)
    first, second = jax.random.split(key)
    rise = 0.6 + 1.2 * jnp.arange(D, dtype=jnp.float32) / D
    noise = jax.random.truncated_normal(first, -3.0, 3.0, (NVEC, D), jnp.float32)
    row = jnp.arange(NVEC)[:, None]
    gain_rows = (row == 1) | (row == 3) | (row == 5)
    gains = rise[None] * (1.0 + 0.1 * noise)
    spread = jnp.where(row == 0, 1.0, 0.3) * noise
    return jnp.where(gain_rows, gains, spread)


def draw_embed_first(key, part):
    key = jax.random.fold_in(key, 8)
    return signed(key, (EROWS, D), 0.11 * grad_size())


def draw_embed_second(key, part):
    key = jax.random.fold_in(key, 9)
    return squared(key, (EROWS, D), grad_size())


def draw_vector_first(key, part):
    key = jax.random.fold_in(key, 10)
    return signed(key, (NVEC, D), 0.33 * grad_size())


def draw_vector_second(key, part):
    key = jax.random.fold_in(key, 11)
    return squared(key, (NVEC, D), 3.0 * grad_size())


def draw_head_first(key, part):
    key = jax.random.fold_in(key, 12)
    return signed(key, (D, VARS * 4), 0.11 * grad_size())


def draw_head_second(key, part):
    key = jax.random.fold_in(key, 13)
    return squared(key, (D, VARS * 4), grad_size())


def block_levels(own_key, dims, cuts, least, top_value):
    def one(axis_at, blocks):
        draws = jax.random.uniform(jax.random.fold_in(jax.random.fold_in(own_key, 6), axis_at), (blocks,), jnp.float32, least / len(cuts), top_value / len(cuts))
        return jnp.repeat(jnp.exp(draws), dims[axis_at] // blocks).reshape((-1,) + (1,) * (len(dims) - axis_at - 1))

    factor_of = one(*cuts[0])
    for cut in cuts[1:]:
        factor_of = factor_of * one(*cut)
    return factor_of


def scatter_about(key, shape, scale, bound, cuts=(), kind=jnp.bfloat16):
    drawn = scale * jax.random.normal(key, shape, jnp.float32)
    if cuts:
        drawn = drawn * block_levels(key, shape, cuts, -0.22, 0.18)
    return jnp.clip(drawn, -bound, bound).astype(kind)


def setup_inputs(seed: int = 0) -> dict:
    key_of = jax.random.split(jax.random.key(seed), 21)
    inputs = scatter_about(key_of[0], (SEQS, LENGTH, HOUT), 1.0, 6.0, ((0, 2), (1, 16)))
    targets = draw_targets(jax.random.fold_in(key_of[20], 71), 0)
    var_ids = jax.vmap(lambda own: jax.random.permutation(own, VARS))(jax.random.split(key_of[2], SEQS)).reshape((SEQS, VARS)).astype(jnp.int32)
    lead_ids = jax.random.randint(key_of[3], (SEQS,), 0, LEADS).astype(jnp.int32)
    block_order = jax.random.permutation(key_of[4], NBLK).astype(jnp.int32)
    blocks = scatter_about(key_of[5], (NBLK, BLK, BLK), D ** -0.5, 0.1875, ((0, 32),), jnp.float32)
    block_momentum = draw_block_momentum(jax.random.fold_in(key_of[20], 71), 0)
    left_stats = draw_left_stats(jax.random.fold_in(key_of[20], 71), 0)
    right_stats = draw_right_stats(jax.random.fold_in(key_of[20], 71), 0)
    left_roots = draw_left_roots(jax.random.fold_in(key_of[20], 71), 0)
    right_roots = draw_right_roots(jax.random.fold_in(key_of[20], 71), 0)
    embed_params = scatter_about(key_of[11], (EROWS, D), 0.5, 3.0, (), jnp.float32)
    embed_first = draw_embed_first(jax.random.fold_in(key_of[20], 71), 0)
    embed_second = draw_embed_second(jax.random.fold_in(key_of[20], 71), 0)
    vectors = draw_vectors(jax.random.fold_in(key_of[20], 71), 0)
    vector_first = draw_vector_first(jax.random.fold_in(key_of[20], 71), 0)
    vector_second = draw_vector_second(jax.random.fold_in(key_of[20], 71), 0)
    head_weight = scatter_about(key_of[17], (D, HOUT), D ** -0.5, 0.1875, (), jnp.float32)
    head_first = draw_head_first(jax.random.fold_in(key_of[20], 71), 0)
    head_second = draw_head_second(jax.random.fold_in(key_of[20], 71), 0)
    return dict(inputs=inputs, targets=targets, var_ids=var_ids, lead_ids=lead_ids, block_order=block_order, blocks=blocks, block_momentum=block_momentum, left_stats=left_stats, right_stats=right_stats, left_roots=left_roots, right_roots=right_roots, embed_params=embed_params, embed_first=embed_first, embed_second=embed_second, vectors=vectors, vector_first=vector_first, vector_second=vector_second, head_weight=head_weight, head_first=head_first, head_second=head_second)


HIGH = lax.Precision.HIGHEST
EPS = 1e-05
CLIP_NORM = 0.001
SPECTRAL = 0.5
BETA_ONE = 0.9
BETA_TWO = 0.95
SHAMPOO_RATE = 0.1
DECAY = 0.01
ADAM_EPS = 1e-08
EMBED_RATE = 0.2
VECTOR_RATE = 0.5
HEAD_RATE = 0.05

@jax.custom_vjp
def low(v):
    return lax.optimization_barrier(v.astype(jnp.bfloat16)).astype(jnp.float32)

@jax.custom_vjp
def low_back(v):
    return v

def low_keep(v):
    return (low(v), None)

def low_pass(kept, grad):
    return (grad,)

def back_keep(v):
    return (v, None)

def back_low(kept, grad):
    return (low(grad),)
low.defvjp(low_keep, low_pass)
low_back.defvjp(back_keep, back_low)

def layer_norm(rows, gain, shift):
    mean = lax.optimization_barrier(jnp.mean(rows, -1, keepdims=True))
    centred = rows - mean
    return centred * lax.rsqrt(lax.optimization_barrier(jnp.mean(centred * centred, -1, keepdims=True)) + EPS) * gain + shift

def to_blocks(matrix, size):
    rows, cols = matrix.shape
    return matrix.reshape(rows // size, size, cols // size, size).transpose(0, 2, 1, 3).reshape(-1, size, size)

def from_blocks(stack, rows, cols):
    size = stack.shape[-1]
    return stack.reshape(rows // size, cols // size, size, size).transpose(0, 2, 1, 3).reshape(rows, cols)

def split_matrices(stack):
    size = stack.shape[-1]
    found = []
    begin = 0
    for rows, cols in ((D, 3 * D), (D, D), (D, FF), (FF, D)):
        count = rows * cols // (size * size)
        found.append(from_blocks(stack[begin:begin + count], rows, cols))
        begin += count
    return found

def mat(left, right):
    return jnp.dot(left, right, precision=HIGH)

def embed_block(pix, tok_sel, emb_sel, query):
    tokens = jnp.einsum('pvc,vcd->pvd', pix, tok_sel, precision=HIGH) + emb_sel[None]
    logits = jnp.einsum('pvd,d->pv', tokens, query, precision=HIGH) * (1.0 / math.sqrt(D))
    weights = jax.nn.softmax(logits, -1)
    return jnp.einsum('pv,pvd->pd', weights, tokens, precision=HIGH)

def attend(query, keys, values):
    rows = min(512, LENGTH)
    heads_k = keys.reshape(LENGTH, HEADS, HD)
    heads_v = values.reshape(LENGTH, HEADS, HD)

    def one(block):
        scores = low_back(jnp.einsum('phd,nhd->hpn', block, heads_k, precision=HIGH) * (1.0 / math.sqrt(HD)))
        probs = low(jax.nn.softmax(scores, -1))
        return jnp.einsum('hpn,nhd->phd', probs, heads_v, precision=HIGH)
    out = lax.map(jax.checkpoint(one), query.reshape(LENGTH // rows, rows, HEADS, HD))
    return out.reshape(LENGTH, D)

def sequence_loss(pix, goal, ids, lead, params):
    embed, vec, head, w_qkv, w_out, w_up, w_down = params
    pick = (ids[:, None] == jnp.arange(VARS, dtype=jnp.int32)[None]).astype(jnp.float32)
    tok_sel = jnp.einsum('vw,wcd->vcd', pick, embed[:VARS * 4].reshape(VARS, 4, D), precision=HIGH)
    emb_sel = mat(pick, embed[VARS * 4:VARS * 5])
    lead_row = mat((lead == jnp.arange(LEADS, dtype=jnp.int32)).astype(jnp.float32), embed[VARS * 5:])
    rows = min(512, LENGTH)
    pieces = pix.reshape(LENGTH // rows, rows, VARS, 4)
    stream = lax.map(jax.checkpoint(lambda piece: embed_block(piece, tok_sel, emb_sel, vec[0])), pieces)
    stream = stream.reshape(LENGTH, D) + lead_row
    normed = low(layer_norm(stream, vec[1], vec[2]))
    bias = jnp.concatenate([vec[9], jnp.zeros_like(vec[9]), vec[10]])
    qkv = low(low_back(mat(normed, low(w_qkv)) + bias))
    attended = low(low_back(attend(qkv[:, :D], qkv[:, D:2 * D], qkv[:, 2 * D:])))
    mid = stream + low_back(mat(attended, low(w_out)) + vec[7])
    normed_two = low(layer_norm(mid, vec[3], vec[4]))
    upper = low_back(mat(normed_two, low(w_up)) + vec[11:].reshape(-1))
    out = mid + low_back(mat(low(jax.nn.gelu(upper)), low(w_down)) + vec[8])
    final = low(layer_norm(out, vec[5], vec[6]))
    pred = low_back(mat(final, low(head)))
    grid = (pred - goal).reshape(LENGTH // LAT_P, LAT_P, VARS, 2, 2).transpose(2, 1, 3, 0, 4).reshape(VARS, NLAT, NLON)
    lat = ((jnp.arange(NLAT, dtype=jnp.float32) + 0.5) / NLAT - 0.5) * math.pi
    weight = jnp.cos(lat)
    weight = (weight / jnp.mean(weight))[None, :, None]
    column = jnp.arange(NLON, dtype=jnp.int32)
    modes = jnp.arange(KMODES, dtype=jnp.int32)
    angle = (column[:, None] * modes[None] % NLON).astype(jnp.float32) * (2.0 * math.pi / NLON)
    part_c = jnp.einsum('vrc,ck->vrk', grid, jnp.cos(angle), precision=HIGH)
    part_s = jnp.einsum('vrc,ck->vrk', grid, jnp.sin(angle), precision=HIGH)
    mse = jnp.sum(weight * grid * grid) / (SEQS * VARS * NLAT * NLON)
    spectral = SPECTRAL * jnp.sum(weight * (part_c * part_c + part_s * part_s)) / (NLON * SEQS * VARS * NLAT * KMODES)
    return mse + spectral

def adam(value, first, second, grad, rate):
    first = BETA_ONE * first + (1.0 - BETA_ONE) * grad
    second = BETA_TWO * second + (1.0 - BETA_TWO) * grad * grad
    step = first / (1.0 - BETA_ONE ** STEP) / (jnp.sqrt(second / (1.0 - BETA_TWO ** STEP)) + ADAM_EPS)
    return (first, second, value - rate * (step + DECAY * value))

def reference(inputs, targets, var_ids, lead_ids, block_order, blocks, block_momentum, left_stats, right_stats, left_roots, right_roots, embed_params, embed_first, embed_second, vectors, vector_first, vector_second, head_weight, head_first, head_second):
    natural = jnp.zeros_like(blocks).at[block_order].set(blocks)
    params = tuple([embed_params, vectors, head_weight] + split_matrices(natural))
    pixels = inputs.astype(jnp.float32)
    goals = targets.astype(jnp.float32)

    def total(params):

        def step(acc, item):
            pix, goal, ids, lead = item
            return (acc + jax.checkpoint(sequence_loss)(pix, goal, ids, lead, params), None)
        acc, _ = lax.scan(step, jnp.zeros((), jnp.float32), (pixels, goals, var_ids, lead_ids))
        return acc
    loss_total, back = jax.vjp(total, params)
    grads = back(jnp.ones((), jnp.float32))[0]
    g_embed, g_vectors, g_head = (grads[0], grads[1], grads[2])
    size = blocks.shape[-1]
    slot_grads = jnp.concatenate([to_blocks(grad, size) for grad in grads[3:]])[block_order]
    grad_norm = jnp.sqrt(jnp.sum(slot_grads * slot_grads) + jnp.sum(g_embed * g_embed) + jnp.sum(g_vectors * g_vectors) + jnp.sum(g_head * g_head))
    clip = CLIP_NORM / jnp.maximum(grad_norm, CLIP_NORM)
    owned = slot_grads * clip
    new_momentum = BETA_ONE * block_momentum + (1.0 - BETA_ONE) * owned
    new_left = BETA_TWO * left_stats + (1.0 - BETA_TWO) * jnp.einsum('bij,bkj->bik', owned, owned, precision=HIGH)
    new_right = BETA_TWO * right_stats + (1.0 - BETA_TWO) * jnp.einsum('bji,bjk->bik', owned, owned, precision=HIGH)
    direction = jnp.einsum('bij,bjk->bik', jnp.einsum('bij,bjk->bik', left_roots, new_momentum, precision=HIGH), right_roots, precision=HIGH)
    new_blocks = blocks - SHAMPOO_RATE * (direction + DECAY * blocks)
    e_one, e_two, e_new = adam(embed_params, embed_first, embed_second, g_embed * clip, EMBED_RATE)
    v_one, v_two, v_new = adam(vectors, vector_first, vector_second, g_vectors * clip, VECTOR_RATE)
    h_one, h_two, h_new = adam(head_weight, head_first, head_second, g_head * clip, HEAD_RATE)
    return (loss_total, grad_norm, new_blocks, new_momentum, new_left, new_right, e_one, e_two, e_new, v_one, v_two, v_new, h_one, h_two, h_new)
```

```python
import math

import jax
import jax.numpy as jnp
from jax import lax
from jax.experimental import pallas as pl
from jax.experimental.pallas import tpu as pltpu
from jax.sharding import PartitionSpec as P

D = 1024
HEADS = 16
HD = 64
FF = 4096
VARS = 48
LEADS = 32
LAT_P = 64
KMODES = 32
STEP = 10


HIGH = lax.Precision.HIGHEST
EPS = 1e-05
CLIP_NORM = 0.001
SPECTRAL = 0.5
BETA_ONE = 0.9
BETA_TWO = 0.95
SHAMPOO_RATE = 0.1
DECAY = 0.01
ADAM_EPS = 1e-08
EMBED_RATE = 0.2
VECTOR_RATE = 0.5
HEAD_RATE = 0.05
FLOOR = -1e30
EROWS = VARS * 5 + LEADS
HOUT = VARS * 4
MSE_COUNT = 786432.0
DFT_COUNT = 25165824.0


def layer_norm(rows, gain, shift):
    mean = jnp.mean(rows, -1, keepdims=True)
    centred = rows - mean
    return centred * lax.rsqrt(jnp.mean(centred * centred, -1, keepdims=True) + EPS) * gain + shift


def to_blocks(matrix, size):
    rows, cols = matrix.shape
    return (
        matrix.reshape(rows // size, size, cols // size, size)
        .transpose(0, 2, 1, 3)
        .reshape(-1, size, size)
    )


def from_blocks(stack, rows, cols):
    size = stack.shape[-1]
    return (
        stack.reshape(rows // size, cols // size, size, size)
        .transpose(0, 2, 1, 3)
        .reshape(rows, cols)
    )


def split_matrices(stack):
    size = stack.shape[-1]
    found = []
    begin = 0
    for rows, cols in ((D, 3 * D), (D, D), (D, FF), (FF, D)):
        count = rows * cols // (size * size)
        found.append(from_blocks(stack[begin : begin + count], rows, cols))
        begin += count
    return found


def embed_patches(pixels, tok_sel, emb_sel, query, lead_rows):
    tokens = jnp.einsum("spvc,svcd->spvd", pixels, tok_sel, precision=HIGH) + emb_sel[:, None]
    logits = jnp.einsum("spvd,d->spv", tokens, query, precision=HIGH) * (1.0 / math.sqrt(D))
    weights = jax.nn.softmax(logits, -1)
    return jnp.einsum("spv,spvd->spd", weights, tokens, precision=HIGH) + lead_rows[:, None]


def split_heads(rows):
    return rows.reshape(rows.shape[0], rows.shape[1], HEADS, HD)


def attention_forward(query, keys, values):
    seqs, length, _ = query.shape
    scale = 1.0 / math.sqrt(HD)
    heads_q = split_heads(query)
    start_state = (
        jnp.zeros((seqs, HEADS, length, HD), jnp.float32),
        jnp.full((seqs, HEADS, length), FLOOR, jnp.float32),
        jnp.zeros((seqs, HEADS, length), jnp.float32),
    )
    key_rows = lax.all_gather(keys, "seq", axis=1, tiled=True)
    value_rows = lax.all_gather(values, "seq", axis=1, tiled=True)
    count = key_rows.shape[1] // length
    key_blocks = key_rows.reshape(seqs, count, length, HEADS, HD)
    value_blocks = value_rows.reshape(seqs, count, length, HEADS, HD)

    def visit(inner, index):
        acc, top, total = inner
        scores = (
            jnp.einsum(
                "sphd,snhd->shpn", heads_q, key_blocks[:, index], preferred_element_type=jnp.float32
            )
            * scale
        )
        new_top = jnp.maximum(top, jnp.max(scores, -1))
        fade = jnp.exp(top - new_top)
        probs = jnp.exp(scores - new_top[..., None])
        total = total * fade + jnp.sum(probs, -1)
        acc = acc * fade[..., None] + jnp.einsum(
            "shpn,snhd->shpd",
            probs.astype(jnp.bfloat16),
            value_blocks[:, index],
            preferred_element_type=jnp.float32,
        )
        return ((acc, new_top, total), None)

    inner, _ = lax.scan(visit, start_state, jnp.arange(count))
    acc, top, total = inner
    attended = (acc / total[..., None]).transpose(0, 2, 1, 3).reshape(seqs, length, HEADS * HD)
    return (attended, (top + jnp.log(total)).transpose(0, 2, 1))


def attention_backward(query, keys, values, attended, lse, d_att):
    seqs, length, _ = query.shape
    scale = 1.0 / math.sqrt(HD)
    heads_q = split_heads(query)
    heads_k = split_heads(keys)
    heads_v = split_heads(values)
    heads_d = split_heads(d_att)
    delta = jnp.sum(heads_d.astype(jnp.float32) * split_heads(attended), -1)
    lse_h = lse.transpose(0, 2, 1)
    delta_h = delta.transpose(0, 2, 1)
    key_rows = lax.all_gather(keys, "seq", axis=1, tiled=True)
    value_rows = lax.all_gather(values, "seq", axis=1, tiled=True)
    count = key_rows.shape[1] // length
    key_blocks = key_rows.reshape(seqs, count, length, HEADS, HD)
    value_blocks = value_rows.reshape(seqs, count, length, HEADS, HD)

    def visit(inner, index):
        k_part = key_blocks[:, index]
        scores = (
            jnp.einsum("sphd,snhd->shpn", heads_q, k_part, preferred_element_type=jnp.float32)
            * scale
        )
        probs = jnp.exp(scores - lse_h[..., None])
        d_prob = jnp.einsum(
            "sphd,snhd->shpn", heads_d, value_blocks[:, index], preferred_element_type=jnp.float32
        )
        d_score = (probs * (d_prob - delta_h[..., None])).astype(jnp.bfloat16)
        return (
            inner
            + jnp.einsum("shpn,snhd->sphd", d_score, k_part, preferred_element_type=jnp.float32)
            * scale,
            None,
        )

    inner, _ = lax.scan(visit, jnp.zeros((seqs, length, HEADS, HD), jnp.float32), jnp.arange(count))
    d_query = inner
    all_lse, all_delta = (
        lax.all_gather(lse, "seq", axis=1, tiled=True),
        lax.all_gather(delta, "seq", axis=1, tiled=True),
    )
    empty = jnp.zeros((seqs, length, HEADS, HD), jnp.float32)
    q_rows = lax.all_gather(query, "seq", axis=1, tiled=True)
    g_rows = lax.all_gather(d_att, "seq", axis=1, tiled=True)
    count = q_rows.shape[1] // length
    q_blocks = q_rows.reshape(seqs, count, length, HEADS, HD)
    g_blocks = g_rows.reshape(seqs, count, length, HEADS, HD)
    lse_rows = all_lse.reshape(seqs, count, length, HEADS)
    delta_rows = all_delta.reshape(seqs, count, length, HEADS)

    def visit(inner, index):
        d_key, d_value = inner
        q_part = q_blocks[:, index]
        g_part = g_blocks[:, index]
        scores = (
            jnp.einsum("snhd,sphd->shnp", q_part, heads_k, preferred_element_type=jnp.float32)
            * scale
        )
        probs = jnp.exp(scores - lse_rows[:, index].transpose(0, 2, 1)[..., None])
        d_value = d_value + jnp.einsum(
            "shnp,snhd->sphd",
            probs.astype(jnp.bfloat16),
            g_part,
            preferred_element_type=jnp.float32,
        )
        d_prob = jnp.einsum("snhd,sphd->shnp", g_part, heads_v, preferred_element_type=jnp.float32)
        d_score = (probs * (d_prob - delta_rows[:, index].transpose(0, 2, 1)[..., None])).astype(
            jnp.bfloat16
        )
        d_key = (
            d_key
            + jnp.einsum("shnp,snhd->sphd", d_score, q_part, preferred_element_type=jnp.float32)
            * scale
        )
        return ((d_key, d_value), None)

    inner, _ = lax.scan(visit, (empty, empty), jnp.arange(count))
    d_key, d_value = inner
    return (d_query, d_key, d_value)


def feed_inner(normed_two, w_up, vectors):
    upper = jnp.dot(normed_two, w_up, preferred_element_type=jnp.float32) + vectors[11:].reshape(-1)
    return (upper, jax.nn.gelu(upper).astype(jnp.bfloat16))


def layer_forward(rows, seqs, mats, vectors):
    w_qkv, w_out, w_up, w_down = mats
    normed = layer_norm(rows, vectors[1], vectors[2]).astype(jnp.bfloat16)
    bias = jnp.concatenate([vectors[9], jnp.zeros_like(vectors[9]), vectors[10]])
    qkv = (jnp.dot(normed, w_qkv, preferred_element_type=jnp.float32) + bias).astype(jnp.bfloat16)
    query = qkv[:, :D].reshape(seqs, -1, D)
    keys = qkv[:, D : 2 * D].reshape(seqs, -1, D)
    values = qkv[:, 2 * D :].reshape(seqs, -1, D)
    attended, lse = attention_forward(query, keys, values)
    att_low = attended.reshape(-1, D).astype(jnp.bfloat16)
    mid = rows + jnp.dot(att_low, w_out, preferred_element_type=jnp.float32) + vectors[7]
    normed_two = layer_norm(mid, vectors[3], vectors[4]).astype(jnp.bfloat16)
    upper, active = feed_inner(normed_two, w_up, vectors)
    out = mid + jnp.dot(active, w_down, preferred_element_type=jnp.float32) + vectors[8]
    saved = (upper, active)
    return (out, (rows, normed, query, keys, values, attended, lse, mid, normed_two, saved))


def layer_backward(d_out, kept, mats, vectors):
    rows, normed, query, keys, values, attended, lse, mid, normed_two, saved = kept
    w_qkv, w_out, w_up, w_down = mats
    upper, active = saved
    d_branch = d_out.astype(jnp.bfloat16)
    g_down = jnp.einsum("rf,rd->fd", active, d_branch, preferred_element_type=jnp.float32)
    d_active = jnp.einsum("rd,fd->rf", d_branch, w_down, preferred_element_type=jnp.float32)
    d_upper = jax.vjp(jax.nn.gelu, upper)[1](d_active)[0].astype(jnp.bfloat16)
    g_up = jnp.einsum("rd,rf->df", normed_two, d_upper, preferred_element_type=jnp.float32)
    d_normed_two = jnp.einsum("rf,df->rd", d_upper, w_up, preferred_element_type=jnp.float32)
    d_mid_norm, g_gain_two, g_shift_two = jax.vjp(layer_norm, mid, vectors[3], vectors[4])[1](
        d_normed_two
    )
    d_mid = d_out + d_mid_norm
    d_mid_low = d_mid.astype(jnp.bfloat16)
    att_low = attended.reshape(-1, D).astype(jnp.bfloat16)
    g_out = jnp.einsum("ra,rd->ad", att_low, d_mid_low, preferred_element_type=jnp.float32)
    d_att = jnp.einsum("rd,ad->ra", d_mid_low, w_out, preferred_element_type=jnp.float32).astype(
        jnp.bfloat16
    )
    seqs = query.shape[0]
    d_query, d_key, d_value = attention_backward(
        query, keys, values, attended, lse, d_att.reshape(seqs, -1, D)
    )
    d_qkv = jnp.concatenate(
        [d_query.reshape(-1, D), d_key.reshape(-1, D), d_value.reshape(-1, D)], 1
    ).astype(jnp.bfloat16)
    g_qkv = jnp.einsum("rd,re->de", normed, d_qkv, preferred_element_type=jnp.float32)
    d_normed = jnp.einsum("re,de->rd", d_qkv, w_qkv, preferred_element_type=jnp.float32)
    d_rows_norm, g_gain_one, g_shift_one = jax.vjp(layer_norm, rows, vectors[1], vectors[2])[1](
        d_normed
    )
    qkv_sums = jnp.sum(d_qkv.astype(jnp.float32), 0)
    small = (
        g_gain_one,
        g_shift_one,
        g_gain_two,
        g_shift_two,
        jnp.sum(d_mid_low.astype(jnp.float32), 0),
        jnp.sum(d_branch.astype(jnp.float32), 0),
        qkv_sums[:D],
        qkv_sums[2 * D :],
        jnp.sum(d_upper.astype(jnp.float32), 0),
    )
    return (d_mid + d_rows_norm, (g_qkv, g_out, g_up, g_down), small)


def loss_terms(pred, targets, seqs, length):
    strips = lax.axis_size("seq")
    cols = length // LAT_P
    nlat = 2 * LAT_P
    nlon = 2 * cols * strips
    all_seqs = seqs * lax.axis_size("batch")
    diff = pred.reshape(seqs, length, -1) - targets.astype(jnp.float32)
    grid = (
        diff.reshape(seqs, cols, LAT_P, VARS, 2, 2)
        .transpose(0, 3, 2, 4, 1, 5)
        .reshape(seqs, VARS, nlat, 2 * cols)
    )
    lat = ((jnp.arange(nlat, dtype=jnp.float32) + 0.5) / nlat - 0.5) * math.pi
    weight = jnp.cos(lat)
    weight = (weight / jnp.mean(weight))[None, None, :, None]
    column = lax.axis_index("seq") * (2 * cols) + jnp.arange(2 * cols, dtype=jnp.int32)
    modes = jnp.arange(KMODES, dtype=jnp.int32)
    angle = (column[:, None] * modes[None] % nlon).astype(jnp.float32) * (2.0 * math.pi / nlon)
    cosine = jnp.cos(angle)
    sine = jnp.sin(angle)
    part_c = jnp.einsum("svrc,ck->svrk", grid, cosine, precision=HIGH)
    part_s = jnp.einsum("svrc,ck->svrk", grid, sine, precision=HIGH)
    full_c, full_s = lax.psum((part_c, part_s), "seq")
    mse_count = all_seqs * VARS * nlat * nlon
    dft_count = nlon * all_seqs * VARS * nlat * KMODES
    mse = jnp.sum(weight * grid * grid) / mse_count
    spectral = SPECTRAL * jnp.sum(weight * (full_c * full_c + full_s * full_s)) / dft_count
    first = (lax.axis_index("seq") == 0).astype(jnp.float32)
    back_wave = jnp.einsum("svrk,ck->svrc", full_c, cosine, precision=HIGH) + jnp.einsum(
        "svrk,ck->svrc", full_s, sine, precision=HIGH
    )
    d_grid = 2.0 * weight * grid / mse_count + 2.0 * SPECTRAL / dft_count * weight * back_wave
    d_pred = (
        d_grid.reshape(seqs, VARS, LAT_P, 2, cols, 2)
        .transpose(0, 4, 2, 1, 3, 5)
        .reshape(seqs * length, VARS * 4)
    )
    return (d_pred, mse + first * spectral)


def adam(value, first, second, grad, rate):
    first = BETA_ONE * first + (1.0 - BETA_ONE) * grad
    second = BETA_TWO * second + (1.0 - BETA_TWO) * grad * grad
    step = first / (1.0 - BETA_ONE**STEP) / (jnp.sqrt(second / (1.0 - BETA_TWO**STEP)) + ADAM_EPS)
    return (first, second, value - rate * (step + DECAY * value))


def shards(
    inputs,
    targets,
    var_ids,
    lead_ids,
    block_order,
    blocks,
    block_momentum,
    left_stats,
    right_stats,
    left_roots,
    right_roots,
    embed_params,
    embed_first,
    embed_second,
    vectors,
    vector_first,
    vector_second,
    head_weight,
    head_first,
    head_second,
):
    seqs, length, _ = inputs.shape
    size = blocks.shape[-1]
    low_blocks = blocks.astype(jnp.bfloat16)
    stack = lax.all_gather(low_blocks, ("seq", "batch"), axis=0, tiled=True)
    natural = jnp.zeros_like(stack).at[block_order].set(stack)
    mats = split_matrices(natural)
    head_low = head_weight.astype(jnp.bfloat16)
    pick = (var_ids[..., None] == jnp.arange(VARS, dtype=jnp.int32)[None, None]).astype(jnp.float32)
    lead_pick = (lead_ids[:, None] == jnp.arange(LEADS, dtype=jnp.int32)[None]).astype(jnp.float32)
    tok_sel = jnp.einsum(
        "svw,wcd->svcd", pick, embed_params[: VARS * 4].reshape(VARS, 4, D), precision=HIGH
    )
    emb_sel = jnp.einsum("svw,wd->svd", pick, embed_params[VARS * 4 : VARS * 5], precision=HIGH)
    lead_rows = jnp.dot(lead_pick, embed_params[VARS * 5 :], precision=HIGH)
    pixels = inputs.astype(jnp.float32).reshape(seqs, length, VARS, 4)

    def embed_local(tok_part, emb_part, query, lead_part):
        return embed_patches(pixels, tok_part, emb_part, query, lead_part)

    stream, embed_back = jax.vjp(embed_local, tok_sel, emb_sel, vectors[0], lead_rows)
    out, kept = layer_forward(stream.reshape(-1, D), seqs, mats, vectors)
    final_rows, final_back = jax.vjp(layer_norm, out, vectors[5], vectors[6])
    final = final_rows.astype(jnp.bfloat16)
    pred = jnp.dot(final, head_low, preferred_element_type=jnp.float32)
    d_pred, loss_part = loss_terms(pred, targets, seqs, length)
    d_low = d_pred.astype(jnp.bfloat16)
    g_head = jnp.einsum("rd,ro->do", final, d_low, preferred_element_type=jnp.float32)
    d_final = jnp.einsum("ro,do->rd", d_low, head_low, preferred_element_type=jnp.float32)
    d_out, g_gain_final, g_shift_final = final_back(d_final)
    d_rows, matrix_grads, small = layer_backward(d_out, kept, mats, vectors)
    d_tok, d_emb, d_query, d_lead = embed_back(d_rows.reshape(seqs, length, D))
    g_embed = jnp.concatenate(
        [
            jnp.einsum("svw,svcd->wcd", pick, d_tok, precision=HIGH).reshape(VARS * 4, D),
            jnp.einsum("svw,svd->wd", pick, d_emb, precision=HIGH),
            jnp.einsum("sl,sd->ld", lead_pick, d_lead, precision=HIGH),
        ]
    )
    g_gain_one, g_shift_one, g_gain_two, g_shift_two, b_out, b_down, b_query, b_value, b_up = small
    g_vectors = jnp.concatenate(
        [
            jnp.stack(
                [
                    d_query,
                    g_gain_one,
                    g_shift_one,
                    g_gain_two,
                    g_shift_two,
                    g_gain_final,
                    g_shift_final,
                    b_out,
                    b_down,
                    b_query,
                    b_value,
                ]
            ),
            b_up.reshape(-1, D),
        ]
    )
    slot_grads = jnp.concatenate([to_blocks(grad, size) for grad in matrix_grads])[block_order]
    owned = lax.psum_scatter(slot_grads, ("seq", "batch"), scatter_dimension=0, tiled=True)
    g_embed, g_vectors, g_head, loss_total = lax.psum(
        (g_embed, g_vectors, g_head, loss_part), ("seq", "batch")
    )
    rest_squares = (
        jnp.sum(g_embed * g_embed) + jnp.sum(g_vectors * g_vectors) + jnp.sum(g_head * g_head)
    )
    grad_norm = jnp.sqrt(lax.psum(jnp.sum(owned * owned), ("seq", "batch")) + rest_squares)
    clip = CLIP_NORM / jnp.maximum(grad_norm, CLIP_NORM)
    owned = owned * clip
    new_momentum = BETA_ONE * block_momentum + (1.0 - BETA_ONE) * owned
    new_left = BETA_TWO * left_stats + (1.0 - BETA_TWO) * jnp.einsum(
        "bij,bkj->bik", owned, owned, precision=HIGH
    )
    new_right = BETA_TWO * right_stats + (1.0 - BETA_TWO) * jnp.einsum(
        "bji,bjk->bik", owned, owned, precision=HIGH
    )
    direction = jnp.einsum(
        "bij,bjk->bik",
        jnp.einsum("bij,bjk->bik", left_roots, new_momentum, precision=HIGH),
        right_roots,
        precision=HIGH,
    )
    new_blocks = blocks - SHAMPOO_RATE * (direction + DECAY * blocks)
    e_one, e_two, e_new = adam(embed_params, embed_first, embed_second, g_embed * clip, EMBED_RATE)
    v_one, v_two, v_new = adam(vectors, vector_first, vector_second, g_vectors * clip, VECTOR_RATE)
    h_one, h_two, h_new = adam(head_weight, head_first, head_second, g_head * clip, HEAD_RATE)
    return (
        loss_total,
        grad_norm,
        new_blocks,
        new_momentum,
        new_left,
        new_right,
        e_one,
        e_two,
        e_new,
        v_one,
        v_two,
        v_new,
        h_one,
        h_two,
        h_new,
    )


TOK = 128
NSEQ = 16
BLOCK = 128
N_LEFT = 56
N_RIGHT = 72
QCH = 256
LOG2E = math.log2(math.e)
MESH_ID = pl.DeviceIdType.MESH
NT = (((1,), (1,)), ((), ()))
TN = (((0,), (0,)), ((), ()))
NN = (((1,), (0,)), ((), ()))
BF = jnp.bfloat16
F32 = jnp.float32
VM = pltpu.VMEM


def mm(a, b, dims=NN):
    return lax.dot_general(a, b, dims, preferred_element_type=F32)


def mmh(a, b, dims=NN):
    return lax.dot_general(a, b, dims, precision=HIGH, preferred_element_type=F32)


def flip(x):
    return jnp.swapaxes(x.astype(F32), 0, 1).astype(x.dtype)


def normalise(x):
    mean = jnp.mean(x, -1, keepdims=True)
    centred = x - mean
    rstd = lax.rsqrt(jnp.mean(centred * centred, -1, keepdims=True) + EPS)
    return centred * rstd, rstd


def normalise_back(grad, unit, rstd, gain):
    inner = grad * gain
    return rstd * (
        inner
        - jnp.mean(inner, -1, keepdims=True)
        - unit * jnp.mean(inner * unit, -1, keepdims=True)
    )


def column_sum(x):
    return jnp.sum(x, 0, keepdims=True)


GELU_K = math.sqrt(2.0 / math.pi)


def gelu_value(x):
    return 0.5 * x * (1.0 + jnp.tanh(GELU_K * (x + 0.044715 * x * x * x)))


def gelu_slope(x):
    t = jnp.tanh(GELU_K * (x + 0.044715 * x * x * x))
    return 0.5 * (1.0 + t) + 0.5 * x * (1.0 - t * t) * GELU_K * (1.0 + 3.0 * 0.044715 * x * x)


def layer_kernel(
    n1_ref,
    h0_ref,
    vec_ref,
    bias_ref,
    bup_ref,
    goal_ref,
    head_ref,
    wlat_ref,
    wqkv_hbm,
    wo_hbm,
    wup_hbm,
    wdown_hbm,
    left_hbm,
    right_hbm,
    drow_ref,
    gvec_ref,
    gup_ref,
    ghead_ref,
    loss_ref,
    wqkv,
    wo,
    wup,
    wdown,
    left,
    right,
    slab,
    qkv_t,
    out_t,
    out_t32,
    lse,
    o_in,
    d_slab,
    do_t,
    dqkv_t,
    dqkv_in,
    k_row,
    v_row,
    q_row,
    do_row,
    s_scr,
    dk_acc,
    dv_acc,
    mid_s,
    up_s,
    acc,
    wave,
    w_sem,
    a_send,
    a_recv,
    x_send,
    x_recv,
    g_local,
    g_send,
    g_recv,
):
    s = lax.axis_index("seq")
    b = lax.axis_index("batch")
    core = lax.rem(s, 2)
    xpos = lax.rem(s // 2, 2)
    zpos = s // 4
    sibling = s + 1 - 2 * core

    copies = []
    for i, (src, dst) in enumerate(((wqkv_hbm, wqkv), (wo_hbm, wo), (wup_hbm, wup), (wdown_hbm, wdown))):
        c = pltpu.make_async_copy(src, dst, w_sem.at[i])
        c.start()
        copies.append(c)

    barrier = pltpu.get_barrier_semaphore()

    def greet(o, _):
        pl.semaphore_signal(
            barrier, inc=1, device_id=(lax.rem(s + o, NSEQ), b), device_id_type=MESH_ID
        )
        return _

    lax.fori_loop(1, NSEQ, greet, 0)
    pl.semaphore_wait(barrier, NSEQ - 1)

    share = []

    def share_group(index, stage, target, begin, count):
        part = pl.ds(begin, count)
        c = pltpu.make_async_copy(stage.at[part], target.at[0, part], g_local.at[index])
        c.start()
        r = pltpu.make_async_remote_copy(
            src_ref=stage.at[part],
            dst_ref=target.at[1, part],
            send_sem=g_send.at[index],
            recv_sem=g_recv.at[index],
            device_id=(sibling, b),
            device_id_type=MESH_ID,
        )
        r.start()
        share.append((c, r))

    def exchange(which, src_at, dst_at):
        def copy(o):
            peer = lax.rem(s + o, NSEQ)
            return pltpu.make_async_remote_copy(
                src_ref=src_at(peer),
                dst_ref=dst_at(s),
                send_sem=a_send.at[which, o],
                recv_sem=a_recv.at[which, o],
                device_id=(peer, b),
                device_id_type=MESH_ID,
            )

        def begin(o, _):
            copy(o).start()
            return _

        def finish(o, _):
            copy(o).wait()
            return _

        def start():
            lax.fori_loop(1, NSEQ, begin, 0)

        def wait():
            lax.fori_loop(1, NSEQ, finish, 0)

        return start, wait

    def lanes(i, size):
        return pl.ds(pl.multiple_of(i * size, size), size)

    n1 = n1_ref[...]
    for k in range(8):
        left[k] = flip(n1[:, k * BLOCK : (k + 1) * BLOCK])
    share_group(0, left, left_hbm, 0, 8)
    copies[0].wait()

    def qkv_tile(t, _):
        part = lanes(t, 512)
        piece = (mm(n1, wqkv[:, part]) + bias_ref[:, part]).astype(BF)
        which = t // 2
        first = lax.rem(t, 2) * 8
        for k in range(4):
            turned = flip(piece[:, k * BLOCK : (k + 1) * BLOCK])
            for half in range(2):
                slab[first + 2 * k + half, pl.ds(which * HD, HD), :] = turned[
                    half * HD : (half + 1) * HD
                ]
        return _

    lax.fori_loop(0, 6, qkv_tile, 0)
    start, wait = exchange(0, lambda p: slab.at[p], lambda p: qkv_t.at[:, lanes(p, TOK)])
    start()
    qkv_t[:, lanes(s, TOK)] = slab[s]
    wait()

    scale2 = LOG2E / math.sqrt(HD)

    def to_rows(t, _):
        part = lanes(t, TOK)
        rows = pl.ds(pl.multiple_of(t * TOK, TOK), TOK)
        q_row[rows, :] = flip(qkv_t[0:HD, part])
        k_row[rows, :] = flip(qkv_t[HD : 2 * HD, part])
        v_row[rows, :] = flip(qkv_t[2 * HD : 3 * HD, part])
        return _

    lax.fori_loop(0, NSEQ, to_rows, 0)
    tiles = (NSEQ * TOK) // QCH

    def forward_chunk(c, _):
        part = lanes(c, QCH)
        q_part = qkv_t[0:HD, part]
        top = None
        for t in range(tiles):
            tile = slice(t * QCH, (t + 1) * QCH)
            scores = mm(k_row[tile, :], q_part)
            s_scr[tile, :] = scores
            best = jnp.max(scores, 0, keepdims=True)
            top = best if top is None else jnp.maximum(top, best)
        top = top * scale2
        total = jnp.zeros((1, QCH), F32)
        mixed = jnp.zeros((HD, QCH), F32)
        for t in range(tiles):
            tile = slice(t * QCH, (t + 1) * QCH)
            probs = jnp.exp2(s_scr[tile, :] * scale2 - top)
            total = total + jnp.sum(probs, 0, keepdims=True)
            mixed = mixed + mm(qkv_t[2 * HD : 3 * HD, tile], probs.astype(BF))
        mixed = mixed / total
        lse[c] = top + jnp.log2(total)
        out_t32[:, part] = mixed
        out_t[:, part] = mixed.astype(BF)
        return _

    lax.fori_loop(0, tiles, forward_chunk, 0)
    start, wait = exchange(1, lambda p: out_t.at[:, lanes(p, TOK)], lambda p: o_in.at[p])
    start()
    o_in[s] = out_t[:, lanes(s, TOK)]
    copies[1].wait()
    wait()

    parts = []
    for k in range(8):
        pair = jnp.concatenate([o_in[2 * k], o_in[2 * k + 1]], 0)
        left[8 + k] = pair
        parts.append(flip(pair))
    share_group(1, left, left_hbm, 8, 8)
    o_low = jnp.concatenate(parts, 1)
    mid = h0_ref[...] + (mm(o_low, wo[...]) + vec_ref[7:8, :])
    mid_s[...] = mid
    unit, _ = normalise(mid)
    n2 = (unit * vec_ref[3:4, :] + vec_ref[4:5, :]).astype(BF)
    for k in range(8):
        left[16 + k] = flip(n2[:, k * BLOCK : (k + 1) * BLOCK])
    share_group(2, left, left_hbm, 16, 8)
    copies[2].wait()
    copies[3].wait()
    acc[...] = mid + vec_ref[8:9, :]

    def up_tile(t, _):
        part = lanes(t, 512)
        upper = mm(n2, wup[:, part]) + bup_ref[:, part]
        up_s[:, part] = upper
        active = gelu_value(upper).astype(BF)
        for k in range(4):
            left[24 + 4 * t + k] = flip(active[:, k * BLOCK : (k + 1) * BLOCK])
        acc[...] += mm(active, wdown[part, :])
        return _

    lax.fori_loop(0, 8, up_tile, 0)
    share_group(3, left, left_hbm, 24, 32)

    unit_f, rstd_f = normalise(acc[...])
    final = (unit_f * vec_ref[5:6, :] + vec_ref[6:7, :]).astype(BF)
    head = head_ref[...]
    diff = mm(final, head) - goal_ref[...].astype(F32)
    wave[0] = diff[0:64] + diff[64:128]
    partners = (
        sibling,
        s + 2 - 4 * xpos,
        s + 4 - 8 * lax.rem(zpos, 2),
        s + 8 - 16 * (zpos // 2),
    )
    for k, partner in enumerate(partners):
        r = pltpu.make_async_remote_copy(
            src_ref=wave.at[2 * k],
            dst_ref=wave.at[2 * k + 1],
            send_sem=x_send.at[k],
            recv_sem=x_recv.at[k],
            device_id=(partner, b),
            device_id_type=MESH_ID,
        )
        r.start()
        r.wait()
        wave[2 * k + 2] = wave[2 * k] + wave[2 * k + 1]
    total_wave = wave[8]
    one = lax.broadcasted_iota(jnp.int32, (HOUT, HOUT), 0)
    two = lax.broadcasted_iota(jnp.int32, (HOUT, HOUT), 1)
    swap = (one == two + 1 - 2 * (two % 2)).astype(F32)
    other = mmh(total_wave, swap)
    weight = wlat_ref[...]
    square = jnp.sum(weight * diff * diff, keepdims=True)
    cross = jnp.sum(weight[0:64] * total_wave * other, keepdims=True) * (1.0 / NSEQ)
    loss_ref[...] = jnp.broadcast_to(
        square * (1.0 / MSE_COUNT)
        + (SPECTRAL / DFT_COUNT) * (float(KMODES) * square + cross),
        loss_ref.shape,
    )
    other2 = jnp.concatenate([other, other], 0)
    d_pred = weight * (
        (2.0 / MSE_COUNT) * diff + (2.0 * SPECTRAL / DFT_COUNT) * (float(KMODES) * diff + other2)
    )
    d_low = d_pred.astype(BF)
    ghead_ref[...] = mm(final, d_low, TN)
    d_final = mm(d_low, head, NT)
    gvec_ref[5:6, :] = column_sum(d_final * unit_f)
    gvec_ref[6:7, :] = column_sum(d_final)
    d_out = normalise_back(d_final, unit_f, rstd_f, vec_ref[5:6, :])
    d_branch = d_out.astype(BF)
    gvec_ref[8:9, :] = column_sum(d_branch.astype(F32))
    for k in range(8):
        right[64 + k] = d_branch[:, k * BLOCK : (k + 1) * BLOCK]
    share_group(4, right, right_hbm, 64, 8)
    acc[...] = jnp.zeros_like(acc)

    def down_tile(t, _):
        part = lanes(t, 512)
        d_active = mm(d_branch, wdown[part, :], NT)
        d_upper = (d_active * gelu_slope(up_s[:, part])).astype(BF)
        gup_ref[:, part] = column_sum(d_upper.astype(F32))
        for k in range(4):
            right[32 + 4 * t + k] = d_upper[:, k * BLOCK : (k + 1) * BLOCK]
        acc[...] += mm(d_upper, wup[:, part], NT)
        return _

    lax.fori_loop(0, 8, down_tile, 0)
    share_group(5, right, right_hbm, 32, 32)
    d_n2 = acc[...]
    unit, rstd = normalise(mid_s[...])
    gvec_ref[3:4, :] = column_sum(d_n2 * unit)
    gvec_ref[4:5, :] = column_sum(d_n2)
    d_mid = d_out + normalise_back(d_n2, unit, rstd, vec_ref[3:4, :])
    mid_s[...] = d_mid
    d_mid_low = d_mid.astype(BF)
    gvec_ref[7:8, :] = column_sum(d_mid_low.astype(F32))
    for k in range(8):
        right[24 + k] = d_mid_low[:, k * BLOCK : (k + 1) * BLOCK]
    share_group(6, right, right_hbm, 24, 8)
    d_att = mm(d_mid_low, wo[...], NT).astype(BF)
    for k in range(8):
        turned = flip(d_att[:, k * BLOCK : (k + 1) * BLOCK])
        d_slab[2 * k] = turned[0:HD]
        d_slab[2 * k + 1] = turned[HD : 2 * HD]
    start, wait = exchange(2, lambda p: d_slab.at[p], lambda p: do_t.at[:, lanes(p, TOK)])
    start()
    do_t[:, lanes(s, TOK)] = d_slab[s]
    wait()

    def do_rows(t, _):
        rows = pl.ds(pl.multiple_of(t * TOK, TOK), TOK)
        do_row[rows, :] = flip(do_t[:, lanes(t, TOK)])
        return _

    lax.fori_loop(0, NSEQ, do_rows, 0)
    dk_acc[...] = jnp.zeros_like(dk_acc)
    dv_acc[...] = jnp.zeros_like(dv_acc)
    scale = 1.0 / math.sqrt(HD)

    def backward_chunk(c, _):
        part = lanes(c, QCH)
        rows = pl.ds(pl.multiple_of(c * QCH, QCH), QCH)
        q_part = qkv_t[0:HD, part]
        do_part = do_t[:, part]
        delta = jnp.sum(do_part.astype(F32) * out_t32[:, part], 0, keepdims=True)
        base = lse[c]
        q_rows = q_row[rows, :]
        g_rows = do_row[rows, :]
        d_query = jnp.zeros((HD, QCH), F32)
        for t in range(tiles):
            tile = slice(t * QCH, (t + 1) * QCH)
            probs = jnp.exp2(mm(k_row[tile, :], q_part) * scale2 - base)
            d_prob = mm(v_row[tile, :], do_part)
            d_score = (probs * (d_prob - delta)).astype(BF)
            dv_acc[tile, :] += mm(probs.astype(BF), g_rows)
            dk_acc[tile, :] += mm(d_score, q_rows)
            d_query = d_query + mm(qkv_t[HD : 2 * HD, tile], d_score)
        dqkv_t[0:HD, part] = (d_query * scale).astype(BF)
        return _

    lax.fori_loop(0, tiles, backward_chunk, 0)

    def turn_back(t, _):
        part = lanes(t, TOK)
        rows = pl.ds(pl.multiple_of(t * TOK, TOK), TOK)
        dqkv_t[HD : 2 * HD, part] = flip((dk_acc[rows, :] * scale)).astype(BF)
        dqkv_t[2 * HD : 3 * HD, part] = flip(dv_acc[rows, :]).astype(BF)
        return _

    lax.fori_loop(0, NSEQ, turn_back, 0)
    start, wait = exchange(3, lambda p: dqkv_t.at[:, lanes(p, TOK)], lambda p: dqkv_in.at[p])
    start()
    dqkv_in[s] = dqkv_t[:, lanes(s, TOK)]
    wait()

    def place(j, _):
        for which in range(3):
            part = slice(which * HD, (which + 1) * HD)
            pair = jnp.concatenate([dqkv_in[2 * j, part, :], dqkv_in[2 * j + 1, part, :]], 0)
            right[8 * which + j] = flip(pair)
        return _

    lax.fori_loop(0, 8, place, 0)
    share_group(7, right, right_hbm, 0, 24)
    acc[...] = jnp.zeros_like(acc)

    def in_tile(t, _):
        piece = jnp.concatenate([right[4 * t + k] for k in range(4)], 1)
        acc[...] += mm(piece, wqkv[:, lanes(t, 512)], NT)
        return _

    lax.fori_loop(0, 6, in_tile, 0)
    for k in range(8):
        part = slice(k * BLOCK, (k + 1) * BLOCK)
        gvec_ref[9:10, part] = column_sum(right[k].astype(F32))
        gvec_ref[10:11, part] = column_sum(right[16 + k].astype(F32))
    d_n1 = acc[...]
    unit, rstd = normalise(h0_ref[...])
    gvec_ref[1:2, :] = column_sum(d_n1 * unit)
    gvec_ref[2:3, :] = column_sum(d_n1)
    drow_ref[...] = mid_s[...] + normalise_back(d_n1, unit, rstd, vec_ref[1:2, :])
    gvec_ref[0:1, :] = jnp.zeros((1, D), F32)
    gvec_ref[11:16, :] = jnp.zeros((5, D), F32)
    for c, r in share:
        c.wait()
        r.wait()


def run_layer(n1, h0, vec, bias, bup, goals, head_low, wlat, mats):
    vmem = pl.BlockSpec(memory_space=VM)
    anyspace = pl.BlockSpec(memory_space=pl.ANY)
    length = NSEQ * TOK
    return pl.pallas_call(
        layer_kernel,
        name="layer",
        out_shape=(
            jax.ShapeDtypeStruct((2, N_LEFT, BLOCK, TOK), BF),
            jax.ShapeDtypeStruct((2, N_RIGHT, TOK, BLOCK), BF),
            jax.ShapeDtypeStruct((TOK, D), F32),
            jax.ShapeDtypeStruct((16, D), F32),
            jax.ShapeDtypeStruct((1, FF), F32),
            jax.ShapeDtypeStruct((D, HOUT), F32),
            jax.ShapeDtypeStruct((8, 128), F32),
        ),
        in_specs=[vmem] * 8 + [anyspace] * 4,
        out_specs=(anyspace, anyspace) + (vmem,) * 5,
        scratch_shapes=[
            VM((D, 3 * D), BF),
            VM((D, D), BF),
            VM((D, FF), BF),
            VM((FF, D), BF),
            VM((N_LEFT, BLOCK, TOK), BF),
            VM((N_RIGHT, TOK, BLOCK), BF),
            VM((HEADS, 3 * HD, TOK), BF),
            VM((3 * HD, length), BF),
            VM((HD, length), BF),
            VM((HD, length), F32),
            VM((length // QCH, 1, QCH), F32),
            VM((HEADS, HD, TOK), BF),
            VM((HEADS, HD, TOK), BF),
            VM((HD, length), BF),
            VM((3 * HD, length), BF),
            VM((HEADS, 3 * HD, TOK), BF),
            VM((length, HD), BF),
            VM((length, HD), BF),
            VM((length, HD), BF),
            VM((length, HD), BF),
            VM((length, QCH), F32),
            VM((length, HD), F32),
            VM((length, HD), F32),
            VM((TOK, D), F32),
            VM((TOK, FF), F32),
            VM((TOK, D), F32),
            VM((9, 64, HOUT), F32),
            pltpu.SemaphoreType.DMA((4,)),
            pltpu.SemaphoreType.DMA((4, NSEQ)),
            pltpu.SemaphoreType.DMA((4, NSEQ)),
            pltpu.SemaphoreType.DMA((4,)),
            pltpu.SemaphoreType.DMA((4,)),
            pltpu.SemaphoreType.DMA((8,)),
            pltpu.SemaphoreType.DMA((8,)),
            pltpu.SemaphoreType.DMA((8,)),
        ],
        compiler_params=pltpu.CompilerParams(
            collective_id=1, has_side_effects=True, vmem_limit_bytes=60 * 1024 * 1024
        ),
    )(n1, h0, vec, bias, bup, goals, head_low, wlat, *mats)


def token_maps():
    row = lax.broadcasted_iota(jnp.int32, (VARS, HOUT), 0)
    col = lax.broadcasted_iota(jnp.int32, (VARS, HOUT), 1)
    return (col // 4 == row).astype(F32)


def embed_kernel(pix_ref, ids_ref, lead_ref, emb_ref, vec_ref, h0_ref, n1_ref, xp_ref, a_ref):
    slot = lax.broadcasted_iota(jnp.int32, (HOUT, HOUT), 1)
    place = (ids_ref[...] == slot).astype(BF)
    pix = mm(pix_ref[...], place)
    xp_ref[...] = pix
    tok = emb_ref[0:HOUT, :]
    emb = emb_ref[HOUT : HOUT + VARS, :]
    query = vec_ref[0:1, :]
    spread = token_maps()
    tok_q = jnp.sum(tok * query, -1, keepdims=True)
    emb_q = mmh(query, emb, NT)
    back = lax.broadcasted_iota(jnp.int32, (HOUT, VARS), 0) // 4
    var = lax.broadcasted_iota(jnp.int32, (HOUT, VARS), 1)
    reduce = jnp.where(back == var, tok_q, 0.0)
    logits = (mmh(pix, reduce) + emb_q) * (1.0 / math.sqrt(D))
    logits = logits - jnp.max(logits, -1, keepdims=True)
    weights = jnp.exp(logits)
    weights = weights / jnp.sum(weights, -1, keepdims=True)
    a_ref[...] = weights
    wide = mmh(weights, spread) * pix
    lead = emb_ref[pl.ds(HOUT + VARS + lead_ref[0], 1), :]
    h0 = mmh(wide, tok) + mmh(weights, emb) + lead
    h0_ref[...] = h0
    unit, _ = normalise(h0)
    n1_ref[...] = (unit * vec_ref[1:2, :] + vec_ref[2:3, :]).astype(BF)


def run_embed(pix, ids, lead, embed, vec):
    vmem = pl.BlockSpec(memory_space=VM)
    smem = pl.BlockSpec(memory_space=pltpu.SMEM)
    return pl.pallas_call(
        embed_kernel,
        name="embed_fwd",
        out_shape=(
            jax.ShapeDtypeStruct((TOK, D), F32),
            jax.ShapeDtypeStruct((TOK, D), BF),
            jax.ShapeDtypeStruct((TOK, HOUT), F32),
            jax.ShapeDtypeStruct((TOK, VARS), F32),
        ),
        in_specs=[vmem, vmem, smem, vmem, vmem],
        out_specs=(vmem,) * 4,
    )(pix, ids, lead, embed, vec)


def embed_back_kernel(drow_ref, xp_ref, a_ref, lead_ref, emb_ref, vec_ref, gemb_ref, gq_ref):
    d_rows = drow_ref[...]
    pix = xp_ref[...]
    weights = a_ref[...]
    tok = emb_ref[0:HOUT, :]
    emb = emb_ref[HOUT : HOUT + VARS, :]
    query = vec_ref[0:1, :]
    spread = token_maps()
    d_wide = mmh(d_rows, tok, NT)
    d_weight = mmh(pix * d_wide, spread, NT) + mmh(d_rows, emb, NT)
    d_logit = (
        weights
        * (d_weight - jnp.sum(weights * d_weight, -1, keepdims=True))
        * (1.0 / math.sqrt(D))
    )
    wide = mmh(weights, spread) * pix
    d_wide_l = mmh(d_logit, spread) * pix
    ones = jnp.ones((TOK, 1), F32)
    d_tok_q = mmh(d_wide_l, ones, TN)
    d_emb_q = mmh(d_logit, ones, TN)
    gemb_ref[0:HOUT, :] = mmh(wide, d_rows, TN) + d_tok_q * query
    gemb_ref[HOUT : HOUT + VARS, :] = mmh(weights, d_rows, TN) + d_emb_q * query
    row = lax.broadcasted_iota(jnp.int32, (LEADS, D), 0)
    gemb_ref[HOUT + VARS :, :] = jnp.where(row == lead_ref[0], column_sum(d_rows), 0.0)
    gq_ref[...] = column_sum(d_tok_q * tok) + column_sum(d_emb_q * emb)


def run_embed_back(d_rows, pix, weights, lead, embed, vec):
    vmem = pl.BlockSpec(memory_space=VM)
    smem = pl.BlockSpec(memory_space=pltpu.SMEM)
    return pl.pallas_call(
        embed_back_kernel,
        name="embed_bwd",
        out_shape=(
            jax.ShapeDtypeStruct((EROWS, D), F32),
            jax.ShapeDtypeStruct((1, D), F32),
        ),
        in_specs=[vmem, vmem, vmem, smem, vmem, vmem],
        out_specs=(vmem,) * 2,
    )(d_rows, pix, weights, lead, embed, vec)


def fast_shards(
    inputs,
    targets,
    var_ids,
    lead_ids,
    block_order,
    blocks,
    block_momentum,
    left_stats,
    right_stats,
    left_roots,
    right_roots,
    embed_params,
    embed_first,
    embed_second,
    vectors,
    vector_first,
    vector_second,
    head_weight,
    head_first,
    head_second,
):
    stack = lax.all_gather(blocks.astype(BF), ("seq", "batch"), axis=0, tiled=True)
    natural = jnp.zeros_like(stack).at[block_order].set(stack)
    mats = split_matrices(natural)
    ids = (4 * var_ids[0][:, None] + jnp.arange(4, dtype=jnp.int32)[None]).reshape(HOUT, 1)
    h0, n1, pix, weights = run_embed(inputs[0], ids, lead_ids, embed_params, vectors)
    bias = jnp.concatenate([vectors[9], jnp.zeros_like(vectors[9]), vectors[10]])[None]
    bup = vectors[11:].reshape(1, FF)
    nlat = 2 * LAT_P
    lat = ((jnp.arange(nlat, dtype=jnp.float32) + 0.5) / nlat - 0.5) * math.pi
    wlat = jnp.cos(lat)
    wlat = wlat / jnp.mean(wlat)
    wlat = jnp.broadcast_to(
        wlat.reshape(1, LAT_P, 1, 2, 1), (TOK // LAT_P, LAT_P, VARS, 2, 2)
    ).reshape(TOK, HOUT)
    left, right, d_rows, g_vec, g_up, g_head, loss = run_layer(
        n1, h0, vectors, bias, bup, targets[0], head_weight.astype(BF), wlat, mats
    )
    g_embed, g_query = run_embed_back(d_rows, pix, weights, lead_ids, embed_params, vectors)
    g_vectors = jnp.concatenate([g_query, g_vec[1:11], g_up.reshape(-1, D)])
    pairs = ((0, 8, 0, 24), (8, 16, 24, 32), (16, 24, 32, 64), (24, 56, 64, 72))
    grads = jnp.concatenate(
        [
            jnp.einsum(
                "rit,ctj->rcij", left[0, a:e], right[0, f:g], preferred_element_type=F32
            ).reshape(-1, BLOCK, BLOCK)
            for a, e, f, g in pairs
        ]
    )
    owned = lax.psum_scatter(
        grads[block_order], ("seq", "batch"), scatter_dimension=0, tiled=True
    )
    g_embed, g_vectors, g_head, loss_total = lax.psum(
        (g_embed, g_vectors, g_head, loss[0, 0]), ("seq", "batch")
    )
    rest_squares = (
        jnp.sum(g_embed * g_embed) + jnp.sum(g_vectors * g_vectors) + jnp.sum(g_head * g_head)
    )
    grad_norm = jnp.sqrt(lax.psum(jnp.sum(owned * owned), ("seq", "batch")) + rest_squares)
    clip = CLIP_NORM / jnp.maximum(grad_norm, CLIP_NORM)
    owned = owned * clip
    new_momentum = BETA_ONE * block_momentum + (1.0 - BETA_ONE) * owned
    new_left = BETA_TWO * left_stats + (1.0 - BETA_TWO) * jnp.einsum(
        "bij,bkj->bik", owned, owned, precision=HIGH
    )
    new_right = BETA_TWO * right_stats + (1.0 - BETA_TWO) * jnp.einsum(
        "bji,bjk->bik", owned, owned, precision=HIGH
    )
    direction = jnp.einsum(
        "bij,bjk->bik",
        jnp.einsum("bij,bjk->bik", left_roots, new_momentum, precision=HIGH),
        right_roots,
        precision=HIGH,
    )
    new_blocks = blocks - SHAMPOO_RATE * (direction + DECAY * blocks)
    e_one, e_two, e_new = adam(embed_params, embed_first, embed_second, g_embed * clip, EMBED_RATE)
    v_one, v_two, v_new = adam(vectors, vector_first, vector_second, g_vectors * clip, VECTOR_RATE)
    h_one, h_two, h_new = adam(head_weight, head_first, head_second, g_head * clip, HEAD_RATE)
    return (
        loss_total,
        grad_norm,
        new_blocks,
        new_momentum,
        new_left,
        new_right,
        e_one,
        e_two,
        e_new,
        v_one,
        v_two,
        v_new,
        h_one,
        h_two,
        h_new,
    )


def solution(mesh):
    in_specs = (
        P("batch", "seq", None),
        P("batch", "seq", None),
        P("batch", None),
        P("batch"),
        P(),
        P(("seq", "batch"), None, None),
        P(("seq", "batch"), None, None),
        P(("seq", "batch"), None, None),
        P(("seq", "batch"), None, None),
        P(("seq", "batch"), None, None),
        P(("seq", "batch"), None, None),
        P(),
        P(),
        P(),
        P(),
        P(),
        P(),
        P(),
        P(),
        P(),
    )
    out_specs = (
        P(),
        P(),
        P(("seq", "batch"), None, None),
        P(("seq", "batch"), None, None),
        P(("seq", "batch"), None, None),
        P(("seq", "batch"), None, None),
        P(),
        P(),
        P(),
        P(),
        P(),
        P(),
        P(),
        P(),
        P(),
    )
    sizes = dict(mesh.shape)
    fast = sizes == {"seq": NSEQ, "batch": 2}
    return jax.shard_map(fast_shards if fast else shards, mesh=mesh, in_specs=in_specs, out_specs=out_specs, check_vma=False)
```

```python
import math

import jax
import jax.numpy as jnp
from jax import lax
from jax.experimental import pallas as pl
from jax.experimental.pallas import tpu as pltpu
from jax.sharding import PartitionSpec as P

D = 1024
HEADS = 16
HD = 64
FF = 4096
VARS = 48
LEADS = 32
LAT_P = 64
KMODES = 32
STEP = 10


HIGH = lax.Precision.HIGHEST
EPS = 1e-05
CLIP_NORM = 0.001
SPECTRAL = 0.5
BETA_ONE = 0.9
BETA_TWO = 0.95
SHAMPOO_RATE = 0.1
DECAY = 0.01
ADAM_EPS = 1e-08
EMBED_RATE = 0.2
VECTOR_RATE = 0.5
HEAD_RATE = 0.05
FLOOR = -1e30
EROWS = VARS * 5 + LEADS
HOUT = VARS * 4
MSE_COUNT = 786432.0
DFT_COUNT = 25165824.0


def layer_norm(rows, gain, shift):
    mean = jnp.mean(rows, -1, keepdims=True)
    centred = rows - mean
    return centred * lax.rsqrt(jnp.mean(centred * centred, -1, keepdims=True) + EPS) * gain + shift


def to_blocks(matrix, size):
    rows, cols = matrix.shape
    return (
        matrix.reshape(rows // size, size, cols // size, size)
        .transpose(0, 2, 1, 3)
        .reshape(-1, size, size)
    )


def from_blocks(stack, rows, cols):
    size = stack.shape[-1]
    return (
        stack.reshape(rows // size, cols // size, size, size)
        .transpose(0, 2, 1, 3)
        .reshape(rows, cols)
    )


def split_matrices(stack):
    size = stack.shape[-1]
    found = []
    begin = 0
    for rows, cols in ((D, 3 * D), (D, D), (D, FF), (FF, D)):
        count = rows * cols // (size * size)
        found.append(from_blocks(stack[begin : begin + count], rows, cols))
        begin += count
    return found


def embed_patches(pixels, tok_sel, emb_sel, query, lead_rows):
    tokens = jnp.einsum("spvc,svcd->spvd", pixels, tok_sel, precision=HIGH) + emb_sel[:, None]
    logits = jnp.einsum("spvd,d->spv", tokens, query, precision=HIGH) * (1.0 / math.sqrt(D))
    weights = jax.nn.softmax(logits, -1)
    return jnp.einsum("spv,spvd->spd", weights, tokens, precision=HIGH) + lead_rows[:, None]


def split_heads(rows):
    return rows.reshape(rows.shape[0], rows.shape[1], HEADS, HD)


def attention_forward(query, keys, values):
    seqs, length, _ = query.shape
    scale = 1.0 / math.sqrt(HD)
    heads_q = split_heads(query)
    start_state = (
        jnp.zeros((seqs, HEADS, length, HD), jnp.float32),
        jnp.full((seqs, HEADS, length), FLOOR, jnp.float32),
        jnp.zeros((seqs, HEADS, length), jnp.float32),
    )
    key_rows = lax.all_gather(keys, "seq", axis=1, tiled=True)
    value_rows = lax.all_gather(values, "seq", axis=1, tiled=True)
    count = key_rows.shape[1] // length
    key_blocks = key_rows.reshape(seqs, count, length, HEADS, HD)
    value_blocks = value_rows.reshape(seqs, count, length, HEADS, HD)

    def visit(inner, index):
        acc, top, total = inner
        scores = (
            jnp.einsum(
                "sphd,snhd->shpn", heads_q, key_blocks[:, index], preferred_element_type=jnp.float32
            )
            * scale
        )
        new_top = jnp.maximum(top, jnp.max(scores, -1))
        fade = jnp.exp(top - new_top)
        probs = jnp.exp(scores - new_top[..., None])
        total = total * fade + jnp.sum(probs, -1)
        acc = acc * fade[..., None] + jnp.einsum(
            "shpn,snhd->shpd",
            probs.astype(jnp.bfloat16),
            value_blocks[:, index],
            preferred_element_type=jnp.float32,
        )
        return ((acc, new_top, total), None)

    inner, _ = lax.scan(visit, start_state, jnp.arange(count))
    acc, top, total = inner
    attended = (acc / total[..., None]).transpose(0, 2, 1, 3).reshape(seqs, length, HEADS * HD)
    return (attended, (top + jnp.log(total)).transpose(0, 2, 1))


def attention_backward(query, keys, values, attended, lse, d_att):
    seqs, length, _ = query.shape
    scale = 1.0 / math.sqrt(HD)
    heads_q = split_heads(query)
    heads_k = split_heads(keys)
    heads_v = split_heads(values)
    heads_d = split_heads(d_att)
    delta = jnp.sum(heads_d.astype(jnp.float32) * split_heads(attended), -1)
    lse_h = lse.transpose(0, 2, 1)
    delta_h = delta.transpose(0, 2, 1)
    key_rows = lax.all_gather(keys, "seq", axis=1, tiled=True)
    value_rows = lax.all_gather(values, "seq", axis=1, tiled=True)
    count = key_rows.shape[1] // length
    key_blocks = key_rows.reshape(seqs, count, length, HEADS, HD)
    value_blocks = value_rows.reshape(seqs, count, length, HEADS, HD)

    def visit(inner, index):
        k_part = key_blocks[:, index]
        scores = (
            jnp.einsum("sphd,snhd->shpn", heads_q, k_part, preferred_element_type=jnp.float32)
            * scale
        )
        probs = jnp.exp(scores - lse_h[..., None])
        d_prob = jnp.einsum(
            "sphd,snhd->shpn", heads_d, value_blocks[:, index], preferred_element_type=jnp.float32
        )
        d_score = (probs * (d_prob - delta_h[..., None])).astype(jnp.bfloat16)
        return (
            inner
            + jnp.einsum("shpn,snhd->sphd", d_score, k_part, preferred_element_type=jnp.float32)
            * scale,
            None,
        )

    inner, _ = lax.scan(visit, jnp.zeros((seqs, length, HEADS, HD), jnp.float32), jnp.arange(count))
    d_query = inner
    all_lse, all_delta = (
        lax.all_gather(lse, "seq", axis=1, tiled=True),
        lax.all_gather(delta, "seq", axis=1, tiled=True),
    )
    empty = jnp.zeros((seqs, length, HEADS, HD), jnp.float32)
    q_rows = lax.all_gather(query, "seq", axis=1, tiled=True)
    g_rows = lax.all_gather(d_att, "seq", axis=1, tiled=True)
    count = q_rows.shape[1] // length
    q_blocks = q_rows.reshape(seqs, count, length, HEADS, HD)
    g_blocks = g_rows.reshape(seqs, count, length, HEADS, HD)
    lse_rows = all_lse.reshape(seqs, count, length, HEADS)
    delta_rows = all_delta.reshape(seqs, count, length, HEADS)

    def visit(inner, index):
        d_key, d_value = inner
        q_part = q_blocks[:, index]
        g_part = g_blocks[:, index]
        scores = (
            jnp.einsum("snhd,sphd->shnp", q_part, heads_k, preferred_element_type=jnp.float32)
            * scale
        )
        probs = jnp.exp(scores - lse_rows[:, index].transpose(0, 2, 1)[..., None])
        d_value = d_value + jnp.einsum(
            "shnp,snhd->sphd",
            probs.astype(jnp.bfloat16),
            g_part,
            preferred_element_type=jnp.float32,
        )
        d_prob = jnp.einsum("snhd,sphd->shnp", g_part, heads_v, preferred_element_type=jnp.float32)
        d_score = (probs * (d_prob - delta_rows[:, index].transpose(0, 2, 1)[..., None])).astype(
            jnp.bfloat16
        )
        d_key = (
            d_key
            + jnp.einsum("shnp,snhd->sphd", d_score, q_part, preferred_element_type=jnp.float32)
            * scale
        )
        return ((d_key, d_value), None)

    inner, _ = lax.scan(visit, (empty, empty), jnp.arange(count))
    d_key, d_value = inner
    return (d_query, d_key, d_value)


def feed_inner(normed_two, w_up, vectors):
    upper = jnp.dot(normed_two, w_up, preferred_element_type=jnp.float32) + vectors[11:].reshape(-1)
    return (upper, jax.nn.gelu(upper).astype(jnp.bfloat16))


def layer_forward(rows, seqs, mats, vectors):
    w_qkv, w_out, w_up, w_down = mats
    normed = layer_norm(rows, vectors[1], vectors[2]).astype(jnp.bfloat16)
    bias = jnp.concatenate([vectors[9], jnp.zeros_like(vectors[9]), vectors[10]])
    qkv = (jnp.dot(normed, w_qkv, preferred_element_type=jnp.float32) + bias).astype(jnp.bfloat16)
    query = qkv[:, :D].reshape(seqs, -1, D)
    keys = qkv[:, D : 2 * D].reshape(seqs, -1, D)
    values = qkv[:, 2 * D :].reshape(seqs, -1, D)
    attended, lse = attention_forward(query, keys, values)
    att_low = attended.reshape(-1, D).astype(jnp.bfloat16)
    mid = rows + jnp.dot(att_low, w_out, preferred_element_type=jnp.float32) + vectors[7]
    normed_two = layer_norm(mid, vectors[3], vectors[4]).astype(jnp.bfloat16)
    upper, active = feed_inner(normed_two, w_up, vectors)
    out = mid + jnp.dot(active, w_down, preferred_element_type=jnp.float32) + vectors[8]
    saved = (upper, active)
    return (out, (rows, normed, query, keys, values, attended, lse, mid, normed_two, saved))


def layer_backward(d_out, kept, mats, vectors):
    rows, normed, query, keys, values, attended, lse, mid, normed_two, saved = kept
    w_qkv, w_out, w_up, w_down = mats
    upper, active = saved
    d_branch = d_out.astype(jnp.bfloat16)
    g_down = jnp.einsum("rf,rd->fd", active, d_branch, preferred_element_type=jnp.float32)
    d_active = jnp.einsum("rd,fd->rf", d_branch, w_down, preferred_element_type=jnp.float32)
    d_upper = jax.vjp(jax.nn.gelu, upper)[1](d_active)[0].astype(jnp.bfloat16)
    g_up = jnp.einsum("rd,rf->df", normed_two, d_upper, preferred_element_type=jnp.float32)
    d_normed_two = jnp.einsum("rf,df->rd", d_upper, w_up, preferred_element_type=jnp.float32)
    d_mid_norm, g_gain_two, g_shift_two = jax.vjp(layer_norm, mid, vectors[3], vectors[4])[1](
        d_normed_two
    )
    d_mid = d_out + d_mid_norm
    d_mid_low = d_mid.astype(jnp.bfloat16)
    att_low = attended.reshape(-1, D).astype(jnp.bfloat16)
    g_out = jnp.einsum("ra,rd->ad", att_low, d_mid_low, preferred_element_type=jnp.float32)
    d_att = jnp.einsum("rd,ad->ra", d_mid_low, w_out, preferred_element_type=jnp.float32).astype(
        jnp.bfloat16
    )
    seqs = query.shape[0]
    d_query, d_key, d_value = attention_backward(
        query, keys, values, attended, lse, d_att.reshape(seqs, -1, D)
    )
    d_qkv = jnp.concatenate(
        [d_query.reshape(-1, D), d_key.reshape(-1, D), d_value.reshape(-1, D)], 1
    ).astype(jnp.bfloat16)
    g_qkv = jnp.einsum("rd,re->de", normed, d_qkv, preferred_element_type=jnp.float32)
    d_normed = jnp.einsum("re,de->rd", d_qkv, w_qkv, preferred_element_type=jnp.float32)
    d_rows_norm, g_gain_one, g_shift_one = jax.vjp(layer_norm, rows, vectors[1], vectors[2])[1](
        d_normed
    )
    qkv_sums = jnp.sum(d_qkv.astype(jnp.float32), 0)
    small = (
        g_gain_one,
        g_shift_one,
        g_gain_two,
        g_shift_two,
        jnp.sum(d_mid_low.astype(jnp.float32), 0),
        jnp.sum(d_branch.astype(jnp.float32), 0),
        qkv_sums[:D],
        qkv_sums[2 * D :],
        jnp.sum(d_upper.astype(jnp.float32), 0),
    )
    return (d_mid + d_rows_norm, (g_qkv, g_out, g_up, g_down), small)


def loss_terms(pred, targets, seqs, length):
    strips = lax.axis_size("seq")
    cols = length // LAT_P
    nlat = 2 * LAT_P
    nlon = 2 * cols * strips
    all_seqs = seqs * lax.axis_size("batch")
    diff = pred.reshape(seqs, length, -1) - targets.astype(jnp.float32)
    grid = (
        diff.reshape(seqs, cols, LAT_P, VARS, 2, 2)
        .transpose(0, 3, 2, 4, 1, 5)
        .reshape(seqs, VARS, nlat, 2 * cols)
    )
    lat = ((jnp.arange(nlat, dtype=jnp.float32) + 0.5) / nlat - 0.5) * math.pi
    weight = jnp.cos(lat)
    weight = (weight / jnp.mean(weight))[None, None, :, None]
    column = lax.axis_index("seq") * (2 * cols) + jnp.arange(2 * cols, dtype=jnp.int32)
    modes = jnp.arange(KMODES, dtype=jnp.int32)
    angle = (column[:, None] * modes[None] % nlon).astype(jnp.float32) * (2.0 * math.pi / nlon)
    cosine = jnp.cos(angle)
    sine = jnp.sin(angle)
    part_c = jnp.einsum("svrc,ck->svrk", grid, cosine, precision=HIGH)
    part_s = jnp.einsum("svrc,ck->svrk", grid, sine, precision=HIGH)
    full_c, full_s = lax.psum((part_c, part_s), "seq")
    mse_count = all_seqs * VARS * nlat * nlon
    dft_count = nlon * all_seqs * VARS * nlat * KMODES
    mse = jnp.sum(weight * grid * grid) / mse_count
    spectral = SPECTRAL * jnp.sum(weight * (full_c * full_c + full_s * full_s)) / dft_count
    first = (lax.axis_index("seq") == 0).astype(jnp.float32)
    back_wave = jnp.einsum("svrk,ck->svrc", full_c, cosine, precision=HIGH) + jnp.einsum(
        "svrk,ck->svrc", full_s, sine, precision=HIGH
    )
    d_grid = 2.0 * weight * grid / mse_count + 2.0 * SPECTRAL / dft_count * weight * back_wave
    d_pred = (
        d_grid.reshape(seqs, VARS, LAT_P, 2, cols, 2)
        .transpose(0, 4, 2, 1, 3, 5)
        .reshape(seqs * length, VARS * 4)
    )
    return (d_pred, mse + first * spectral)


def adam(value, first, second, grad, rate):
    first = BETA_ONE * first + (1.0 - BETA_ONE) * grad
    second = BETA_TWO * second + (1.0 - BETA_TWO) * grad * grad
    step = first / (1.0 - BETA_ONE**STEP) / (jnp.sqrt(second / (1.0 - BETA_TWO**STEP)) + ADAM_EPS)
    return (first, second, value - rate * (step + DECAY * value))


def shards(
    inputs,
    targets,
    var_ids,
    lead_ids,
    block_order,
    blocks,
    block_momentum,
    left_stats,
    right_stats,
    left_roots,
    right_roots,
    embed_params,
    embed_first,
    embed_second,
    vectors,
    vector_first,
    vector_second,
    head_weight,
    head_first,
    head_second,
):
    seqs, length, _ = inputs.shape
    size = blocks.shape[-1]
    low_blocks = blocks.astype(jnp.bfloat16)
    stack = lax.all_gather(low_blocks, ("seq", "batch"), axis=0, tiled=True)
    natural = jnp.zeros_like(stack).at[block_order].set(stack)
    mats = split_matrices(natural)
    head_low = head_weight.astype(jnp.bfloat16)
    pick = (var_ids[..., None] == jnp.arange(VARS, dtype=jnp.int32)[None, None]).astype(jnp.float32)
    lead_pick = (lead_ids[:, None] == jnp.arange(LEADS, dtype=jnp.int32)[None]).astype(jnp.float32)
    tok_sel = jnp.einsum(
        "svw,wcd->svcd", pick, embed_params[: VARS * 4].reshape(VARS, 4, D), precision=HIGH
    )
    emb_sel = jnp.einsum("svw,wd->svd", pick, embed_params[VARS * 4 : VARS * 5], precision=HIGH)
    lead_rows = jnp.dot(lead_pick, embed_params[VARS * 5 :], precision=HIGH)
    pixels = inputs.astype(jnp.float32).reshape(seqs, length, VARS, 4)

    def embed_local(tok_part, emb_part, query, lead_part):
        return embed_patches(pixels, tok_part, emb_part, query, lead_part)

    stream, embed_back = jax.vjp(embed_local, tok_sel, emb_sel, vectors[0], lead_rows)
    out, kept = layer_forward(stream.reshape(-1, D), seqs, mats, vectors)
    final_rows, final_back = jax.vjp(layer_norm, out, vectors[5], vectors[6])
    final = final_rows.astype(jnp.bfloat16)
    pred = jnp.dot(final, head_low, preferred_element_type=jnp.float32)
    d_pred, loss_part = loss_terms(pred, targets, seqs, length)
    d_low = d_pred.astype(jnp.bfloat16)
    g_head = jnp.einsum("rd,ro->do", final, d_low, preferred_element_type=jnp.float32)
    d_final = jnp.einsum("ro,do->rd", d_low, head_low, preferred_element_type=jnp.float32)
    d_out, g_gain_final, g_shift_final = final_back(d_final)
    d_rows, matrix_grads, small = layer_backward(d_out, kept, mats, vectors)
    d_tok, d_emb, d_query, d_lead = embed_back(d_rows.reshape(seqs, length, D))
    g_embed = jnp.concatenate(
        [
            jnp.einsum("svw,svcd->wcd", pick, d_tok, precision=HIGH).reshape(VARS * 4, D),
            jnp.einsum("svw,svd->wd", pick, d_emb, precision=HIGH),
            jnp.einsum("sl,sd->ld", lead_pick, d_lead, precision=HIGH),
        ]
    )
    g_gain_one, g_shift_one, g_gain_two, g_shift_two, b_out, b_down, b_query, b_value, b_up = small
    g_vectors = jnp.concatenate(
        [
            jnp.stack(
                [
                    d_query,
                    g_gain_one,
                    g_shift_one,
                    g_gain_two,
                    g_shift_two,
                    g_gain_final,
                    g_shift_final,
                    b_out,
                    b_down,
                    b_query,
                    b_value,
                ]
            ),
            b_up.reshape(-1, D),
        ]
    )
    slot_grads = jnp.concatenate([to_blocks(grad, size) for grad in matrix_grads])[block_order]
    owned = lax.psum_scatter(slot_grads, ("seq", "batch"), scatter_dimension=0, tiled=True)
    g_embed, g_vectors, g_head, loss_total = lax.psum(
        (g_embed, g_vectors, g_head, loss_part), ("seq", "batch")
    )
    rest_squares = (
        jnp.sum(g_embed * g_embed) + jnp.sum(g_vectors * g_vectors) + jnp.sum(g_head * g_head)
    )
    grad_norm = jnp.sqrt(lax.psum(jnp.sum(owned * owned), ("seq", "batch")) + rest_squares)
    clip = CLIP_NORM / jnp.maximum(grad_norm, CLIP_NORM)
    owned = owned * clip
    new_momentum = BETA_ONE * block_momentum + (1.0 - BETA_ONE) * owned
    new_left = BETA_TWO * left_stats + (1.0 - BETA_TWO) * jnp.einsum(
        "bij,bkj->bik", owned, owned, precision=HIGH
    )
    new_right = BETA_TWO * right_stats + (1.0 - BETA_TWO) * jnp.einsum(
        "bji,bjk->bik", owned, owned, precision=HIGH
    )
    direction = jnp.einsum(
        "bij,bjk->bik",
        jnp.einsum("bij,bjk->bik", left_roots, new_momentum, precision=HIGH),
        right_roots,
        precision=HIGH,
    )
    new_blocks = blocks - SHAMPOO_RATE * (direction + DECAY * blocks)
    e_one, e_two, e_new = adam(embed_params, embed_first, embed_second, g_embed * clip, EMBED_RATE)
    v_one, v_two, v_new = adam(vectors, vector_first, vector_second, g_vectors * clip, VECTOR_RATE)
    h_one, h_two, h_new = adam(head_weight, head_first, head_second, g_head * clip, HEAD_RATE)
    return (
        loss_total,
        grad_norm,
        new_blocks,
        new_momentum,
        new_left,
        new_right,
        e_one,
        e_two,
        e_new,
        v_one,
        v_two,
        v_new,
        h_one,
        h_two,
        h_new,
    )


SHARE = 24
PIECE = 6
MAIN = ("zxy", "zyx", "xzy", "yzx")
SMALL = ("xyz", "yxz")
TAIL = ("xzy", "yzx")
GATHER_ORDER = (
    (0, 0, 0, 3), (3, 0, 0, 3), (1, 0, 0, 3), (2, 0, 0, 3), (0, 1, 0, 3), (1, 0, 0, 2), (0, 0, 0, 2), (1, 0, 0, 1),
    (1, 0, 1, 3), (0, 0, 0, 1), (3, 0, 0, 2), (0, 0, 1, 3), (3, 0, 1, 3), (2, 1, 0, 3), (1, 1, 0, 3), (2, 0, 0, 2),
    (1, 1, 1, 3), (0, 0, 0, 0), (1, 1, 0, 2), (2, 0, 1, 3), (1, 0, 1, 2), (2, 1, 0, 2), (3, 0, 1, 2), (0, 1, 0, 2),
    (2, 0, 0, 1), (3, 1, 0, 3), (2, 0, 0, 0), (0, 0, 1, 2), (0, 1, 1, 3), (2, 0, 1, 2), (3, 0, 0, 1), (3, 1, 1, 3),
    (0, 1, 0, 1), (2, 1, 1, 3), (3, 1, 0, 2), (1, 1, 0, 1), (2, 1, 0, 0), (1, 0, 0, 0), (3, 0, 0, 0), (1, 0, 1, 1),
    (0, 1, 1, 2), (0, 0, 1, 1), (3, 0, 1, 0), (2, 1, 1, 2), (2, 1, 0, 1), (0, 1, 1, 1), (3, 1, 0, 1), (2, 0, 1, 1),
    (0, 1, 0, 0), (3, 0, 1, 1), (1, 1, 1, 2), (1, 0, 1, 0), (3, 1, 0, 0), (1, 1, 0, 0), (0, 0, 1, 0), (3, 1, 1, 1),
    (3, 1, 1, 0), (1, 1, 1, 0), (2, 1, 1, 1), (2, 1, 1, 0), (1, 1, 1, 1), (3, 1, 1, 2), (2, 0, 1, 0), (0, 1, 1, 0),
)
REDUCE_ORDER = (
    (5, 0, 1, 0), (4, 0, 1, 0), (3, 1, 1, 1), (2, 1, 1, 0), (4, 1, 0, 0), (4, 0, 0, 0), (5, 0, 0, 0), (3, 1, 1, 0),
    (3, 1, 0, 0), (2, 1, 1, 1), (5, 1, 1, 0), (4, 1, 0, 1), (1, 1, 1, 1), (4, 1, 1, 0), (4, 1, 1, 1), (4, 0, 1, 2),
    (5, 1, 0, 1), (5, 1, 1, 2), (2, 0, 1, 0), (0, 1, 1, 0), (0, 0, 1, 0), (4, 0, 0, 2), (1, 1, 1, 0), (1, 1, 1, 3),
    (5, 0, 1, 2), (5, 1, 0, 0), (5, 1, 1, 1), (0, 0, 1, 1), (1, 1, 0, 1), (5, 1, 0, 2), (2, 1, 0, 0), (2, 0, 1, 2),
    (2, 1, 1, 2), (1, 1, 0, 2), (5, 1, 1, 3), (5, 0, 0, 1), (5, 0, 1, 1), (3, 0, 1, 0), (2, 0, 1, 1), (4, 0, 0, 1),
    (5, 0, 0, 2), (4, 1, 0, 2), (3, 1, 0, 1), (3, 1, 0, 2), (3, 1, 0, 3), (0, 1, 1, 2), (4, 1, 1, 2), (0, 1, 1, 1),
    (2, 1, 0, 1), (2, 0, 1, 3), (3, 1, 1, 2), (3, 0, 0, 0), (0, 1, 0, 0), (2, 0, 0, 0), (4, 0, 1, 1), (0, 1, 1, 3),
    (3, 0, 1, 1), (2, 1, 0, 2), (2, 0, 0, 1), (1, 1, 1, 2), (1, 0, 1, 1), (3, 0, 0, 1), (1, 0, 1, 0), (2, 1, 1, 3),
    (1, 1, 0, 0), (4, 0, 1, 3), (3, 0, 1, 2), (4, 1, 1, 3), (3, 1, 1, 3), (0, 1, 0, 1), (2, 0, 0, 2), (0, 0, 1, 2),
    (3, 0, 0, 2), (1, 0, 1, 3), (5, 1, 0, 3), (1, 0, 0, 0), (0, 0, 1, 3), (0, 1, 0, 2), (1, 0, 1, 2), (0, 0, 0, 0),
    (2, 1, 0, 3), (3, 0, 1, 3), (0, 0, 0, 1), (5, 0, 1, 3), (0, 1, 0, 3), (1, 0, 0, 1), (0, 0, 0, 2), (1, 1, 0, 3),
    (4, 1, 0, 3), (1, 0, 0, 2), (0, 0, 0, 3), (3, 0, 0, 3), (5, 0, 0, 3), (2, 0, 0, 3), (4, 0, 0, 3), (1, 0, 0, 3),
)
TAIL_ORDER = (
    (0, 0, 0, 3), (1, 0, 0, 3), (0, 0, 0, 2), (0, 1, 0, 3), (1, 0, 0, 2), (1, 0, 1, 3), (1, 1, 0, 3), (0, 0, 1, 3),
    (0, 0, 0, 1), (0, 0, 0, 0), (0, 1, 0, 1), (0, 0, 1, 2), (1, 0, 0, 1), (0, 1, 0, 2), (0, 1, 1, 3), (1, 0, 1, 2),
    (1, 0, 1, 1), (0, 0, 1, 1), (1, 1, 0, 2), (1, 0, 0, 0), (1, 1, 1, 3), (0, 1, 0, 0), (0, 1, 1, 1), (1, 1, 0, 1),
    (1, 0, 1, 0), (1, 1, 0, 0), (0, 1, 1, 2), (1, 1, 1, 1), (1, 1, 1, 2), (0, 0, 1, 0), (1, 1, 1, 0), (0, 1, 1, 0),
)


class Place:
    def __init__(self):
        s = lax.axis_index("seq")
        self.y = lax.axis_index("batch")
        self.core = lax.rem(s, 2)
        self.x = lax.rem(s // 2, 2)
        self.z = s // 4
        self.s = s

    def chip(self, z, x, y):
        return (z * 2 + x) * 2 + y

    def linear(self, z, x, y):
        return ((z * 2 + x) * 2 + self.core) * 2 + y

    def device(self, z, x, y):
        return ((z * 2 + x) * 2 + self.core, y)

    def sibling(self):
        return (self.s + 1 - 2 * self.core, self.y)

    def far(self, rank):
        z = self.z
        if rank == 3:
            return z
        if rank == 2:
            return z + 1 - 2 * lax.rem(z, 2)
        low = z // 2
        return (3 - 3 * low) if rank == 0 else (2 - low)

    def flipped(self, dx, dy):
        x = self.x if dx == 0 else 1 - self.x
        y = self.y if dy == 0 else 1 - self.y
        return x, y

    def greet(self):
        barrier = pltpu.get_barrier_semaphore()

        def hail(device):
            pl.semaphore_signal(barrier, inc=1, device_id=device, device_id_type=MESH_ID)

        hail(self.sibling())
        hail(self.device(self.z, 1 - self.x, self.y))
        hail(self.device(self.z, self.x, 1 - self.y))

        @pl.when(self.z < 3)
        def _():
            hail(self.device(self.z + 1, self.x, self.y))

        @pl.when(self.z > 0)
        def _():
            hail(self.device(self.z - 1, self.x, self.y))

        ends = (self.z == 0).astype(jnp.int32) + (self.z == 3).astype(jnp.int32)
        pl.semaphore_wait(barrier, 5 - ends)


def last_move(order, dx, dy, rank):
    found = -1
    for i, c in enumerate(order):
        if (c == "x" and dx) or (c == "y" and dy) or (c == "z" and rank != 3):
            found = i
    return found


def sends_before(order, axis):
    count = 1
    for c in order:
        if c == axis:
            return count
        count *= 4 if c == "z" else 2
    return count


def drain(place, orders, total, sem, hops):
    count = {c: sum(sends_before(order, c) for order in orders) for c in "xyz"}

    def finish(i, pieces):
        ref = total(pieces)
        pltpu.make_async_remote_copy(
            ref, ref, sem.at[i], sem.at[i], place.sibling(), MESH_ID
        ).wait_send()

    finish(0, count["x"])
    finish(1, count["y"])
    for z in range(4):
        for i in (2, 3):
            if hops[i - 2][z]:

                @pl.when(place.z == z)
                def _(i=i, z=z):
                    finish(i, count["z"] * hops[i - 2][z])


GATHER_HOPS = ((1, 2, 3, 0), (0, 3, 2, 1))
REDUCE_HOPS = ((3, 2, 1, 0), (0, 1, 2, 3))


def gather_tree(place, orders, steps, piece, total, recv, send, sib_send, sib_recv, between=None):
    z = place.z
    parts = len(orders)

    def copy(ref, device, send_sem, recv_sem):
        return pltpu.make_async_remote_copy(ref, ref, send_sem, recv_sem, device, MESH_ID)

    for number, (part, dx, dy, rank) in enumerate(steps):
        order = orders[part]
        tz = place.far(rank)
        sx, sy = place.flipped(dx, dy)
        ref = piece(place.linear(tz, sx, sy) * parts + part)
        landed = recv.at[part, place.chip(tz, sx, sy)]
        own = dx == 0 and dy == 0 and rank == 3
        if not own:
            copy(ref, place.sibling(), landed, landed).wait_recv()
        last = last_move(order, dx, dy, rank)
        if last >= 0 and order[last] == "z" and rank != 3:
            up = (z > tz).astype(jnp.int32)
            nz = z + 2 * up - 1

            @pl.when(jnp.logical_and(nz >= 0, nz <= 3))
            def _():
                copy(ref, place.device(nz, place.x, place.y), send.at[3 - up], landed).start()

        for c in order[last + 1 :]:
            if c == "x":
                copy(ref, place.device(z, 1 - place.x, place.y), send.at[0], landed).start()
            elif c == "y":
                copy(ref, place.device(z, place.x, 1 - place.y), send.at[1], landed).start()
            else:

                @pl.when(z < 3)
                def _():
                    copy(ref, place.device(z + 1, place.x, place.y), send.at[2], landed).start()

                @pl.when(z > 0)
                def _():
                    copy(ref, place.device(z - 1, place.x, place.y), send.at[3], landed).start()

        copy(ref, place.sibling(), sib_send.at[0], sib_recv.at[0]).start()
        if between is not None:
            between(number)
    drain(place, orders, total, send, GATHER_HOPS)
    whole = total(16 * parts)
    copy(whole, place.sibling(), sib_send.at[0], sib_recv.at[0]).wait()


def radix(order, stop, dx, dy, tz):
    index = 0
    size = 1
    for c in order[: order.index(stop)]:
        value, base = {"x": (dx, 2), "y": (dy, 2), "z": (tz, 4)}[c]
        index = index * base + value
        size *= base
    if stop == "z":
        index = index * 4 + tz
        size *= 4
    return index, size


def landing_base(orders):
    base = {}
    at = 0
    for axis in ("x", "y", "z+", "z-"):
        for part, order in enumerate(orders):
            base[(axis, part)] = at
            at += radix(order, axis[0], 0, 0, 0)[1]
    return base, at


def reduce_step(place, orders, base, step, own_piece, add_landed, land, recv, out, send, keep, offset):
    part, dx, dy, rank = step
    order = orders[part]
    z = place.z
    tz = place.far(rank)
    tx, ty = place.flipped(dx, dy)
    chip = place.chip(tz, tx, ty)
    root = dx == 0 and dy == 0 and rank == 3
    last = last_move(order, dx, dy, rank)
    out_at = part * 16 + chip
    own_piece(part + offset, place.linear(tz, tx, ty), chip, out_at)

    def slot(axis):
        return base[(axis, part)] + radix(order, axis[0], dx, dy, tz)[0]

    def take(index):
        ref = land.at[index]
        sem = recv.at[index]
        pltpu.make_async_remote_copy(ref, ref, sem, sem, place.sibling(), MESH_ID).wait_recv()
        add_landed(part + offset, index)

    if last >= 0 and order[last] == "z" and rank != 3:
        up = (z > tz).astype(jnp.int32)
        nz = z + 2 * up - 1
        plus = base[("z+", part)]
        minus = base[("z-", part)]
        here = radix(order, "z", dx, dy, tz)[0]

        @pl.when(jnp.logical_and(nz >= 0, nz <= 3))
        def _():
            take(up * plus + (1 - up) * minus + here)

    for c in order[last + 1 :]:
        if c == "z":

            @pl.when(z < 3)
            def _():
                take(slot("z+"))

            @pl.when(z > 0)
            def _():
                take(slot("z-"))

        else:
            take(slot(c))
    keep(part + offset, out_at, root)
    if root:
        return
    ref = out.at[out_at]

    def push(device, index, direction):
        pltpu.make_async_remote_copy(
            ref, land.at[index], send.at[direction], recv.at[index], device, MESH_ID
        ).start()

    axis = order[last]
    if axis == "x":
        index = base[("x", part)] + radix(order, "x", 0, dy, tz)[0]
        push(place.device(z, 1 - place.x, place.y), index, 0)
    elif axis == "y":
        index = base[("y", part)] + radix(order, "y", dx, 0, tz)[0]
        push(place.device(z, place.x, 1 - place.y), index, 1)
    else:
        down = (z > tz).astype(jnp.int32)
        here = radix(order, "z", dx, dy, tz)[0]
        index = down * base[("z+", part)] + (1 - down) * base[("z-", part)] + here
        push(place.device(z + 1 - 2 * down, place.x, place.y), index, 2 + down)


TOK = 128
NSEQ = 16
BLOCK = 128
N_LEFT = 56
N_RIGHT = 72
QCH = 256
LOG2E = math.log2(math.e)
MESH_ID = pl.DeviceIdType.MESH
NT = (((1,), (1,)), ((), ()))
TN = (((0,), (0,)), ((), ()))
NN = (((1,), (0,)), ((), ()))
BF = jnp.bfloat16
F32 = jnp.float32
VM = pltpu.VMEM


def mm(a, b, dims=NN):
    return lax.dot_general(a, b, dims, preferred_element_type=F32)


def mmh(a, b, dims=NN):
    return lax.dot_general(a, b, dims, precision=HIGH, preferred_element_type=F32)


def flip(x):
    return jnp.swapaxes(x.astype(F32), 0, 1).astype(x.dtype)


def normalise(x):
    mean = jnp.mean(x, -1, keepdims=True)
    centred = x - mean
    rstd = lax.rsqrt(jnp.mean(centred * centred, -1, keepdims=True) + EPS)
    return centred * rstd, rstd


def normalise_back(grad, unit, rstd, gain):
    inner = grad * gain
    return rstd * (
        inner
        - jnp.mean(inner, -1, keepdims=True)
        - unit * jnp.mean(inner * unit, -1, keepdims=True)
    )


def column_sum(x):
    return jnp.sum(x, 0, keepdims=True)


GELU_K = math.sqrt(2.0 / math.pi)


def gelu_value(x):
    return 0.5 * x * (1.0 + jnp.tanh(GELU_K * (x + 0.044715 * x * x * x)))


def gelu_slope(x):
    t = jnp.tanh(GELU_K * (x + 0.044715 * x * x * x))
    return 0.5 * (1.0 + t) + 0.5 * x * (1.0 - t * t) * GELU_K * (1.0 + 3.0 * 0.044715 * x * x)


def layer_kernel(
    n1_ref,
    h0_ref,
    vec_ref,
    bias_ref,
    bup_ref,
    goal_ref,
    head_ref,
    wlat_ref,
    wqkv_hbm,
    wo_hbm,
    wup_hbm,
    wdown_hbm,
    left_hbm,
    right_hbm,
    drow_ref,
    gvec_ref,
    gup_ref,
    ghead_ref,
    loss_ref,
    wqkv,
    wo,
    wup,
    wdown,
    left,
    right,
    slab,
    qkv_t,
    out_t,
    out_t32,
    lse,
    o_in,
    d_slab,
    do_t,
    dqkv_t,
    dqkv_in,
    k_row,
    v_row,
    q_row,
    do_row,
    s_scr,
    dk_acc,
    dv_acc,
    mid_s,
    up_s,
    acc,
    wave,
    w_sem,
    a_send,
    a_recv,
    x_send,
    x_recv,
    g_local,
    g_send,
    g_recv,
):
    s = lax.axis_index("seq")
    b = lax.axis_index("batch")
    core = lax.rem(s, 2)
    xpos = lax.rem(s // 2, 2)
    zpos = s // 4
    sibling = s + 1 - 2 * core

    copies = []
    for i, (src, dst) in enumerate(((wqkv_hbm, wqkv), (wo_hbm, wo), (wup_hbm, wup), (wdown_hbm, wdown))):
        c = pltpu.make_async_copy(src, dst, w_sem.at[i])
        c.start()
        copies.append(c)

    barrier = pltpu.get_barrier_semaphore()

    def greet(o, _):
        pl.semaphore_signal(
            barrier, inc=1, device_id=(lax.rem(s + o, NSEQ), b), device_id_type=MESH_ID
        )
        return _

    lax.fori_loop(1, NSEQ, greet, 0)
    pl.semaphore_wait(barrier, NSEQ - 1)

    share = []

    def share_group(index, stage, target, begin, count):
        part = pl.ds(begin, count)
        c = pltpu.make_async_copy(stage.at[part], target.at[0, part], g_local.at[index])
        c.start()
        r = pltpu.make_async_remote_copy(
            src_ref=stage.at[part],
            dst_ref=target.at[1, part],
            send_sem=g_send.at[index],
            recv_sem=g_recv.at[index],
            device_id=(sibling, b),
            device_id_type=MESH_ID,
        )
        r.start()
        share.append((c, r))

    def exchange(which, src_at, dst_at):
        def copy(o):
            peer = lax.rem(s + o, NSEQ)
            return pltpu.make_async_remote_copy(
                src_ref=src_at(peer),
                dst_ref=dst_at(s),
                send_sem=a_send.at[which, o],
                recv_sem=a_recv.at[which, o],
                device_id=(peer, b),
                device_id_type=MESH_ID,
            )

        def begin(o, _):
            copy(o).start()
            return _

        def finish(o, _):
            copy(o).wait()
            return _

        def start():
            lax.fori_loop(1, NSEQ, begin, 0)

        def wait():
            lax.fori_loop(1, NSEQ, finish, 0)

        return start, wait

    def lanes(i, size):
        return pl.ds(pl.multiple_of(i * size, size), size)

    n1 = n1_ref[...]
    for k in range(8):
        left[k] = flip(n1[:, k * BLOCK : (k + 1) * BLOCK])
    share_group(0, left, left_hbm, 0, 8)
    copies[0].wait()

    def qkv_tile(t, _):
        part = lanes(t, 512)
        piece = (mm(n1, wqkv[:, part]) + bias_ref[:, part]).astype(BF)
        which = t // 2
        first = lax.rem(t, 2) * 8
        for k in range(4):
            turned = flip(piece[:, k * BLOCK : (k + 1) * BLOCK])
            for half in range(2):
                slab[first + 2 * k + half, pl.ds(which * HD, HD), :] = turned[
                    half * HD : (half + 1) * HD
                ]
        return _

    lax.fori_loop(0, 6, qkv_tile, 0)
    start, wait = exchange(0, lambda p: slab.at[p], lambda p: qkv_t.at[:, lanes(p, TOK)])
    start()
    qkv_t[:, lanes(s, TOK)] = slab[s]
    wait()

    scale2 = LOG2E / math.sqrt(HD)

    def to_rows(t, _):
        part = lanes(t, TOK)
        rows = pl.ds(pl.multiple_of(t * TOK, TOK), TOK)
        q_row[rows, :] = flip(qkv_t[0:HD, part])
        k_row[rows, :] = flip(qkv_t[HD : 2 * HD, part])
        v_row[rows, :] = flip(qkv_t[2 * HD : 3 * HD, part])
        return _

    lax.fori_loop(0, NSEQ, to_rows, 0)
    tiles = (NSEQ * TOK) // QCH

    def forward_chunk(c, _):
        part = lanes(c, QCH)
        q_part = qkv_t[0:HD, part]
        top = None
        for t in range(tiles):
            tile = slice(t * QCH, (t + 1) * QCH)
            scores = mm(k_row[tile, :], q_part)
            s_scr[tile, :] = scores
            best = jnp.max(scores, 0, keepdims=True)
            top = best if top is None else jnp.maximum(top, best)
        top = top * scale2
        total = jnp.zeros((1, QCH), F32)
        mixed = jnp.zeros((HD, QCH), F32)
        for t in range(tiles):
            tile = slice(t * QCH, (t + 1) * QCH)
            probs = jnp.exp2(s_scr[tile, :] * scale2 - top)
            total = total + jnp.sum(probs, 0, keepdims=True)
            mixed = mixed + mm(qkv_t[2 * HD : 3 * HD, tile], probs.astype(BF))
        mixed = mixed / total
        lse[c] = top + jnp.log2(total)
        out_t32[:, part] = mixed
        out_t[:, part] = mixed.astype(BF)
        return _

    lax.fori_loop(0, tiles, forward_chunk, 0)
    start, wait = exchange(1, lambda p: out_t.at[:, lanes(p, TOK)], lambda p: o_in.at[p])
    start()
    o_in[s] = out_t[:, lanes(s, TOK)]
    copies[1].wait()
    wait()

    parts = []
    for k in range(8):
        pair = jnp.concatenate([o_in[2 * k], o_in[2 * k + 1]], 0)
        left[8 + k] = pair
        parts.append(flip(pair))
    share_group(1, left, left_hbm, 8, 8)
    o_low = jnp.concatenate(parts, 1)
    mid = h0_ref[...] + (mm(o_low, wo[...]) + vec_ref[7:8, :])
    mid_s[...] = mid
    unit, _ = normalise(mid)
    n2 = (unit * vec_ref[3:4, :] + vec_ref[4:5, :]).astype(BF)
    for k in range(8):
        left[16 + k] = flip(n2[:, k * BLOCK : (k + 1) * BLOCK])
    share_group(2, left, left_hbm, 16, 8)
    copies[2].wait()
    copies[3].wait()
    acc[...] = mid + vec_ref[8:9, :]

    def up_tile(t, _):
        part = lanes(t, 512)
        upper = mm(n2, wup[:, part]) + bup_ref[:, part]
        up_s[:, part] = upper
        active = gelu_value(upper).astype(BF)
        for k in range(4):
            left[24 + 4 * t + k] = flip(active[:, k * BLOCK : (k + 1) * BLOCK])
        acc[...] += mm(active, wdown[part, :])
        return _

    lax.fori_loop(0, 8, up_tile, 0)
    share_group(3, left, left_hbm, 24, 32)

    unit_f, rstd_f = normalise(acc[...])
    final = (unit_f * vec_ref[5:6, :] + vec_ref[6:7, :]).astype(BF)
    head = head_ref[...]
    diff = mm(final, head) - goal_ref[...].astype(F32)
    wave[0] = diff[0:64] + diff[64:128]
    partners = (
        sibling,
        s + 2 - 4 * xpos,
        s + 4 - 8 * lax.rem(zpos, 2),
        s + 8 - 16 * (zpos // 2),
    )
    for k, partner in enumerate(partners):
        r = pltpu.make_async_remote_copy(
            src_ref=wave.at[2 * k],
            dst_ref=wave.at[2 * k + 1],
            send_sem=x_send.at[k],
            recv_sem=x_recv.at[k],
            device_id=(partner, b),
            device_id_type=MESH_ID,
        )
        r.start()
        r.wait()
        wave[2 * k + 2] = wave[2 * k] + wave[2 * k + 1]
    total_wave = wave[8]
    one = lax.broadcasted_iota(jnp.int32, (HOUT, HOUT), 0)
    two = lax.broadcasted_iota(jnp.int32, (HOUT, HOUT), 1)
    swap = (one == two + 1 - 2 * (two % 2)).astype(F32)
    other = mmh(total_wave, swap)
    weight = wlat_ref[...]
    square = jnp.sum(weight * diff * diff, keepdims=True)
    cross = jnp.sum(weight[0:64] * total_wave * other, keepdims=True) * (1.0 / NSEQ)
    loss_ref[...] = jnp.broadcast_to(
        square * (1.0 / MSE_COUNT)
        + (SPECTRAL / DFT_COUNT) * (float(KMODES) * square + cross),
        loss_ref.shape,
    )
    other2 = jnp.concatenate([other, other], 0)
    d_pred = weight * (
        (2.0 / MSE_COUNT) * diff + (2.0 * SPECTRAL / DFT_COUNT) * (float(KMODES) * diff + other2)
    )
    d_low = d_pred.astype(BF)
    ghead_ref[...] = mm(final, d_low, TN)
    d_final = mm(d_low, head, NT)
    gvec_ref[5:6, :] = column_sum(d_final * unit_f)
    gvec_ref[6:7, :] = column_sum(d_final)
    d_out = normalise_back(d_final, unit_f, rstd_f, vec_ref[5:6, :])
    d_branch = d_out.astype(BF)
    gvec_ref[8:9, :] = column_sum(d_branch.astype(F32))
    for k in range(8):
        right[64 + k] = d_branch[:, k * BLOCK : (k + 1) * BLOCK]
    share_group(4, right, right_hbm, 64, 8)
    acc[...] = jnp.zeros_like(acc)

    def down_tile(t, _):
        part = lanes(t, 512)
        d_active = mm(d_branch, wdown[part, :], NT)
        d_upper = (d_active * gelu_slope(up_s[:, part])).astype(BF)
        gup_ref[:, part] = column_sum(d_upper.astype(F32))
        for k in range(4):
            right[32 + 4 * t + k] = d_upper[:, k * BLOCK : (k + 1) * BLOCK]
        acc[...] += mm(d_upper, wup[:, part], NT)
        return _

    lax.fori_loop(0, 8, down_tile, 0)
    share_group(5, right, right_hbm, 32, 32)
    d_n2 = acc[...]
    unit, rstd = normalise(mid_s[...])
    gvec_ref[3:4, :] = column_sum(d_n2 * unit)
    gvec_ref[4:5, :] = column_sum(d_n2)
    d_mid = d_out + normalise_back(d_n2, unit, rstd, vec_ref[3:4, :])
    mid_s[...] = d_mid
    d_mid_low = d_mid.astype(BF)
    gvec_ref[7:8, :] = column_sum(d_mid_low.astype(F32))
    for k in range(8):
        right[24 + k] = d_mid_low[:, k * BLOCK : (k + 1) * BLOCK]
    share_group(6, right, right_hbm, 24, 8)
    d_att = mm(d_mid_low, wo[...], NT).astype(BF)
    for k in range(8):
        turned = flip(d_att[:, k * BLOCK : (k + 1) * BLOCK])
        d_slab[2 * k] = turned[0:HD]
        d_slab[2 * k + 1] = turned[HD : 2 * HD]
    start, wait = exchange(2, lambda p: d_slab.at[p], lambda p: do_t.at[:, lanes(p, TOK)])
    start()
    do_t[:, lanes(s, TOK)] = d_slab[s]
    wait()

    def do_rows(t, _):
        rows = pl.ds(pl.multiple_of(t * TOK, TOK), TOK)
        do_row[rows, :] = flip(do_t[:, lanes(t, TOK)])
        return _

    lax.fori_loop(0, NSEQ, do_rows, 0)
    dk_acc[...] = jnp.zeros_like(dk_acc)
    dv_acc[...] = jnp.zeros_like(dv_acc)
    scale = 1.0 / math.sqrt(HD)

    def backward_chunk(c, _):
        part = lanes(c, QCH)
        rows = pl.ds(pl.multiple_of(c * QCH, QCH), QCH)
        q_part = qkv_t[0:HD, part]
        do_part = do_t[:, part]
        delta = jnp.sum(do_part.astype(F32) * out_t32[:, part], 0, keepdims=True)
        base = lse[c]
        q_rows = q_row[rows, :]
        g_rows = do_row[rows, :]
        d_query = jnp.zeros((HD, QCH), F32)
        for t in range(tiles):
            tile = slice(t * QCH, (t + 1) * QCH)
            probs = jnp.exp2(mm(k_row[tile, :], q_part) * scale2 - base)
            d_prob = mm(v_row[tile, :], do_part)
            d_score = (probs * (d_prob - delta)).astype(BF)
            dv_acc[tile, :] += mm(probs.astype(BF), g_rows)
            dk_acc[tile, :] += mm(d_score, q_rows)
            d_query = d_query + mm(qkv_t[HD : 2 * HD, tile], d_score)
        dqkv_t[0:HD, part] = (d_query * scale).astype(BF)
        return _

    lax.fori_loop(0, tiles, backward_chunk, 0)

    def turn_back(t, _):
        part = lanes(t, TOK)
        rows = pl.ds(pl.multiple_of(t * TOK, TOK), TOK)
        dqkv_t[HD : 2 * HD, part] = flip((dk_acc[rows, :] * scale)).astype(BF)
        dqkv_t[2 * HD : 3 * HD, part] = flip(dv_acc[rows, :]).astype(BF)
        return _

    lax.fori_loop(0, NSEQ, turn_back, 0)
    start, wait = exchange(3, lambda p: dqkv_t.at[:, lanes(p, TOK)], lambda p: dqkv_in.at[p])
    start()
    dqkv_in[s] = dqkv_t[:, lanes(s, TOK)]
    wait()

    def place(j, _):
        for which in range(3):
            part = slice(which * HD, (which + 1) * HD)
            pair = jnp.concatenate([dqkv_in[2 * j, part, :], dqkv_in[2 * j + 1, part, :]], 0)
            right[8 * which + j] = flip(pair)
        return _

    lax.fori_loop(0, 8, place, 0)
    share_group(7, right, right_hbm, 0, 24)
    acc[...] = jnp.zeros_like(acc)

    def in_tile(t, _):
        piece = jnp.concatenate([right[4 * t + k] for k in range(4)], 1)
        acc[...] += mm(piece, wqkv[:, lanes(t, 512)], NT)
        return _

    lax.fori_loop(0, 6, in_tile, 0)
    for k in range(8):
        part = slice(k * BLOCK, (k + 1) * BLOCK)
        gvec_ref[9:10, part] = column_sum(right[k].astype(F32))
        gvec_ref[10:11, part] = column_sum(right[16 + k].astype(F32))
    d_n1 = acc[...]
    unit, rstd = normalise(h0_ref[...])
    gvec_ref[1:2, :] = column_sum(d_n1 * unit)
    gvec_ref[2:3, :] = column_sum(d_n1)
    drow_ref[...] = mid_s[...] + normalise_back(d_n1, unit, rstd, vec_ref[1:2, :])
    gvec_ref[0:1, :] = jnp.zeros((1, D), F32)
    gvec_ref[11:16, :] = jnp.zeros((5, D), F32)
    for c, r in share:
        c.wait()
        r.wait()


def run_layer(n1, h0, vec, bias, bup, goals, head_low, wlat, mats):
    vmem = pl.BlockSpec(memory_space=VM)
    anyspace = pl.BlockSpec(memory_space=pl.ANY)
    length = NSEQ * TOK
    return pl.pallas_call(
        layer_kernel,
        name="layer",
        out_shape=(
            jax.ShapeDtypeStruct((2, N_LEFT, BLOCK, TOK), BF),
            jax.ShapeDtypeStruct((2, N_RIGHT, TOK, BLOCK), BF),
            jax.ShapeDtypeStruct((TOK, D), F32),
            jax.ShapeDtypeStruct((16, D), F32),
            jax.ShapeDtypeStruct((1, FF), F32),
            jax.ShapeDtypeStruct((D, HOUT), F32),
            jax.ShapeDtypeStruct((8, 128), F32),
        ),
        in_specs=[vmem] * 8 + [anyspace] * 4,
        out_specs=(anyspace, anyspace) + (vmem,) * 5,
        scratch_shapes=[
            VM((D, 3 * D), BF),
            VM((D, D), BF),
            VM((D, FF), BF),
            VM((FF, D), BF),
            VM((N_LEFT, BLOCK, TOK), BF),
            VM((N_RIGHT, TOK, BLOCK), BF),
            VM((HEADS, 3 * HD, TOK), BF),
            VM((3 * HD, length), BF),
            VM((HD, length), BF),
            VM((HD, length), F32),
            VM((length // QCH, 1, QCH), F32),
            VM((HEADS, HD, TOK), BF),
            VM((HEADS, HD, TOK), BF),
            VM((HD, length), BF),
            VM((3 * HD, length), BF),
            VM((HEADS, 3 * HD, TOK), BF),
            VM((length, HD), BF),
            VM((length, HD), BF),
            VM((length, HD), BF),
            VM((length, HD), BF),
            VM((length, QCH), F32),
            VM((length, HD), F32),
            VM((length, HD), F32),
            VM((TOK, D), F32),
            VM((TOK, FF), F32),
            VM((TOK, D), F32),
            VM((9, 64, HOUT), F32),
            pltpu.SemaphoreType.DMA((4,)),
            pltpu.SemaphoreType.DMA((4, NSEQ)),
            pltpu.SemaphoreType.DMA((4, NSEQ)),
            pltpu.SemaphoreType.DMA((4,)),
            pltpu.SemaphoreType.DMA((4,)),
            pltpu.SemaphoreType.DMA((8,)),
            pltpu.SemaphoreType.DMA((8,)),
            pltpu.SemaphoreType.DMA((8,)),
        ],
        compiler_params=pltpu.CompilerParams(
            collective_id=1, has_side_effects=True, vmem_limit_bytes=60 * 1024 * 1024
        ),
    )(n1, h0, vec, bias, bup, goals, head_low, wlat, *mats)


def token_maps():
    row = lax.broadcasted_iota(jnp.int32, (VARS, HOUT), 0)
    col = lax.broadcasted_iota(jnp.int32, (VARS, HOUT), 1)
    return (col // 4 == row).astype(F32)


def embed_kernel(pix_ref, ids_ref, lead_ref, emb_ref, vec_ref, h0_ref, n1_ref, xp_ref, a_ref):
    slot = lax.broadcasted_iota(jnp.int32, (HOUT, HOUT), 1)
    place = (ids_ref[...] == slot).astype(BF)
    pix = mm(pix_ref[...], place)
    xp_ref[...] = pix
    tok = emb_ref[0:HOUT, :]
    emb = emb_ref[HOUT : HOUT + VARS, :]
    query = vec_ref[0:1, :]
    spread = token_maps()
    tok_q = jnp.sum(tok * query, -1, keepdims=True)
    emb_q = mmh(query, emb, NT)
    back = lax.broadcasted_iota(jnp.int32, (HOUT, VARS), 0) // 4
    var = lax.broadcasted_iota(jnp.int32, (HOUT, VARS), 1)
    reduce = jnp.where(back == var, tok_q, 0.0)
    logits = (mmh(pix, reduce) + emb_q) * (1.0 / math.sqrt(D))
    logits = logits - jnp.max(logits, -1, keepdims=True)
    weights = jnp.exp(logits)
    weights = weights / jnp.sum(weights, -1, keepdims=True)
    a_ref[...] = weights
    wide = mmh(weights, spread) * pix
    lead = emb_ref[pl.ds(HOUT + VARS + lead_ref[0], 1), :]
    h0 = mmh(wide, tok) + mmh(weights, emb) + lead
    h0_ref[...] = h0
    unit, _ = normalise(h0)
    n1_ref[...] = (unit * vec_ref[1:2, :] + vec_ref[2:3, :]).astype(BF)


def embed_back_kernel(
    drow_ref, xp_ref, a_ref, lead_ref, emb_ref, vec_ref, gvec_ref, gup_ref, ghead_ref, loss_ref, small_ref
):
    d_rows = drow_ref[...]
    pix = xp_ref[...]
    weights = a_ref[...]
    tok = emb_ref[0:HOUT, :]
    emb = emb_ref[HOUT : HOUT + VARS, :]
    query = vec_ref[0:1, :]
    spread = token_maps()
    d_wide = mmh(d_rows, tok, NT)
    d_weight = mmh(pix * d_wide, spread, NT) + mmh(d_rows, emb, NT)
    d_logit = (
        weights
        * (d_weight - jnp.sum(weights * d_weight, -1, keepdims=True))
        * (1.0 / math.sqrt(D))
    )
    wide = mmh(weights, spread) * pix
    d_wide_l = mmh(d_logit, spread) * pix
    ones = jnp.ones((TOK, 1), F32)
    d_tok_q = mmh(d_wide_l, ones, TN)
    d_emb_q = mmh(d_logit, ones, TN)
    g_tok = mmh(wide, d_rows, TN) + d_tok_q * query
    g_emb = mmh(weights, d_rows, TN) + d_emb_q * query
    row = lax.broadcasted_iota(jnp.int32, (LEADS, D), 0)
    g_lead = jnp.where(row == lead_ref[0], column_sum(d_rows), 0.0)
    g_query = column_sum(d_tok_q * tok) + column_sum(d_emb_q * emb)

    def put(begin, value):
        rows = value.shape[0]
        at = 0
        while at < rows:
            device, inside = divmod(begin + at, ROWS)
            count = min(rows - at, ROWS - inside)
            small_ref[device, inside : inside + count, :] = value[at : at + count]
            at += count

    for k in range(8):
        part = slice(k * BLOCK, (k + 1) * BLOCK)
        put(EROWS * k, g_tok[:, part])
        put(EROWS * k + HOUT, g_emb[:, part])
        put(EROWS * k + HOUT + VARS, g_lead[:, part])
        rows = [g_query[:, part], gvec_ref[1:11, part]]
        rows += [gup_ref[:, r * D + k * BLOCK : r * D + (k + 1) * BLOCK] for r in range(4)]
        put(VEC_AT + 16 * k, jnp.concatenate(rows + [jnp.zeros((1, BLOCK), F32)], 0))
    put(HEAD_AT, ghead_ref[:, 0:BLOCK])
    rest = jnp.concatenate(
        [ghead_ref[:, BLOCK:HOUT], jnp.zeros((D, 2 * BLOCK - HOUT), F32)], 1
    )
    put(HEAD_AT + D, rest)
    for d in range(32):
        small_ref[d, ROWS : 2 * HALF, :] = loss_ref[...]


VEC_AT = 8 * EROWS
HEAD_AT = VEC_AT + 128


def run_embed_back(d_rows, pix, weights, lead, embed, vec, g_vec, g_up, g_head, loss):
    vmem = pl.BlockSpec(memory_space=VM)
    smem = pl.BlockSpec(memory_space=pltpu.SMEM)
    return pl.pallas_call(
        embed_back_kernel,
        name="embed_bwd",
        out_shape=jax.ShapeDtypeStruct((32, 2 * HALF, BLOCK), F32),
        in_specs=[vmem, vmem, vmem, smem] + [vmem] * 6,
        out_specs=vmem,
        compiler_params=pltpu.CompilerParams(vmem_limit_bytes=40 * 1024 * 1024),
    )(d_rows, pix, weights, lead, embed, vec, g_vec, g_up, g_head, loss)


MATRICES = ((D, 3 * D), (D, D), (D, FF), (FF, D))
SLOTS = 768


def gather_kernel(
    place_ref,
    lead_ref,
    blocks_ref,
    left_ref,
    mom_ref,
    right_ref,
    pix_ref,
    ids_ref,
    emb_ref,
    vec_ref,
    wqkv_hbm,
    wo_hbm,
    wup_hbm,
    wdown_hbm,
    turned_ref,
    h0_ref,
    n1_ref,
    xp_ref,
    a_ref,
    stack,
    strip_qkv,
    strip_o,
    strip_up,
    strip_down,
    recv,
    send,
    sib_send,
    sib_recv,
    strip_sem,
):
    place = Place()
    place.greet()
    mine = place.linear(place.z, place.x, place.y)
    stack[pl.ds(mine * SHARE, SHARE)] = blocks_ref[...].astype(BF)

    def between(number):
        if number == 3:
            embed_kernel(pix_ref, ids_ref, lead_ref, emb_ref, vec_ref, h0_ref, n1_ref, xp_ref, a_ref)
        at = number - 12
        if 0 <= at < 48 and at % 2 == 0:
            i = at // 2
            turned_ref[i] = mmh(mmh(left_ref[i], mom_ref[i]), right_ref[i])

    gather_tree(
        place,
        MAIN,
        GATHER_ORDER,
        lambda i: stack.at[pl.ds(i * PIECE, PIECE)],
        lambda n: stack.at[pl.ds(0, n * PIECE)],
        recv,
        send,
        sib_send,
        sib_recv,
        between,
    )

    begin = 0
    groups = (
        (strip_qkv, wqkv_hbm),
        (strip_o, wo_hbm),
        (strip_up, wup_hbm),
        (strip_down, wdown_hbm),
    )
    for which, ((rows, cols), (strip, target)) in enumerate(zip(MATRICES, groups)):
        across = cols // BLOCK
        count = rows // BLOCK

        def out(r, which=which, strip=strip, target=target):
            two = lax.rem(r, 2)
            return pltpu.make_async_copy(
                strip.at[two],
                target.at[pl.ds(pl.multiple_of(r * BLOCK, BLOCK), BLOCK)],
                strip_sem.at[which, two],
            )

        def fill(r, _, begin=begin, across=across, strip=strip, out=out):
            @pl.when(r >= 2)
            def _():
                out(r - 2).wait()

            two = lax.rem(r, 2)
            for c in range(across):
                strip[two, :, c * BLOCK : (c + 1) * BLOCK] = stack[
                    place_ref[begin + r * across + c]
                ]
            out(r).start()
            return 0

        lax.fori_loop(0, count, fill, 0)
        begin += count * across
    for which, ((rows, cols), (strip, target)) in enumerate(zip(MATRICES, groups)):
        count = rows // BLOCK
        for r in (count - 2, count - 1):
            pltpu.make_async_copy(
                strip.at[r % 2], target.at[pl.ds(r * BLOCK, BLOCK)], strip_sem.at[which, r % 2]
            ).wait()


def run_gather(place, lead, blocks, left, momentum, right, pix, ids, embed, vec):
    vmem = pl.BlockSpec(memory_space=VM)
    smem = pl.BlockSpec(memory_space=pltpu.SMEM)
    anyspace = pl.BlockSpec(memory_space=pl.ANY)
    dma = pltpu.SemaphoreType.DMA
    return pl.pallas_call(
        gather_kernel,
        name="gather",
        out_shape=tuple(jax.ShapeDtypeStruct(m, BF) for m in MATRICES)
        + (
            jax.ShapeDtypeStruct((SHARE, BLOCK, BLOCK), F32),
            jax.ShapeDtypeStruct((TOK, D), F32),
            jax.ShapeDtypeStruct((TOK, D), BF),
            jax.ShapeDtypeStruct((TOK, HOUT), F32),
            jax.ShapeDtypeStruct((TOK, VARS), F32),
        ),
        in_specs=[smem, smem] + [vmem] * 8,
        out_specs=(anyspace,) * 4 + (vmem,) * 5,
        scratch_shapes=[
            VM((SLOTS, BLOCK, BLOCK), BF),
            VM((2, BLOCK, 3 * D), BF),
            VM((2, BLOCK, D), BF),
            VM((2, BLOCK, FF), BF),
            VM((2, BLOCK, D), BF),
            dma((4, 16)),
            dma((4,)),
            dma((1,)),
            dma((1,)),
            dma((4, 2)),
        ],
        compiler_params=pltpu.CompilerParams(
            collective_id=2, has_side_effects=True, vmem_limit_bytes=60 * 1024 * 1024
        ),
    )(place, lead, blocks, left, momentum, right, pix, ids, embed, vec)


ROWS = 136
HALF = 72


def reduce_kernel(
    li_ref,
    ri_ref,
    left_hbm,
    right_hbm,
    small_ref,
    lroot_ref,
    rroot_ref,
    own_ref,
    ggt_ref,
    gtg_ref,
    lgr_ref,
    all_ref,
    sum_ref,
    lt,
    rt,
    mine,
    theirs,
    acc,
    acc_small,
    land,
    land_small,
    out,
    out_small,
    tail,
    in_sem,
    swap_sem,
    recv,
    send,
    recv_small,
    send_small,
    t_recv,
    t_send,
    t_sib,
):
    place = Place()
    loads = [
        pltpu.make_async_copy(left_hbm.at[0], lt.at[:, :, pl.ds(0, TOK)], in_sem.at[0]),
        pltpu.make_async_copy(left_hbm.at[1], lt.at[:, :, pl.ds(TOK, TOK)], in_sem.at[1]),
        pltpu.make_async_copy(right_hbm.at[0], rt.at[:, pl.ds(0, TOK), :], in_sem.at[2]),
        pltpu.make_async_copy(right_hbm.at[1], rt.at[:, pl.ds(TOK, TOK), :], in_sem.at[3]),
    ]
    for c in loads:
        c.start()
    place.greet()
    swap = pltpu.make_async_remote_copy(
        small_ref.at[:, 1 - place.core],
        theirs,
        swap_sem.at[0],
        swap_sem.at[1],
        place.sibling(),
        MESH_ID,
    )
    swap.start()
    for c in loads:
        c.wait()
    swap.wait()
    mine[...] = small_ref[:, place.core] + theirs[...]

    def own_piece(part, device, chip, out_at):
        if part < 4:

            def block(j, _):
                slot = device * SHARE + part * PIECE + j
                acc[j] = mm(lt[li_ref[slot]], rt[ri_ref[slot]])
                return 0

            lax.fori_loop(0, PIECE, block, 0, unroll=3)
        else:
            acc_small[...] = mine[chip // 2, lax.rem(chip, 2), pl.ds((part - 4) * HALF, HALF), :]

    def add_landed(part, index):
        if part < 4:
            acc[...] += land[index].astype(F32)
        else:
            acc_small[...] += land_small[index]

    me = place.linear(place.z, place.x, place.y)

    def keep(part, out_at, root):
        if part < 4:
            if root:
                own_ref[pl.ds(part * PIECE, PIECE)] = acc[...]
            else:
                out[out_at] = acc[...].astype(BF)
        elif root:
            tail[me * 2 + part - 4] = acc_small[...]
        else:
            out_small[out_at] = acc_small[...]

    base, _ = landing_base(MAIN)
    base_small, _ = landing_base(SMALL)
    for part, dx, dy, rank in REDUCE_ORDER:
        if part < 4:
            reduce_step(
                place, MAIN, base, (part, dx, dy, rank), own_piece, add_landed,
                land, recv, out, send, keep, 0,
            )
        else:
            reduce_step(
                place, SMALL, base_small, (part - 4, dx, dy, rank), own_piece, add_landed,
                land_small, recv_small, out_small, send_small, keep, 4,
            )
    drain(place, MAIN, lambda n: out.at[pl.ds(0, n)], send, REDUCE_HOPS)
    drain(place, SMALL, lambda n: out_small.at[pl.ds(0, n)], send_small, REDUCE_HOPS)

    squares = jnp.zeros((BLOCK, BLOCK), F32)
    for i in range(SHARE):
        squares = squares + own_ref[i] * own_ref[i]
    first = tail[me * 2]
    second = tail[me * 2 + 1]
    data = second[0 : ROWS - HALF]
    norm = (
        jnp.sum(squares, keepdims=True)
        + jnp.sum(first * first, keepdims=True)
        + jnp.sum(data * data, keepdims=True)
    )
    row = lax.broadcasted_iota(jnp.int32, (8, BLOCK), 0)
    tail[me * 2 + 1, ROWS - HALF : HALF, :] = jnp.where(row < 4, norm, second[ROWS - HALF : HALF])

    def between(number):
        if number < SHARE:
            g = own_ref[number]
            ggt_ref[number] = mmh(g, g, NT)
            gtg_ref[number] = mmh(g, g, TN)
            lgr_ref[number] = mmh(mmh(lroot_ref[number], g), rroot_ref[number])

    gather_tree(
        place,
        TAIL,
        TAIL_ORDER,
        lambda i: tail.at[i],
        lambda n: tail.at[pl.ds(0, n)],
        t_recv,
        t_send,
        t_sib.at[pl.ds(0, 1)],
        t_sib.at[pl.ds(1, 1)],
        between,
    )
    total = jnp.zeros((8, BLOCK), F32)
    for d in range(32):
        all_ref[d, 0:HALF, :] = tail[2 * d]
        all_ref[d, HALF:ROWS, :] = tail[2 * d + 1, 0 : ROWS - HALF, :]
        total = total + tail[2 * d + 1, ROWS - HALF : HALF, :]
    sum_ref[0] = total
    sum_ref[1] = tail[1, ROWS - HALF : HALF, :]


def run_reduce(li, ri, left, right, small, lroots, rroots):
    vmem = pl.BlockSpec(memory_space=VM)
    smem = pl.BlockSpec(memory_space=pltpu.SMEM)
    anyspace = pl.BlockSpec(memory_space=pl.ANY)
    dma = pltpu.SemaphoreType.DMA
    _, count = landing_base(MAIN)
    _, count_small = landing_base(SMALL)
    stack = jax.ShapeDtypeStruct((SHARE, BLOCK, BLOCK), F32)
    return pl.pallas_call(
        reduce_kernel,
        name="reduce",
        out_shape=(stack,) * 4
        + (
            jax.ShapeDtypeStruct((32, ROWS, BLOCK), F32),
            jax.ShapeDtypeStruct((2, 8, BLOCK), F32),
        ),
        in_specs=[smem, smem, anyspace, anyspace, vmem, vmem, vmem],
        out_specs=(vmem,) * 6,
        scratch_shapes=[
            VM((N_LEFT, BLOCK, 2 * TOK), BF),
            VM((N_RIGHT, 2 * TOK, BLOCK), BF),
            VM((8, 2, 2 * HALF, BLOCK), F32),
            VM((8, 2, 2 * HALF, BLOCK), F32),
            VM((PIECE, BLOCK, BLOCK), F32),
            VM((HALF, BLOCK), F32),
            VM((count, PIECE, BLOCK, BLOCK), BF),
            VM((count_small, HALF, BLOCK), F32),
            VM((64, PIECE, BLOCK, BLOCK), BF),
            VM((32, HALF, BLOCK), F32),
            VM((64, HALF, BLOCK), F32),
            dma((4,)),
            dma((2,)),
            dma((count,)),
            dma((4,)),
            dma((count_small,)),
            dma((4,)),
            dma((2, 16)),
            dma((4,)),
            dma((2,)),
        ],
        compiler_params=pltpu.CompilerParams(
            collective_id=3, has_side_effects=True, vmem_limit_bytes=60 * 1024 * 1024
        ),
    )(li, ri, left, right, small, lroots, rroots)


def fast_shards(
    inputs,
    targets,
    var_ids,
    lead_ids,
    block_order,
    blocks,
    block_momentum,
    left_stats,
    right_stats,
    left_roots,
    right_roots,
    embed_params,
    embed_first,
    embed_second,
    vectors,
    vector_first,
    vector_second,
    head_weight,
    head_first,
    head_second,
):
    slots = jnp.arange(SLOTS, dtype=jnp.int32)
    hit = block_order[None, :] == slots[:, None]
    place = jnp.sum(jnp.where(hit, slots[None, :], 0), 1)
    ids = (4 * var_ids[0][:, None] + jnp.arange(4, dtype=jnp.int32)[None]).reshape(HOUT, 1)
    *mats, turned, h0, n1, pix, weights = run_gather(
        place, lead_ids, blocks, left_roots, block_momentum, right_roots,
        inputs[0], ids, embed_params, vectors,
    )
    bias = jnp.concatenate([vectors[9], jnp.zeros_like(vectors[9]), vectors[10]])[None]
    bup = vectors[11:].reshape(1, FF)
    nlat = 2 * LAT_P
    lat = ((jnp.arange(nlat, dtype=jnp.float32) + 0.5) / nlat - 0.5) * math.pi
    wlat = jnp.cos(lat)
    wlat = wlat / jnp.mean(wlat)
    wlat = jnp.broadcast_to(
        wlat.reshape(1, LAT_P, 1, 2, 1), (TOK // LAT_P, LAT_P, VARS, 2, 2)
    ).reshape(TOK, HOUT)
    left, right, d_rows, g_vec, g_up, g_head, loss = run_layer(
        n1, h0, vectors, bias, bup, targets[0], head_weight.astype(BF), wlat, mats
    )
    small = run_embed_back(
        d_rows, pix, weights, lead_ids, embed_params, vectors, g_vec, g_up, g_head, loss
    )
    o = block_order
    li = jnp.where(
        o < 192, o // 24, jnp.where(o < 256, o // 8 - 16, jnp.where(o < 512, o // 32 + 8, o // 8 - 40))
    )
    ri = jnp.where(
        o < 192, o % 24, jnp.where(o < 256, 24 + o % 8, jnp.where(o < 512, 32 + o % 32, 64 + o % 8))
    )
    owned, ggt, gtg, lgr, every, sums = run_reduce(
        li, ri, left, right, small.reshape(8, 2, 2, 2 * HALF, BLOCK), left_roots, right_roots
    )
    flat = every.reshape(32 * ROWS, BLOCK)
    g_embed = flat[:VEC_AT].reshape(8, EROWS, BLOCK).transpose(1, 0, 2).reshape(EROWS, D)
    g_vectors = flat[VEC_AT:HEAD_AT].reshape(8, 16, BLOCK).transpose(1, 0, 2).reshape(16, D)[:15]
    g_head = jnp.concatenate(
        [flat[HEAD_AT : HEAD_AT + D], flat[HEAD_AT + D :, : HOUT - BLOCK]], 1
    )
    loss_total = sums[1, 4, 0]
    grad_norm = jnp.sqrt(sums[0, 0, 0])
    clip = CLIP_NORM / jnp.maximum(grad_norm, CLIP_NORM)
    scaled = owned * clip
    new_momentum = BETA_ONE * block_momentum + (1.0 - BETA_ONE) * scaled
    new_left = BETA_TWO * left_stats + ((1.0 - BETA_TWO) * clip) * (ggt * clip)
    new_right = BETA_TWO * right_stats + ((1.0 - BETA_TWO) * clip) * (gtg * clip)
    direction = BETA_ONE * turned + ((1.0 - BETA_ONE) * clip) * lgr
    new_blocks = blocks - SHAMPOO_RATE * (direction + DECAY * blocks)
    e_one, e_two, e_new = adam(embed_params, embed_first, embed_second, g_embed * clip, EMBED_RATE)
    v_one, v_two, v_new = adam(vectors, vector_first, vector_second, g_vectors * clip, VECTOR_RATE)
    h_one, h_two, h_new = adam(head_weight, head_first, head_second, g_head * clip, HEAD_RATE)
    return (
        loss_total,
        grad_norm,
        new_blocks,
        new_momentum,
        new_left,
        new_right,
        e_one,
        e_two,
        e_new,
        v_one,
        v_two,
        v_new,
        h_one,
        h_two,
        h_new,
    )


def solution(mesh):
    in_specs = (
        P("batch", "seq", None),
        P("batch", "seq", None),
        P("batch", None),
        P("batch"),
        P(),
        P(("seq", "batch"), None, None),
        P(("seq", "batch"), None, None),
        P(("seq", "batch"), None, None),
        P(("seq", "batch"), None, None),
        P(("seq", "batch"), None, None),
        P(("seq", "batch"), None, None),
        P(),
        P(),
        P(),
        P(),
        P(),
        P(),
        P(),
        P(),
        P(),
    )
    out_specs = (
        P(),
        P(),
        P(("seq", "batch"), None, None),
        P(("seq", "batch"), None, None),
        P(("seq", "batch"), None, None),
        P(("seq", "batch"), None, None),
        P(),
        P(),
        P(),
        P(),
        P(),
        P(),
        P(),
        P(),
        P(),
    )
    sizes = dict(mesh.shape)
    fast = sizes == {"seq": NSEQ, "batch": 2}
    return jax.shard_map(fast_shards if fast else shards, mesh=mesh, in_specs=in_specs, out_specs=out_specs, check_vma=False)
```

```python
import math

import jax
import jax.numpy as jnp
import numpy as np
from jax import lax
from jax.experimental import pallas as pl
from jax.experimental.pallas import tpu as pltpu
from jax.sharding import PartitionSpec as P

D = 1024
HEADS = 16
HD = 64
FF = 4096
VARS = 48
LEADS = 32
LAT_P = 64
KMODES = 32
STEP = 10


HIGH = lax.Precision.HIGHEST
EPS = 1e-05
CLIP_NORM = 0.001
SPECTRAL = 0.5
BETA_ONE = 0.9
BETA_TWO = 0.95
SHAMPOO_RATE = 0.1
DECAY = 0.01
ADAM_EPS = 1e-08
EMBED_RATE = 0.2
VECTOR_RATE = 0.5
HEAD_RATE = 0.05
FLOOR = -1e30
EROWS = VARS * 5 + LEADS
HOUT = VARS * 4
MSE_COUNT = 786432.0
DFT_COUNT = 25165824.0


def layer_norm(rows, gain, shift):
    mean = jnp.mean(rows, -1, keepdims=True)
    centred = rows - mean
    return centred * lax.rsqrt(jnp.mean(centred * centred, -1, keepdims=True) + EPS) * gain + shift


def to_blocks(matrix, size):
    rows, cols = matrix.shape
    return (
        matrix.reshape(rows // size, size, cols // size, size)
        .transpose(0, 2, 1, 3)
        .reshape(-1, size, size)
    )


def from_blocks(stack, rows, cols):
    size = stack.shape[-1]
    return (
        stack.reshape(rows // size, cols // size, size, size)
        .transpose(0, 2, 1, 3)
        .reshape(rows, cols)
    )


def split_matrices(stack):
    size = stack.shape[-1]
    found = []
    begin = 0
    for rows, cols in ((D, 3 * D), (D, D), (D, FF), (FF, D)):
        count = rows * cols // (size * size)
        found.append(from_blocks(stack[begin : begin + count], rows, cols))
        begin += count
    return found


def embed_patches(pixels, tok_sel, emb_sel, query, lead_rows):
    tokens = jnp.einsum("spvc,svcd->spvd", pixels, tok_sel, precision=HIGH) + emb_sel[:, None]
    logits = jnp.einsum("spvd,d->spv", tokens, query, precision=HIGH) * (1.0 / math.sqrt(D))
    weights = jax.nn.softmax(logits, -1)
    return jnp.einsum("spv,spvd->spd", weights, tokens, precision=HIGH) + lead_rows[:, None]


def split_heads(rows):
    return rows.reshape(rows.shape[0], rows.shape[1], HEADS, HD)


def attention_forward(query, keys, values):
    seqs, length, _ = query.shape
    scale = 1.0 / math.sqrt(HD)
    heads_q = split_heads(query)
    start_state = (
        jnp.zeros((seqs, HEADS, length, HD), jnp.float32),
        jnp.full((seqs, HEADS, length), FLOOR, jnp.float32),
        jnp.zeros((seqs, HEADS, length), jnp.float32),
    )
    key_rows = lax.all_gather(keys, "seq", axis=1, tiled=True)
    value_rows = lax.all_gather(values, "seq", axis=1, tiled=True)
    count = key_rows.shape[1] // length
    key_blocks = key_rows.reshape(seqs, count, length, HEADS, HD)
    value_blocks = value_rows.reshape(seqs, count, length, HEADS, HD)

    def visit(inner, index):
        acc, top, total = inner
        scores = (
            jnp.einsum(
                "sphd,snhd->shpn", heads_q, key_blocks[:, index], preferred_element_type=jnp.float32
            )
            * scale
        )
        new_top = jnp.maximum(top, jnp.max(scores, -1))
        fade = jnp.exp(top - new_top)
        probs = jnp.exp(scores - new_top[..., None])
        total = total * fade + jnp.sum(probs, -1)
        acc = acc * fade[..., None] + jnp.einsum(
            "shpn,snhd->shpd",
            probs.astype(jnp.bfloat16),
            value_blocks[:, index],
            preferred_element_type=jnp.float32,
        )
        return ((acc, new_top, total), None)

    inner, _ = lax.scan(visit, start_state, jnp.arange(count))
    acc, top, total = inner
    attended = (acc / total[..., None]).transpose(0, 2, 1, 3).reshape(seqs, length, HEADS * HD)
    return (attended, (top + jnp.log(total)).transpose(0, 2, 1))


def attention_backward(query, keys, values, attended, lse, d_att):
    seqs, length, _ = query.shape
    scale = 1.0 / math.sqrt(HD)
    heads_q = split_heads(query)
    heads_k = split_heads(keys)
    heads_v = split_heads(values)
    heads_d = split_heads(d_att)
    delta = jnp.sum(heads_d.astype(jnp.float32) * split_heads(attended), -1)
    lse_h = lse.transpose(0, 2, 1)
    delta_h = delta.transpose(0, 2, 1)
    key_rows = lax.all_gather(keys, "seq", axis=1, tiled=True)
    value_rows = lax.all_gather(values, "seq", axis=1, tiled=True)
    count = key_rows.shape[1] // length
    key_blocks = key_rows.reshape(seqs, count, length, HEADS, HD)
    value_blocks = value_rows.reshape(seqs, count, length, HEADS, HD)

    def visit(inner, index):
        k_part = key_blocks[:, index]
        scores = (
            jnp.einsum("sphd,snhd->shpn", heads_q, k_part, preferred_element_type=jnp.float32)
            * scale
        )
        probs = jnp.exp(scores - lse_h[..., None])
        d_prob = jnp.einsum(
            "sphd,snhd->shpn", heads_d, value_blocks[:, index], preferred_element_type=jnp.float32
        )
        d_score = (probs * (d_prob - delta_h[..., None])).astype(jnp.bfloat16)
        return (
            inner
            + jnp.einsum("shpn,snhd->sphd", d_score, k_part, preferred_element_type=jnp.float32)
            * scale,
            None,
        )

    inner, _ = lax.scan(visit, jnp.zeros((seqs, length, HEADS, HD), jnp.float32), jnp.arange(count))
    d_query = inner
    all_lse, all_delta = (
        lax.all_gather(lse, "seq", axis=1, tiled=True),
        lax.all_gather(delta, "seq", axis=1, tiled=True),
    )
    empty = jnp.zeros((seqs, length, HEADS, HD), jnp.float32)
    q_rows = lax.all_gather(query, "seq", axis=1, tiled=True)
    g_rows = lax.all_gather(d_att, "seq", axis=1, tiled=True)
    count = q_rows.shape[1] // length
    q_blocks = q_rows.reshape(seqs, count, length, HEADS, HD)
    g_blocks = g_rows.reshape(seqs, count, length, HEADS, HD)
    lse_rows = all_lse.reshape(seqs, count, length, HEADS)
    delta_rows = all_delta.reshape(seqs, count, length, HEADS)

    def visit(inner, index):
        d_key, d_value = inner
        q_part = q_blocks[:, index]
        g_part = g_blocks[:, index]
        scores = (
            jnp.einsum("snhd,sphd->shnp", q_part, heads_k, preferred_element_type=jnp.float32)
            * scale
        )
        probs = jnp.exp(scores - lse_rows[:, index].transpose(0, 2, 1)[..., None])
        d_value = d_value + jnp.einsum(
            "shnp,snhd->sphd",
            probs.astype(jnp.bfloat16),
            g_part,
            preferred_element_type=jnp.float32,
        )
        d_prob = jnp.einsum("snhd,sphd->shnp", g_part, heads_v, preferred_element_type=jnp.float32)
        d_score = (probs * (d_prob - delta_rows[:, index].transpose(0, 2, 1)[..., None])).astype(
            jnp.bfloat16
        )
        d_key = (
            d_key
            + jnp.einsum("shnp,snhd->sphd", d_score, q_part, preferred_element_type=jnp.float32)
            * scale
        )
        return ((d_key, d_value), None)

    inner, _ = lax.scan(visit, (empty, empty), jnp.arange(count))
    d_key, d_value = inner
    return (d_query, d_key, d_value)


def feed_inner(normed_two, w_up, vectors):
    upper = jnp.dot(normed_two, w_up, preferred_element_type=jnp.float32) + vectors[11:].reshape(-1)
    return (upper, jax.nn.gelu(upper).astype(jnp.bfloat16))


def layer_forward(rows, seqs, mats, vectors):
    w_qkv, w_out, w_up, w_down = mats
    normed = layer_norm(rows, vectors[1], vectors[2]).astype(jnp.bfloat16)
    bias = jnp.concatenate([vectors[9], jnp.zeros_like(vectors[9]), vectors[10]])
    qkv = (jnp.dot(normed, w_qkv, preferred_element_type=jnp.float32) + bias).astype(jnp.bfloat16)
    query = qkv[:, :D].reshape(seqs, -1, D)
    keys = qkv[:, D : 2 * D].reshape(seqs, -1, D)
    values = qkv[:, 2 * D :].reshape(seqs, -1, D)
    attended, lse = attention_forward(query, keys, values)
    att_low = attended.reshape(-1, D).astype(jnp.bfloat16)
    mid = rows + jnp.dot(att_low, w_out, preferred_element_type=jnp.float32) + vectors[7]
    normed_two = layer_norm(mid, vectors[3], vectors[4]).astype(jnp.bfloat16)
    upper, active = feed_inner(normed_two, w_up, vectors)
    out = mid + jnp.dot(active, w_down, preferred_element_type=jnp.float32) + vectors[8]
    saved = (upper, active)
    return (out, (rows, normed, query, keys, values, attended, lse, mid, normed_two, saved))


def layer_backward(d_out, kept, mats, vectors):
    rows, normed, query, keys, values, attended, lse, mid, normed_two, saved = kept
    w_qkv, w_out, w_up, w_down = mats
    upper, active = saved
    d_branch = d_out.astype(jnp.bfloat16)
    g_down = jnp.einsum("rf,rd->fd", active, d_branch, preferred_element_type=jnp.float32)
    d_active = jnp.einsum("rd,fd->rf", d_branch, w_down, preferred_element_type=jnp.float32)
    d_upper = jax.vjp(jax.nn.gelu, upper)[1](d_active)[0].astype(jnp.bfloat16)
    g_up = jnp.einsum("rd,rf->df", normed_two, d_upper, preferred_element_type=jnp.float32)
    d_normed_two = jnp.einsum("rf,df->rd", d_upper, w_up, preferred_element_type=jnp.float32)
    d_mid_norm, g_gain_two, g_shift_two = jax.vjp(layer_norm, mid, vectors[3], vectors[4])[1](
        d_normed_two
    )
    d_mid = d_out + d_mid_norm
    d_mid_low = d_mid.astype(jnp.bfloat16)
    att_low = attended.reshape(-1, D).astype(jnp.bfloat16)
    g_out = jnp.einsum("ra,rd->ad", att_low, d_mid_low, preferred_element_type=jnp.float32)
    d_att = jnp.einsum("rd,ad->ra", d_mid_low, w_out, preferred_element_type=jnp.float32).astype(
        jnp.bfloat16
    )
    seqs = query.shape[0]
    d_query, d_key, d_value = attention_backward(
        query, keys, values, attended, lse, d_att.reshape(seqs, -1, D)
    )
    d_qkv = jnp.concatenate(
        [d_query.reshape(-1, D), d_key.reshape(-1, D), d_value.reshape(-1, D)], 1
    ).astype(jnp.bfloat16)
    g_qkv = jnp.einsum("rd,re->de", normed, d_qkv, preferred_element_type=jnp.float32)
    d_normed = jnp.einsum("re,de->rd", d_qkv, w_qkv, preferred_element_type=jnp.float32)
    d_rows_norm, g_gain_one, g_shift_one = jax.vjp(layer_norm, rows, vectors[1], vectors[2])[1](
        d_normed
    )
    qkv_sums = jnp.sum(d_qkv.astype(jnp.float32), 0)
    small = (
        g_gain_one,
        g_shift_one,
        g_gain_two,
        g_shift_two,
        jnp.sum(d_mid_low.astype(jnp.float32), 0),
        jnp.sum(d_branch.astype(jnp.float32), 0),
        qkv_sums[:D],
        qkv_sums[2 * D :],
        jnp.sum(d_upper.astype(jnp.float32), 0),
    )
    return (d_mid + d_rows_norm, (g_qkv, g_out, g_up, g_down), small)


def loss_terms(pred, targets, seqs, length):
    strips = lax.axis_size("seq")
    cols = length // LAT_P
    nlat = 2 * LAT_P
    nlon = 2 * cols * strips
    all_seqs = seqs * lax.axis_size("batch")
    diff = pred.reshape(seqs, length, -1) - targets.astype(jnp.float32)
    grid = (
        diff.reshape(seqs, cols, LAT_P, VARS, 2, 2)
        .transpose(0, 3, 2, 4, 1, 5)
        .reshape(seqs, VARS, nlat, 2 * cols)
    )
    lat = ((jnp.arange(nlat, dtype=jnp.float32) + 0.5) / nlat - 0.5) * math.pi
    weight = jnp.cos(lat)
    weight = (weight / jnp.mean(weight))[None, None, :, None]
    column = lax.axis_index("seq") * (2 * cols) + jnp.arange(2 * cols, dtype=jnp.int32)
    modes = jnp.arange(KMODES, dtype=jnp.int32)
    angle = (column[:, None] * modes[None] % nlon).astype(jnp.float32) * (2.0 * math.pi / nlon)
    cosine = jnp.cos(angle)
    sine = jnp.sin(angle)
    part_c = jnp.einsum("svrc,ck->svrk", grid, cosine, precision=HIGH)
    part_s = jnp.einsum("svrc,ck->svrk", grid, sine, precision=HIGH)
    full_c, full_s = lax.psum((part_c, part_s), "seq")
    mse_count = all_seqs * VARS * nlat * nlon
    dft_count = nlon * all_seqs * VARS * nlat * KMODES
    mse = jnp.sum(weight * grid * grid) / mse_count
    spectral = SPECTRAL * jnp.sum(weight * (full_c * full_c + full_s * full_s)) / dft_count
    first = (lax.axis_index("seq") == 0).astype(jnp.float32)
    back_wave = jnp.einsum("svrk,ck->svrc", full_c, cosine, precision=HIGH) + jnp.einsum(
        "svrk,ck->svrc", full_s, sine, precision=HIGH
    )
    d_grid = 2.0 * weight * grid / mse_count + 2.0 * SPECTRAL / dft_count * weight * back_wave
    d_pred = (
        d_grid.reshape(seqs, VARS, LAT_P, 2, cols, 2)
        .transpose(0, 4, 2, 1, 3, 5)
        .reshape(seqs * length, VARS * 4)
    )
    return (d_pred, mse + first * spectral)


def adam(value, first, second, grad, rate):
    first = BETA_ONE * first + (1.0 - BETA_ONE) * grad
    second = BETA_TWO * second + (1.0 - BETA_TWO) * grad * grad
    step = first / (1.0 - BETA_ONE**STEP) / (jnp.sqrt(second / (1.0 - BETA_TWO**STEP)) + ADAM_EPS)
    return (first, second, value - rate * (step + DECAY * value))


def shards(
    inputs,
    targets,
    var_ids,
    lead_ids,
    block_order,
    blocks,
    block_momentum,
    left_stats,
    right_stats,
    left_roots,
    right_roots,
    embed_params,
    embed_first,
    embed_second,
    vectors,
    vector_first,
    vector_second,
    head_weight,
    head_first,
    head_second,
):
    seqs, length, _ = inputs.shape
    size = blocks.shape[-1]
    low_blocks = blocks.astype(jnp.bfloat16)
    stack = lax.all_gather(low_blocks, ("seq", "batch"), axis=0, tiled=True)
    natural = jnp.zeros_like(stack).at[block_order].set(stack)
    mats = split_matrices(natural)
    head_low = head_weight.astype(jnp.bfloat16)
    pick = (var_ids[..., None] == jnp.arange(VARS, dtype=jnp.int32)[None, None]).astype(jnp.float32)
    lead_pick = (lead_ids[:, None] == jnp.arange(LEADS, dtype=jnp.int32)[None]).astype(jnp.float32)
    tok_sel = jnp.einsum(
        "svw,wcd->svcd", pick, embed_params[: VARS * 4].reshape(VARS, 4, D), precision=HIGH
    )
    emb_sel = jnp.einsum("svw,wd->svd", pick, embed_params[VARS * 4 : VARS * 5], precision=HIGH)
    lead_rows = jnp.dot(lead_pick, embed_params[VARS * 5 :], precision=HIGH)
    pixels = inputs.astype(jnp.float32).reshape(seqs, length, VARS, 4)

    def embed_local(tok_part, emb_part, query, lead_part):
        return embed_patches(pixels, tok_part, emb_part, query, lead_part)

    stream, embed_back = jax.vjp(embed_local, tok_sel, emb_sel, vectors[0], lead_rows)
    out, kept = layer_forward(stream.reshape(-1, D), seqs, mats, vectors)
    final_rows, final_back = jax.vjp(layer_norm, out, vectors[5], vectors[6])
    final = final_rows.astype(jnp.bfloat16)
    pred = jnp.dot(final, head_low, preferred_element_type=jnp.float32)
    d_pred, loss_part = loss_terms(pred, targets, seqs, length)
    d_low = d_pred.astype(jnp.bfloat16)
    g_head = jnp.einsum("rd,ro->do", final, d_low, preferred_element_type=jnp.float32)
    d_final = jnp.einsum("ro,do->rd", d_low, head_low, preferred_element_type=jnp.float32)
    d_out, g_gain_final, g_shift_final = final_back(d_final)
    d_rows, matrix_grads, small = layer_backward(d_out, kept, mats, vectors)
    d_tok, d_emb, d_query, d_lead = embed_back(d_rows.reshape(seqs, length, D))
    g_embed = jnp.concatenate(
        [
            jnp.einsum("svw,svcd->wcd", pick, d_tok, precision=HIGH).reshape(VARS * 4, D),
            jnp.einsum("svw,svd->wd", pick, d_emb, precision=HIGH),
            jnp.einsum("sl,sd->ld", lead_pick, d_lead, precision=HIGH),
        ]
    )
    g_gain_one, g_shift_one, g_gain_two, g_shift_two, b_out, b_down, b_query, b_value, b_up = small
    g_vectors = jnp.concatenate(
        [
            jnp.stack(
                [
                    d_query,
                    g_gain_one,
                    g_shift_one,
                    g_gain_two,
                    g_shift_two,
                    g_gain_final,
                    g_shift_final,
                    b_out,
                    b_down,
                    b_query,
                    b_value,
                ]
            ),
            b_up.reshape(-1, D),
        ]
    )
    slot_grads = jnp.concatenate([to_blocks(grad, size) for grad in matrix_grads])[block_order]
    owned = lax.psum_scatter(slot_grads, ("seq", "batch"), scatter_dimension=0, tiled=True)
    g_embed, g_vectors, g_head, loss_total = lax.psum(
        (g_embed, g_vectors, g_head, loss_part), ("seq", "batch")
    )
    rest_squares = (
        jnp.sum(g_embed * g_embed) + jnp.sum(g_vectors * g_vectors) + jnp.sum(g_head * g_head)
    )
    grad_norm = jnp.sqrt(lax.psum(jnp.sum(owned * owned), ("seq", "batch")) + rest_squares)
    clip = CLIP_NORM / jnp.maximum(grad_norm, CLIP_NORM)
    owned = owned * clip
    new_momentum = BETA_ONE * block_momentum + (1.0 - BETA_ONE) * owned
    new_left = BETA_TWO * left_stats + (1.0 - BETA_TWO) * jnp.einsum(
        "bij,bkj->bik", owned, owned, precision=HIGH
    )
    new_right = BETA_TWO * right_stats + (1.0 - BETA_TWO) * jnp.einsum(
        "bji,bjk->bik", owned, owned, precision=HIGH
    )
    direction = jnp.einsum(
        "bij,bjk->bik",
        jnp.einsum("bij,bjk->bik", left_roots, new_momentum, precision=HIGH),
        right_roots,
        precision=HIGH,
    )
    new_blocks = blocks - SHAMPOO_RATE * (direction + DECAY * blocks)
    e_one, e_two, e_new = adam(embed_params, embed_first, embed_second, g_embed * clip, EMBED_RATE)
    v_one, v_two, v_new = adam(vectors, vector_first, vector_second, g_vectors * clip, VECTOR_RATE)
    h_one, h_two, h_new = adam(head_weight, head_first, head_second, g_head * clip, HEAD_RATE)
    return (
        loss_total,
        grad_norm,
        new_blocks,
        new_momentum,
        new_left,
        new_right,
        e_one,
        e_two,
        e_new,
        v_one,
        v_two,
        v_new,
        h_one,
        h_two,
        h_new,
    )


SHARE = 24
PIECE = 6
MAIN = ("zxy", "zyx", "xzy", "yzx")
SMALL = ("xyz", "yxz")
TAIL = ("zxy", "zyx")
GATHER_ORDER = (
    (0, 0, 0, 3), (3, 0, 0, 3), (1, 0, 0, 3), (2, 0, 0, 3), (0, 1, 0, 3), (1, 0, 0, 2), (0, 0, 0, 2), (1, 0, 0, 1),
    (1, 0, 1, 3), (0, 0, 0, 1), (3, 0, 0, 2), (0, 0, 1, 3), (3, 0, 1, 3), (2, 1, 0, 3), (1, 1, 0, 3), (2, 0, 0, 2),
    (1, 1, 1, 3), (0, 0, 0, 0), (1, 1, 0, 2), (2, 0, 1, 3), (1, 0, 1, 2), (2, 1, 0, 2), (3, 0, 1, 2), (0, 1, 0, 2),
    (2, 0, 0, 1), (3, 1, 0, 3), (2, 0, 0, 0), (0, 0, 1, 2), (0, 1, 1, 3), (2, 0, 1, 2), (3, 0, 0, 1), (3, 1, 1, 3),
    (0, 1, 0, 1), (2, 1, 1, 3), (3, 1, 0, 2), (1, 1, 0, 1), (2, 1, 0, 0), (1, 0, 0, 0), (3, 0, 0, 0), (1, 0, 1, 1),
    (0, 1, 1, 2), (0, 0, 1, 1), (3, 0, 1, 0), (2, 1, 1, 2), (2, 1, 0, 1), (0, 1, 1, 1), (3, 1, 0, 1), (2, 0, 1, 1),
    (0, 1, 0, 0), (3, 0, 1, 1), (1, 1, 1, 2), (1, 0, 1, 0), (3, 1, 0, 0), (1, 1, 0, 0), (0, 0, 1, 0), (3, 1, 1, 1),
    (3, 1, 1, 0), (1, 1, 1, 0), (2, 1, 1, 1), (2, 1, 1, 0), (1, 1, 1, 1), (3, 1, 1, 2), (2, 0, 1, 0), (0, 1, 1, 0),
)
REDUCE_PLAN = (
    (0, 5, 1, 1, 0), (0, 5, 1, 1, 1), (0, 3, 1, 1, 0), (0, 4, 1, 0, 0), (0, 2, 1, 1, 1), (0, 4, 1, 0, 1), (0, 5, 0, 0, 1),
    (0, 5, 1, 0, 1), (0, 1, 1, 1, 1), (0, 5, 1, 0, 0), (0, 2, 1, 1, 2), (0, 4, 1, 1, 1), (0, 4, 0, 1, 0), (0, 5, 1, 1, 2),
    (0, 4, 1, 1, 0), (0, 4, 0, 0, 1), (0, 3, 1, 1, 1), (0, 5, 0, 1, 0), (0, 5, 1, 0, 2), (0, 1, 1, 0, 0), (0, 2, 0, 1, 0),
    (0, 5, 0, 1, 1), (0, 4, 0, 1, 2), (0, 2, 1, 1, 0), (0, 0, 1, 1, 1), (0, 2, 1, 0, 1), (0, 5, 1, 1, 3), (0, 0, 1, 1, 0),
    (0, 1, 1, 1, 0), (0, 3, 1, 1, 2), (0, 2, 0, 1, 2), (0, 5, 0, 0, 0), (0, 5, 1, 0, 3), (0, 5, 0, 1, 2), (0, 3, 0, 1, 0),
    (0, 4, 1, 1, 2), (0, 2, 0, 0, 0), (0, 3, 1, 0, 1), (0, 1, 1, 1, 2), (0, 3, 1, 1, 3), (0, 2, 1, 0, 0), (0, 1, 0, 1, 1),
    (0, 1, 1, 0, 1), (0, 4, 1, 1, 3), (0, 4, 0, 1, 1), (0, 1, 0, 1, 0), (0, 4, 1, 0, 2), (0, 0, 0, 1, 0), (0, 3, 0, 1, 1),
    (0, 2, 1, 0, 2), (0, 0, 0, 1, 1), (0, 0, 1, 0, 0), (0, 3, 1, 0, 0), (0, 5, 0, 1, 3), (0, 0, 1, 0, 1), (0, 1, 1, 1, 3),
    (0, 3, 1, 0, 2), (0, 3, 0, 0, 1), (0, 0, 1, 1, 2), (0, 0, 0, 1, 2), (0, 4, 1, 0, 3), (0, 2, 1, 1, 3), (0, 5, 0, 0, 2),
    (0, 2, 0, 1, 1), (0, 3, 0, 1, 2), (0, 0, 1, 1, 3), (0, 1, 0, 0, 1), (0, 1, 1, 0, 2), (0, 0, 0, 0, 0), (0, 4, 0, 0, 0),
    (0, 4, 0, 1, 3), (0, 1, 0, 1, 2), (0, 3, 0, 0, 0), (0, 1, 0, 0, 0), (0, 0, 1, 0, 2), (0, 2, 0, 1, 3), (0, 5, 0, 0, 3),
    (0, 2, 1, 0, 3), (0, 0, 0, 0, 1), (0, 2, 0, 0, 1), (0, 4, 0, 0, 2), (1, 1, 0, 0, 3), (0, 2, 0, 0, 2), (0, 0, 0, 0, 2),
    (0, 4, 0, 0, 3), (1, 0, 0, 0, 3), (1, 1, 0, 0, 2), (0, 1, 1, 0, 3), (0, 1, 0, 1, 3), (0, 0, 0, 1, 3), (0, 3, 0, 1, 3),
    (0, 3, 1, 0, 3), (1, 1, 0, 0, 1), (1, 0, 0, 0, 2), (1, 1, 0, 0, 0), (0, 1, 0, 0, 2), (0, 0, 1, 0, 3), (1, 0, 1, 0, 3),
    (0, 2, 0, 0, 3), (1, 1, 0, 1, 3), (1, 0, 0, 0, 0), (1, 0, 0, 0, 1), (0, 3, 0, 0, 2), (1, 1, 0, 1, 2), (1, 0, 1, 0, 2),
    (1, 1, 1, 0, 2), (0, 1, 0, 0, 3), (0, 0, 0, 0, 3), (1, 0, 1, 1, 3), (1, 1, 0, 1, 1), (1, 0, 0, 1, 2), (1, 1, 1, 0, 0),
    (1, 0, 1, 0, 1), (1, 1, 1, 0, 3), (1, 1, 1, 0, 1), (1, 1, 0, 1, 0), (1, 0, 1, 0, 0), (0, 3, 0, 0, 3), (1, 1, 1, 1, 0),
    (1, 1, 1, 1, 3), (1, 0, 1, 1, 2), (1, 1, 1, 1, 1), (1, 0, 0, 1, 0), (1, 0, 1, 1, 1), (1, 0, 1, 1, 0), (1, 0, 0, 1, 1),
    (1, 0, 0, 1, 3), (1, 1, 1, 1, 2),
)

class Place:
    def __init__(self):
        s = lax.axis_index("seq")
        self.y = lax.axis_index("batch")
        self.core = lax.rem(s, 2)
        self.x = lax.rem(s // 2, 2)
        self.z = s // 4
        self.s = s

    def chip(self, z, x, y):
        return (z * 2 + x) * 2 + y

    def linear(self, z, x, y):
        return ((z * 2 + x) * 2 + self.core) * 2 + y

    def device(self, z, x, y):
        return ((z * 2 + x) * 2 + self.core, y)

    def sibling(self):
        return (self.s + 1 - 2 * self.core, self.y)

    def far(self, rank):
        z = self.z
        if rank == 3:
            return z
        if rank == 2:
            return z + 1 - 2 * lax.rem(z, 2)
        low = z // 2
        return (3 - 3 * low) if rank == 0 else (2 - low)

    def flipped(self, dx, dy):
        x = self.x if dx == 0 else 1 - self.x
        y = self.y if dy == 0 else 1 - self.y
        return x, y

    def greet(self):
        barrier = pltpu.get_barrier_semaphore()

        def hail(o, _):
            peer = lax.rem(self.s + o, NSEQ)
            pl.semaphore_signal(barrier, inc=1, device_id=(peer, self.y), device_id_type=MESH_ID)
            return _

        lax.fori_loop(1, NSEQ, hail, 0)
        pl.semaphore_signal(
            barrier, inc=1, device_id=(self.s, 1 - self.y), device_id_type=MESH_ID
        )
        pl.semaphore_wait(barrier, NSEQ)


def last_move(order, dx, dy, rank):
    found = -1
    for i, c in enumerate(order):
        if (c == "x" and dx) or (c == "y" and dy) or (c == "z" and rank != 3):
            found = i
    return found


def sends_before(order, axis):
    count = 1
    for c in order:
        if c == axis:
            return count
        count *= 4 if c == "z" else 2
    return count


def drain(place, orders, total, sem, hops):
    count = {c: sum(sends_before(order, c) for order in orders) for c in "xyz"}

    def finish(i, pieces):
        ref = total(pieces)
        pltpu.make_async_remote_copy(
            ref, ref, sem.at[i], sem.at[i], place.sibling(), MESH_ID
        ).wait_send()

    finish(0, count["x"])
    finish(1, count["y"])
    for z in range(4):
        for i in (2, 3):
            if hops[i - 2][z]:

                @pl.when(place.z == z)
                def _(i=i, z=z):
                    finish(i, count["z"] * hops[i - 2][z])


GATHER_HOPS = ((1, 2, 3, 0), (0, 3, 2, 1))
REDUCE_HOPS = ((3, 2, 1, 0), (0, 1, 2, 3))


def gather_steps(place, orders, steps, piece, total, recv, send, sib_send, sib_recv):
    z = place.z
    parts = len(orders)

    def copy(ref, device, send_sem, recv_sem):
        return pltpu.make_async_remote_copy(ref, ref, send_sem, recv_sem, device, MESH_ID)

    for number, (part, dx, dy, rank) in enumerate(steps):
        order = orders[part]
        tz = place.far(rank)
        sx, sy = place.flipped(dx, dy)
        ref = piece(place.linear(tz, sx, sy) * parts + part)
        landed = recv.at[part, place.chip(tz, sx, sy)]
        own = dx == 0 and dy == 0 and rank == 3
        if not own:
            copy(ref, place.sibling(), landed, landed).wait_recv()
        last = last_move(order, dx, dy, rank)
        if last >= 0 and order[last] == "z" and rank != 3:
            up = (z > tz).astype(jnp.int32)
            nz = z + 2 * up - 1

            @pl.when(jnp.logical_and(nz >= 0, nz <= 3))
            def _():
                copy(ref, place.device(nz, place.x, place.y), send.at[3 - up], landed).start()

        for c in order[last + 1 :]:
            if c == "x":
                copy(ref, place.device(z, 1 - place.x, place.y), send.at[0], landed).start()
            elif c == "y":
                copy(ref, place.device(z, place.x, 1 - place.y), send.at[1], landed).start()
            else:

                @pl.when(z < 3)
                def _():
                    copy(ref, place.device(z + 1, place.x, place.y), send.at[2], landed).start()

                @pl.when(z > 0)
                def _():
                    copy(ref, place.device(z - 1, place.x, place.y), send.at[3], landed).start()

        copy(ref, place.sibling(), sib_send.at[0], sib_recv.at[0]).start()
        yield number
    drain(place, orders, total, send, GATHER_HOPS)
    whole = total(16 * parts)
    copy(whole, place.sibling(), sib_send.at[0], sib_recv.at[0]).wait()


def radix(order, stop, dx, dy, tz):
    index = 0
    size = 1
    for c in order[: order.index(stop[0])]:
        value, base = {"x": (dx, 2), "y": (dy, 2), "z": (tz, 4)}[c]
        index = index * base + value
        size *= base
    if stop[0] == "z":
        index = index * 3 + (tz if stop == "z+" else tz - 1)
        size *= 3
    return index, size


def landing_base(orders):
    base = {}
    at = 0
    for axis in ("x", "y", "z+", "z-"):
        for part, order in enumerate(orders):
            base[(axis, part)] = at
            at += radix(order, axis, 0, 0, 0)[1]
    return base, at


def reduce_step(place, orders, base, step, own_piece, add_landed, land, recv, out, send, keep, offset):
    part, dx, dy, rank = step
    order = orders[part]
    z = place.z
    tz = place.far(rank)
    tx, ty = place.flipped(dx, dy)
    chip = place.chip(tz, tx, ty)
    root = dx == 0 and dy == 0 and rank == 3
    last = last_move(order, dx, dy, rank)
    out_at = part * 16 + chip
    own_piece(part + offset, place.linear(tz, tx, ty), chip, out_at)

    def slot(axis):
        return base[(axis, part)] + radix(order, axis, dx, dy, tz)[0]

    def take(index):
        ref = land.at[index]
        sem = recv.at[index]
        pltpu.make_async_remote_copy(ref, ref, sem, sem, place.sibling(), MESH_ID).wait_recv()
        add_landed(part + offset, index)

    if last >= 0 and order[last] == "z" and rank != 3:
        up = (z > tz).astype(jnp.int32)
        nz = z + 2 * up - 1
        plus = slot("z+")
        minus = slot("z-")

        @pl.when(jnp.logical_and(nz >= 0, nz <= 3))
        def _():
            take(up * plus + (1 - up) * minus)

    for c in order[last + 1 :]:
        if c == "z":

            @pl.when(z < 3)
            def _():
                take(slot("z+"))

            @pl.when(z > 0)
            def _():
                take(slot("z-"))

        else:
            take(slot(c))
    keep(part + offset, out_at, root)
    if root:
        return
    ref = out.at[out_at]

    def push(device, index, direction):
        pltpu.make_async_remote_copy(
            ref, land.at[index], send.at[direction], recv.at[index], device, MESH_ID
        ).start()

    axis = order[last]
    if axis == "x":
        index = base[("x", part)] + radix(order, "x", 0, dy, tz)[0]
        push(place.device(z, 1 - place.x, place.y), index, 0)
    elif axis == "y":
        index = base[("y", part)] + radix(order, "y", dx, 0, tz)[0]
        push(place.device(z, place.x, 1 - place.y), index, 1)
    else:
        down = (z > tz).astype(jnp.int32)
        index = down * slot("z+") + (1 - down) * slot("z-")
        push(place.device(z + 1 - 2 * down, place.x, place.y), index, 2 + down)


TOK = 128
NSEQ = 16
BLOCK = 128
N_LEFT = 56
N_RIGHT = 72
QCH = 256
LOG2E = math.log2(math.e)
MESH_ID = pl.DeviceIdType.MESH
NT = (((1,), (1,)), ((), ()))
TN = (((0,), (0,)), ((), ()))
NN = (((1,), (0,)), ((), ()))
BF = jnp.bfloat16
F32 = jnp.float32
VM = pltpu.VMEM


def mm(a, b, dims=NN):
    return lax.dot_general(a, b, dims, preferred_element_type=F32)


def mmh(a, b, dims=NN):
    return lax.dot_general(a, b, dims, precision=HIGH, preferred_element_type=F32)


def flip(x):
    return jnp.swapaxes(x.astype(F32), 0, 1).astype(x.dtype)


def normalise(x):
    mean = jnp.mean(x, -1, keepdims=True)
    centred = x - mean
    rstd = lax.rsqrt(jnp.mean(centred * centred, -1, keepdims=True) + EPS)
    return centred * rstd, rstd


def normalise_back(grad, unit, rstd, gain):
    inner = grad * gain
    return rstd * (
        inner
        - jnp.mean(inner, -1, keepdims=True)
        - unit * jnp.mean(inner * unit, -1, keepdims=True)
    )


def column_sum(x):
    return jnp.sum(x, 0, keepdims=True)


GELU_K = math.sqrt(2.0 / math.pi)


def gelu_value(x):
    return 0.5 * x * (1.0 + jnp.tanh(GELU_K * (x + 0.044715 * x * x * x)))


def gelu_slope(x):
    t = jnp.tanh(GELU_K * (x + 0.044715 * x * x * x))
    return 0.5 * (1.0 + t) + 0.5 * x * (1.0 - t * t) * GELU_K * (1.0 + 3.0 * 0.044715 * x * x)


def layer_kernel(
    place_ref,
    lead_ref,
    blocks_ref,
    ids_ref,
    pix_ref,
    goal_ref,
    emb_ref,
    vec_ref,
    head_ref,
    wlat_ref,
    left_hbm,
    right_hbm,
    small_ref,
    stack,
    left,
    right,
    slab,
    qkv_t,
    out_t,
    out_t32,
    lse,
    o_in,
    d_slab,
    do_t,
    dqkv_t,
    dqkv_in,
    k_row,
    v_row,
    q_row,
    do_row,
    s_scr,
    dq_acc,
    h0_s,
    n1_s,
    xp_s,
    a_s,
    mid_s,
    up_s,
    acc,
    wave,
    wave_in,
    wave_tile,
    wave_all,
    pix_s,
    goal_s,
    head_s,
    gvec,
    t_recv,
    t_send,
    t_sib_send,
    t_sib_recv,
    a_send,
    a_recv,
    in_sem,
    g_local,
    g_send,
    g_recv,
):
    s = lax.axis_index("seq")
    b = lax.axis_index("batch")
    place = Place()
    sibling = s + 1 - 2 * place.core

    loads = []
    for i, (src, dst) in enumerate(((pix_ref, pix_s), (goal_ref, goal_s), (head_ref, head_s))):
        c = pltpu.make_async_copy(src, dst, in_sem.at[i])
        c.start()
        loads.append(c)
    mine = place.linear(place.z, place.x, place.y)
    stack[pl.ds(mine * SHARE, SHARE)] = blocks_ref[...].astype(BF)
    place.greet()

    for number in gather_steps(
        place,
        MAIN,
        GATHER_ORDER,
        lambda i: stack.at[pl.ds(i * PIECE, PIECE)],
        lambda n: stack.at[pl.ds(0, n * PIECE)],
        t_recv,
        t_send,
        t_sib_send,
        t_sib_recv,
    ):
        if number == 3:
            loads[0].wait()
            embed_forward(pix_s, ids_ref, lead_ref, emb_ref, vec_ref, h0_s, n1_s, xp_s, a_s)

    def block(begin, across, r, c):
        return stack[place_ref[begin + r * across + c]]

    def two_columns(begin, across, pair):
        return jnp.concatenate(
            [
                jnp.concatenate(
                    [block(begin, across, r, 2 * pair), block(begin, across, r, 2 * pair + 1)], 1
                )
                for r in range(8)
            ],
            0,
        )

    def two_rows(begin, pair):
        return jnp.concatenate(
            [
                jnp.concatenate([block(begin, 8, 2 * pair + r, c) for c in range(8)], 1)
                for r in range(2)
            ],
            0,
        )

    at_qkv, at_o, at_up, at_down = 0, 192, 256, 512
    share = []

    def share_group(index, stage, target, begin, count):
        part = pl.ds(begin, count)
        c = pltpu.make_async_copy(stage.at[part], target.at[0, part], g_local.at[index])
        c.start()
        r = pltpu.make_async_remote_copy(
            src_ref=stage.at[part],
            dst_ref=target.at[1, part],
            send_sem=g_send.at[index],
            recv_sem=g_recv.at[index],
            device_id=(sibling, b),
            device_id_type=MESH_ID,
        )
        r.start()
        share.append((c, r))

    def exchange(which, src_at, dst_at):
        def copy(o):
            peer = lax.rem(s + o, NSEQ)
            return pltpu.make_async_remote_copy(
                src_ref=src_at(peer),
                dst_ref=dst_at(s),
                send_sem=a_send.at[which, o],
                recv_sem=a_recv.at[which, o],
                device_id=(peer, b),
                device_id_type=MESH_ID,
            )

        def begin(o, _):
            copy(o).start()
            return _

        def finish(o, _):
            copy(o).wait()
            return _

        def start():
            lax.fori_loop(1, NSEQ, begin, 0)

        def start_to(peer):
            @pl.when(peer != s)
            def _():
                copy(lax.rem(peer - s + NSEQ, NSEQ)).start()

        def wait():
            lax.fori_loop(1, NSEQ, finish, 0)

        return start, wait, start_to

    def lanes(i, size):
        return pl.ds(pl.multiple_of(i * size, size), size)

    def rows_at(i, size):
        return pl.ds(pl.multiple_of(i * size, size), size)

    n1 = n1_s[...]
    waits = {}
    for which in (1, 0, 2):

        def qkv_tile(t, _, which=which):
            piece = mm(n1, two_columns(at_qkv, 24, 4 * which + t))
            if which != 1:
                piece = piece + vec_ref[9 + which // 2 : 10 + which // 2, lanes(t, 256)]
            piece = piece.astype(BF)
            for k in range(2):
                turned = flip(piece[:, k * BLOCK : (k + 1) * BLOCK])
                for half in range(2):
                    slab[4 * t + 2 * k + half, which * HD : (which + 1) * HD, :] = turned[
                        half * HD : (half + 1) * HD
                    ]
            return _

        lax.fori_loop(0, 4, qkv_tile, 0)
        part = pl.ds(which * HD, HD)
        start, waits[which], _ = exchange(
            which,
            lambda p, part=part: slab.at[p, part],
            lambda p, part=part: qkv_t.at[part, lanes(p, TOK)],
        )
        start()
    qkv_t[:, lanes(s, TOK)] = slab[s]
    for k in range(8):
        left[k] = flip(n1[:, k * BLOCK : (k + 1) * BLOCK])

    scale2 = LOG2E / math.sqrt(HD)

    def turn_rows(source, begin, target):
        def one(t, _):
            target[rows_at(t, TOK), :] = flip(source[begin : begin + HD, lanes(t, TOK)])
            return _

        lax.fori_loop(0, NSEQ, one, 0)

    waits[1]()
    turn_rows(qkv_t, HD, k_row)
    waits[0]()
    tiles = (NSEQ * TOK) // QCH
    start, wait_o, send_o = exchange(
        3, lambda p: out_t.at[:, lanes(p, TOK)], lambda p: o_in.at[p]
    )

    def forward_chunk(i, _):
        c = lax.rem(i + s // 2, tiles)
        part = lanes(c, QCH)
        q_part = qkv_t[0:HD, part]
        top = None
        for t in range(tiles):
            tile = slice(t * QCH, (t + 1) * QCH)
            scores = mm(k_row[tile, :], q_part)
            s_scr[tile, :] = scores
            best = jnp.max(scores, 0, keepdims=True)
            top = best if top is None else jnp.maximum(top, best)
        top = top * scale2

        @pl.when(i == 0)
        def _():
            waits[2]()

        total = jnp.zeros((1, QCH), F32)
        mixed = jnp.zeros((HD, QCH), F32)
        for t in range(tiles):
            tile = slice(t * QCH, (t + 1) * QCH)
            probs = jnp.exp2(s_scr[tile, :] * scale2 - top)
            total = total + jnp.sum(probs, 0, keepdims=True)
            mixed = mixed + mm(qkv_t[2 * HD : 3 * HD, tile], probs.astype(BF))
        mixed = mixed / total
        lse[c] = top + jnp.log2(total)
        out_t32[:, part] = mixed
        out_t[:, part] = mixed.astype(BF)
        send_o(2 * c)
        send_o(2 * c + 1)
        return 0

    lax.fori_loop(0, tiles, forward_chunk, 0)
    share_group(0, left, left_hbm, 0, 8)
    o_in[s] = out_t[:, lanes(s, TOK)]
    turn_rows(qkv_t, 0, q_row)
    turn_rows(qkv_t, 2 * HD, v_row)
    wait_o()

    parts = []
    for k in range(8):
        pair = jnp.concatenate([o_in[2 * k], o_in[2 * k + 1]], 0)
        left[8 + k] = pair
        parts.append(flip(pair))
    share_group(1, left, left_hbm, 8, 8)
    o_low = jnp.concatenate(parts, 1)

    def out_tile(t, _):
        part = lanes(t, 256)
        mid_s[:, part] = h0_s[:, part] + (
            mm(o_low, two_columns(at_o, 8, t)) + vec_ref[7:8, part]
        )
        return _

    lax.fori_loop(0, 4, out_tile, 0)
    mid = mid_s[...]
    unit, _ = normalise(mid)
    n2 = (unit * vec_ref[3:4, :] + vec_ref[4:5, :]).astype(BF)
    for k in range(8):
        left[16 + k] = flip(n2[:, k * BLOCK : (k + 1) * BLOCK])
    share_group(2, left, left_hbm, 16, 8)
    acc[...] = mid + vec_ref[8:9, :]

    def up_tile(t, _):
        part = lanes(t, 256)
        bias = vec_ref[pl.ds(11 + t // 4, 1), lanes(lax.rem(t, 4), 256)]
        upper = mm(n2, two_columns(at_up, 32, t)) + bias
        up_s[:, part] = upper
        active = gelu_value(upper).astype(BF)
        for k in range(2):
            left[24 + 2 * t + k] = flip(active[:, k * BLOCK : (k + 1) * BLOCK])
        acc[...] += mm(active, two_rows(at_down, t))
        return _

    lax.fori_loop(0, 16, up_tile, 0)
    share_group(3, left, left_hbm, 24, 32)

    unit_f, rstd_f = normalise(acc[...])
    final = (unit_f * vec_ref[5:6, :] + vec_ref[6:7, :]).astype(BF)
    loads[2].wait()
    head = head_s[...].astype(BF)
    loads[1].wait()
    diff = mm(final, head, NT) - jnp.swapaxes(goal_s[0].astype(F32), 0, 1)
    wave[...] = jnp.concatenate(
        [diff[0:64] + diff[64:128], jnp.zeros((64, 2 * BLOCK - HOUT), F32)], 1
    )

    def tile_of(ref, j):
        return ref.at[
            pl.ds(pl.multiple_of(j // 2 * 8, 8), 8),
            pl.ds(pl.multiple_of(lax.rem(j, 2) * BLOCK, BLOCK), BLOCK),
        ]

    start, wait, _ = exchange(7, lambda p: tile_of(wave, p), lambda p: wave_in.at[p])
    start()
    wave_in[s] = tile_of(wave, s)[...]
    wait()
    tile = wave_in[0]
    for k in range(1, NSEQ):
        tile = tile + wave_in[k]
    wave_tile[...] = tile
    start, wait, _ = exchange(8, lambda p: wave_tile, lambda p: tile_of(wave_all, p))
    start()
    tile_of(wave_all, s)[...] = tile
    wait()
    total_wave = wave_all[:, 0:HOUT]
    one = lax.broadcasted_iota(jnp.int32, (HOUT, HOUT), 0)
    two = lax.broadcasted_iota(jnp.int32, (HOUT, HOUT), 1)
    swap = (one == two + 1 - 2 * (two % 2)).astype(F32)
    other = mmh(total_wave, swap)
    weight = wlat_ref[...]
    square = jnp.sum(weight * diff * diff, keepdims=True)
    cross = jnp.sum(weight[0:64] * total_wave * other, keepdims=True) * (1.0 / NSEQ)
    loss = square * (1.0 / MSE_COUNT) + (SPECTRAL / DFT_COUNT) * (float(KMODES) * square + cross)
    other2 = jnp.concatenate([other, other], 0)
    d_pred = weight * (
        (2.0 / MSE_COUNT) * diff + (2.0 * SPECTRAL / DFT_COUNT) * (float(KMODES) * diff + other2)
    )
    d_low = d_pred.astype(BF)
    put_head(small_ref, mm(d_low, final, TN), loss)
    d_final = mm(d_low, head)
    gvec[5:6, :] = column_sum(d_final * unit_f)
    gvec[6:7, :] = column_sum(d_final)
    d_out = normalise_back(d_final, unit_f, rstd_f, vec_ref[5:6, :])
    d_branch = d_out.astype(BF)
    gvec[8:9, :] = column_sum(d_branch.astype(F32))
    for k in range(8):
        right[64 + k] = d_branch[:, k * BLOCK : (k + 1) * BLOCK]
    share_group(4, right, right_hbm, 64, 8)
    acc[...] = jnp.zeros_like(acc)

    def down_tile(t, _):
        part = lanes(t, 256)
        d_active = mm(d_branch, two_rows(at_down, t), NT)
        d_upper = (d_active * gelu_slope(up_s[:, part])).astype(BF)
        gvec[pl.ds(11 + t // 4, 1), lanes(lax.rem(t, 4), 256)] = column_sum(d_upper.astype(F32))
        for k in range(2):
            right[32 + 2 * t + k] = d_upper[:, k * BLOCK : (k + 1) * BLOCK]
        acc[...] += mm(d_upper, two_columns(at_up, 32, t), NT)
        return _

    lax.fori_loop(0, 16, down_tile, 0)
    share_group(5, right, right_hbm, 32, 32)
    d_n2 = acc[...]
    unit, rstd = normalise(mid_s[...])
    gvec[3:4, :] = column_sum(d_n2 * unit)
    gvec[4:5, :] = column_sum(d_n2)
    d_mid = d_out + normalise_back(d_n2, unit, rstd, vec_ref[3:4, :])
    mid_s[...] = d_mid
    d_mid_low = d_mid.astype(BF)
    start, wait_d, send_d = exchange(
        4, lambda p: d_slab.at[p], lambda p: do_t.at[:, lanes(p, TOK)]
    )

    def att_tile(t, _):
        piece = mm(d_mid_low, two_rows(at_o, t), NT).astype(BF)
        for k in range(2):
            turned = flip(piece[:, k * BLOCK : (k + 1) * BLOCK])
            for half in range(2):
                d_slab[4 * t + 2 * k + half] = turned[half * HD : (half + 1) * HD]
        for k in range(4):
            send_d(4 * t + k)
        return _

    lax.fori_loop(0, 4, att_tile, 0)
    do_t[:, lanes(s, TOK)] = d_slab[s]
    gvec[7:8, :] = column_sum(d_mid_low.astype(F32))
    for k in range(8):
        right[24 + k] = d_mid_low[:, k * BLOCK : (k + 1) * BLOCK]
    share_group(6, right, right_hbm, 24, 8)
    dq_acc[...] = jnp.zeros_like(dq_acc)
    wait_d()

    turn_rows(do_t, 0, do_row)
    scale = 1.0 / math.sqrt(HD)

    def deltas(c, _):
        part = lanes(c, QCH)
        s_scr[pl.ds(c, 1), :] = jnp.sum(
            do_t[:, part].astype(F32) * out_t32[:, part], 0, keepdims=True
        )
        return _

    lax.fori_loop(0, tiles, deltas, 0)
    start, wait_kv, send_kv = exchange(
        5,
        lambda p: dqkv_t.at[pl.ds(HD, 2 * HD), lanes(p, TOK)],
        lambda p: dqkv_in.at[p, pl.ds(HD, 2 * HD)],
    )

    def backward_tile(i, _):
        c = lax.rem(i + s // 2, tiles)
        keys = rows_at(c, QCH)
        k_part = k_row[keys, :]
        v_part = v_row[keys, :]
        k_turned = qkv_t[HD : 2 * HD, lanes(c, QCH)]
        d_key = jnp.zeros((QCH, HD), F32)
        d_value = jnp.zeros((QCH, HD), F32)
        for t in range(tiles):
            tile = slice(t * QCH, (t + 1) * QCH)
            probs = jnp.exp2(mm(k_part, qkv_t[0:HD, tile]) * scale2 - lse[t])
            d_prob = mm(v_part, do_t[:, tile])
            d_score = (probs * (d_prob - s_scr[t : t + 1, :])).astype(BF)
            d_value = d_value + mm(probs.astype(BF), do_row[tile, :])
            d_key = d_key + mm(d_score, q_row[tile, :])
            dq_acc[:, tile] += mm(k_turned, d_score)
        d_key = d_key * scale
        for k in range(2):
            part = lanes(2 * c + k, TOK)
            half = slice(k * TOK, (k + 1) * TOK)
            dqkv_t[HD : 2 * HD, part] = flip(d_key[half]).astype(BF)
            dqkv_t[2 * HD : 3 * HD, part] = flip(d_value[half]).astype(BF)
            send_kv(2 * c + k)
        return _

    lax.fori_loop(0, tiles, backward_tile, 0)
    dqkv_t[0:HD, :] = (dq_acc[...] * scale).astype(BF)
    start_q, wait_q, _ = exchange(
        6,
        lambda p: dqkv_t.at[pl.ds(0, HD), lanes(p, TOK)],
        lambda p: dqkv_in.at[p, pl.ds(0, HD)],
    )
    start_q()
    dqkv_in[s] = dqkv_t[:, lanes(s, TOK)]
    acc[...] = jnp.zeros_like(acc)

    def finish_part(which):
        def one(t, _):
            parts = []
            for k in range(2):
                j = 2 * t + k
                part = slice(which * HD, (which + 1) * HD)
                pair = jnp.concatenate([dqkv_in[2 * j, part, :], dqkv_in[2 * j + 1, part, :]], 0)
                piece = flip(pair)
                right[8 * which + j] = piece
                parts.append(piece)
            piece = jnp.concatenate(parts, 1)
            if which != 1:
                gvec[9 + which // 2 : 10 + which // 2, lanes(t, 256)] = column_sum(
                    piece.astype(F32)
                )
            acc[...] += mm(piece, two_columns(at_qkv, 24, 4 * which + t), NT)
            return _

        lax.fori_loop(0, 4, one, 0)

    wait_kv()
    finish_part(1)
    finish_part(2)
    wait_q()
    finish_part(0)
    share_group(7, right, right_hbm, 0, 24)
    d_n1 = acc[...]
    unit, rstd = normalise(h0_s[...])
    gvec[1:2, :] = column_sum(d_n1 * unit)
    gvec[2:3, :] = column_sum(d_n1)
    d_rows = mid_s[...] + normalise_back(d_n1, unit, rstd, vec_ref[1:2, :])
    embed_backward(d_rows, xp_s, a_s, lead_ref, emb_ref, vec_ref, gvec, small_ref)
    for c, r in share:
        c.wait()
        r.wait()


def run_layer(place, lead, blocks, ids, pix, goals, embed, vec, head, wlat):
    vmem = pl.BlockSpec(memory_space=VM)
    smem = pl.BlockSpec(memory_space=pltpu.SMEM)
    anyspace = pl.BlockSpec(memory_space=pl.ANY)
    dma = pltpu.SemaphoreType.DMA
    length = NSEQ * TOK
    return pl.pallas_call(
        layer_kernel,
        name="layer",
        out_shape=(
            jax.ShapeDtypeStruct((2, N_LEFT, BLOCK, TOK), BF),
            jax.ShapeDtypeStruct((2, N_RIGHT, TOK, BLOCK), BF),
            jax.ShapeDtypeStruct((32, 2 * HALF, BLOCK), F32),
        ),
        in_specs=[smem, smem, vmem, vmem, anyspace, anyspace, vmem, vmem, anyspace, vmem],
        out_specs=(anyspace, anyspace, vmem),
        scratch_shapes=[
            VM((SLOTS, BLOCK, BLOCK), BF),
            VM((N_LEFT, BLOCK, TOK), BF),
            VM((N_RIGHT, TOK, BLOCK), BF),
            VM((HEADS, 3 * HD, TOK), BF),
            VM((3 * HD, length), BF),
            VM((HD, length), BF),
            VM((HD, length), F32),
            VM((length // QCH, 1, QCH), F32),
            VM((HEADS, HD, TOK), BF),
            VM((HEADS, HD, TOK), BF),
            VM((HD, length), BF),
            VM((3 * HD, length), BF),
            VM((HEADS, 3 * HD, TOK), BF),
            VM((length, HD), BF),
            VM((length, HD), BF),
            VM((length, HD), BF),
            VM((length, HD), BF),
            VM((length, QCH), F32),
            VM((HD, length), F32),
            VM((TOK, D), F32),
            VM((TOK, D), BF),
            VM((TOK, HOUT), F32),
            VM((TOK, VARS), F32),
            VM((TOK, D), F32),
            VM((TOK, FF), F32),
            VM((TOK, D), F32),
            VM((64, 2 * BLOCK), F32),
            VM((NSEQ, 8, BLOCK), F32),
            VM((8, BLOCK), F32),
            VM((64, 2 * BLOCK), F32),
            VM((1, HOUT, TOK), BF),
            VM((1, HOUT, TOK), BF),
            VM((HOUT, D), F32),
            VM((16, D), F32),
            dma((4, 16)),
            dma((4,)),
            dma((1,)),
            dma((1,)),
            dma((9, NSEQ)),
            dma((9, NSEQ)),
            dma((3,)),
            dma((8,)),
            dma((8,)),
            dma((8,)),
        ],
        compiler_params=pltpu.CompilerParams(
            collective_id=1, has_side_effects=True, vmem_limit_bytes=60 * 1024 * 1024
        ),
    )(place, lead, blocks, ids, pix, goals, embed, vec, head, wlat)


def token_maps():
    row = lax.broadcasted_iota(jnp.int32, (VARS, HOUT), 0)
    col = lax.broadcasted_iota(jnp.int32, (VARS, HOUT), 1)
    return (col // 4 == row).astype(F32)


def embed_forward(pix_ref, ids_ref, lead_ref, emb_ref, vec_ref, h0_ref, n1_ref, xp_ref, a_ref):
    spread = token_maps()
    var = lax.broadcasted_iota(jnp.int32, (VARS, VARS), 0)
    chosen = (ids_ref[...] == var).astype(BF)
    low = spread.astype(BF)
    wide_ids = mm(chosen, low)
    routes = mm(wide_ids.astype(BF), low, TN)
    one = lax.broadcasted_iota(jnp.int32, (HOUT, HOUT), 0)
    two = lax.broadcasted_iota(jnp.int32, (HOUT, HOUT), 1)
    routes = jnp.where(one % 4 == two % 4, routes, 0.0).astype(BF)
    pix = mm(pix_ref[0], routes, TN)
    xp_ref[...] = pix
    tok = emb_ref[0:HOUT, :]
    emb = emb_ref[HOUT : HOUT + VARS, :]
    query = vec_ref[0:1, :]
    tok_q = jnp.sum(tok * query, -1, keepdims=True)
    emb_q = mmh(query, emb, NT)
    back = lax.broadcasted_iota(jnp.int32, (HOUT, VARS), 0) // 4
    col = lax.broadcasted_iota(jnp.int32, (HOUT, VARS), 1)
    reduce = jnp.where(back == col, tok_q, 0.0)
    logits = (mmh(pix, reduce) + emb_q) * (1.0 / math.sqrt(D))
    logits = logits - jnp.max(logits, -1, keepdims=True)
    weights = jnp.exp(logits)
    weights = weights / jnp.sum(weights, -1, keepdims=True)
    a_ref[...] = weights
    wide = mmh(weights, spread) * pix
    lead = emb_ref[pl.ds(HOUT + VARS + lead_ref[0], 1), :]
    h0 = mmh(wide, tok) + mmh(weights, emb) + lead
    h0_ref[...] = h0
    unit, _ = normalise(h0)
    n1_ref[...] = (unit * vec_ref[1:2, :] + vec_ref[2:3, :]).astype(BF)


VEC_AT = 8 * EROWS
HEAD_AT = VEC_AT + 128


def put(small_ref, begin, value):
    rows = value.shape[0]
    at = 0
    while at < rows:
        device, inside = divmod(begin + at, ROWS)
        count = min(rows - at, ROWS - inside)
        small_ref[device, inside : inside + count, :] = value[at : at + count]
        at += count


def put_head(small_ref, grad, loss):
    for k in range(8):
        put(small_ref, HEAD_AT + HOUT * k, grad[:, k * BLOCK : (k + 1) * BLOCK])
    tile = jnp.broadcast_to(loss, (8, BLOCK))
    for d in range(32):
        small_ref[d, ROWS : 2 * HALF, :] = tile


def embed_backward(d_rows, xp_ref, a_ref, lead_ref, emb_ref, vec_ref, gvec, small_ref):
    pix = xp_ref[...]
    weights = a_ref[...]
    tok = emb_ref[0:HOUT, :]
    emb = emb_ref[HOUT : HOUT + VARS, :]
    query = vec_ref[0:1, :]
    spread = token_maps()
    d_wide = mmh(d_rows, tok, NT)
    d_weight = mmh(pix * d_wide, spread, NT) + mmh(d_rows, emb, NT)
    d_logit = (
        weights
        * (d_weight - jnp.sum(weights * d_weight, -1, keepdims=True))
        * (1.0 / math.sqrt(D))
    )
    wide = mmh(weights, spread) * pix
    d_wide_l = mmh(d_logit, spread) * pix
    ones = jnp.ones((TOK, 1), F32)
    d_tok_q = mmh(d_wide_l, ones, TN)
    d_emb_q = mmh(d_logit, ones, TN)
    g_tok = mmh(wide, d_rows, TN) + d_tok_q * query
    g_emb = mmh(weights, d_rows, TN) + d_emb_q * query
    row = lax.broadcasted_iota(jnp.int32, (LEADS, D), 0)
    g_lead = jnp.where(row == lead_ref[0], column_sum(d_rows), 0.0)
    gvec[0:1, :] = column_sum(d_tok_q * tok) + column_sum(d_emb_q * emb)
    gvec[15:16, :] = jnp.zeros((1, D), F32)
    for k in range(8):
        part = slice(k * BLOCK, (k + 1) * BLOCK)
        put(small_ref, EROWS * k, g_tok[:, part])
        put(small_ref, EROWS * k + HOUT, g_emb[:, part])
        put(small_ref, EROWS * k + HOUT + VARS, g_lead[:, part])
        put(small_ref, VEC_AT + 16 * k, gvec[:, part])


SLOTS = 768
ROWS = 120
HALF = 64


def sides_of(b):
    li = jnp.where(
        b < 192, b // 24, jnp.where(b < 256, b // 8 - 16, jnp.where(b < 512, b // 32 + 8, b // 8 - 40))
    )
    ri = jnp.where(
        b < 192,
        lax.rem(b, 24),
        jnp.where(
            b < 256,
            24 + lax.rem(b, 8),
            jnp.where(b < 512, 32 + lax.rem(b, 32), 64 + lax.rem(b, 8)),
        ),
    )
    return li, ri


def reduce_kernel(
    order_ref,
    left_hbm,
    right_hbm,
    small_ref,
    lroot_ref,
    mom_ref,
    rroot_ref,
    own_ref,
    ggt_ref,
    gtg_ref,
    lgr_ref,
    turned_ref,
    all_ref,
    sum_ref,
    lt,
    rt,
    mine,
    theirs,
    acc,
    acc_small,
    land,
    land_small,
    out,
    out_small,
    tail,
    in_sem,
    swap_sem,
    recv,
    send,
    recv_small,
    send_small,
    norms,
    across,
    t_recv,
    t_send,
    t_sib,
    n_send,
    n_recv,
):
    place = Place()
    loads = [
        pltpu.make_async_copy(left_hbm.at[0], lt.at[:, :, pl.ds(0, TOK)], in_sem.at[0]),
        pltpu.make_async_copy(left_hbm.at[1], lt.at[:, :, pl.ds(TOK, TOK)], in_sem.at[1]),
        pltpu.make_async_copy(right_hbm.at[0], rt.at[:, pl.ds(0, TOK), :], in_sem.at[2]),
        pltpu.make_async_copy(right_hbm.at[1], rt.at[:, pl.ds(TOK, TOK), :], in_sem.at[3]),
    ]
    loads.append(pltpu.make_async_copy(small_ref.at[:, place.core], mine, in_sem.at[4]))
    for c in loads:
        c.start()
    place.greet()
    swap = pltpu.make_async_remote_copy(
        small_ref.at[:, 1 - place.core],
        theirs,
        swap_sem.at[0],
        swap_sem.at[1],
        place.sibling(),
        MESH_ID,
    )
    swap.start()
    for c in loads:
        c.wait()
    swap.wait()
    mine[...] += theirs[...]

    def own_piece(part, device, chip, out_at):
        if part < 4:

            def block(j, _):
                slot = device * SHARE + part * PIECE + j
                li, ri = sides_of(order_ref[slot])
                acc[j] = mm(lt[li], rt[ri])
                return 0

            lax.fori_loop(0, PIECE, block, 0, unroll=3)
        else:
            acc_small[...] = mine[chip // 2, lax.rem(chip, 2), pl.ds((part - 4) * HALF, HALF), :]

    def add_landed(part, index):
        if part < 4:
            acc[...] += land[index].astype(F32)
        else:
            acc_small[...] += land_small[index]

    me = place.linear(place.z, place.x, place.y)

    def keep(part, out_at, root):
        if part < 4:
            if root:
                own_ref[pl.ds(part * PIECE, PIECE)] = acc[...]
            else:
                out[out_at] = acc[...].astype(BF)
        elif root:
            tail[me * 2 + part - 4] = acc_small[...]
        else:
            out_small[out_at] = acc_small[...]

    base, _ = landing_base(MAIN)
    base_small, _ = landing_base(SMALL)

    def main_step(step):
        reduce_step(
            place, MAIN, base, step, own_piece, add_landed, land, recv, out, send, keep, 0
        )

    def small_step(step):
        reduce_step(
            place, SMALL, base_small, step, own_piece, add_landed,
            land_small, recv_small, out_small, send_small, keep, 4,
        )

    def products(part):
        for i in range(part * PIECE, (part + 1) * PIECE):
            g = own_ref[i]
            ggt_ref[i] = mmh(g, g, NT)
            gtg_ref[i] = mmh(g, g, TN)
            lgr_ref[i] = mmh(mmh(lroot_ref[i], g), rroot_ref[i])

    def small_root():
        first = tail[me * 2]
        data = tail[me * 2 + 1, 0 : ROWS - HALF, :]
        return jnp.sum(first * first, keepdims=True) + jnp.sum(data * data, keepdims=True)

    spread = gather_steps(
        place,
        TAIL,
        [step[1:] for step in REDUCE_PLAN if step[0]],
        lambda i: tail.at[i],
        lambda n: tail.at[pl.ds(0, n)],
        t_recv,
        t_send,
        t_sib.at[pl.ds(0, 1)],
        t_sib.at[pl.ds(1, 1)],
    )
    squares = jnp.zeros((BLOCK, BLOCK), F32)
    done = 0
    roots = []
    for kind, part, dx, dy, rank in REDUCE_PLAN:
        if kind:
            next(spread)
            continue
        root = dx == 0 and dy == 0 and rank == 3
        if part >= 4:
            small_step((part - 4, dx, dy, rank))
            continue
        main_step((part, dx, dy, rank))
        if done % 2 == 0 and done // 2 < SHARE:
            i = done // 2
            turned_ref[i] = mmh(mmh(lroot_ref[i], mom_ref[i]), rroot_ref[i])
        done += 1
        if root:
            for i in range(part * PIECE, (part + 1) * PIECE):
                squares = squares + own_ref[i] * own_ref[i]
            roots.append(part)
    small_squares = small_root()

    norms[place.s] = jnp.broadcast_to(jnp.sum(squares, keepdims=True) + small_squares, (8, BLOCK))

    def norm_copy(o):
        peer = lax.rem(place.s + o, NSEQ)
        return pltpu.make_async_remote_copy(
            norms.at[place.s],
            norms.at[place.s],
            n_send.at[o],
            n_recv.at[o],
            (peer, place.y),
            MESH_ID,
        )

    lax.fori_loop(1, NSEQ, lambda o, _: (norm_copy(o).start(), 0)[1], 0)
    for part in roots[:2]:
        products(part)
    for _ in spread:
        pass
    for d in range(32):
        all_ref[d, 0:HALF, :] = tail[2 * d]
        all_ref[d, HALF:ROWS, :] = tail[2 * d + 1, 0 : ROWS - HALF, :]
    lax.fori_loop(1, NSEQ, lambda o, _: (norm_copy(o).wait(), 0)[1], 0)
    total = norms[0]
    for k in range(1, NSEQ):
        total = total + norms[k]
    across[0] = total
    over = pltpu.make_async_remote_copy(
        across.at[0], across.at[1], n_send.at[0], n_recv.at[0], (place.s, 1 - place.y), MESH_ID
    )
    over.start()
    for part in roots[2:]:
        products(part)
    drain(place, MAIN, lambda n: out.at[pl.ds(0, n)], send, REDUCE_HOPS)
    drain(place, SMALL, lambda n: out_small.at[pl.ds(0, n)], send_small, REDUCE_HOPS)
    over.wait()
    sum_ref[0] = across[0] + across[1]
    sum_ref[1] = tail[1, ROWS - HALF : HALF, :]


def run_reduce(order, left, right, small, lroots, momentum, rroots):
    vmem = pl.BlockSpec(memory_space=VM)
    smem = pl.BlockSpec(memory_space=pltpu.SMEM)
    anyspace = pl.BlockSpec(memory_space=pl.ANY)
    dma = pltpu.SemaphoreType.DMA
    _, count = landing_base(MAIN)
    _, count_small = landing_base(SMALL)
    stack = jax.ShapeDtypeStruct((SHARE, BLOCK, BLOCK), F32)
    return pl.pallas_call(
        reduce_kernel,
        name="reduce",
        out_shape=(stack,) * 5
        + (
            jax.ShapeDtypeStruct((32, ROWS, BLOCK), F32),
            jax.ShapeDtypeStruct((2, 8, BLOCK), F32),
        ),
        in_specs=[smem, anyspace, anyspace, anyspace] + [vmem] * 3,
        out_specs=(vmem,) * 7,
        scratch_shapes=[
            VM((N_LEFT, BLOCK, 2 * TOK), BF),
            VM((N_RIGHT, 2 * TOK, BLOCK), BF),
            VM((8, 2, 2 * HALF, BLOCK), F32),
            VM((8, 2, 2 * HALF, BLOCK), F32),
            VM((PIECE, BLOCK, BLOCK), F32),
            VM((HALF, BLOCK), F32),
            VM((count, PIECE, BLOCK, BLOCK), BF),
            VM((count_small, HALF, BLOCK), F32),
            VM((64, PIECE, BLOCK, BLOCK), BF),
            VM((32, HALF, BLOCK), F32),
            VM((64, HALF, BLOCK), F32),
            dma((5,)),
            dma((2,)),
            dma((count,)),
            dma((4,)),
            dma((count_small,)),
            dma((4,)),
            VM((NSEQ, 8, BLOCK), F32),
            VM((2, 8, BLOCK), F32),
            dma((2, 16)),
            dma((4,)),
            dma((2,)),
            dma((NSEQ,)),
            dma((NSEQ,)),
        ],
        compiler_params=pltpu.CompilerParams(
            collective_id=3, has_side_effects=True, vmem_limit_bytes=60 * 1024 * 1024
        ),
    )(order, left, right, small, lroots, momentum, rroots)


def final_kernel(
    sums_ref, own, ggt, gtg, lgr, turned, mom, stat_l, stat_r, blk,
    ge, gv, gh, e, e1, e2, v, v1, v2, h, h1, h2,
    loss_o, norm_o, blk_o, mom_o, l_o, r_o,
    e1_o, e2_o, e_o, v1_o, v2_o, v_o, h1_o, h2_o, h_o,
):
    norm = jnp.sqrt(sums_ref[0, 0:1, 0:1])
    loss_o[...] = sums_ref[1, 4:5, 0:1]
    norm_o[...] = norm
    clip = CLIP_NORM / jnp.maximum(norm, CLIP_NORM)
    for i in range(3):
        mom_o[i] = BETA_ONE * mom[i] + (1.0 - BETA_ONE) * (own[i] * clip)
        l_o[i] = BETA_TWO * stat_l[i] + (1.0 - BETA_TWO) * ((ggt[i] * clip) * clip)
        r_o[i] = BETA_TWO * stat_r[i] + (1.0 - BETA_TWO) * ((gtg[i] * clip) * clip)
        direction = BETA_ONE * turned[i] + (1.0 - BETA_ONE) * (lgr[i] * clip)
        blk_o[i] = blk[i] - SHAMPOO_RATE * (direction + DECAY * blk[i])
    e1_o[...], e2_o[...], e_o[...] = adam(e[...], e1[...], e2[...], ge[...] * clip, EMBED_RATE)
    v1_o[...], v2_o[...], v_o[...] = adam(
        v[...], v1[...], v2[...], gv[0:15, :] * clip, VECTOR_RATE
    )
    h1_o[...], h2_o[...], h_o[...] = adam(h[...], h1[...], h2[...], gh[...] * clip, HEAD_RATE)


def run_final(sums, stacks, flat, embed, vec, head):
    slots = pl.BlockSpec((3, BLOCK, BLOCK), lambda k: (k, 0, 0))
    table = pl.BlockSpec((EROWS, BLOCK), lambda k: (0, k))
    rows = pl.BlockSpec((15, BLOCK), lambda k: (0, k))
    wide = pl.BlockSpec((HOUT, BLOCK), lambda k: (0, k))
    one = pl.BlockSpec((1, 1), lambda k: (0, 0))
    stack = jax.ShapeDtypeStruct((SHARE, BLOCK, BLOCK), F32)
    shapes = (
        (jax.ShapeDtypeStruct((1, 1), F32),) * 2
        + (stack,) * 4
        + (jax.ShapeDtypeStruct((EROWS, D), F32),) * 3
        + (jax.ShapeDtypeStruct((15, D), F32),) * 3
        + (jax.ShapeDtypeStruct((HOUT, D), F32),) * 3
    )
    return pl.pallas_call(
        final_kernel,
        name="final",
        grid=(8,),
        out_shape=shapes,
        in_specs=[pl.BlockSpec((2, 8, BLOCK), lambda k: (0, 0, 0))]
        + [slots] * 9
        + [
            pl.BlockSpec((EROWS, BLOCK), lambda k: (k, 0)),
            pl.BlockSpec((16, BLOCK), lambda k: (VEC_AT // 16 + k, 0)),
            pl.BlockSpec((HOUT, BLOCK), lambda k: (HEAD_AT // HOUT + k, 0)),
        ]
        + [table] * 3
        + [rows] * 3
        + [wide] * 3,
        out_specs=(one,) * 2 + (slots,) * 4 + (table,) * 3 + (rows,) * 3 + (wide,) * 3,
        compiler_params=pltpu.CompilerParams(vmem_limit_bytes=60 * 1024 * 1024),
    )(sums, *stacks, flat, flat, flat, *embed, *vec, *head)


def fast_shards(
    inputs,
    targets,
    var_ids,
    lead_ids,
    block_order,
    blocks,
    block_momentum,
    left_stats,
    right_stats,
    left_roots,
    right_roots,
    embed_params,
    embed_first,
    embed_second,
    vectors,
    vector_first,
    vector_second,
    head_weight,
    head_first,
    head_second,
):
    slots = jnp.arange(SLOTS, dtype=jnp.int32)
    hit = block_order[None, :] == slots[:, None]
    place = jnp.sum(jnp.where(hit, slots[None, :], 0), 1)
    lat = ((np.arange(2 * LAT_P, dtype=np.float64) + 0.5) / (2 * LAT_P) - 0.5) * math.pi
    wlat = np.cos(lat)
    wlat = (wlat / np.mean(wlat)).reshape(1, LAT_P, 1, 2, 1)
    wlat = np.broadcast_to(wlat, (TOK // LAT_P, LAT_P, VARS, 2, 2)).reshape(TOK, HOUT)
    left, right, small = run_layer(
        place, lead_ids, blocks, var_ids, jnp.swapaxes(inputs, 1, 2), jnp.swapaxes(targets, 1, 2),
        embed_params, vectors, head_weight.T,
        jnp.asarray(wlat, F32),
    )
    owned, ggt, gtg, lgr, turned, every, sums = run_reduce(
        block_order, left, right, small.reshape(8, 2, 2, 2 * HALF, BLOCK),
        left_roots, block_momentum, right_roots,
    )
    loss, norm, *rest = run_final(
        sums,
        (owned, ggt, gtg, lgr, turned, block_momentum, left_stats, right_stats, blocks),
        every.reshape(32 * ROWS, BLOCK),
        (embed_params, embed_first, embed_second),
        (vectors, vector_first, vector_second),
        (head_weight.T, head_first.T, head_second.T),
    )
    return (loss.reshape(()), norm.reshape(()), *rest[:-3], *(a.T for a in rest[-3:]))


def solution(mesh):
    in_specs = (
        P("batch", "seq", None),
        P("batch", "seq", None),
        P("batch", None),
        P("batch"),
        P(),
        P(("seq", "batch"), None, None),
        P(("seq", "batch"), None, None),
        P(("seq", "batch"), None, None),
        P(("seq", "batch"), None, None),
        P(("seq", "batch"), None, None),
        P(("seq", "batch"), None, None),
        P(),
        P(),
        P(),
        P(),
        P(),
        P(),
        P(),
        P(),
        P(),
    )
    out_specs = (
        P(),
        P(),
        P(("seq", "batch"), None, None),
        P(("seq", "batch"), None, None),
        P(("seq", "batch"), None, None),
        P(("seq", "batch"), None, None),
        P(),
        P(),
        P(),
        P(),
        P(),
        P(),
        P(),
        P(),
        P(),
    )
    sizes = dict(mesh.shape)
    fast = sizes == {"seq": NSEQ, "batch": 2}
    return jax.shard_map(fast_shards if fast else shards, mesh=mesh, in_specs=in_specs, out_specs=out_specs, check_vma=False)
```

```python
import math

import jax
import jax.numpy as jnp
import numpy as np
from jax import lax
from jax.experimental import pallas as pl
from jax.experimental.pallas import tpu as pltpu
from jax.sharding import PartitionSpec as P

D = 1024
HEADS = 16
HD = 64
FF = 4096
VARS = 48
LEADS = 32
LAT_P = 64
KMODES = 32
STEP = 10


HIGH = lax.Precision.HIGHEST
EPS = 1e-05
CLIP_NORM = 0.001
SPECTRAL = 0.5
BETA_ONE = 0.9
BETA_TWO = 0.95
SHAMPOO_RATE = 0.1
DECAY = 0.01
ADAM_EPS = 1e-08
EMBED_RATE = 0.2
VECTOR_RATE = 0.5
HEAD_RATE = 0.05
FLOOR = -1e30
EROWS = VARS * 5 + LEADS
HOUT = VARS * 4
MSE_COUNT = 786432.0
DFT_COUNT = 25165824.0


def layer_norm(rows, gain, shift):
    mean = jnp.mean(rows, -1, keepdims=True)
    centred = rows - mean
    return centred * lax.rsqrt(jnp.mean(centred * centred, -1, keepdims=True) + EPS) * gain + shift


def to_blocks(matrix, size):
    rows, cols = matrix.shape
    return (
        matrix.reshape(rows // size, size, cols // size, size)
        .transpose(0, 2, 1, 3)
        .reshape(-1, size, size)
    )


def from_blocks(stack, rows, cols):
    size = stack.shape[-1]
    return (
        stack.reshape(rows // size, cols // size, size, size)
        .transpose(0, 2, 1, 3)
        .reshape(rows, cols)
    )


def split_matrices(stack):
    size = stack.shape[-1]
    found = []
    begin = 0
    for rows, cols in ((D, 3 * D), (D, D), (D, FF), (FF, D)):
        count = rows * cols // (size * size)
        found.append(from_blocks(stack[begin : begin + count], rows, cols))
        begin += count
    return found


def embed_patches(pixels, tok_sel, emb_sel, query, lead_rows):
    tokens = jnp.einsum("spvc,svcd->spvd", pixels, tok_sel, precision=HIGH) + emb_sel[:, None]
    logits = jnp.einsum("spvd,d->spv", tokens, query, precision=HIGH) * (1.0 / math.sqrt(D))
    weights = jax.nn.softmax(logits, -1)
    return jnp.einsum("spv,spvd->spd", weights, tokens, precision=HIGH) + lead_rows[:, None]


def split_heads(rows):
    return rows.reshape(rows.shape[0], rows.shape[1], HEADS, HD)


def attention_forward(query, keys, values):
    seqs, length, _ = query.shape
    scale = 1.0 / math.sqrt(HD)
    heads_q = split_heads(query)
    start_state = (
        jnp.zeros((seqs, HEADS, length, HD), jnp.float32),
        jnp.full((seqs, HEADS, length), FLOOR, jnp.float32),
        jnp.zeros((seqs, HEADS, length), jnp.float32),
    )
    key_rows = lax.all_gather(keys, "seq", axis=1, tiled=True)
    value_rows = lax.all_gather(values, "seq", axis=1, tiled=True)
    count = key_rows.shape[1] // length
    key_blocks = key_rows.reshape(seqs, count, length, HEADS, HD)
    value_blocks = value_rows.reshape(seqs, count, length, HEADS, HD)

    def visit(inner, index):
        acc, top, total = inner
        scores = (
            jnp.einsum(
                "sphd,snhd->shpn", heads_q, key_blocks[:, index], preferred_element_type=jnp.float32
            )
            * scale
        )
        new_top = jnp.maximum(top, jnp.max(scores, -1))
        fade = jnp.exp(top - new_top)
        probs = jnp.exp(scores - new_top[..., None])
        total = total * fade + jnp.sum(probs, -1)
        acc = acc * fade[..., None] + jnp.einsum(
            "shpn,snhd->shpd",
            probs.astype(jnp.bfloat16),
            value_blocks[:, index],
            preferred_element_type=jnp.float32,
        )
        return ((acc, new_top, total), None)

    inner, _ = lax.scan(visit, start_state, jnp.arange(count))
    acc, top, total = inner
    attended = (acc / total[..., None]).transpose(0, 2, 1, 3).reshape(seqs, length, HEADS * HD)
    return (attended, (top + jnp.log(total)).transpose(0, 2, 1))


def attention_backward(query, keys, values, attended, lse, d_att):
    seqs, length, _ = query.shape
    scale = 1.0 / math.sqrt(HD)
    heads_q = split_heads(query)
    heads_k = split_heads(keys)
    heads_v = split_heads(values)
    heads_d = split_heads(d_att)
    delta = jnp.sum(heads_d.astype(jnp.float32) * split_heads(attended), -1)
    lse_h = lse.transpose(0, 2, 1)
    delta_h = delta.transpose(0, 2, 1)
    key_rows = lax.all_gather(keys, "seq", axis=1, tiled=True)
    value_rows = lax.all_gather(values, "seq", axis=1, tiled=True)
    count = key_rows.shape[1] // length
    key_blocks = key_rows.reshape(seqs, count, length, HEADS, HD)
    value_blocks = value_rows.reshape(seqs, count, length, HEADS, HD)

    def visit(inner, index):
        k_part = key_blocks[:, index]
        scores = (
            jnp.einsum("sphd,snhd->shpn", heads_q, k_part, preferred_element_type=jnp.float32)
            * scale
        )
        probs = jnp.exp(scores - lse_h[..., None])
        d_prob = jnp.einsum(
            "sphd,snhd->shpn", heads_d, value_blocks[:, index], preferred_element_type=jnp.float32
        )
        d_score = (probs * (d_prob - delta_h[..., None])).astype(jnp.bfloat16)
        return (
            inner
            + jnp.einsum("shpn,snhd->sphd", d_score, k_part, preferred_element_type=jnp.float32)
            * scale,
            None,
        )

    inner, _ = lax.scan(visit, jnp.zeros((seqs, length, HEADS, HD), jnp.float32), jnp.arange(count))
    d_query = inner
    all_lse, all_delta = (
        lax.all_gather(lse, "seq", axis=1, tiled=True),
        lax.all_gather(delta, "seq", axis=1, tiled=True),
    )
    empty = jnp.zeros((seqs, length, HEADS, HD), jnp.float32)
    q_rows = lax.all_gather(query, "seq", axis=1, tiled=True)
    g_rows = lax.all_gather(d_att, "seq", axis=1, tiled=True)
    count = q_rows.shape[1] // length
    q_blocks = q_rows.reshape(seqs, count, length, HEADS, HD)
    g_blocks = g_rows.reshape(seqs, count, length, HEADS, HD)
    lse_rows = all_lse.reshape(seqs, count, length, HEADS)
    delta_rows = all_delta.reshape(seqs, count, length, HEADS)

    def visit(inner, index):
        d_key, d_value = inner
        q_part = q_blocks[:, index]
        g_part = g_blocks[:, index]
        scores = (
            jnp.einsum("snhd,sphd->shnp", q_part, heads_k, preferred_element_type=jnp.float32)
            * scale
        )
        probs = jnp.exp(scores - lse_rows[:, index].transpose(0, 2, 1)[..., None])
        d_value = d_value + jnp.einsum(
            "shnp,snhd->sphd",
            probs.astype(jnp.bfloat16),
            g_part,
            preferred_element_type=jnp.float32,
        )
        d_prob = jnp.einsum("snhd,sphd->shnp", g_part, heads_v, preferred_element_type=jnp.float32)
        d_score = (probs * (d_prob - delta_rows[:, index].transpose(0, 2, 1)[..., None])).astype(
            jnp.bfloat16
        )
        d_key = (
            d_key
            + jnp.einsum("shnp,snhd->sphd", d_score, q_part, preferred_element_type=jnp.float32)
            * scale
        )
        return ((d_key, d_value), None)

    inner, _ = lax.scan(visit, (empty, empty), jnp.arange(count))
    d_key, d_value = inner
    return (d_query, d_key, d_value)


def feed_inner(normed_two, w_up, vectors):
    upper = jnp.dot(normed_two, w_up, preferred_element_type=jnp.float32) + vectors[11:].reshape(-1)
    return (upper, jax.nn.gelu(upper).astype(jnp.bfloat16))


def layer_forward(rows, seqs, mats, vectors):
    w_qkv, w_out, w_up, w_down = mats
    normed = layer_norm(rows, vectors[1], vectors[2]).astype(jnp.bfloat16)
    bias = jnp.concatenate([vectors[9], jnp.zeros_like(vectors[9]), vectors[10]])
    qkv = (jnp.dot(normed, w_qkv, preferred_element_type=jnp.float32) + bias).astype(jnp.bfloat16)
    query = qkv[:, :D].reshape(seqs, -1, D)
    keys = qkv[:, D : 2 * D].reshape(seqs, -1, D)
    values = qkv[:, 2 * D :].reshape(seqs, -1, D)
    attended, lse = attention_forward(query, keys, values)
    att_low = attended.reshape(-1, D).astype(jnp.bfloat16)
    mid = rows + jnp.dot(att_low, w_out, preferred_element_type=jnp.float32) + vectors[7]
    normed_two = layer_norm(mid, vectors[3], vectors[4]).astype(jnp.bfloat16)
    upper, active = feed_inner(normed_two, w_up, vectors)
    out = mid + jnp.dot(active, w_down, preferred_element_type=jnp.float32) + vectors[8]
    saved = (upper, active)
    return (out, (rows, normed, query, keys, values, attended, lse, mid, normed_two, saved))


def layer_backward(d_out, kept, mats, vectors):
    rows, normed, query, keys, values, attended, lse, mid, normed_two, saved = kept
    w_qkv, w_out, w_up, w_down = mats
    upper, active = saved
    d_branch = d_out.astype(jnp.bfloat16)
    g_down = jnp.einsum("rf,rd->fd", active, d_branch, preferred_element_type=jnp.float32)
    d_active = jnp.einsum("rd,fd->rf", d_branch, w_down, preferred_element_type=jnp.float32)
    d_upper = jax.vjp(jax.nn.gelu, upper)[1](d_active)[0].astype(jnp.bfloat16)
    g_up = jnp.einsum("rd,rf->df", normed_two, d_upper, preferred_element_type=jnp.float32)
    d_normed_two = jnp.einsum("rf,df->rd", d_upper, w_up, preferred_element_type=jnp.float32)
    d_mid_norm, g_gain_two, g_shift_two = jax.vjp(layer_norm, mid, vectors[3], vectors[4])[1](
        d_normed_two
    )
    d_mid = d_out + d_mid_norm
    d_mid_low = d_mid.astype(jnp.bfloat16)
    att_low = attended.reshape(-1, D).astype(jnp.bfloat16)
    g_out = jnp.einsum("ra,rd->ad", att_low, d_mid_low, preferred_element_type=jnp.float32)
    d_att = jnp.einsum("rd,ad->ra", d_mid_low, w_out, preferred_element_type=jnp.float32).astype(
        jnp.bfloat16
    )
    seqs = query.shape[0]
    d_query, d_key, d_value = attention_backward(
        query, keys, values, attended, lse, d_att.reshape(seqs, -1, D)
    )
    d_qkv = jnp.concatenate(
        [d_query.reshape(-1, D), d_key.reshape(-1, D), d_value.reshape(-1, D)], 1
    ).astype(jnp.bfloat16)
    g_qkv = jnp.einsum("rd,re->de", normed, d_qkv, preferred_element_type=jnp.float32)
    d_normed = jnp.einsum("re,de->rd", d_qkv, w_qkv, preferred_element_type=jnp.float32)
    d_rows_norm, g_gain_one, g_shift_one = jax.vjp(layer_norm, rows, vectors[1], vectors[2])[1](
        d_normed
    )
    qkv_sums = jnp.sum(d_qkv.astype(jnp.float32), 0)
    small = (
        g_gain_one,
        g_shift_one,
        g_gain_two,
        g_shift_two,
        jnp.sum(d_mid_low.astype(jnp.float32), 0),
        jnp.sum(d_branch.astype(jnp.float32), 0),
        qkv_sums[:D],
        qkv_sums[2 * D :],
        jnp.sum(d_upper.astype(jnp.float32), 0),
    )
    return (d_mid + d_rows_norm, (g_qkv, g_out, g_up, g_down), small)


def loss_terms(pred, targets, seqs, length):
    strips = lax.axis_size("seq")
    cols = length // LAT_P
    nlat = 2 * LAT_P
    nlon = 2 * cols * strips
    all_seqs = seqs * lax.axis_size("batch")
    diff = pred.reshape(seqs, length, -1) - targets.astype(jnp.float32)
    grid = (
        diff.reshape(seqs, cols, LAT_P, VARS, 2, 2)
        .transpose(0, 3, 2, 4, 1, 5)
        .reshape(seqs, VARS, nlat, 2 * cols)
    )
    lat = ((jnp.arange(nlat, dtype=jnp.float32) + 0.5) / nlat - 0.5) * math.pi
    weight = jnp.cos(lat)
    weight = (weight / jnp.mean(weight))[None, None, :, None]
    column = lax.axis_index("seq") * (2 * cols) + jnp.arange(2 * cols, dtype=jnp.int32)
    modes = jnp.arange(KMODES, dtype=jnp.int32)
    angle = (column[:, None] * modes[None] % nlon).astype(jnp.float32) * (2.0 * math.pi / nlon)
    cosine = jnp.cos(angle)
    sine = jnp.sin(angle)
    part_c = jnp.einsum("svrc,ck->svrk", grid, cosine, precision=HIGH)
    part_s = jnp.einsum("svrc,ck->svrk", grid, sine, precision=HIGH)
    full_c, full_s = lax.psum((part_c, part_s), "seq")
    mse_count = all_seqs * VARS * nlat * nlon
    dft_count = nlon * all_seqs * VARS * nlat * KMODES
    mse = jnp.sum(weight * grid * grid) / mse_count
    spectral = SPECTRAL * jnp.sum(weight * (full_c * full_c + full_s * full_s)) / dft_count
    first = (lax.axis_index("seq") == 0).astype(jnp.float32)
    back_wave = jnp.einsum("svrk,ck->svrc", full_c, cosine, precision=HIGH) + jnp.einsum(
        "svrk,ck->svrc", full_s, sine, precision=HIGH
    )
    d_grid = 2.0 * weight * grid / mse_count + 2.0 * SPECTRAL / dft_count * weight * back_wave
    d_pred = (
        d_grid.reshape(seqs, VARS, LAT_P, 2, cols, 2)
        .transpose(0, 4, 2, 1, 3, 5)
        .reshape(seqs * length, VARS * 4)
    )
    return (d_pred, mse + first * spectral)


def adam(value, first, second, grad, rate):
    first = BETA_ONE * first + (1.0 - BETA_ONE) * grad
    second = BETA_TWO * second + (1.0 - BETA_TWO) * grad * grad
    step = first / (1.0 - BETA_ONE**STEP) / (jnp.sqrt(second / (1.0 - BETA_TWO**STEP)) + ADAM_EPS)
    return (first, second, value - rate * (step + DECAY * value))


def shards(
    inputs,
    targets,
    var_ids,
    lead_ids,
    block_order,
    blocks,
    block_momentum,
    left_stats,
    right_stats,
    left_roots,
    right_roots,
    embed_params,
    embed_first,
    embed_second,
    vectors,
    vector_first,
    vector_second,
    head_weight,
    head_first,
    head_second,
):
    seqs, length, _ = inputs.shape
    size = blocks.shape[-1]
    low_blocks = blocks.astype(jnp.bfloat16)
    stack = lax.all_gather(low_blocks, ("seq", "batch"), axis=0, tiled=True)
    natural = jnp.zeros_like(stack).at[block_order].set(stack)
    mats = split_matrices(natural)
    head_low = head_weight.astype(jnp.bfloat16)
    pick = (var_ids[..., None] == jnp.arange(VARS, dtype=jnp.int32)[None, None]).astype(jnp.float32)
    lead_pick = (lead_ids[:, None] == jnp.arange(LEADS, dtype=jnp.int32)[None]).astype(jnp.float32)
    tok_sel = jnp.einsum(
        "svw,wcd->svcd", pick, embed_params[: VARS * 4].reshape(VARS, 4, D), precision=HIGH
    )
    emb_sel = jnp.einsum("svw,wd->svd", pick, embed_params[VARS * 4 : VARS * 5], precision=HIGH)
    lead_rows = jnp.dot(lead_pick, embed_params[VARS * 5 :], precision=HIGH)
    pixels = inputs.astype(jnp.float32).reshape(seqs, length, VARS, 4)

    def embed_local(tok_part, emb_part, query, lead_part):
        return embed_patches(pixels, tok_part, emb_part, query, lead_part)

    stream, embed_back = jax.vjp(embed_local, tok_sel, emb_sel, vectors[0], lead_rows)
    out, kept = layer_forward(stream.reshape(-1, D), seqs, mats, vectors)
    final_rows, final_back = jax.vjp(layer_norm, out, vectors[5], vectors[6])
    final = final_rows.astype(jnp.bfloat16)
    pred = jnp.dot(final, head_low, preferred_element_type=jnp.float32)
    d_pred, loss_part = loss_terms(pred, targets, seqs, length)
    d_low = d_pred.astype(jnp.bfloat16)
    g_head = jnp.einsum("rd,ro->do", final, d_low, preferred_element_type=jnp.float32)
    d_final = jnp.einsum("ro,do->rd", d_low, head_low, preferred_element_type=jnp.float32)
    d_out, g_gain_final, g_shift_final = final_back(d_final)
    d_rows, matrix_grads, small = layer_backward(d_out, kept, mats, vectors)
    d_tok, d_emb, d_query, d_lead = embed_back(d_rows.reshape(seqs, length, D))
    g_embed = jnp.concatenate(
        [
            jnp.einsum("svw,svcd->wcd", pick, d_tok, precision=HIGH).reshape(VARS * 4, D),
            jnp.einsum("svw,svd->wd", pick, d_emb, precision=HIGH),
            jnp.einsum("sl,sd->ld", lead_pick, d_lead, precision=HIGH),
        ]
    )
    g_gain_one, g_shift_one, g_gain_two, g_shift_two, b_out, b_down, b_query, b_value, b_up = small
    g_vectors = jnp.concatenate(
        [
            jnp.stack(
                [
                    d_query,
                    g_gain_one,
                    g_shift_one,
                    g_gain_two,
                    g_shift_two,
                    g_gain_final,
                    g_shift_final,
                    b_out,
                    b_down,
                    b_query,
                    b_value,
                ]
            ),
            b_up.reshape(-1, D),
        ]
    )
    slot_grads = jnp.concatenate([to_blocks(grad, size) for grad in matrix_grads])[block_order]
    owned = lax.psum_scatter(slot_grads, ("seq", "batch"), scatter_dimension=0, tiled=True)
    g_embed, g_vectors, g_head, loss_total = lax.psum(
        (g_embed, g_vectors, g_head, loss_part), ("seq", "batch")
    )
    rest_squares = (
        jnp.sum(g_embed * g_embed) + jnp.sum(g_vectors * g_vectors) + jnp.sum(g_head * g_head)
    )
    grad_norm = jnp.sqrt(lax.psum(jnp.sum(owned * owned), ("seq", "batch")) + rest_squares)
    clip = CLIP_NORM / jnp.maximum(grad_norm, CLIP_NORM)
    owned = owned * clip
    new_momentum = BETA_ONE * block_momentum + (1.0 - BETA_ONE) * owned
    new_left = BETA_TWO * left_stats + (1.0 - BETA_TWO) * jnp.einsum(
        "bij,bkj->bik", owned, owned, precision=HIGH
    )
    new_right = BETA_TWO * right_stats + (1.0 - BETA_TWO) * jnp.einsum(
        "bji,bjk->bik", owned, owned, precision=HIGH
    )
    direction = jnp.einsum(
        "bij,bjk->bik",
        jnp.einsum("bij,bjk->bik", left_roots, new_momentum, precision=HIGH),
        right_roots,
        precision=HIGH,
    )
    new_blocks = blocks - SHAMPOO_RATE * (direction + DECAY * blocks)
    e_one, e_two, e_new = adam(embed_params, embed_first, embed_second, g_embed * clip, EMBED_RATE)
    v_one, v_two, v_new = adam(vectors, vector_first, vector_second, g_vectors * clip, VECTOR_RATE)
    h_one, h_two, h_new = adam(head_weight, head_first, head_second, g_head * clip, HEAD_RATE)
    return (
        loss_total,
        grad_norm,
        new_blocks,
        new_momentum,
        new_left,
        new_right,
        e_one,
        e_two,
        e_new,
        v_one,
        v_two,
        v_new,
        h_one,
        h_two,
        h_new,
    )


SHARE = 24
PIECE = 6
MAIN = ("zxy", "zyx", "xzy", "yzx")
SMALL = ("xyz", "yxz")
TAIL = ("zxy", "zyx")
GATHER_ORDER = (
    (0, 0, 0, 3), (3, 0, 0, 3), (1, 0, 0, 3), (2, 0, 0, 3), (0, 1, 0, 3), (1, 0, 0, 2), (0, 0, 0, 2), (1, 0, 0, 1),
    (1, 0, 1, 3), (0, 0, 0, 1), (3, 0, 0, 2), (0, 0, 1, 3), (3, 0, 1, 3), (2, 1, 0, 3), (1, 1, 0, 3), (2, 0, 0, 2),
    (1, 1, 1, 3), (0, 0, 0, 0), (1, 1, 0, 2), (2, 0, 1, 3), (1, 0, 1, 2), (2, 1, 0, 2), (3, 0, 1, 2), (0, 1, 0, 2),
    (2, 0, 0, 1), (3, 1, 0, 3), (2, 0, 0, 0), (0, 0, 1, 2), (0, 1, 1, 3), (2, 0, 1, 2), (3, 0, 0, 1), (3, 1, 1, 3),
    (0, 1, 0, 1), (2, 1, 1, 3), (3, 1, 0, 2), (1, 1, 0, 1), (2, 1, 0, 0), (1, 0, 0, 0), (3, 0, 0, 0), (1, 0, 1, 1),
    (0, 1, 1, 2), (0, 0, 1, 1), (3, 0, 1, 0), (2, 1, 1, 2), (2, 1, 0, 1), (0, 1, 1, 1), (3, 1, 0, 1), (2, 0, 1, 1),
    (0, 1, 0, 0), (3, 0, 1, 1), (1, 1, 1, 2), (1, 0, 1, 0), (3, 1, 0, 0), (1, 1, 0, 0), (0, 0, 1, 0), (3, 1, 1, 1),
    (3, 1, 1, 0), (1, 1, 1, 0), (2, 1, 1, 1), (2, 1, 1, 0), (1, 1, 1, 1), (3, 1, 1, 2), (2, 0, 1, 0), (0, 1, 1, 0),
)
REDUCE_PLAN = (
    (0, 4, 0, 0, 1), (0, 5, 1, 1, 0), (0, 3, 1, 1, 0), (0, 5, 0, 1, 1), (0, 2, 0, 1, 0), (0, 5, 1, 0, 0), (0, 4, 1, 0, 0),
    (0, 2, 1, 1, 0), (0, 4, 1, 1, 0), (0, 5, 0, 0, 0), (0, 2, 1, 1, 1), (0, 5, 1, 1, 1), (0, 1, 1, 1, 0), (0, 4, 1, 0, 1),
    (0, 5, 1, 0, 2), (0, 4, 0, 1, 0), (0, 4, 1, 0, 2), (0, 3, 1, 1, 2), (0, 0, 1, 1, 1), (0, 5, 1, 1, 2), (0, 4, 1, 1, 1),
    (3, 0, 0, 0, 0), (0, 4, 1, 1, 2), (0, 3, 1, 0, 1), (0, 5, 1, 0, 1), (0, 4, 0, 1, 2), (3, 0, 0, 0, 0), (0, 5, 0, 1, 0),
    (3, 0, 0, 0, 0), (3, 0, 0, 0, 0), (0, 1, 1, 1, 1), (0, 4, 0, 1, 1), (0, 3, 1, 1, 1), (0, 3, 0, 1, 0), (0, 2, 1, 1, 2),
    (0, 0, 1, 1, 2), (0, 5, 0, 1, 2), (0, 4, 1, 1, 3), (0, 2, 1, 0, 0), (0, 3, 0, 1, 2), (3, 0, 0, 0, 0), (0, 0, 1, 1, 0),
    (3, 0, 0, 0, 0), (0, 0, 1, 0, 1), (0, 1, 1, 0, 1), (0, 5, 1, 1, 3), (0, 0, 1, 1, 3), (0, 2, 1, 0, 1), (3, 0, 0, 0, 0),
    (0, 5, 1, 0, 3), (3, 0, 0, 0, 0), (3, 0, 0, 0, 0), (3, 0, 0, 0, 0), (3, 0, 0, 0, 0), (0, 0, 0, 1, 1), (0, 3, 1, 0, 0),
    (3, 0, 0, 0, 0), (0, 5, 0, 0, 2), (3, 0, 0, 0, 0), (0, 4, 0, 0, 0), (0, 4, 0, 1, 3), (0, 2, 1, 0, 2), (3, 0, 0, 0, 0),
    (0, 2, 1, 1, 3), (0, 1, 1, 1, 3), (0, 5, 0, 0, 1), (0, 1, 1, 0, 0), (0, 1, 1, 1, 2), (0, 0, 1, 0, 0), (0, 3, 0, 0, 1),
    (3, 0, 0, 0, 0), (0, 5, 0, 1, 3), (3, 0, 0, 0, 0), (0, 1, 0, 1, 0), (0, 2, 0, 0, 0), (0, 0, 0, 1, 0), (0, 3, 1, 1, 3),
    (3, 0, 0, 0, 0), (0, 1, 0, 1, 1), (0, 0, 1, 0, 2), (0, 4, 1, 0, 3), (0, 3, 0, 1, 1), (0, 0, 0, 1, 2), (0, 1, 1, 0, 2),
    (0, 2, 0, 1, 1), (0, 0, 0, 0, 1), (0, 2, 0, 1, 2), (0, 2, 1, 0, 3), (0, 3, 1, 0, 2), (0, 1, 0, 0, 0), (3, 0, 0, 0, 0),
    (0, 1, 0, 1, 2), (3, 0, 0, 0, 0), (0, 3, 0, 0, 0), (0, 2, 0, 1, 3), (0, 0, 1, 0, 3), (0, 1, 1, 0, 3), (0, 3, 1, 0, 3),
    (0, 5, 0, 0, 3), (0, 0, 0, 0, 0), (0, 0, 0, 1, 3), (3, 0, 0, 0, 0), (0, 1, 0, 1, 3), (0, 1, 0, 0, 1), (3, 0, 0, 0, 0),
    (3, 0, 0, 0, 0), (3, 0, 0, 0, 0), (3, 0, 0, 0, 0), (0, 2, 0, 0, 1), (1, 1, 0, 0, 3), (0, 4, 0, 0, 2), (0, 2, 0, 0, 2),
    (0, 4, 0, 0, 3), (1, 0, 0, 0, 3), (0, 0, 0, 0, 2), (0, 1, 0, 0, 2), (0, 3, 0, 1, 3), (0, 3, 0, 0, 2), (1, 1, 0, 0, 2),
    (0, 2, 0, 0, 3), (2, 2, 0, 0, 0), (1, 0, 0, 0, 2), (2, 2, 1, 0, 0), (0, 0, 0, 0, 3), (2, 2, 2, 0, 0), (2, 0, 0, 0, 0),
    (2, 2, 3, 0, 0), (2, 2, 4, 0, 0), (2, 0, 1, 0, 0), (2, 2, 5, 0, 0), (0, 1, 0, 0, 3), (2, 1, 0, 0, 0), (1, 1, 0, 1, 3),
    (2, 0, 2, 0, 0), (1, 0, 0, 1, 3), (2, 0, 3, 0, 0), (2, 1, 1, 0, 0), (2, 1, 2, 0, 0), (1, 0, 0, 0, 1), (2, 1, 3, 0, 0),
    (2, 0, 4, 0, 0), (1, 1, 0, 0, 0), (2, 1, 4, 0, 0), (1, 0, 0, 0, 0), (2, 0, 5, 0, 0), (1, 1, 1, 0, 2), (1, 1, 1, 0, 3),
    (1, 1, 0, 0, 1), (1, 1, 0, 1, 2), (1, 0, 1, 0, 1), (1, 0, 0, 1, 2), (1, 0, 0, 1, 1), (0, 3, 0, 0, 3), (1, 0, 1, 0, 2),
    (2, 3, 0, 0, 0), (1, 1, 0, 1, 1), (1, 1, 1, 1, 3), (1, 0, 1, 0, 0), (1, 0, 1, 0, 3), (2, 3, 1, 0, 0), (1, 1, 0, 1, 0),
    (1, 0, 1, 1, 1), (2, 3, 2, 0, 0), (2, 3, 3, 0, 0), (2, 1, 5, 0, 0), (2, 3, 4, 0, 0), (1, 1, 1, 0, 1), (1, 1, 1, 1, 1),
    (2, 3, 5, 0, 0), (1, 0, 1, 1, 0), (1, 1, 1, 0, 0), (1, 0, 0, 1, 0), (1, 1, 1, 1, 0), (1, 0, 1, 1, 3), (1, 1, 1, 1, 2),
    (1, 0, 1, 1, 2),
)

class Place:
    def __init__(self):
        s = lax.axis_index("seq")
        self.y = lax.axis_index("batch")
        self.core = lax.rem(s, 2)
        self.x = lax.rem(s // 2, 2)
        self.z = s // 4
        self.s = s

    def chip(self, z, x, y):
        return (z * 2 + x) * 2 + y

    def linear(self, z, x, y):
        return ((z * 2 + x) * 2 + self.core) * 2 + y

    def device(self, z, x, y):
        return ((z * 2 + x) * 2 + self.core, y)

    def sibling(self):
        return (self.s + 1 - 2 * self.core, self.y)

    def far(self, rank):
        z = self.z
        if rank == 3:
            return z
        if rank == 2:
            return z + 1 - 2 * lax.rem(z, 2)
        low = z // 2
        return (3 - 3 * low) if rank == 0 else (2 - low)

    def flipped(self, dx, dy):
        x = self.x if dx == 0 else 1 - self.x
        y = self.y if dy == 0 else 1 - self.y
        return x, y

    def greet(self):
        barrier = pltpu.get_barrier_semaphore()

        def hail(o, _):
            peer = lax.rem(self.s + o, NSEQ)
            pl.semaphore_signal(barrier, inc=1, device_id=(peer, self.y), device_id_type=MESH_ID)
            return _

        lax.fori_loop(1, NSEQ, hail, 0)
        pl.semaphore_signal(
            barrier, inc=1, device_id=(self.s, 1 - self.y), device_id_type=MESH_ID
        )
        pl.semaphore_wait(barrier, NSEQ)


def last_move(order, dx, dy, rank):
    found = -1
    for i, c in enumerate(order):
        if (c == "x" and dx) or (c == "y" and dy) or (c == "z" and rank != 3):
            found = i
    return found


def sends_before(order, axis):
    count = 1
    for c in order:
        if c == axis:
            return count
        count *= 4 if c == "z" else 2
    return count


def drain(place, orders, total, sem, hops):
    count = {c: sum(sends_before(order, c) for order in orders) for c in "xyz"}

    def finish(i, pieces):
        ref = total(pieces)
        pltpu.make_async_remote_copy(
            ref, ref, sem.at[i], sem.at[i], place.sibling(), MESH_ID
        ).wait_send()

    finish(0, count["x"])
    finish(1, count["y"])
    for z in range(4):
        for i in (2, 3):
            if hops[i - 2][z]:

                @pl.when(place.z == z)
                def _(i=i, z=z):
                    finish(i, count["z"] * hops[i - 2][z])


GATHER_HOPS = ((1, 2, 3, 0), (0, 3, 2, 1))
REDUCE_HOPS = ((3, 2, 1, 0), (0, 1, 2, 3))


def gather_steps(place, orders, steps, piece, total, recv, send, sib_send, sib_recv):
    z = place.z
    parts = len(orders)

    def copy(ref, device, send_sem, recv_sem):
        return pltpu.make_async_remote_copy(ref, ref, send_sem, recv_sem, device, MESH_ID)

    for number, (part, dx, dy, rank) in enumerate(steps):
        order = orders[part]
        tz = place.far(rank)
        sx, sy = place.flipped(dx, dy)
        ref = piece(place.linear(tz, sx, sy) * parts + part)
        landed = recv.at[part, place.chip(tz, sx, sy)]
        own = dx == 0 and dy == 0 and rank == 3
        if not own:
            copy(ref, place.sibling(), landed, landed).wait_recv()
        last = last_move(order, dx, dy, rank)
        if last >= 0 and order[last] == "z" and rank != 3:
            up = (z > tz).astype(jnp.int32)
            nz = z + 2 * up - 1

            @pl.when(jnp.logical_and(nz >= 0, nz <= 3))
            def _():
                copy(ref, place.device(nz, place.x, place.y), send.at[3 - up], landed).start()

        for c in order[last + 1 :]:
            if c == "x":
                copy(ref, place.device(z, 1 - place.x, place.y), send.at[0], landed).start()
            elif c == "y":
                copy(ref, place.device(z, place.x, 1 - place.y), send.at[1], landed).start()
            else:

                @pl.when(z < 3)
                def _():
                    copy(ref, place.device(z + 1, place.x, place.y), send.at[2], landed).start()

                @pl.when(z > 0)
                def _():
                    copy(ref, place.device(z - 1, place.x, place.y), send.at[3], landed).start()

        copy(ref, place.sibling(), sib_send.at[0], sib_recv.at[0]).start()
        yield number
    drain(place, orders, total, send, GATHER_HOPS)
    whole = total(16 * parts)
    copy(whole, place.sibling(), sib_send.at[0], sib_recv.at[0]).wait()


def radix(order, stop, dx, dy, tz):
    index = 0
    size = 1
    for c in order[: order.index(stop[0])]:
        value, base = {"x": (dx, 2), "y": (dy, 2), "z": (tz, 4)}[c]
        index = index * base + value
        size *= base
    if stop[0] == "z":
        index = index * 3 + (tz if stop == "z+" else tz - 1)
        size *= 3
    return index, size


def landing_base(orders):
    base = {}
    at = 0
    for axis in ("x", "y", "z+", "z-"):
        for part, order in enumerate(orders):
            base[(axis, part)] = at
            at += radix(order, axis, 0, 0, 0)[1]
    return base, at


def reduce_step(place, orders, base, step, own_piece, add_landed, land, recv, out, send, keep, offset):
    part, dx, dy, rank = step
    order = orders[part]
    z = place.z
    tz = place.far(rank)
    tx, ty = place.flipped(dx, dy)
    chip = place.chip(tz, tx, ty)
    root = dx == 0 and dy == 0 and rank == 3
    last = last_move(order, dx, dy, rank)
    out_at = part * 16 + chip
    own_piece(part + offset, place.linear(tz, tx, ty), chip, out_at)

    def slot(axis):
        return base[(axis, part)] + radix(order, axis, dx, dy, tz)[0]

    def take(index):
        ref = land.at[index]
        sem = recv.at[index]
        pltpu.make_async_remote_copy(ref, ref, sem, sem, place.sibling(), MESH_ID).wait_recv()
        add_landed(part + offset, index)

    if last >= 0 and order[last] == "z" and rank != 3:
        up = (z > tz).astype(jnp.int32)
        nz = z + 2 * up - 1
        plus = slot("z+")
        minus = slot("z-")

        @pl.when(jnp.logical_and(nz >= 0, nz <= 3))
        def _():
            take(up * plus + (1 - up) * minus)

    for c in order[last + 1 :]:
        if c == "z":

            @pl.when(z < 3)
            def _():
                take(slot("z+"))

            @pl.when(z > 0)
            def _():
                take(slot("z-"))

        else:
            take(slot(c))
    keep(part + offset, out_at, root)
    if root:
        return
    ref = out.at[out_at]

    def push(device, index, direction):
        pltpu.make_async_remote_copy(
            ref, land.at[index], send.at[direction], recv.at[index], device, MESH_ID
        ).start()

    axis = order[last]
    if axis == "x":
        index = base[("x", part)] + radix(order, "x", 0, dy, tz)[0]
        push(place.device(z, 1 - place.x, place.y), index, 0)
    elif axis == "y":
        index = base[("y", part)] + radix(order, "y", dx, 0, tz)[0]
        push(place.device(z, place.x, 1 - place.y), index, 1)
    else:
        down = (z > tz).astype(jnp.int32)
        index = down * slot("z+") + (1 - down) * slot("z-")
        push(place.device(z + 1 - 2 * down, place.x, place.y), index, 2 + down)


TOK = 128
NSEQ = 16
BLOCK = 128
N_LEFT = 56
N_RIGHT = 72
QCH = 256
LOG2E = math.log2(math.e)
MESH_ID = pl.DeviceIdType.MESH
NT = (((1,), (1,)), ((), ()))
TN = (((0,), (0,)), ((), ()))
NN = (((1,), (0,)), ((), ()))
BF = jnp.bfloat16
F32 = jnp.float32
VM = pltpu.VMEM


def mm(a, b, dims=NN):
    return lax.dot_general(a, b, dims, preferred_element_type=F32)


def mmh(a, b, dims=NN):
    return lax.dot_general(a, b, dims, precision=HIGH, preferred_element_type=F32)


def flip(x):
    return jnp.swapaxes(x.astype(F32), 0, 1).astype(x.dtype)


def normalise(x):
    mean = jnp.mean(x, -1, keepdims=True)
    centred = x - mean
    rstd = lax.rsqrt(jnp.mean(centred * centred, -1, keepdims=True) + EPS)
    return centred * rstd, rstd


def normalise_back(grad, unit, rstd, gain):
    inner = grad * gain
    return rstd * (
        inner
        - jnp.mean(inner, -1, keepdims=True)
        - unit * jnp.mean(inner * unit, -1, keepdims=True)
    )


def column_sum(x):
    return jnp.sum(x, 0, keepdims=True)


GELU_K = math.sqrt(2.0 / math.pi)


def gelu_value(x):
    return 0.5 * x * (1.0 + jnp.tanh(GELU_K * (x + 0.044715 * x * x * x)))


def gelu_slope(x):
    t = jnp.tanh(GELU_K * (x + 0.044715 * x * x * x))
    return 0.5 * (1.0 + t) + 0.5 * x * (1.0 - t * t) * GELU_K * (1.0 + 3.0 * 0.044715 * x * x)


def layer_kernel(
    place_ref,
    lead_ref,
    blocks_ref,
    ids_ref,
    pix_ref,
    goal_ref,
    emb_ref,
    vec_ref,
    head_ref,
    wlat_ref,
    left_hbm,
    right_hbm,
    small_ref,
    stack,
    left,
    right,
    slab,
    qkv_t,
    out_t,
    out_t32,
    lse,
    o_in,
    d_slab,
    do_t,
    dqkv_t,
    dqkv_in,
    k_row,
    v_row,
    q_row,
    do_row,
    s_scr,
    dq_acc,
    h0_s,
    n1_s,
    xp_s,
    a_s,
    mid_s,
    up_s,
    act_s,
    acc,
    wave,
    wave_in,
    wave_tile,
    wave_all,
    pix_s,
    goal_s,
    head_s,
    gvec,
    t_recv,
    t_send,
    t_sib_send,
    t_sib_recv,
    a_send,
    a_recv,
    in_sem,
    g_local,
    g_send,
    g_recv,
):
    s = lax.axis_index("seq")
    b = lax.axis_index("batch")
    place = Place()
    sibling = s + 1 - 2 * place.core

    loads = []
    for i, (src, dst) in enumerate(((pix_ref, pix_s), (goal_ref, goal_s), (head_ref, head_s))):
        c = pltpu.make_async_copy(src, dst, in_sem.at[i])
        c.start()
        loads.append(c)
    mine = place.linear(place.z, place.x, place.y)
    stack[pl.ds(mine * SHARE, SHARE)] = blocks_ref[...].astype(BF)
    place.greet()

    for number in gather_steps(
        place,
        MAIN,
        GATHER_ORDER,
        lambda i: stack.at[pl.ds(i * PIECE, PIECE)],
        lambda n: stack.at[pl.ds(0, n * PIECE)],
        t_recv,
        t_send,
        t_sib_send,
        t_sib_recv,
    ):
        if number == 3:
            loads[0].wait()
            embed_forward(pix_s, ids_ref, lead_ref, emb_ref, vec_ref, h0_s, n1_s, xp_s, a_s)

    def block(begin, across, r, c):
        return stack[place_ref[begin + r * across + c]]

    def two_columns(begin, across, pair):
        return jnp.concatenate(
            [
                jnp.concatenate(
                    [block(begin, across, r, 2 * pair), block(begin, across, r, 2 * pair + 1)], 1
                )
                for r in range(8)
            ],
            0,
        )

    def two_rows(begin, pair):
        return jnp.concatenate(
            [
                jnp.concatenate([block(begin, 8, 2 * pair + r, c) for c in range(8)], 1)
                for r in range(2)
            ],
            0,
        )

    at_qkv, at_o, at_up, at_down = 0, 192, 256, 512
    share = []

    def share_group(index, stage, target, begin, count):
        part = pl.ds(begin, count)
        c = pltpu.make_async_copy(stage.at[part], target.at[0, part], g_local.at[index])
        c.start()
        r = pltpu.make_async_remote_copy(
            src_ref=stage.at[part],
            dst_ref=target.at[1, part],
            send_sem=g_send.at[index],
            recv_sem=g_recv.at[index],
            device_id=(sibling, b),
            device_id_type=MESH_ID,
        )
        r.start()
        share.append((c, r))

    def exchange(which, src_at, dst_at):
        def copy(o):
            peer = lax.rem(s + o, NSEQ)
            return pltpu.make_async_remote_copy(
                src_ref=src_at(peer),
                dst_ref=dst_at(s),
                send_sem=a_send.at[which, o],
                recv_sem=a_recv.at[which, o],
                device_id=(peer, b),
                device_id_type=MESH_ID,
            )

        def begin(o, _):
            copy(o).start()
            return _

        def finish(o, _):
            copy(o).wait()
            return _

        def start():
            lax.fori_loop(1, NSEQ, begin, 0)

        def start_to(peer):
            @pl.when(peer != s)
            def _():
                copy(lax.rem(peer - s + NSEQ, NSEQ)).start()

        def wait():
            lax.fori_loop(1, NSEQ, finish, 0)

        return start, wait, start_to

    def lanes(i, size):
        return pl.ds(pl.multiple_of(i * size, size), size)

    def rows_at(i, size):
        return pl.ds(pl.multiple_of(i * size, size), size)

    n1 = n1_s[...]
    waits = {}
    for which in (1, 0, 2):

        def qkv_tile(t, _, which=which):
            piece = mm(n1, two_columns(at_qkv, 24, 4 * which + t))
            if which != 1:
                piece = piece + vec_ref[9 + which // 2 : 10 + which // 2, lanes(t, 256)]
            piece = piece.astype(BF)
            for k in range(2):
                turned = flip(piece[:, k * BLOCK : (k + 1) * BLOCK])
                for half in range(2):
                    slab[4 * t + 2 * k + half, which * HD : (which + 1) * HD, :] = turned[
                        half * HD : (half + 1) * HD
                    ]
            return _

        lax.fori_loop(0, 4, qkv_tile, 0)
        part = pl.ds(which * HD, HD)
        start, waits[which], _ = exchange(
            which,
            lambda p, part=part: slab.at[p, part],
            lambda p, part=part: qkv_t.at[part, lanes(p, TOK)],
        )
        start()
    qkv_t[:, lanes(s, TOK)] = slab[s]
    for k in range(8):
        left[k] = flip(n1[:, k * BLOCK : (k + 1) * BLOCK])

    scale2 = LOG2E / math.sqrt(HD)

    def turn_rows(source, begin, target):
        def one(t, _):
            target[rows_at(t, TOK), :] = flip(source[begin : begin + HD, lanes(t, TOK)])
            return _

        lax.fori_loop(0, NSEQ, one, 0)

    waits[1]()
    turn_rows(qkv_t, HD, k_row)
    waits[0]()
    tiles = (NSEQ * TOK) // QCH
    start, wait_o, send_o = exchange(
        3, lambda p: out_t.at[:, lanes(p, TOK)], lambda p: o_in.at[p]
    )

    def forward_chunk(i, _):
        c = lax.rem(i + s // 2, tiles)
        part = lanes(c, QCH)
        q_part = qkv_t[0:HD, part]
        top = None
        for t in range(tiles):
            tile = slice(t * QCH, (t + 1) * QCH)
            scores = mm(k_row[tile, :], q_part)
            s_scr[tile, :] = scores
            best = jnp.max(scores, 0, keepdims=True)
            top = best if top is None else jnp.maximum(top, best)
        top = top * scale2

        @pl.when(i == 0)
        def _():
            waits[2]()

        total = jnp.zeros((1, QCH), F32)
        mixed = jnp.zeros((HD, QCH), F32)
        for t in range(2):
            tile = slice(4 * t * QCH, (4 * t + 4) * QCH)
            probs = jnp.exp2(s_scr[tile, :] * scale2 - top)
            total = total + jnp.sum(probs, 0, keepdims=True)
            mixed = mixed + mm(qkv_t[2 * HD : 3 * HD, tile], probs.astype(BF))
        mixed = mixed / total
        lse[c] = top + jnp.log2(total)
        out_t32[:, part] = mixed
        out_t[:, part] = mixed.astype(BF)
        send_o(2 * c)
        send_o(2 * c + 1)
        return 0

    lax.fori_loop(0, tiles, forward_chunk, 0)
    share_group(0, left, left_hbm, 0, 8)
    o_in[s] = out_t[:, lanes(s, TOK)]
    turn_rows(qkv_t, 0, q_row)
    turn_rows(qkv_t, 2 * HD, v_row)
    wait_o()

    parts = []
    for k in range(8):
        pair = jnp.concatenate([o_in[2 * k], o_in[2 * k + 1]], 0)
        left[8 + k] = pair
        parts.append(flip(pair))
    share_group(1, left, left_hbm, 8, 8)
    o_low = jnp.concatenate(parts, 1)

    def out_tile(t, _):
        part = lanes(t, 256)
        mid_s[:, part] = h0_s[:, part] + (
            mm(o_low, two_columns(at_o, 8, t)) + vec_ref[7:8, part]
        )
        return _

    lax.fori_loop(0, 4, out_tile, 0)
    mid = mid_s[...]
    unit, _ = normalise(mid)
    n2 = (unit * vec_ref[3:4, :] + vec_ref[4:5, :]).astype(BF)
    acc[...] = mid + vec_ref[8:9, :]

    def up_tile(t, _):
        part = lanes(t, 256)
        bias = vec_ref[pl.ds(11 + t // 4, 1), lanes(lax.rem(t, 4), 256)]
        upper = mm(n2, two_columns(at_up, 32, t)) + bias
        up_s[:, part] = upper
        active = gelu_value(upper).astype(BF)
        act_s[:, part] = active
        acc[...] += mm(active, two_rows(at_down, t))
        return _

    lax.fori_loop(0, 16, up_tile, 0)

    unit_f, rstd_f = normalise(acc[...])
    final = (unit_f * vec_ref[5:6, :] + vec_ref[6:7, :]).astype(BF)
    loads[2].wait()
    head = head_s[...].astype(BF)
    loads[1].wait()
    diff = mm(final, head, NT) - jnp.swapaxes(goal_s[0].astype(F32), 0, 1)
    wave[...] = jnp.concatenate(
        [diff[0:64] + diff[64:128], jnp.zeros((64, 2 * BLOCK - HOUT), F32)], 1
    )

    def tile_of(ref, j):
        return ref.at[
            pl.ds(pl.multiple_of(j // 2 * 8, 8), 8),
            pl.ds(pl.multiple_of(lax.rem(j, 2) * BLOCK, BLOCK), BLOCK),
        ]

    start, wait, _ = exchange(7, lambda p: tile_of(wave, p), lambda p: wave_in.at[p])
    start()
    wave_in[s] = tile_of(wave, s)[...]
    for k in range(8):
        left[16 + k] = flip(n2[:, k * BLOCK : (k + 1) * BLOCK])
    share_group(2, left, left_hbm, 16, 8)
    wait()
    tile = wave_in[0]
    for k in range(1, NSEQ):
        tile = tile + wave_in[k]
    wave_tile[...] = tile
    start, wait, _ = exchange(8, lambda p: wave_tile, lambda p: tile_of(wave_all, p))
    start()
    tile_of(wave_all, s)[...] = tile

    def turn_active(k, _):
        left[24 + k] = flip(act_s[:, lanes(k, BLOCK)])
        return _

    lax.fori_loop(0, 12, turn_active, 0)
    wait()
    total_wave = wave_all[:, 0:HOUT]
    one = lax.broadcasted_iota(jnp.int32, (HOUT, HOUT), 0)
    two = lax.broadcasted_iota(jnp.int32, (HOUT, HOUT), 1)
    swap = (one == two + 1 - 2 * (two % 2)).astype(F32)
    other = mmh(total_wave, swap)
    weight = wlat_ref[...]
    square = jnp.sum(weight * diff * diff, keepdims=True)
    cross = jnp.sum(weight[0:64] * total_wave * other, keepdims=True) * (1.0 / NSEQ)
    loss = square * (1.0 / MSE_COUNT) + (SPECTRAL / DFT_COUNT) * (float(KMODES) * square + cross)
    other2 = jnp.concatenate([other, other], 0)
    d_pred = weight * (
        (2.0 / MSE_COUNT) * diff + (2.0 * SPECTRAL / DFT_COUNT) * (float(KMODES) * diff + other2)
    )
    d_low = d_pred.astype(BF)
    put_head(small_ref, mm(d_low, final, TN), loss)
    d_final = mm(d_low, head)
    gvec[5:6, :] = column_sum(d_final * unit_f)
    gvec[6:7, :] = column_sum(d_final)
    d_out = normalise_back(d_final, unit_f, rstd_f, vec_ref[5:6, :])
    d_branch = d_out.astype(BF)
    gvec[8:9, :] = column_sum(d_branch.astype(F32))
    for k in range(8):
        right[64 + k] = d_branch[:, k * BLOCK : (k + 1) * BLOCK]
    share_group(4, right, right_hbm, 64, 8)
    acc[...] = jnp.zeros_like(acc)

    def down_tile(t, _):
        part = lanes(t, 256)
        d_active = mm(d_branch, two_rows(at_down, t), NT)
        d_upper = (d_active * gelu_slope(up_s[:, part])).astype(BF)
        gvec[pl.ds(11 + t // 4, 1), lanes(lax.rem(t, 4), 256)] = column_sum(d_upper.astype(F32))
        for k in range(2):
            right[32 + 2 * t + k] = d_upper[:, k * BLOCK : (k + 1) * BLOCK]
        acc[...] += mm(d_upper, two_columns(at_up, 32, t), NT)
        return _

    lax.fori_loop(0, 16, down_tile, 0)
    share_group(5, right, right_hbm, 32, 32)
    d_n2 = acc[...]
    unit, rstd = normalise(mid_s[...])
    gvec[3:4, :] = column_sum(d_n2 * unit)
    gvec[4:5, :] = column_sum(d_n2)
    d_mid = d_out + normalise_back(d_n2, unit, rstd, vec_ref[3:4, :])
    mid_s[...] = d_mid
    d_mid_low = d_mid.astype(BF)
    start, wait_d, send_d = exchange(
        4, lambda p: d_slab.at[p], lambda p: do_t.at[:, lanes(p, TOK)]
    )

    def att_tile(t, _):
        piece = mm(d_mid_low, two_rows(at_o, t), NT).astype(BF)
        for k in range(2):
            turned = flip(piece[:, k * BLOCK : (k + 1) * BLOCK])
            for half in range(2):
                d_slab[4 * t + 2 * k + half] = turned[half * HD : (half + 1) * HD]
        for k in range(4):
            send_d(4 * t + k)
        return _

    lax.fori_loop(0, 4, att_tile, 0)
    do_t[:, lanes(s, TOK)] = d_slab[s]
    gvec[7:8, :] = column_sum(d_mid_low.astype(F32))
    for k in range(8):
        right[24 + k] = d_mid_low[:, k * BLOCK : (k + 1) * BLOCK]
    share_group(6, right, right_hbm, 24, 8)
    dq_acc[...] = jnp.zeros_like(dq_acc)
    lax.fori_loop(12, 32, turn_active, 0)
    share_group(3, left, left_hbm, 24, 32)
    wait_d()

    turn_rows(do_t, 0, do_row)
    scale = 1.0 / math.sqrt(HD)

    def deltas(c, _):
        part = lanes(c, QCH)
        s_scr[pl.ds(c, 1), :] = jnp.sum(
            do_t[:, part].astype(F32) * out_t32[:, part], 0, keepdims=True
        )
        return _

    lax.fori_loop(0, tiles, deltas, 0)
    start, wait_kv, send_kv = exchange(
        5,
        lambda p: dqkv_t.at[pl.ds(HD, 2 * HD), lanes(p, TOK)],
        lambda p: dqkv_in.at[p, pl.ds(HD, 2 * HD)],
    )

    def backward_tile(i, _):
        c = lax.rem(i + s // 2, tiles)
        keys = rows_at(c, QCH)
        k_part = k_row[keys, :]
        v_part = v_row[keys, :]
        k_turned = qkv_t[HD : 2 * HD, lanes(c, QCH)]
        d_key = jnp.zeros((QCH, HD), F32)
        d_value = jnp.zeros((QCH, HD), F32)
        for t in range(tiles // 2):
            tile = slice(2 * t * QCH, (2 * t + 2) * QCH)
            base = jnp.concatenate([lse[2 * t], lse[2 * t + 1]], 1)
            delta = jnp.concatenate([s_scr[2 * t : 2 * t + 1, :], s_scr[2 * t + 1 : 2 * t + 2, :]], 1)
            probs = jnp.exp2(mm(k_part, qkv_t[0:HD, tile]) * scale2 - base)
            d_prob = mm(v_part, do_t[:, tile])
            d_score = (probs * (d_prob - delta)).astype(BF)
            d_value = d_value + mm(probs.astype(BF), do_row[tile, :])
            d_key = d_key + mm(d_score, q_row[tile, :])
            dq_acc[:, tile] += mm(k_turned, d_score)
        d_key = d_key * scale
        for k in range(2):
            part = lanes(2 * c + k, TOK)
            half = slice(k * TOK, (k + 1) * TOK)
            dqkv_t[HD : 2 * HD, part] = flip(d_key[half]).astype(BF)
            dqkv_t[2 * HD : 3 * HD, part] = flip(d_value[half]).astype(BF)
            send_kv(2 * c + k)
        return _

    lax.fori_loop(0, tiles, backward_tile, 0)
    dqkv_t[0:HD, :] = (dq_acc[...] * scale).astype(BF)
    start_q, wait_q, _ = exchange(
        6,
        lambda p: dqkv_t.at[pl.ds(0, HD), lanes(p, TOK)],
        lambda p: dqkv_in.at[p, pl.ds(0, HD)],
    )
    start_q()
    dqkv_in[s] = dqkv_t[:, lanes(s, TOK)]
    acc[...] = jnp.zeros_like(acc)

    def finish_part(which):
        def one(t, _):
            parts = []
            for k in range(2):
                j = 2 * t + k
                part = slice(which * HD, (which + 1) * HD)
                pair = jnp.concatenate([dqkv_in[2 * j, part, :], dqkv_in[2 * j + 1, part, :]], 0)
                piece = flip(pair)
                right[8 * which + j] = piece
                parts.append(piece)
            piece = jnp.concatenate(parts, 1)
            if which != 1:
                gvec[9 + which // 2 : 10 + which // 2, lanes(t, 256)] = column_sum(
                    piece.astype(F32)
                )
            acc[...] += mm(piece, two_columns(at_qkv, 24, 4 * which + t), NT)
            return _

        lax.fori_loop(0, 4, one, 0)

    wait_kv()
    finish_part(1)
    finish_part(2)
    wait_q()
    finish_part(0)
    share_group(7, right, right_hbm, 0, 24)
    d_n1 = acc[...]
    unit, rstd = normalise(h0_s[...])
    gvec[1:2, :] = column_sum(d_n1 * unit)
    gvec[2:3, :] = column_sum(d_n1)
    d_rows = mid_s[...] + normalise_back(d_n1, unit, rstd, vec_ref[1:2, :])
    embed_backward(d_rows, xp_s, a_s, lead_ref, emb_ref, vec_ref, gvec, small_ref)
    for c, r in share:
        c.wait()
        r.wait()


def run_layer(place, lead, blocks, ids, pix, goals, embed, vec, head, wlat):
    vmem = pl.BlockSpec(memory_space=VM)
    smem = pl.BlockSpec(memory_space=pltpu.SMEM)
    anyspace = pl.BlockSpec(memory_space=pl.ANY)
    dma = pltpu.SemaphoreType.DMA
    length = NSEQ * TOK
    return pl.pallas_call(
        layer_kernel,
        name="layer",
        out_shape=(
            jax.ShapeDtypeStruct((2, N_LEFT, BLOCK, TOK), BF),
            jax.ShapeDtypeStruct((2, N_RIGHT, TOK, BLOCK), BF),
            jax.ShapeDtypeStruct((32, 2 * HALF, BLOCK), F32),
        ),
        in_specs=[smem, smem, vmem, vmem, anyspace, anyspace, vmem, vmem, anyspace, vmem],
        out_specs=(anyspace, anyspace, vmem),
        scratch_shapes=[
            VM((SLOTS, BLOCK, BLOCK), BF),
            VM((N_LEFT, BLOCK, TOK), BF),
            VM((N_RIGHT, TOK, BLOCK), BF),
            VM((HEADS, 3 * HD, TOK), BF),
            VM((3 * HD, length), BF),
            VM((HD, length), BF),
            VM((HD, length), F32),
            VM((length // QCH, 1, QCH), F32),
            VM((HEADS, HD, TOK), BF),
            VM((HEADS, HD, TOK), BF),
            VM((HD, length), BF),
            VM((3 * HD, length), BF),
            VM((HEADS, 3 * HD, TOK), BF),
            VM((length, HD), BF),
            VM((length, HD), BF),
            VM((length, HD), BF),
            VM((length, HD), BF),
            VM((length, QCH), F32),
            VM((HD, length), F32),
            VM((TOK, D), F32),
            VM((TOK, D), BF),
            VM((TOK, HOUT), F32),
            VM((TOK, VARS), F32),
            VM((TOK, D), F32),
            VM((TOK, FF), F32),
            VM((TOK, FF), BF),
            VM((TOK, D), F32),
            VM((64, 2 * BLOCK), F32),
            VM((NSEQ, 8, BLOCK), F32),
            VM((8, BLOCK), F32),
            VM((64, 2 * BLOCK), F32),
            VM((1, HOUT, TOK), BF),
            VM((1, HOUT, TOK), BF),
            VM((HOUT, D), F32),
            VM((16, D), F32),
            dma((4, 16)),
            dma((4,)),
            dma((1,)),
            dma((1,)),
            dma((9, NSEQ)),
            dma((9, NSEQ)),
            dma((3,)),
            dma((8,)),
            dma((8,)),
            dma((8,)),
        ],
        compiler_params=pltpu.CompilerParams(
            collective_id=1, has_side_effects=True, vmem_limit_bytes=60 * 1024 * 1024
        ),
    )(place, lead, blocks, ids, pix, goals, embed, vec, head, wlat)


def token_maps():
    row = lax.broadcasted_iota(jnp.int32, (VARS, HOUT), 0)
    col = lax.broadcasted_iota(jnp.int32, (VARS, HOUT), 1)
    return (col // 4 == row).astype(F32)


def embed_forward(pix_ref, ids_ref, lead_ref, emb_ref, vec_ref, h0_ref, n1_ref, xp_ref, a_ref):
    spread = token_maps()
    var = lax.broadcasted_iota(jnp.int32, (VARS, VARS), 0)
    chosen = (ids_ref[...] == var).astype(BF)
    low = spread.astype(BF)
    wide_ids = mm(chosen, low)
    routes = mm(wide_ids.astype(BF), low, TN)
    one = lax.broadcasted_iota(jnp.int32, (HOUT, HOUT), 0)
    two = lax.broadcasted_iota(jnp.int32, (HOUT, HOUT), 1)
    routes = jnp.where(one % 4 == two % 4, routes, 0.0).astype(BF)
    pix = mm(pix_ref[0], routes, TN)
    xp_ref[...] = pix
    tok = emb_ref[0:HOUT, :]
    emb = emb_ref[HOUT : HOUT + VARS, :]
    query = vec_ref[0:1, :]
    tok_q = jnp.sum(tok * query, -1, keepdims=True)
    emb_q = mmh(query, emb, NT)
    back = lax.broadcasted_iota(jnp.int32, (HOUT, VARS), 0) // 4
    col = lax.broadcasted_iota(jnp.int32, (HOUT, VARS), 1)
    reduce = jnp.where(back == col, tok_q, 0.0)
    logits = (mmh(pix, reduce) + emb_q) * (1.0 / math.sqrt(D))
    logits = logits - jnp.max(logits, -1, keepdims=True)
    weights = jnp.exp(logits)
    weights = weights / jnp.sum(weights, -1, keepdims=True)
    a_ref[...] = weights
    wide = mmh(weights, spread) * pix
    lead = emb_ref[pl.ds(HOUT + VARS + lead_ref[0], 1), :]
    h0 = mmh(wide, tok) + mmh(weights, emb) + lead
    h0_ref[...] = h0
    unit, _ = normalise(h0)
    n1_ref[...] = (unit * vec_ref[1:2, :] + vec_ref[2:3, :]).astype(BF)


VEC_AT = 8 * EROWS
HEAD_AT = VEC_AT + 128


def put(small_ref, begin, value):
    rows = value.shape[0]
    at = 0
    while at < rows:
        device, inside = divmod(begin + at, ROWS)
        count = min(rows - at, ROWS - inside)
        small_ref[device, inside : inside + count, :] = value[at : at + count]
        at += count


def put_head(small_ref, grad, loss):
    for k in range(8):
        put(small_ref, HEAD_AT + HOUT * k, grad[:, k * BLOCK : (k + 1) * BLOCK])
    tile = jnp.broadcast_to(loss, (8, BLOCK))
    for d in range(32):
        small_ref[d, ROWS : 2 * HALF, :] = tile


def embed_backward(d_rows, xp_ref, a_ref, lead_ref, emb_ref, vec_ref, gvec, small_ref):
    pix = xp_ref[...]
    weights = a_ref[...]
    tok = emb_ref[0:HOUT, :]
    emb = emb_ref[HOUT : HOUT + VARS, :]
    query = vec_ref[0:1, :]
    spread = token_maps()
    d_wide = mmh(d_rows, tok, NT)
    d_weight = mmh(pix * d_wide, spread, NT) + mmh(d_rows, emb, NT)
    d_logit = (
        weights
        * (d_weight - jnp.sum(weights * d_weight, -1, keepdims=True))
        * (1.0 / math.sqrt(D))
    )
    wide = mmh(weights, spread) * pix
    d_wide_l = mmh(d_logit, spread) * pix
    ones = jnp.ones((TOK, 1), F32)
    d_tok_q = mmh(d_wide_l, ones, TN)
    d_emb_q = mmh(d_logit, ones, TN)
    g_tok = mmh(wide, d_rows, TN) + d_tok_q * query
    g_emb = mmh(weights, d_rows, TN) + d_emb_q * query
    row = lax.broadcasted_iota(jnp.int32, (LEADS, D), 0)
    g_lead = jnp.where(row == lead_ref[0], column_sum(d_rows), 0.0)
    gvec[0:1, :] = column_sum(d_tok_q * tok) + column_sum(d_emb_q * emb)
    gvec[15:16, :] = jnp.zeros((1, D), F32)
    for k in range(8):
        part = slice(k * BLOCK, (k + 1) * BLOCK)
        put(small_ref, EROWS * k, g_tok[:, part])
        put(small_ref, EROWS * k + HOUT, g_emb[:, part])
        put(small_ref, EROWS * k + HOUT + VARS, g_lead[:, part])
        put(small_ref, VEC_AT + 16 * k, gvec[:, part])


SLOTS = 768
ROWS = 120
HALF = 64


def sides_of(b):
    li = jnp.where(
        b < 192, b // 24, jnp.where(b < 256, b // 8 - 16, jnp.where(b < 512, b // 32 + 8, b // 8 - 40))
    )
    ri = jnp.where(
        b < 192,
        lax.rem(b, 24),
        jnp.where(
            b < 256,
            24 + lax.rem(b, 8),
            jnp.where(b < 512, 32 + lax.rem(b, 32), 64 + lax.rem(b, 8)),
        ),
    )
    return li, ri


def reduce_kernel(
    order_ref,
    left_hbm,
    right_hbm,
    small_ref,
    lroot_hbm,
    mom_hbm,
    rroot_hbm,
    own_hbm,
    ggt_hbm,
    gtg_hbm,
    lgr_hbm,
    turned_hbm,
    all_ref,
    sum_ref,
    lroot_ref,
    mom_ref,
    rroot_ref,
    own_ref,
    ggt_ref,
    gtg_ref,
    lgr_ref,
    turned_ref,
    lt,
    rt,
    mine,
    theirs,
    acc,
    acc_small,
    land,
    land_small,
    out,
    out_small,
    tail,
    in_sem,
    swap_sem,
    recv,
    send,
    recv_small,
    send_small,
    norms,
    across,
    t_recv,
    t_send,
    t_sib,
    n_send,
    n_recv,
    root_sem,
    out_sem,
):
    place = Place()
    loads = [
        pltpu.make_async_copy(left_hbm.at[0], lt.at[:, :, pl.ds(0, TOK)], in_sem.at[0]),
        pltpu.make_async_copy(left_hbm.at[1], lt.at[:, :, pl.ds(TOK, TOK)], in_sem.at[1]),
        pltpu.make_async_copy(right_hbm.at[0], rt.at[:, pl.ds(0, TOK), :], in_sem.at[2]),
        pltpu.make_async_copy(right_hbm.at[1], rt.at[:, pl.ds(TOK, TOK), :], in_sem.at[3]),
    ]
    loads.append(pltpu.make_async_copy(small_ref.at[:, place.core], mine, in_sem.at[4]))
    for c in loads:
        c.start()
    later = [
        pltpu.make_async_copy(src, dst, root_sem.at[i])
        for i, (src, dst) in enumerate(
            ((lroot_hbm, lroot_ref), (mom_hbm, mom_ref), (rroot_hbm, rroot_ref))
        )
    ]
    place.greet()
    swap = pltpu.make_async_remote_copy(
        small_ref.at[:, 1 - place.core],
        theirs,
        swap_sem.at[0],
        swap_sem.at[1],
        place.sibling(),
        MESH_ID,
    )
    swap.start()
    for c in later:
        c.start()
    for c in loads:
        c.wait()

    def own_piece(part, device, chip, out_at):
        if part < 4:

            def block(j, _):
                slot = device * SHARE + part * PIECE + j
                li, ri = sides_of(order_ref[slot])
                acc[j] = mm(lt[li], rt[ri])
                return 0

            lax.fori_loop(0, PIECE, block, 0, unroll=3)
        else:
            acc_small[...] = mine[chip // 2, lax.rem(chip, 2), pl.ds((part - 4) * HALF, HALF), :]

    def add_landed(part, index):
        if part < 4:
            acc[...] += land[index].astype(F32)
        else:
            acc_small[...] += land_small[index]

    me = place.linear(place.z, place.x, place.y)

    def keep(part, out_at, root):
        if part < 4:
            if root:
                own_ref[pl.ds(part * PIECE, PIECE)] = acc[...]
            else:
                out[out_at] = acc[...].astype(BF)
        elif root:
            tail[me * 2 + part - 4] = acc_small[...]
        else:
            out_small[out_at] = acc_small[...]

    base, _ = landing_base(MAIN)
    base_small, _ = landing_base(SMALL)

    def main_step(step):
        reduce_step(
            place, MAIN, base, step, own_piece, add_landed, land, recv, out, send, keep, 0
        )

    def small_step(step):
        reduce_step(
            place, SMALL, base_small, step, own_piece, add_landed,
            land_small, recv_small, out_small, send_small, keep, 4,
        )

    stores = []

    def store(index, source, target, begin, count):
        part = pl.ds(begin, count)
        copy = pltpu.make_async_copy(source.at[part], target.at[part], out_sem.at[index])
        copy.start()
        stores.append(copy)

    def product(part, j):
        i = part * PIECE + j
        g = own_ref[i]
        ggt_ref[i] = mmh(g, g, NT)
        gtg_ref[i] = mmh(g, g, TN)
        lgr_ref[i] = mmh(mmh(lroot_ref[i], g), rroot_ref[i])
        if j == PIECE - 1:
            store(4 * part, own_ref, own_hbm, part * PIECE, PIECE)
            store(4 * part + 1, ggt_ref, ggt_hbm, part * PIECE, PIECE)
            store(4 * part + 2, gtg_ref, gtg_hbm, part * PIECE, PIECE)
            store(4 * part + 3, lgr_ref, lgr_hbm, part * PIECE, PIECE)

    def small_root():
        first = tail[me * 2]
        data = tail[me * 2 + 1, 0 : ROWS - HALF, :]
        return jnp.sum(first * first, keepdims=True) + jnp.sum(data * data, keepdims=True)

    spread = gather_steps(
        place,
        TAIL,
        [step[1:] for step in REDUCE_PLAN if step[0] == 1],
        lambda i: tail.at[i],
        lambda n: tail.at[pl.ds(0, n)],
        t_recv,
        t_send,
        t_sib.at[pl.ds(0, 1)],
        t_sib.at[pl.ds(1, 1)],
    )
    def send_norm(squares):
        norms[place.s] = jnp.broadcast_to(
            jnp.sum(squares, keepdims=True) + small_root(), (8, BLOCK)
        )
        lax.fori_loop(1, NSEQ, lambda o, _: (norm_copy(o).start(), 0)[1], 0)

    def norm_copy(o):
        peer = lax.rem(place.s + o, NSEQ)
        return pltpu.make_async_remote_copy(
            norms.at[place.s],
            norms.at[place.s],
            n_send.at[o],
            n_recv.at[o],
            (peer, place.y),
            MESH_ID,
        )

    squares = jnp.zeros((BLOCK, BLOCK), F32)
    roots = 0
    turned = 0
    small_roots = 0
    swapped = False
    for kind, part, dx, dy, rank in REDUCE_PLAN:
        root = dx == 0 and dy == 0 and rank == 3
        if kind == 1:
            next(spread)
        elif kind == 2:
            product(part, dx)
        elif kind == 3:
            if turned == 0:
                for c in later:
                    c.wait()
            turned_ref[turned] = mmh(mmh(lroot_ref[turned], mom_ref[turned]), rroot_ref[turned])
            turned += 1
            if turned == SHARE:
                store(16, turned_ref, turned_hbm, 0, SHARE)
        elif part >= 4:
            if not swapped:
                swapped = True
                swap.wait()
                mine[...] += theirs[...]
            small_step((part - 4, dx, dy, rank))
            small_roots += root
        else:
            main_step((part, dx, dy, rank))
            if root:
                for i in range(part * PIECE, (part + 1) * PIECE):
                    squares = squares + own_ref[i] * own_ref[i]
                roots += 1
        if kind == 0 and root and roots == 4 and small_roots == 2:
            send_norm(squares)

    for _ in spread:
        pass
    for d in range(32):
        all_ref[d, 0:HALF, :] = tail[2 * d]
        all_ref[d, HALF:ROWS, :] = tail[2 * d + 1, 0 : ROWS - HALF, :]
    lax.fori_loop(1, NSEQ, lambda o, _: (norm_copy(o).wait(), 0)[1], 0)
    total = norms[0]
    for k in range(1, NSEQ):
        total = total + norms[k]
    across[0] = total
    over = pltpu.make_async_remote_copy(
        across.at[0], across.at[1], n_send.at[0], n_recv.at[0], (place.s, 1 - place.y), MESH_ID
    )
    over.start()
    drain(place, MAIN, lambda n: out.at[pl.ds(0, n)], send, REDUCE_HOPS)
    drain(place, SMALL, lambda n: out_small.at[pl.ds(0, n)], send_small, REDUCE_HOPS)
    for copy in stores:
        copy.wait()
    over.wait()
    sum_ref[0] = across[0] + across[1]
    sum_ref[1] = tail[1, ROWS - HALF : HALF, :]


def run_reduce(order, left, right, small, lroots, momentum, rroots):
    vmem = pl.BlockSpec(memory_space=VM)
    smem = pl.BlockSpec(memory_space=pltpu.SMEM)
    anyspace = pl.BlockSpec(memory_space=pl.ANY)
    dma = pltpu.SemaphoreType.DMA
    _, count = landing_base(MAIN)
    _, count_small = landing_base(SMALL)
    stack = jax.ShapeDtypeStruct((SHARE, BLOCK, BLOCK), F32)
    return pl.pallas_call(
        reduce_kernel,
        name="reduce",
        out_shape=(stack,) * 5
        + (
            jax.ShapeDtypeStruct((32, ROWS, BLOCK), F32),
            jax.ShapeDtypeStruct((2, 8, BLOCK), F32),
        ),
        in_specs=[smem] + [anyspace] * 6,
        out_specs=(anyspace,) * 5 + (vmem, vmem),
        scratch_shapes=[VM((SHARE, BLOCK, BLOCK), F32)] * 8
        + [
            VM((N_LEFT, BLOCK, 2 * TOK), BF),
            VM((N_RIGHT, 2 * TOK, BLOCK), BF),
            VM((8, 2, 2 * HALF, BLOCK), F32),
            VM((8, 2, 2 * HALF, BLOCK), F32),
            VM((PIECE, BLOCK, BLOCK), F32),
            VM((HALF, BLOCK), F32),
            VM((count, PIECE, BLOCK, BLOCK), BF),
            VM((count_small, HALF, BLOCK), F32),
            VM((64, PIECE, BLOCK, BLOCK), BF),
            VM((32, HALF, BLOCK), F32),
            VM((64, HALF, BLOCK), F32),
            dma((5,)),
            dma((2,)),
            dma((count,)),
            dma((4,)),
            dma((count_small,)),
            dma((4,)),
            VM((NSEQ, 8, BLOCK), F32),
            VM((2, 8, BLOCK), F32),
            dma((2, 16)),
            dma((4,)),
            dma((2,)),
            dma((NSEQ,)),
            dma((NSEQ,)),
            dma((3,)),
            dma((17,)),
        ],
        compiler_params=pltpu.CompilerParams(
            collective_id=3, has_side_effects=True, vmem_limit_bytes=60 * 1024 * 1024
        ),
    )(order, left, right, small, lroots, momentum, rroots)


def final_kernel(
    sums_ref, own, ggt, gtg, lgr, turned, mom, stat_l, stat_r, blk,
    ge, gv, gh, e, e1, e2, v, v1, v2, h, h1, h2,
    loss_o, norm_o, blk_o, mom_o, l_o, r_o,
    e1_o, e2_o, e_o, v1_o, v2_o, v_o, h1_o, h2_o, h_o,
):
    norm = jnp.sqrt(sums_ref[0, 0:1, 0:1])
    loss_o[...] = sums_ref[1, 4:5, 0:1]
    norm_o[...] = norm
    clip = CLIP_NORM / jnp.maximum(norm, CLIP_NORM)
    for i in range(6):
        mom_o[i] = BETA_ONE * mom[i] + (1.0 - BETA_ONE) * (own[i] * clip)
        l_o[i] = BETA_TWO * stat_l[i] + (1.0 - BETA_TWO) * ((ggt[i] * clip) * clip)
        r_o[i] = BETA_TWO * stat_r[i] + (1.0 - BETA_TWO) * ((gtg[i] * clip) * clip)
        direction = BETA_ONE * turned[i] + (1.0 - BETA_ONE) * (lgr[i] * clip)
        blk_o[i] = blk[i] - SHAMPOO_RATE * (direction + DECAY * blk[i])
    e1_o[...], e2_o[...], e_o[...] = adam(e[...], e1[...], e2[...], jnp.concatenate([ge[0:EROWS], ge[EROWS:]], 1) * clip, EMBED_RATE)
    v1_o[...], v2_o[...], v_o[...] = adam(
        v[...], v1[...], v2[...], jnp.concatenate([gv[0:15, :], gv[16:31, :]], 1) * clip, VECTOR_RATE
    )
    h1_o[...], h2_o[...], h_o[...] = adam(h[...], h1[...], h2[...], jnp.concatenate([gh[0:HOUT], gh[HOUT:]], 1) * clip, HEAD_RATE)


def run_final(sums, stacks, flat, embed, vec, head):
    slots = pl.BlockSpec((6, BLOCK, BLOCK), lambda k: (k, 0, 0))
    table = pl.BlockSpec((EROWS, 2 * BLOCK), lambda k: (0, k))
    rows = pl.BlockSpec((15, 2 * BLOCK), lambda k: (0, k))
    wide = pl.BlockSpec((HOUT, 2 * BLOCK), lambda k: (0, k))
    one = pl.BlockSpec((1, 1), lambda k: (0, 0))
    stack = jax.ShapeDtypeStruct((SHARE, BLOCK, BLOCK), F32)
    shapes = (
        (jax.ShapeDtypeStruct((1, 1), F32),) * 2
        + (stack,) * 4
        + (jax.ShapeDtypeStruct((EROWS, D), F32),) * 3
        + (jax.ShapeDtypeStruct((15, D), F32),) * 3
        + (jax.ShapeDtypeStruct((HOUT, D), F32),) * 3
    )
    return pl.pallas_call(
        final_kernel,
        name="final",
        grid=(4,),
        out_shape=shapes,
        in_specs=[pl.BlockSpec((2, 8, BLOCK), lambda k: (0, 0, 0))]
        + [slots] * 9
        + [
            pl.BlockSpec((2 * EROWS, BLOCK), lambda k: (k, 0)),
            pl.BlockSpec((32, BLOCK), lambda k: (VEC_AT // 32 + k, 0)),
            pl.BlockSpec((2 * HOUT, BLOCK), lambda k: (HEAD_AT // HOUT // 2 + k, 0)),
        ]
        + [table] * 3
        + [rows] * 3
        + [wide] * 3,
        out_specs=(one,) * 2 + (slots,) * 4 + (table,) * 3 + (rows,) * 3 + (wide,) * 3,
        compiler_params=pltpu.CompilerParams(vmem_limit_bytes=60 * 1024 * 1024),
    )(sums, *stacks, flat, flat, flat, *embed, *vec, *head)


def fast_shards(
    inputs,
    targets,
    var_ids,
    lead_ids,
    block_order,
    blocks,
    block_momentum,
    left_stats,
    right_stats,
    left_roots,
    right_roots,
    embed_params,
    embed_first,
    embed_second,
    vectors,
    vector_first,
    vector_second,
    head_weight,
    head_first,
    head_second,
):
    slots = jnp.arange(SLOTS, dtype=jnp.int32)
    hit = block_order[None, :] == slots[:, None]
    place = jnp.sum(jnp.where(hit, slots[None, :], 0), 1)
    lat = ((np.arange(2 * LAT_P, dtype=np.float64) + 0.5) / (2 * LAT_P) - 0.5) * math.pi
    wlat = np.cos(lat)
    wlat = (wlat / np.mean(wlat)).reshape(1, LAT_P, 1, 2, 1)
    wlat = np.broadcast_to(wlat, (TOK // LAT_P, LAT_P, VARS, 2, 2)).reshape(TOK, HOUT)
    left, right, small = run_layer(
        place, lead_ids, blocks, var_ids, jnp.swapaxes(inputs, 1, 2), jnp.swapaxes(targets, 1, 2),
        embed_params, vectors, head_weight.T,
        jnp.asarray(wlat, F32),
    )
    owned, ggt, gtg, lgr, turned, every, sums = run_reduce(
        block_order, left, right, small.reshape(8, 2, 2, 2 * HALF, BLOCK),
        left_roots, block_momentum, right_roots,
    )
    loss, norm, *rest = run_final(
        sums,
        (owned, ggt, gtg, lgr, turned, block_momentum, left_stats, right_stats, blocks),
        every.reshape(32 * ROWS, BLOCK),
        (embed_params, embed_first, embed_second),
        (vectors, vector_first, vector_second),
        (head_weight.T, head_first.T, head_second.T),
    )
    return (loss.reshape(()), norm.reshape(()), *rest[:-3], *(a.T for a in rest[-3:]))


def solution(mesh):
    in_specs = (
        P("batch", "seq", None),
        P("batch", "seq", None),
        P("batch", None),
        P("batch"),
        P(),
        P(("seq", "batch"), None, None),
        P(("seq", "batch"), None, None),
        P(("seq", "batch"), None, None),
        P(("seq", "batch"), None, None),
        P(("seq", "batch"), None, None),
        P(("seq", "batch"), None, None),
        P(),
        P(),
        P(),
        P(),
        P(),
        P(),
        P(),
        P(),
        P(),
    )
    out_specs = (
        P(),
        P(),
        P(("seq", "batch"), None, None),
        P(("seq", "batch"), None, None),
        P(("seq", "batch"), None, None),
        P(("seq", "batch"), None, None),
        P(),
        P(),
        P(),
        P(),
        P(),
        P(),
        P(),
        P(),
        P(),
    )
    sizes = dict(mesh.shape)
    fast = sizes == {"seq": NSEQ, "batch": 2}
    return jax.shard_map(fast_shards if fast else shards, mesh=mesh, in_specs=in_specs, out_specs=out_specs, check_vma=False)
```

```python
import math

import jax
import jax.numpy as jnp
import numpy as np
from jax import lax
from jax.experimental import pallas as pl
from jax.experimental.pallas import tpu as pltpu
from jax.sharding import PartitionSpec as P

D = 1024
HEADS = 16
HD = 64
FF = 4096
VARS = 48
LEADS = 32
LAT_P = 64
KMODES = 32
STEP = 10


HIGH = lax.Precision.HIGHEST
EPS = 1e-05
CLIP_NORM = 0.001
SPECTRAL = 0.5
BETA_ONE = 0.9
BETA_TWO = 0.95
SHAMPOO_RATE = 0.1
DECAY = 0.01
ADAM_EPS = 1e-08
EMBED_RATE = 0.2
VECTOR_RATE = 0.5
HEAD_RATE = 0.05
FLOOR = -1e30
EROWS = VARS * 5 + LEADS
HOUT = VARS * 4
MSE_COUNT = 786432.0
DFT_COUNT = 25165824.0


def layer_norm(rows, gain, shift):
    mean = jnp.mean(rows, -1, keepdims=True)
    centred = rows - mean
    return centred * lax.rsqrt(jnp.mean(centred * centred, -1, keepdims=True) + EPS) * gain + shift


def to_blocks(matrix, size):
    rows, cols = matrix.shape
    return (
        matrix.reshape(rows // size, size, cols // size, size)
        .transpose(0, 2, 1, 3)
        .reshape(-1, size, size)
    )


def from_blocks(stack, rows, cols):
    size = stack.shape[-1]
    return (
        stack.reshape(rows // size, cols // size, size, size)
        .transpose(0, 2, 1, 3)
        .reshape(rows, cols)
    )


def split_matrices(stack):
    size = stack.shape[-1]
    found = []
    begin = 0
    for rows, cols in ((D, 3 * D), (D, D), (D, FF), (FF, D)):
        count = rows * cols // (size * size)
        found.append(from_blocks(stack[begin : begin + count], rows, cols))
        begin += count
    return found


def embed_patches(pixels, tok_sel, emb_sel, query, lead_rows):
    tokens = jnp.einsum("spvc,svcd->spvd", pixels, tok_sel, precision=HIGH) + emb_sel[:, None]
    logits = jnp.einsum("spvd,d->spv", tokens, query, precision=HIGH) * (1.0 / math.sqrt(D))
    weights = jax.nn.softmax(logits, -1)
    return jnp.einsum("spv,spvd->spd", weights, tokens, precision=HIGH) + lead_rows[:, None]


def split_heads(rows):
    return rows.reshape(rows.shape[0], rows.shape[1], HEADS, HD)


def attention_forward(query, keys, values):
    seqs, length, _ = query.shape
    scale = 1.0 / math.sqrt(HD)
    heads_q = split_heads(query)
    start_state = (
        jnp.zeros((seqs, HEADS, length, HD), jnp.float32),
        jnp.full((seqs, HEADS, length), FLOOR, jnp.float32),
        jnp.zeros((seqs, HEADS, length), jnp.float32),
    )
    key_rows = lax.all_gather(keys, "seq", axis=1, tiled=True)
    value_rows = lax.all_gather(values, "seq", axis=1, tiled=True)
    count = key_rows.shape[1] // length
    key_blocks = key_rows.reshape(seqs, count, length, HEADS, HD)
    value_blocks = value_rows.reshape(seqs, count, length, HEADS, HD)

    def visit(inner, index):
        acc, top, total = inner
        scores = (
            jnp.einsum(
                "sphd,snhd->shpn", heads_q, key_blocks[:, index], preferred_element_type=jnp.float32
            )
            * scale
        )
        new_top = jnp.maximum(top, jnp.max(scores, -1))
        fade = jnp.exp(top - new_top)
        probs = jnp.exp(scores - new_top[..., None])
        total = total * fade + jnp.sum(probs, -1)
        acc = acc * fade[..., None] + jnp.einsum(
            "shpn,snhd->shpd",
            probs.astype(jnp.bfloat16),
            value_blocks[:, index],
            preferred_element_type=jnp.float32,
        )
        return ((acc, new_top, total), None)

    inner, _ = lax.scan(visit, start_state, jnp.arange(count))
    acc, top, total = inner
    attended = (acc / total[..., None]).transpose(0, 2, 1, 3).reshape(seqs, length, HEADS * HD)
    return (attended, (top + jnp.log(total)).transpose(0, 2, 1))


def attention_backward(query, keys, values, attended, lse, d_att):
    seqs, length, _ = query.shape
    scale = 1.0 / math.sqrt(HD)
    heads_q = split_heads(query)
    heads_k = split_heads(keys)
    heads_v = split_heads(values)
    heads_d = split_heads(d_att)
    delta = jnp.sum(heads_d.astype(jnp.float32) * split_heads(attended), -1)
    lse_h = lse.transpose(0, 2, 1)
    delta_h = delta.transpose(0, 2, 1)
    key_rows = lax.all_gather(keys, "seq", axis=1, tiled=True)
    value_rows = lax.all_gather(values, "seq", axis=1, tiled=True)
    count = key_rows.shape[1] // length
    key_blocks = key_rows.reshape(seqs, count, length, HEADS, HD)
    value_blocks = value_rows.reshape(seqs, count, length, HEADS, HD)

    def visit(inner, index):
        k_part = key_blocks[:, index]
        scores = (
            jnp.einsum("sphd,snhd->shpn", heads_q, k_part, preferred_element_type=jnp.float32)
            * scale
        )
        probs = jnp.exp(scores - lse_h[..., None])
        d_prob = jnp.einsum(
            "sphd,snhd->shpn", heads_d, value_blocks[:, index], preferred_element_type=jnp.float32
        )
        d_score = (probs * (d_prob - delta_h[..., None])).astype(jnp.bfloat16)
        return (
            inner
            + jnp.einsum("shpn,snhd->sphd", d_score, k_part, preferred_element_type=jnp.float32)
            * scale,
            None,
        )

    inner, _ = lax.scan(visit, jnp.zeros((seqs, length, HEADS, HD), jnp.float32), jnp.arange(count))
    d_query = inner
    all_lse, all_delta = (
        lax.all_gather(lse, "seq", axis=1, tiled=True),
        lax.all_gather(delta, "seq", axis=1, tiled=True),
    )
    empty = jnp.zeros((seqs, length, HEADS, HD), jnp.float32)
    q_rows = lax.all_gather(query, "seq", axis=1, tiled=True)
    g_rows = lax.all_gather(d_att, "seq", axis=1, tiled=True)
    count = q_rows.shape[1] // length
    q_blocks = q_rows.reshape(seqs, count, length, HEADS, HD)
    g_blocks = g_rows.reshape(seqs, count, length, HEADS, HD)
    lse_rows = all_lse.reshape(seqs, count, length, HEADS)
    delta_rows = all_delta.reshape(seqs, count, length, HEADS)

    def visit(inner, index):
        d_key, d_value = inner
        q_part = q_blocks[:, index]
        g_part = g_blocks[:, index]
        scores = (
            jnp.einsum("snhd,sphd->shnp", q_part, heads_k, preferred_element_type=jnp.float32)
            * scale
        )
        probs = jnp.exp(scores - lse_rows[:, index].transpose(0, 2, 1)[..., None])
        d_value = d_value + jnp.einsum(
            "shnp,snhd->sphd",
            probs.astype(jnp.bfloat16),
            g_part,
            preferred_element_type=jnp.float32,
        )
        d_prob = jnp.einsum("snhd,sphd->shnp", g_part, heads_v, preferred_element_type=jnp.float32)
        d_score = (probs * (d_prob - delta_rows[:, index].transpose(0, 2, 1)[..., None])).astype(
            jnp.bfloat16
        )
        d_key = (
            d_key
            + jnp.einsum("shnp,snhd->sphd", d_score, q_part, preferred_element_type=jnp.float32)
            * scale
        )
        return ((d_key, d_value), None)

    inner, _ = lax.scan(visit, (empty, empty), jnp.arange(count))
    d_key, d_value = inner
    return (d_query, d_key, d_value)


def feed_inner(normed_two, w_up, vectors):
    upper = jnp.dot(normed_two, w_up, preferred_element_type=jnp.float32) + vectors[11:].reshape(-1)
    return (upper, jax.nn.gelu(upper).astype(jnp.bfloat16))


def layer_forward(rows, seqs, mats, vectors):
    w_qkv, w_out, w_up, w_down = mats
    normed = layer_norm(rows, vectors[1], vectors[2]).astype(jnp.bfloat16)
    bias = jnp.concatenate([vectors[9], jnp.zeros_like(vectors[9]), vectors[10]])
    qkv = (jnp.dot(normed, w_qkv, preferred_element_type=jnp.float32) + bias).astype(jnp.bfloat16)
    query = qkv[:, :D].reshape(seqs, -1, D)
    keys = qkv[:, D : 2 * D].reshape(seqs, -1, D)
    values = qkv[:, 2 * D :].reshape(seqs, -1, D)
    attended, lse = attention_forward(query, keys, values)
    att_low = attended.reshape(-1, D).astype(jnp.bfloat16)
    mid = rows + jnp.dot(att_low, w_out, preferred_element_type=jnp.float32) + vectors[7]
    normed_two = layer_norm(mid, vectors[3], vectors[4]).astype(jnp.bfloat16)
    upper, active = feed_inner(normed_two, w_up, vectors)
    out = mid + jnp.dot(active, w_down, preferred_element_type=jnp.float32) + vectors[8]
    saved = (upper, active)
    return (out, (rows, normed, query, keys, values, attended, lse, mid, normed_two, saved))


def layer_backward(d_out, kept, mats, vectors):
    rows, normed, query, keys, values, attended, lse, mid, normed_two, saved = kept
    w_qkv, w_out, w_up, w_down = mats
    upper, active = saved
    d_branch = d_out.astype(jnp.bfloat16)
    g_down = jnp.einsum("rf,rd->fd", active, d_branch, preferred_element_type=jnp.float32)
    d_active = jnp.einsum("rd,fd->rf", d_branch, w_down, preferred_element_type=jnp.float32)
    d_upper = jax.vjp(jax.nn.gelu, upper)[1](d_active)[0].astype(jnp.bfloat16)
    g_up = jnp.einsum("rd,rf->df", normed_two, d_upper, preferred_element_type=jnp.float32)
    d_normed_two = jnp.einsum("rf,df->rd", d_upper, w_up, preferred_element_type=jnp.float32)
    d_mid_norm, g_gain_two, g_shift_two = jax.vjp(layer_norm, mid, vectors[3], vectors[4])[1](
        d_normed_two
    )
    d_mid = d_out + d_mid_norm
    d_mid_low = d_mid.astype(jnp.bfloat16)
    att_low = attended.reshape(-1, D).astype(jnp.bfloat16)
    g_out = jnp.einsum("ra,rd->ad", att_low, d_mid_low, preferred_element_type=jnp.float32)
    d_att = jnp.einsum("rd,ad->ra", d_mid_low, w_out, preferred_element_type=jnp.float32).astype(
        jnp.bfloat16
    )
    seqs = query.shape[0]
    d_query, d_key, d_value = attention_backward(
        query, keys, values, attended, lse, d_att.reshape(seqs, -1, D)
    )
    d_qkv = jnp.concatenate(
        [d_query.reshape(-1, D), d_key.reshape(-1, D), d_value.reshape(-1, D)], 1
    ).astype(jnp.bfloat16)
    g_qkv = jnp.einsum("rd,re->de", normed, d_qkv, preferred_element_type=jnp.float32)
    d_normed = jnp.einsum("re,de->rd", d_qkv, w_qkv, preferred_element_type=jnp.float32)
    d_rows_norm, g_gain_one, g_shift_one = jax.vjp(layer_norm, rows, vectors[1], vectors[2])[1](
        d_normed
    )
    qkv_sums = jnp.sum(d_qkv.astype(jnp.float32), 0)
    small = (
        g_gain_one,
        g_shift_one,
        g_gain_two,
        g_shift_two,
        jnp.sum(d_mid_low.astype(jnp.float32), 0),
        jnp.sum(d_branch.astype(jnp.float32), 0),
        qkv_sums[:D],
        qkv_sums[2 * D :],
        jnp.sum(d_upper.astype(jnp.float32), 0),
    )
    return (d_mid + d_rows_norm, (g_qkv, g_out, g_up, g_down), small)


def loss_terms(pred, targets, seqs, length):
    strips = lax.axis_size("seq")
    cols = length // LAT_P
    nlat = 2 * LAT_P
    nlon = 2 * cols * strips
    all_seqs = seqs * lax.axis_size("batch")
    diff = pred.reshape(seqs, length, -1) - targets.astype(jnp.float32)
    grid = (
        diff.reshape(seqs, cols, LAT_P, VARS, 2, 2)
        .transpose(0, 3, 2, 4, 1, 5)
        .reshape(seqs, VARS, nlat, 2 * cols)
    )
    lat = ((jnp.arange(nlat, dtype=jnp.float32) + 0.5) / nlat - 0.5) * math.pi
    weight = jnp.cos(lat)
    weight = (weight / jnp.mean(weight))[None, None, :, None]
    column = lax.axis_index("seq") * (2 * cols) + jnp.arange(2 * cols, dtype=jnp.int32)
    modes = jnp.arange(KMODES, dtype=jnp.int32)
    angle = (column[:, None] * modes[None] % nlon).astype(jnp.float32) * (2.0 * math.pi / nlon)
    cosine = jnp.cos(angle)
    sine = jnp.sin(angle)
    part_c = jnp.einsum("svrc,ck->svrk", grid, cosine, precision=HIGH)
    part_s = jnp.einsum("svrc,ck->svrk", grid, sine, precision=HIGH)
    full_c, full_s = lax.psum((part_c, part_s), "seq")
    mse_count = all_seqs * VARS * nlat * nlon
    dft_count = nlon * all_seqs * VARS * nlat * KMODES
    mse = jnp.sum(weight * grid * grid) / mse_count
    spectral = SPECTRAL * jnp.sum(weight * (full_c * full_c + full_s * full_s)) / dft_count
    first = (lax.axis_index("seq") == 0).astype(jnp.float32)
    back_wave = jnp.einsum("svrk,ck->svrc", full_c, cosine, precision=HIGH) + jnp.einsum(
        "svrk,ck->svrc", full_s, sine, precision=HIGH
    )
    d_grid = 2.0 * weight * grid / mse_count + 2.0 * SPECTRAL / dft_count * weight * back_wave
    d_pred = (
        d_grid.reshape(seqs, VARS, LAT_P, 2, cols, 2)
        .transpose(0, 4, 2, 1, 3, 5)
        .reshape(seqs * length, VARS * 4)
    )
    return (d_pred, mse + first * spectral)


def adam(value, first, second, grad, rate):
    first = BETA_ONE * first + (1.0 - BETA_ONE) * grad
    second = BETA_TWO * second + (1.0 - BETA_TWO) * grad * grad
    step = first / (1.0 - BETA_ONE**STEP) / (jnp.sqrt(second / (1.0 - BETA_TWO**STEP)) + ADAM_EPS)
    return (first, second, value - rate * (step + DECAY * value))


def shards(
    inputs,
    targets,
    var_ids,
    lead_ids,
    block_order,
    blocks,
    block_momentum,
    left_stats,
    right_stats,
    left_roots,
    right_roots,
    embed_params,
    embed_first,
    embed_second,
    vectors,
    vector_first,
    vector_second,
    head_weight,
    head_first,
    head_second,
):
    seqs, length, _ = inputs.shape
    size = blocks.shape[-1]
    low_blocks = blocks.astype(jnp.bfloat16)
    stack = lax.all_gather(low_blocks, ("seq", "batch"), axis=0, tiled=True)
    natural = jnp.zeros_like(stack).at[block_order].set(stack)
    mats = split_matrices(natural)
    head_low = head_weight.astype(jnp.bfloat16)
    pick = (var_ids[..., None] == jnp.arange(VARS, dtype=jnp.int32)[None, None]).astype(jnp.float32)
    lead_pick = (lead_ids[:, None] == jnp.arange(LEADS, dtype=jnp.int32)[None]).astype(jnp.float32)
    tok_sel = jnp.einsum(
        "svw,wcd->svcd", pick, embed_params[: VARS * 4].reshape(VARS, 4, D), precision=HIGH
    )
    emb_sel = jnp.einsum("svw,wd->svd", pick, embed_params[VARS * 4 : VARS * 5], precision=HIGH)
    lead_rows = jnp.dot(lead_pick, embed_params[VARS * 5 :], precision=HIGH)
    pixels = inputs.astype(jnp.float32).reshape(seqs, length, VARS, 4)

    def embed_local(tok_part, emb_part, query, lead_part):
        return embed_patches(pixels, tok_part, emb_part, query, lead_part)

    stream, embed_back = jax.vjp(embed_local, tok_sel, emb_sel, vectors[0], lead_rows)
    out, kept = layer_forward(stream.reshape(-1, D), seqs, mats, vectors)
    final_rows, final_back = jax.vjp(layer_norm, out, vectors[5], vectors[6])
    final = final_rows.astype(jnp.bfloat16)
    pred = jnp.dot(final, head_low, preferred_element_type=jnp.float32)
    d_pred, loss_part = loss_terms(pred, targets, seqs, length)
    d_low = d_pred.astype(jnp.bfloat16)
    g_head = jnp.einsum("rd,ro->do", final, d_low, preferred_element_type=jnp.float32)
    d_final = jnp.einsum("ro,do->rd", d_low, head_low, preferred_element_type=jnp.float32)
    d_out, g_gain_final, g_shift_final = final_back(d_final)
    d_rows, matrix_grads, small = layer_backward(d_out, kept, mats, vectors)
    d_tok, d_emb, d_query, d_lead = embed_back(d_rows.reshape(seqs, length, D))
    g_embed = jnp.concatenate(
        [
            jnp.einsum("svw,svcd->wcd", pick, d_tok, precision=HIGH).reshape(VARS * 4, D),
            jnp.einsum("svw,svd->wd", pick, d_emb, precision=HIGH),
            jnp.einsum("sl,sd->ld", lead_pick, d_lead, precision=HIGH),
        ]
    )
    g_gain_one, g_shift_one, g_gain_two, g_shift_two, b_out, b_down, b_query, b_value, b_up = small
    g_vectors = jnp.concatenate(
        [
            jnp.stack(
                [
                    d_query,
                    g_gain_one,
                    g_shift_one,
                    g_gain_two,
                    g_shift_two,
                    g_gain_final,
                    g_shift_final,
                    b_out,
                    b_down,
                    b_query,
                    b_value,
                ]
            ),
            b_up.reshape(-1, D),
        ]
    )
    slot_grads = jnp.concatenate([to_blocks(grad, size) for grad in matrix_grads])[block_order]
    owned = lax.psum_scatter(slot_grads, ("seq", "batch"), scatter_dimension=0, tiled=True)
    g_embed, g_vectors, g_head, loss_total = lax.psum(
        (g_embed, g_vectors, g_head, loss_part), ("seq", "batch")
    )
    rest_squares = (
        jnp.sum(g_embed * g_embed) + jnp.sum(g_vectors * g_vectors) + jnp.sum(g_head * g_head)
    )
    grad_norm = jnp.sqrt(lax.psum(jnp.sum(owned * owned), ("seq", "batch")) + rest_squares)
    clip = CLIP_NORM / jnp.maximum(grad_norm, CLIP_NORM)
    owned = owned * clip
    new_momentum = BETA_ONE * block_momentum + (1.0 - BETA_ONE) * owned
    new_left = BETA_TWO * left_stats + (1.0 - BETA_TWO) * jnp.einsum(
        "bij,bkj->bik", owned, owned, precision=HIGH
    )
    new_right = BETA_TWO * right_stats + (1.0 - BETA_TWO) * jnp.einsum(
        "bji,bjk->bik", owned, owned, precision=HIGH
    )
    direction = jnp.einsum(
        "bij,bjk->bik",
        jnp.einsum("bij,bjk->bik", left_roots, new_momentum, precision=HIGH),
        right_roots,
        precision=HIGH,
    )
    new_blocks = blocks - SHAMPOO_RATE * (direction + DECAY * blocks)
    e_one, e_two, e_new = adam(embed_params, embed_first, embed_second, g_embed * clip, EMBED_RATE)
    v_one, v_two, v_new = adam(vectors, vector_first, vector_second, g_vectors * clip, VECTOR_RATE)
    h_one, h_two, h_new = adam(head_weight, head_first, head_second, g_head * clip, HEAD_RATE)
    return (
        loss_total,
        grad_norm,
        new_blocks,
        new_momentum,
        new_left,
        new_right,
        e_one,
        e_two,
        e_new,
        v_one,
        v_two,
        v_new,
        h_one,
        h_two,
        h_new,
    )


SHARE = 24
PIECE = 6
MAIN = ("zxy", "zyx", "xzy", "yzx")
SMALL = ("xyz", "yxz")
TAIL = ("zxy", "zyx")
GATHER_ORDER = (
    (0, 0, 0, 3), (3, 0, 0, 3), (1, 0, 0, 3), (2, 0, 0, 3), (0, 1, 0, 3), (1, 0, 0, 2), (0, 0, 0, 2), (1, 0, 0, 1),
    (1, 0, 1, 3), (0, 0, 0, 1), (3, 0, 0, 2), (0, 0, 1, 3), (3, 0, 1, 3), (2, 1, 0, 3), (1, 1, 0, 3), (2, 0, 0, 2),
    (1, 1, 1, 3), (0, 0, 0, 0), (1, 1, 0, 2), (2, 0, 1, 3), (1, 0, 1, 2), (2, 1, 0, 2), (3, 0, 1, 2), (0, 1, 0, 2),
    (2, 0, 0, 1), (3, 1, 0, 3), (2, 0, 0, 0), (0, 0, 1, 2), (0, 1, 1, 3), (2, 0, 1, 2), (3, 0, 0, 1), (3, 1, 1, 3),
    (0, 1, 0, 1), (2, 1, 1, 3), (3, 1, 0, 2), (1, 1, 0, 1), (2, 1, 0, 0), (1, 0, 0, 0), (3, 0, 0, 0), (1, 0, 1, 1),
    (0, 1, 1, 2), (0, 0, 1, 1), (3, 0, 1, 0), (2, 1, 1, 2), (2, 1, 0, 1), (0, 1, 1, 1), (3, 1, 0, 1), (2, 0, 1, 1),
    (0, 1, 0, 0), (3, 0, 1, 1), (1, 1, 1, 2), (1, 0, 1, 0), (3, 1, 0, 0), (1, 1, 0, 0), (0, 0, 1, 0), (3, 1, 1, 1),
    (3, 1, 1, 0), (1, 1, 1, 0), (2, 1, 1, 1), (2, 1, 1, 0), (1, 1, 1, 1), (3, 1, 1, 2), (2, 0, 1, 0), (0, 1, 1, 0),
)
REDUCE_PLAN = (
    (0, 4, 1, 1, 1), (0, 4, 0, 0, 0), (0, 3, 1, 0, 1), (0, 4, 1, 1, 0), (0, 0, 1, 1, 1), (0, 4, 0, 1, 0), (0, 5, 0, 0, 1),
    (3, 0, 0, 0, 0), (3, 0, 0, 0, 0), (0, 5, 1, 1, 0), (0, 5, 0, 1, 0), (0, 3, 1, 0, 0), (0, 2, 1, 1, 0), (0, 5, 1, 0, 0),
    (3, 0, 0, 0, 0), (0, 4, 1, 0, 0), (0, 5, 1, 1, 1), (0, 5, 1, 0, 1), (0, 1, 1, 1, 0), (0, 5, 0, 1, 1), (0, 5, 1, 1, 2),
    (0, 4, 1, 1, 2), (0, 2, 0, 1, 0), (0, 2, 1, 1, 2), (3, 0, 0, 0, 0), (0, 4, 0, 1, 1), (0, 3, 1, 1, 2), (0, 1, 1, 1, 1),
    (0, 4, 1, 0, 2), (3, 0, 0, 0, 0), (3, 0, 0, 0, 0), (0, 4, 0, 1, 2), (0, 5, 0, 0, 0), (0, 3, 0, 0, 1), (3, 0, 0, 0, 0),
    (3, 0, 0, 0, 0), (0, 0, 1, 1, 0), (0, 0, 1, 1, 3), (0, 3, 1, 1, 0), (0, 3, 0, 0, 0), (3, 0, 0, 0, 0), (0, 5, 0, 1, 2),
    (0, 3, 1, 1, 1), (0, 0, 1, 0, 1), (3, 0, 0, 0, 0), (3, 0, 0, 0, 0), (0, 4, 1, 1, 3), (3, 0, 0, 0, 0), (3, 0, 0, 0, 0),
    (0, 2, 1, 0, 0), (0, 5, 1, 1, 3), (0, 2, 1, 1, 1), (3, 0, 0, 0, 0), (0, 0, 0, 1, 1), (0, 0, 1, 1, 2), (0, 5, 1, 0, 2),
    (3, 0, 0, 0, 0), (0, 2, 0, 0, 0), (0, 1, 1, 1, 2), (0, 0, 0, 1, 0), (0, 2, 1, 0, 2), (0, 1, 1, 0, 0), (0, 1, 0, 1, 0),
    (0, 2, 1, 1, 3), (3, 0, 0, 0, 0), (3, 0, 0, 0, 0), (0, 4, 1, 0, 1), (0, 1, 1, 1, 3), (0, 0, 1, 0, 0), (0, 1, 1, 0, 1),
    (3, 0, 0, 0, 0), (0, 2, 1, 0, 1), (0, 1, 0, 1, 1), (0, 5, 0, 1, 3), (0, 3, 0, 1, 1), (3, 0, 0, 0, 0), (0, 2, 0, 1, 1),
    (0, 4, 1, 0, 3), (3, 0, 0, 0, 0), (0, 5, 1, 0, 3), (0, 5, 0, 0, 2), (3, 0, 0, 0, 0), (0, 3, 0, 1, 0), (0, 2, 0, 1, 2),
    (0, 0, 0, 1, 2), (0, 3, 1, 0, 2), (0, 1, 0, 1, 2), (0, 3, 1, 1, 3), (3, 0, 0, 0, 0), (0, 0, 0, 0, 1), (0, 4, 0, 1, 3),
    (0, 0, 1, 0, 2), (0, 2, 0, 1, 3), (3, 0, 0, 0, 0), (0, 1, 0, 0, 0), (0, 0, 0, 1, 3), (0, 0, 0, 0, 0), (0, 1, 1, 0, 2),
    (0, 2, 1, 0, 3), (3, 0, 0, 0, 0), (0, 0, 1, 0, 3), (0, 1, 0, 0, 1), (0, 3, 0, 1, 2), (0, 1, 1, 0, 3), (0, 1, 0, 1, 3),
    (0, 3, 1, 0, 3), (0, 5, 0, 0, 3), (0, 2, 0, 0, 1), (0, 4, 0, 0, 1), (1, 1, 0, 0, 3), (0, 4, 0, 0, 2), (0, 2, 0, 0, 2),
    (0, 0, 0, 0, 2), (1, 1, 0, 0, 2), (0, 1, 0, 0, 2), (0, 3, 0, 1, 3), (0, 4, 0, 0, 3), (1, 0, 0, 0, 3), (0, 2, 0, 0, 3),
    (2, 2, 0, 0, 0), (2, 2, 1, 0, 0), (2, 2, 2, 0, 0), (0, 3, 0, 0, 2), (2, 2, 3, 0, 0), (0, 0, 0, 0, 3), (2, 2, 4, 0, 0),
    (2, 2, 5, 0, 0), (2, 0, 0, 0, 0), (1, 0, 0, 0, 2), (2, 0, 1, 0, 0), (2, 0, 2, 0, 0), (0, 1, 0, 0, 3), (2, 1, 0, 0, 0),
    (1, 1, 0, 1, 3), (2, 1, 1, 0, 0), (2, 1, 2, 0, 0), (1, 1, 0, 1, 2), (2, 1, 3, 0, 0), (1, 1, 0, 0, 0), (2, 1, 4, 0, 0),
    (2, 0, 3, 0, 0), (1, 0, 0, 0, 0), (1, 1, 1, 0, 3), (2, 1, 5, 0, 0), (1, 0, 0, 0, 1), (2, 0, 4, 0, 0), (2, 0, 5, 0, 0),
    (1, 1, 0, 0, 1), (1, 1, 0, 1, 0), (1, 0, 1, 0, 3), (1, 0, 1, 0, 2), (0, 3, 0, 0, 3), (1, 0, 1, 0, 1), (2, 3, 0, 0, 0),
    (1, 0, 1, 0, 0), (1, 1, 0, 1, 1), (1, 0, 0, 1, 1), (2, 3, 1, 0, 0), (2, 3, 2, 0, 0), (2, 3, 3, 0, 0), (1, 1, 1, 1, 2),
    (2, 3, 4, 0, 0), (1, 1, 1, 1, 0), (1, 1, 1, 0, 0), (1, 0, 0, 1, 2), (1, 0, 1, 1, 1), (1, 0, 0, 1, 0), (1, 1, 1, 0, 1),
    (2, 3, 5, 0, 0), (1, 0, 1, 1, 2), (1, 0, 1, 1, 0), (1, 0, 0, 1, 3), (1, 1, 1, 0, 2), (1, 1, 1, 1, 1), (1, 0, 1, 1, 3),
    (1, 1, 1, 1, 3),
)

class Place:
    def __init__(self):
        s = lax.axis_index("seq")
        self.y = lax.axis_index("batch")
        self.core = lax.rem(s, 2)
        self.x = lax.rem(s // 2, 2)
        self.z = s // 4
        self.s = s

    def chip(self, z, x, y):
        return (z * 2 + x) * 2 + y

    def linear(self, z, x, y):
        return ((z * 2 + x) * 2 + self.core) * 2 + y

    def device(self, z, x, y):
        return ((z * 2 + x) * 2 + self.core, y)

    def sibling(self):
        return (self.s + 1 - 2 * self.core, self.y)

    def far(self, rank):
        z = self.z
        if rank == 3:
            return z
        if rank == 2:
            return z + 1 - 2 * lax.rem(z, 2)
        low = z // 2
        return (3 - 3 * low) if rank == 0 else (2 - low)

    def flipped(self, dx, dy):
        x = self.x if dx == 0 else 1 - self.x
        y = self.y if dy == 0 else 1 - self.y
        return x, y

    def greet(self):
        barrier = pltpu.get_barrier_semaphore()

        def hail(o, _):
            peer = lax.rem(self.s + o, NSEQ)
            pl.semaphore_signal(barrier, inc=1, device_id=(peer, self.y), device_id_type=MESH_ID)
            return _

        lax.fori_loop(1, NSEQ, hail, 0)
        pl.semaphore_signal(
            barrier, inc=1, device_id=(self.s, 1 - self.y), device_id_type=MESH_ID
        )
        pl.semaphore_wait(barrier, NSEQ)


def last_move(order, dx, dy, rank):
    found = -1
    for i, c in enumerate(order):
        if (c == "x" and dx) or (c == "y" and dy) or (c == "z" and rank != 3):
            found = i
    return found


def sends_before(order, axis):
    count = 1
    for c in order:
        if c == axis:
            return count
        count *= 4 if c == "z" else 2
    return count


def drain(place, orders, total, sem, hops):
    count = {c: sum(sends_before(order, c) for order in orders) for c in "xyz"}

    def finish(i, pieces):
        ref = total(pieces)
        pltpu.make_async_remote_copy(
            ref, ref, sem.at[i], sem.at[i], place.sibling(), MESH_ID
        ).wait_send()

    finish(0, count["x"])
    finish(1, count["y"])
    for z in range(4):
        for i in (2, 3):
            if hops[i - 2][z]:

                @pl.when(place.z == z)
                def _(i=i, z=z):
                    finish(i, count["z"] * hops[i - 2][z])


GATHER_HOPS = ((1, 2, 3, 0), (0, 3, 2, 1))
REDUCE_HOPS = ((3, 2, 1, 0), (0, 1, 2, 3))


def gather_steps(place, orders, steps, piece, total, recv, send, sib_send, sib_recv):
    z = place.z
    parts = len(orders)

    def copy(ref, device, send_sem, recv_sem):
        return pltpu.make_async_remote_copy(ref, ref, send_sem, recv_sem, device, MESH_ID)

    for number, (part, dx, dy, rank) in enumerate(steps):
        order = orders[part]
        tz = place.far(rank)
        sx, sy = place.flipped(dx, dy)
        ref = piece(place.linear(tz, sx, sy) * parts + part)
        landed = recv.at[part, place.chip(tz, sx, sy)]
        own = dx == 0 and dy == 0 and rank == 3
        if not own:
            copy(ref, place.sibling(), landed, landed).wait_recv()
        last = last_move(order, dx, dy, rank)
        if last >= 0 and order[last] == "z" and rank != 3:
            up = (z > tz).astype(jnp.int32)
            nz = z + 2 * up - 1

            @pl.when(jnp.logical_and(nz >= 0, nz <= 3))
            def _():
                copy(ref, place.device(nz, place.x, place.y), send.at[3 - up], landed).start()

        for c in order[last + 1 :]:
            if c == "x":
                copy(ref, place.device(z, 1 - place.x, place.y), send.at[0], landed).start()
            elif c == "y":
                copy(ref, place.device(z, place.x, 1 - place.y), send.at[1], landed).start()
            else:

                @pl.when(z < 3)
                def _():
                    copy(ref, place.device(z + 1, place.x, place.y), send.at[2], landed).start()

                @pl.when(z > 0)
                def _():
                    copy(ref, place.device(z - 1, place.x, place.y), send.at[3], landed).start()

        copy(ref, place.sibling(), sib_send.at[0], sib_recv.at[0]).start()
        yield number
    drain(place, orders, total, send, GATHER_HOPS)
    whole = total(16 * parts)
    copy(whole, place.sibling(), sib_send.at[0], sib_recv.at[0]).wait()


def radix(order, stop, dx, dy, tz):
    index = 0
    size = 1
    for c in order[: order.index(stop[0])]:
        value, base = {"x": (dx, 2), "y": (dy, 2), "z": (tz, 4)}[c]
        index = index * base + value
        size *= base
    if stop[0] == "z":
        index = index * 3 + (tz if stop == "z+" else tz - 1)
        size *= 3
    return index, size


def landing_base(orders):
    base = {}
    at = 0
    for axis in ("x", "y", "z+", "z-"):
        for part, order in enumerate(orders):
            base[(axis, part)] = at
            at += radix(order, axis, 0, 0, 0)[1]
    return base, at


def reduce_step(place, orders, base, step, own_piece, add_landed, land, recv, out, send, keep, offset):
    part, dx, dy, rank = step
    order = orders[part]
    z = place.z
    tz = place.far(rank)
    tx, ty = place.flipped(dx, dy)
    chip = place.chip(tz, tx, ty)
    root = dx == 0 and dy == 0 and rank == 3
    last = last_move(order, dx, dy, rank)
    out_at = part * 16 + chip
    own_piece(part + offset, place.linear(tz, tx, ty), chip, out_at)

    def slot(axis):
        return base[(axis, part)] + radix(order, axis, dx, dy, tz)[0]

    def take(index):
        ref = land.at[index]
        sem = recv.at[index]
        pltpu.make_async_remote_copy(ref, ref, sem, sem, place.sibling(), MESH_ID).wait_recv()
        add_landed(part + offset, index)

    if last >= 0 and order[last] == "z" and rank != 3:
        up = (z > tz).astype(jnp.int32)
        nz = z + 2 * up - 1
        plus = slot("z+")
        minus = slot("z-")

        @pl.when(jnp.logical_and(nz >= 0, nz <= 3))
        def _():
            take(up * plus + (1 - up) * minus)

    for c in order[last + 1 :]:
        if c == "z":

            @pl.when(z < 3)
            def _():
                take(slot("z+"))

            @pl.when(z > 0)
            def _():
                take(slot("z-"))

        else:
            take(slot(c))
    keep(part + offset, out_at, root)
    if root:
        return
    ref = out.at[out_at]

    def push(device, index, direction):
        pltpu.make_async_remote_copy(
            ref, land.at[index], send.at[direction], recv.at[index], device, MESH_ID
        ).start()

    axis = order[last]
    if axis == "x":
        index = base[("x", part)] + radix(order, "x", 0, dy, tz)[0]
        push(place.device(z, 1 - place.x, place.y), index, 0)
    elif axis == "y":
        index = base[("y", part)] + radix(order, "y", dx, 0, tz)[0]
        push(place.device(z, place.x, 1 - place.y), index, 1)
    else:
        down = (z > tz).astype(jnp.int32)
        index = down * slot("z+") + (1 - down) * slot("z-")
        push(place.device(z + 1 - 2 * down, place.x, place.y), index, 2 + down)


TOK = 128
NSEQ = 16
BLOCK = 128
N_LEFT = 56
N_RIGHT = 72
QCH = 256
LOG2E = math.log2(math.e)
MESH_ID = pl.DeviceIdType.MESH
NT = (((1,), (1,)), ((), ()))
TN = (((0,), (0,)), ((), ()))
NN = (((1,), (0,)), ((), ()))
BF = jnp.bfloat16
F32 = jnp.float32
VM = pltpu.VMEM


def mm(a, b, dims=NN):
    return lax.dot_general(a, b, dims, preferred_element_type=F32)


def mmh(a, b, dims=NN):
    return lax.dot_general(a, b, dims, precision=HIGH, preferred_element_type=F32)


def flip(x):
    return jnp.swapaxes(x.astype(F32), 0, 1).astype(x.dtype)


def normalise(x):
    mean = jnp.mean(x, -1, keepdims=True)
    centred = x - mean
    rstd = lax.rsqrt(jnp.mean(centred * centred, -1, keepdims=True) + EPS)
    return centred * rstd, rstd


def normalise_back(grad, unit, rstd, gain):
    inner = grad * gain
    return rstd * (
        inner
        - jnp.mean(inner, -1, keepdims=True)
        - unit * jnp.mean(inner * unit, -1, keepdims=True)
    )


def column_sum(x):
    return jnp.sum(x, 0, keepdims=True)


GELU_K = math.sqrt(2.0 / math.pi)


def gelu_value(x):
    return 0.5 * x * (1.0 + jnp.tanh(GELU_K * (x + 0.044715 * x * x * x)))


def gelu_slope(x):
    t = jnp.tanh(GELU_K * (x + 0.044715 * x * x * x))
    return 0.5 * (1.0 + t) + 0.5 * x * (1.0 - t * t) * GELU_K * (1.0 + 3.0 * 0.044715 * x * x)


def layer_kernel(
    place_ref,
    lead_ref,
    blocks_ref,
    ids_ref,
    pix_ref,
    goal_ref,
    emb_ref,
    vec_ref,
    head_ref,
    wlat_ref,
    left_hbm,
    right_hbm,
    small_ref,
    stack,
    left,
    right,
    slab,
    qkv_t,
    out_t,
    out_t32,
    lse,
    o_in,
    d_slab,
    do_t,
    dqkv_t,
    dqkv_in,
    k_row,
    v_row,
    q_row,
    do_row,
    s_scr,
    dq_acc,
    h0_s,
    n1_s,
    xp_s,
    a_s,
    mid_s,
    up_s,
    act_s,
    acc,
    wave,
    wave_in,
    wave_tile,
    wave_all,
    pix_s,
    goal_s,
    head_s,
    gvec,
    t_recv,
    t_send,
    t_sib_send,
    t_sib_recv,
    a_send,
    a_recv,
    in_sem,
    g_local,
    g_send,
    g_recv,
):
    s = lax.axis_index("seq")
    b = lax.axis_index("batch")
    place = Place()
    sibling = s + 1 - 2 * place.core

    loads = []
    for i, (src, dst) in enumerate(((pix_ref, pix_s), (goal_ref, goal_s), (head_ref, head_s))):
        c = pltpu.make_async_copy(src, dst, in_sem.at[i])
        c.start()
        loads.append(c)
    mine = place.linear(place.z, place.x, place.y)
    stack[pl.ds(mine * SHARE, SHARE)] = blocks_ref[...].astype(BF)
    place.greet()

    for number in gather_steps(
        place,
        MAIN,
        GATHER_ORDER,
        lambda i: stack.at[pl.ds(i * PIECE, PIECE)],
        lambda n: stack.at[pl.ds(0, n * PIECE)],
        t_recv,
        t_send,
        t_sib_send,
        t_sib_recv,
    ):
        if number == 3:
            loads[0].wait()
            embed_forward(pix_s, ids_ref, lead_ref, emb_ref, vec_ref, h0_s, n1_s, xp_s, a_s)

    def block(begin, across, r, c):
        return stack[place_ref[begin + r * across + c]]

    def two_columns(begin, across, pair):
        return jnp.concatenate(
            [
                jnp.concatenate(
                    [block(begin, across, r, 2 * pair), block(begin, across, r, 2 * pair + 1)], 1
                )
                for r in range(8)
            ],
            0,
        )

    def two_rows(begin, pair):
        return jnp.concatenate(
            [
                jnp.concatenate([block(begin, 8, 2 * pair + r, c) for c in range(8)], 1)
                for r in range(2)
            ],
            0,
        )

    def eight_columns(begin, across, quad):
        return jnp.concatenate(
            [
                jnp.concatenate([block(begin, across, r, 8 * quad + k) for k in range(8)], 1)
                for r in range(8)
            ],
            0,
        )

    def eight_rows(begin, quad):
        return jnp.concatenate(
            [
                jnp.concatenate([block(begin, 8, 8 * quad + r, c) for c in range(8)], 1)
                for r in range(8)
            ],
            0,
        )

    at_qkv, at_o, at_up, at_down = 0, 192, 256, 512
    share = []

    def share_group(index, stage, target, begin, count):
        part = pl.ds(begin, count)
        c = pltpu.make_async_copy(stage.at[part], target.at[0, part], g_local.at[index])
        c.start()
        r = pltpu.make_async_remote_copy(
            src_ref=stage.at[part],
            dst_ref=target.at[1, part],
            send_sem=g_send.at[index],
            recv_sem=g_recv.at[index],
            device_id=(sibling, b),
            device_id_type=MESH_ID,
        )
        r.start()
        share.append((c, r))

    def exchange(which, src_at, dst_at):
        def copy(o):
            peer = lax.rem(s + o, NSEQ)
            return pltpu.make_async_remote_copy(
                src_ref=src_at(peer),
                dst_ref=dst_at(s),
                send_sem=a_send.at[which, o],
                recv_sem=a_recv.at[which, o],
                device_id=(peer, b),
                device_id_type=MESH_ID,
            )

        def begin(o, _):
            copy(o).start()
            return _

        def finish(o, _):
            copy(o).wait()
            return _

        def start():
            lax.fori_loop(1, NSEQ, begin, 0)

        def start_to(peer):
            @pl.when(peer != s)
            def _():
                copy(lax.rem(peer - s + NSEQ, NSEQ)).start()

        def wait():
            lax.fori_loop(1, NSEQ, finish, 0)

        return start, wait, start_to

    def lanes(i, size):
        return pl.ds(pl.multiple_of(i * size, size), size)

    def rows_at(i, size):
        return pl.ds(pl.multiple_of(i * size, size), size)

    n1 = n1_s[...]
    waits = {}
    for which in (1, 0, 2):

        def qkv_tile(t, _, which=which):
            piece = mm(n1, two_columns(at_qkv, 24, 4 * which + t))
            if which != 1:
                piece = piece + vec_ref[9 + which // 2 : 10 + which // 2, lanes(t, 256)]
            piece = piece.astype(BF)
            for k in range(2):
                turned = flip(piece[:, k * BLOCK : (k + 1) * BLOCK])
                for half in range(2):
                    slab[4 * t + 2 * k + half, which * HD : (which + 1) * HD, :] = turned[
                        half * HD : (half + 1) * HD
                    ]
            return _

        lax.fori_loop(0, 4, qkv_tile, 0, unroll=4)
        part = pl.ds(which * HD, HD)
        start, waits[which], _ = exchange(
            which,
            lambda p, part=part: slab.at[p, part],
            lambda p, part=part: qkv_t.at[part, lanes(p, TOK)],
        )
        start()
    qkv_t[:, lanes(s, TOK)] = slab[s]
    for k in range(8):
        left[k] = flip(n1[:, k * BLOCK : (k + 1) * BLOCK])

    scale2 = LOG2E / math.sqrt(HD)

    def turn_rows(source, begin, target):
        def one(t, _):
            target[rows_at(t, TOK), :] = flip(source[begin : begin + HD, lanes(t, TOK)])
            return _

        lax.fori_loop(0, NSEQ, one, 0, unroll=4)

    waits[1]()
    turn_rows(qkv_t, HD, k_row)
    waits[0]()
    tiles = (NSEQ * TOK) // QCH
    start, wait_o, send_o = exchange(
        3, lambda p: out_t.at[:, lanes(p, TOK)], lambda p: o_in.at[p]
    )

    def forward_chunk(i, _):
        c = lax.rem(i + s // 2, tiles)
        part = lanes(c, QCH)
        q_part = qkv_t[0:HD, part]
        top = None
        for t in range(tiles):
            tile = slice(t * QCH, (t + 1) * QCH)
            scores = mm(k_row[tile, :], q_part)
            s_scr[tile, :] = scores
            best = jnp.max(scores, 0, keepdims=True)
            top = best if top is None else jnp.maximum(top, best)
        top = top * scale2

        @pl.when(i == 0)
        def _():
            waits[2]()

        total = jnp.zeros((1, QCH), F32)
        mixed = jnp.zeros((HD, QCH), F32)
        for t in range(2):
            tile = slice(4 * t * QCH, (4 * t + 4) * QCH)
            probs = jnp.exp2(s_scr[tile, :] * scale2 - top)
            total = total + jnp.sum(probs, 0, keepdims=True)
            mixed = mixed + mm(qkv_t[2 * HD : 3 * HD, tile], probs.astype(BF))
        mixed = mixed / total
        lse[c] = top + jnp.log2(total)
        out_t32[:, part] = mixed
        out_t[:, part] = mixed.astype(BF)
        send_o(2 * c)
        send_o(2 * c + 1)
        return 0

    lax.fori_loop(0, tiles, forward_chunk, 0)
    share_group(0, left, left_hbm, 0, 8)
    o_in[s] = out_t[:, lanes(s, TOK)]
    turn_rows(qkv_t, 0, q_row)
    turn_rows(qkv_t, 2 * HD, v_row)
    wait_o()

    parts = []
    for k in range(8):
        pair = jnp.concatenate([o_in[2 * k], o_in[2 * k + 1]], 0)
        left[8 + k] = pair
        parts.append(flip(pair))
    share_group(1, left, left_hbm, 8, 8)
    o_low = jnp.concatenate(parts, 1)

    def out_tile(t, _):
        part = lanes(t, 256)
        mid_s[:, part] = h0_s[:, part] + (
            mm(o_low, two_columns(at_o, 8, t)) + vec_ref[7:8, part]
        )
        return _

    lax.fori_loop(0, 4, out_tile, 0, unroll=4)
    mid = mid_s[...]
    unit, _ = normalise(mid)
    n2 = (unit * vec_ref[3:4, :] + vec_ref[4:5, :]).astype(BF)
    acc[...] = mid + vec_ref[8:9, :]

    def up_tile(t, _):
        part = lanes(t, 1024)
        bias = vec_ref[pl.ds(11 + t, 1), :]
        upper = mm(n2, eight_columns(at_up, 32, t)) + bias
        up_s[:, part] = upper
        active = gelu_value(upper).astype(BF)
        act_s[:, part] = active
        acc[...] += mm(active, eight_rows(at_down, t))
        return _

    lax.fori_loop(0, 4, up_tile, 0)

    unit_f, rstd_f = normalise(acc[...])
    final = (unit_f * vec_ref[5:6, :] + vec_ref[6:7, :]).astype(BF)
    loads[2].wait()
    head = head_s[...].astype(BF)
    loads[1].wait()
    diff = mm(final, head, NT) - jnp.swapaxes(goal_s[0].astype(F32), 0, 1)
    wave[...] = jnp.concatenate(
        [diff[0:64] + diff[64:128], jnp.zeros((64, 2 * BLOCK - HOUT), F32)], 1
    )

    def tile_of(ref, j):
        return ref.at[
            pl.ds(pl.multiple_of(j // 2 * 8, 8), 8),
            pl.ds(pl.multiple_of(lax.rem(j, 2) * BLOCK, BLOCK), BLOCK),
        ]

    start, wait, _ = exchange(7, lambda p: tile_of(wave, p), lambda p: wave_in.at[p])
    start()
    wave_in[s] = tile_of(wave, s)[...]
    for k in range(8):
        left[16 + k] = flip(n2[:, k * BLOCK : (k + 1) * BLOCK])
    share_group(2, left, left_hbm, 16, 8)
    wait()
    tile = wave_in[0]
    for k in range(1, NSEQ):
        tile = tile + wave_in[k]
    wave_tile[...] = tile
    start, wait, _ = exchange(8, lambda p: wave_tile, lambda p: tile_of(wave_all, p))
    start()
    tile_of(wave_all, s)[...] = tile

    def turn_active(k, _):
        left[24 + k] = flip(act_s[:, lanes(k, BLOCK)])
        return _

    lax.fori_loop(0, 12, turn_active, 0)
    wait()
    total_wave = wave_all[:, 0:HOUT]
    one = lax.broadcasted_iota(jnp.int32, (HOUT, HOUT), 0)
    two = lax.broadcasted_iota(jnp.int32, (HOUT, HOUT), 1)
    swap = (one == two + 1 - 2 * (two % 2)).astype(F32)
    other = mmh(total_wave, swap)
    weight = wlat_ref[...]
    square = jnp.sum(weight * diff * diff, keepdims=True)
    cross = jnp.sum(weight[0:64] * total_wave * other, keepdims=True) * (1.0 / NSEQ)
    loss = square * (1.0 / MSE_COUNT) + (SPECTRAL / DFT_COUNT) * (float(KMODES) * square + cross)
    other2 = jnp.concatenate([other, other], 0)
    d_pred = weight * (
        (2.0 / MSE_COUNT) * diff + (2.0 * SPECTRAL / DFT_COUNT) * (float(KMODES) * diff + other2)
    )
    d_low = d_pred.astype(BF)
    put_head(small_ref, mm(d_low, final, TN), loss)
    d_final = mm(d_low, head)
    gvec[5:6, :] = column_sum(d_final * unit_f)
    gvec[6:7, :] = column_sum(d_final)
    d_out = normalise_back(d_final, unit_f, rstd_f, vec_ref[5:6, :])
    d_branch = d_out.astype(BF)
    gvec[8:9, :] = column_sum(d_branch.astype(F32))
    for k in range(8):
        right[64 + k] = d_branch[:, k * BLOCK : (k + 1) * BLOCK]
    share_group(4, right, right_hbm, 64, 8)
    acc[...] = jnp.zeros_like(acc)

    def down_tile(t, _):
        part = lanes(t, 1024)
        d_active = mm(d_branch, eight_rows(at_down, t), NT)
        d_upper = (d_active * gelu_slope(up_s[:, part])).astype(BF)
        gvec[pl.ds(11 + t, 1), :] = column_sum(d_upper.astype(F32))
        for k in range(8):
            right[32 + 8 * t + k] = d_upper[:, k * BLOCK : (k + 1) * BLOCK]
        acc[...] += mm(d_upper, eight_columns(at_up, 32, t), NT)
        return _

    lax.fori_loop(0, 4, down_tile, 0)
    share_group(5, right, right_hbm, 32, 32)
    d_n2 = acc[...]
    unit, rstd = normalise(mid_s[...])
    gvec[3:4, :] = column_sum(d_n2 * unit)
    gvec[4:5, :] = column_sum(d_n2)
    d_mid = d_out + normalise_back(d_n2, unit, rstd, vec_ref[3:4, :])
    mid_s[...] = d_mid
    d_mid_low = d_mid.astype(BF)
    start, wait_d, send_d = exchange(
        4, lambda p: d_slab.at[p], lambda p: do_t.at[:, lanes(p, TOK)]
    )

    def att_tile(t, _):
        piece = mm(d_mid_low, two_rows(at_o, t), NT).astype(BF)
        for k in range(2):
            turned = flip(piece[:, k * BLOCK : (k + 1) * BLOCK])
            for half in range(2):
                d_slab[4 * t + 2 * k + half] = turned[half * HD : (half + 1) * HD]
        for k in range(4):
            send_d(4 * t + k)
        return _

    lax.fori_loop(0, 4, att_tile, 0, unroll=4)
    do_t[:, lanes(s, TOK)] = d_slab[s]
    gvec[7:8, :] = column_sum(d_mid_low.astype(F32))
    for k in range(8):
        right[24 + k] = d_mid_low[:, k * BLOCK : (k + 1) * BLOCK]
    share_group(6, right, right_hbm, 24, 8)
    dq_acc[...] = jnp.zeros_like(dq_acc)
    lax.fori_loop(12, 32, turn_active, 0)
    share_group(3, left, left_hbm, 24, 32)
    wait_d()

    turn_rows(do_t, 0, do_row)
    scale = 1.0 / math.sqrt(HD)

    def deltas(c, _):
        part = lanes(c, QCH)
        s_scr[pl.ds(c, 1), :] = jnp.sum(
            do_t[:, part].astype(F32) * out_t32[:, part], 0, keepdims=True
        )
        return _

    lax.fori_loop(0, tiles, deltas, 0)
    start, wait_kv, send_kv = exchange(
        5,
        lambda p: dqkv_t.at[pl.ds(HD, 2 * HD), lanes(p, TOK)],
        lambda p: dqkv_in.at[p, pl.ds(HD, 2 * HD)],
    )

    def backward_tile(i, _):
        c = lax.rem(i + s // 2, tiles)
        keys = rows_at(c, QCH)
        k_part = k_row[keys, :]
        v_part = v_row[keys, :]
        k_turned = qkv_t[HD : 2 * HD, lanes(c, QCH)]
        d_key = jnp.zeros((QCH, HD), F32)
        d_value = jnp.zeros((QCH, HD), F32)
        for t in range(tiles // 2):
            tile = slice(2 * t * QCH, (2 * t + 2) * QCH)
            base = jnp.concatenate([lse[2 * t], lse[2 * t + 1]], 1)
            delta = jnp.concatenate([s_scr[2 * t : 2 * t + 1, :], s_scr[2 * t + 1 : 2 * t + 2, :]], 1)
            probs = jnp.exp2(mm(k_part, qkv_t[0:HD, tile]) * scale2 - base)
            d_prob = mm(v_part, do_t[:, tile])
            d_score = (probs * (d_prob - delta)).astype(BF)
            d_value = d_value + mm(probs.astype(BF), do_row[tile, :])
            d_key = d_key + mm(d_score, q_row[tile, :])
            dq_acc[:, tile] += mm(k_turned, d_score)
        d_key = d_key * scale
        for k in range(2):
            part = lanes(2 * c + k, TOK)
            half = slice(k * TOK, (k + 1) * TOK)
            dqkv_t[HD : 2 * HD, part] = flip(d_key[half]).astype(BF)
            dqkv_t[2 * HD : 3 * HD, part] = flip(d_value[half]).astype(BF)
            send_kv(2 * c + k)
        return _

    lax.fori_loop(0, tiles, backward_tile, 0)
    dqkv_t[0:HD, :] = (dq_acc[...] * scale).astype(BF)
    start_q, wait_q, _ = exchange(
        6,
        lambda p: dqkv_t.at[pl.ds(0, HD), lanes(p, TOK)],
        lambda p: dqkv_in.at[p, pl.ds(0, HD)],
    )
    start_q()
    dqkv_in[s] = dqkv_t[:, lanes(s, TOK)]
    acc[...] = jnp.zeros_like(acc)

    def finish_part(which):
        def one(t, _):
            parts = []
            for k in range(2):
                j = 2 * t + k
                part = slice(which * HD, (which + 1) * HD)
                pair = jnp.concatenate([dqkv_in[2 * j, part, :], dqkv_in[2 * j + 1, part, :]], 0)
                piece = flip(pair)
                right[8 * which + j] = piece
                parts.append(piece)
            piece = jnp.concatenate(parts, 1)
            if which != 1:
                gvec[9 + which // 2 : 10 + which // 2, lanes(t, 256)] = column_sum(
                    piece.astype(F32)
                )
            acc[...] += mm(piece, two_columns(at_qkv, 24, 4 * which + t), NT)
            return _

        lax.fori_loop(0, 4, one, 0, unroll=4)

    wait_kv()
    finish_part(1)
    finish_part(2)
    wait_q()
    finish_part(0)
    share_group(7, right, right_hbm, 0, 24)
    d_n1 = acc[...]
    unit, rstd = normalise(h0_s[...])
    gvec[1:2, :] = column_sum(d_n1 * unit)
    gvec[2:3, :] = column_sum(d_n1)
    d_rows = mid_s[...] + normalise_back(d_n1, unit, rstd, vec_ref[1:2, :])
    embed_backward(d_rows, xp_s, a_s, lead_ref, emb_ref, vec_ref, gvec, small_ref)
    for c, r in share:
        c.wait()
        r.wait()


def run_layer(place, lead, blocks, ids, pix, goals, embed, vec, head, wlat):
    vmem = pl.BlockSpec(memory_space=VM)
    smem = pl.BlockSpec(memory_space=pltpu.SMEM)
    anyspace = pl.BlockSpec(memory_space=pl.ANY)
    dma = pltpu.SemaphoreType.DMA
    length = NSEQ * TOK
    return pl.pallas_call(
        layer_kernel,
        name="layer",
        out_shape=(
            jax.ShapeDtypeStruct((2, N_LEFT, BLOCK, TOK), BF),
            jax.ShapeDtypeStruct((2, N_RIGHT, TOK, BLOCK), BF),
            jax.ShapeDtypeStruct((32, 2 * HALF, BLOCK), F32),
        ),
        in_specs=[smem, smem, vmem, vmem, anyspace, anyspace, vmem, vmem, anyspace, vmem],
        out_specs=(anyspace, anyspace, vmem),
        scratch_shapes=[
            VM((SLOTS, BLOCK, BLOCK), BF),
            VM((N_LEFT, BLOCK, TOK), BF),
            VM((N_RIGHT, TOK, BLOCK), BF),
            VM((HEADS, 3 * HD, TOK), BF),
            VM((3 * HD, length), BF),
            VM((HD, length), BF),
            VM((HD, length), F32),
            VM((length // QCH, 1, QCH), F32),
            VM((HEADS, HD, TOK), BF),
            VM((HEADS, HD, TOK), BF),
            VM((HD, length), BF),
            VM((3 * HD, length), BF),
            VM((HEADS, 3 * HD, TOK), BF),
            VM((length, HD), BF),
            VM((length, HD), BF),
            VM((length, HD), BF),
            VM((length, HD), BF),
            VM((length, QCH), F32),
            VM((HD, length), F32),
            VM((TOK, D), F32),
            VM((TOK, D), BF),
            VM((TOK, HOUT), F32),
            VM((TOK, VARS), F32),
            VM((TOK, D), F32),
            VM((TOK, FF), F32),
            VM((TOK, FF), BF),
            VM((TOK, D), F32),
            VM((64, 2 * BLOCK), F32),
            VM((NSEQ, 8, BLOCK), F32),
            VM((8, BLOCK), F32),
            VM((64, 2 * BLOCK), F32),
            VM((1, HOUT, TOK), BF),
            VM((1, HOUT, TOK), BF),
            VM((HOUT, D), F32),
            VM((16, D), F32),
            dma((4, 16)),
            dma((4,)),
            dma((1,)),
            dma((1,)),
            dma((9, NSEQ)),
            dma((9, NSEQ)),
            dma((3,)),
            dma((8,)),
            dma((8,)),
            dma((8,)),
        ],
        compiler_params=pltpu.CompilerParams(
            collective_id=1, has_side_effects=True, vmem_limit_bytes=60 * 1024 * 1024
        ),
    )(place, lead, blocks, ids, pix, goals, embed, vec, head, wlat)


def token_maps():
    row = lax.broadcasted_iota(jnp.int32, (VARS, HOUT), 0)
    col = lax.broadcasted_iota(jnp.int32, (VARS, HOUT), 1)
    return (col // 4 == row).astype(F32)


def embed_forward(pix_ref, ids_ref, lead_ref, emb_ref, vec_ref, h0_ref, n1_ref, xp_ref, a_ref):
    spread = token_maps()
    var = lax.broadcasted_iota(jnp.int32, (VARS, VARS), 0)
    chosen = (ids_ref[...] == var).astype(BF)
    low = spread.astype(BF)
    wide_ids = mm(chosen, low)
    routes = mm(wide_ids.astype(BF), low, TN)
    one = lax.broadcasted_iota(jnp.int32, (HOUT, HOUT), 0)
    two = lax.broadcasted_iota(jnp.int32, (HOUT, HOUT), 1)
    routes = jnp.where(one % 4 == two % 4, routes, 0.0).astype(BF)
    pix = mm(pix_ref[0], routes, TN)
    xp_ref[...] = pix
    tok = emb_ref[0:HOUT, :]
    emb = emb_ref[HOUT : HOUT + VARS, :]
    query = vec_ref[0:1, :]
    tok_q = jnp.sum(tok * query, -1, keepdims=True)
    emb_q = mmh(query, emb, NT)
    back = lax.broadcasted_iota(jnp.int32, (HOUT, VARS), 0) // 4
    col = lax.broadcasted_iota(jnp.int32, (HOUT, VARS), 1)
    reduce = jnp.where(back == col, tok_q, 0.0)
    logits = (mmh(pix, reduce) + emb_q) * (1.0 / math.sqrt(D))
    logits = logits - jnp.max(logits, -1, keepdims=True)
    weights = jnp.exp(logits)
    weights = weights / jnp.sum(weights, -1, keepdims=True)
    a_ref[...] = weights
    wide = mmh(weights, spread) * pix
    lead = emb_ref[pl.ds(HOUT + VARS + lead_ref[0], 1), :]
    h0 = mmh(wide, tok) + mmh(weights, emb) + lead
    h0_ref[...] = h0
    unit, _ = normalise(h0)
    n1_ref[...] = (unit * vec_ref[1:2, :] + vec_ref[2:3, :]).astype(BF)


VEC_AT = 8 * EROWS
HEAD_AT = VEC_AT + 128


def put(small_ref, begin, value):
    rows = value.shape[0]
    at = 0
    while at < rows:
        device, inside = divmod(begin + at, ROWS)
        count = min(rows - at, ROWS - inside)
        small_ref[device, inside : inside + count, :] = value[at : at + count]
        at += count


def put_head(small_ref, grad, loss):
    for k in range(8):
        put(small_ref, HEAD_AT + HOUT * k, grad[:, k * BLOCK : (k + 1) * BLOCK])
    tile = jnp.broadcast_to(loss, (8, BLOCK))
    for d in range(32):
        small_ref[d, ROWS : 2 * HALF, :] = tile


def embed_backward(d_rows, xp_ref, a_ref, lead_ref, emb_ref, vec_ref, gvec, small_ref):
    pix = xp_ref[...]
    weights = a_ref[...]
    tok = emb_ref[0:HOUT, :]
    emb = emb_ref[HOUT : HOUT + VARS, :]
    query = vec_ref[0:1, :]
    spread = token_maps()
    d_wide = mmh(d_rows, tok, NT)
    d_weight = mmh(pix * d_wide, spread, NT) + mmh(d_rows, emb, NT)
    d_logit = (
        weights
        * (d_weight - jnp.sum(weights * d_weight, -1, keepdims=True))
        * (1.0 / math.sqrt(D))
    )
    wide = mmh(weights, spread) * pix
    d_wide_l = mmh(d_logit, spread) * pix
    ones = jnp.ones((TOK, 1), F32)
    d_tok_q = mmh(d_wide_l, ones, TN)
    d_emb_q = mmh(d_logit, ones, TN)
    g_tok = mmh(wide, d_rows, TN) + d_tok_q * query
    g_emb = mmh(weights, d_rows, TN) + d_emb_q * query
    row = lax.broadcasted_iota(jnp.int32, (LEADS, D), 0)
    g_lead = jnp.where(row == lead_ref[0], column_sum(d_rows), 0.0)
    gvec[0:1, :] = column_sum(d_tok_q * tok) + column_sum(d_emb_q * emb)
    gvec[15:16, :] = jnp.zeros((1, D), F32)
    for k in range(8):
        part = slice(k * BLOCK, (k + 1) * BLOCK)
        put(small_ref, EROWS * k, g_tok[:, part])
        put(small_ref, EROWS * k + HOUT, g_emb[:, part])
        put(small_ref, EROWS * k + HOUT + VARS, g_lead[:, part])
        put(small_ref, VEC_AT + 16 * k, gvec[:, part])


SLOTS = 768
ROWS = 120
HALF = 64


def sides_of(b):
    li = jnp.where(
        b < 192, b // 24, jnp.where(b < 256, b // 8 - 16, jnp.where(b < 512, b // 32 + 8, b // 8 - 40))
    )
    ri = jnp.where(
        b < 192,
        lax.rem(b, 24),
        jnp.where(
            b < 256,
            24 + lax.rem(b, 8),
            jnp.where(b < 512, 32 + lax.rem(b, 32), 64 + lax.rem(b, 8)),
        ),
    )
    return li, ri


def reduce_kernel(
    order_ref,
    left_hbm,
    right_hbm,
    small_ref,
    lroot_hbm,
    mom_hbm,
    rroot_hbm,
    own_hbm,
    ggt_hbm,
    gtg_hbm,
    lgr_hbm,
    turned_hbm,
    all_ref,
    sum_ref,
    lroot_ref,
    mom_ref,
    rroot_ref,
    own_ref,
    ggt_ref,
    gtg_ref,
    lgr_ref,
    turned_ref,
    lt,
    rt,
    mine,
    theirs,
    acc,
    acc_small,
    land,
    land_small,
    out,
    out_small,
    tail,
    in_sem,
    swap_sem,
    recv,
    send,
    recv_small,
    send_small,
    norms,
    across,
    t_recv,
    t_send,
    t_sib,
    n_send,
    n_recv,
    root_sem,
    out_sem,
):
    place = Place()
    loads = [
        pltpu.make_async_copy(left_hbm.at[0], lt.at[:, :, pl.ds(0, TOK)], in_sem.at[0]),
        pltpu.make_async_copy(left_hbm.at[1], lt.at[:, :, pl.ds(TOK, TOK)], in_sem.at[1]),
        pltpu.make_async_copy(right_hbm.at[0], rt.at[:, pl.ds(0, TOK), :], in_sem.at[2]),
        pltpu.make_async_copy(right_hbm.at[1], rt.at[:, pl.ds(TOK, TOK), :], in_sem.at[3]),
    ]
    loads.append(pltpu.make_async_copy(small_ref.at[:, place.core], mine, in_sem.at[4]))
    for c in loads:
        c.start()
    later = [
        pltpu.make_async_copy(src, dst, root_sem.at[i])
        for i, (src, dst) in enumerate(
            ((lroot_hbm, lroot_ref), (mom_hbm, mom_ref), (rroot_hbm, rroot_ref))
        )
    ]
    place.greet()
    swap = pltpu.make_async_remote_copy(
        small_ref.at[:, 1 - place.core],
        theirs,
        swap_sem.at[0],
        swap_sem.at[1],
        place.sibling(),
        MESH_ID,
    )
    swap.start()
    for c in later:
        c.start()
    for c in loads:
        c.wait()

    def own_piece(part, device, chip, out_at):
        if part < 4:

            def block(j, _):
                slot = device * SHARE + part * PIECE + j
                li, ri = sides_of(order_ref[slot])
                acc[j] = mm(lt[li], rt[ri])
                return 0

            lax.fori_loop(0, PIECE, block, 0, unroll=3)
        else:
            acc_small[...] = mine[chip // 2, lax.rem(chip, 2), pl.ds((part - 4) * HALF, HALF), :]

    def add_landed(part, index):
        if part < 4:
            acc[...] += land[index].astype(F32)
        else:
            acc_small[...] += land_small[index]

    me = place.linear(place.z, place.x, place.y)

    def keep(part, out_at, root):
        if part < 4:
            if root:
                own_ref[pl.ds(part * PIECE, PIECE)] = acc[...]
            else:
                out[out_at] = acc[...].astype(BF)
        elif root:
            tail[me * 2 + part - 4] = acc_small[...]
        else:
            out_small[out_at] = acc_small[...]

    base, _ = landing_base(MAIN)
    base_small, _ = landing_base(SMALL)

    def main_step(step):
        reduce_step(
            place, MAIN, base, step, own_piece, add_landed, land, recv, out, send, keep, 0
        )

    def small_step(step):
        reduce_step(
            place, SMALL, base_small, step, own_piece, add_landed,
            land_small, recv_small, out_small, send_small, keep, 4,
        )

    stores = []

    def store(index, source, target, begin, count):
        part = pl.ds(begin, count)
        copy = pltpu.make_async_copy(source.at[part], target.at[part], out_sem.at[index])
        copy.start()
        stores.append(copy)

    def product(part, j):
        i = part * PIECE + j
        g = own_ref[i]
        ggt_ref[i] = mmh(g, g, NT)
        gtg_ref[i] = mmh(g, g, TN)
        lgr_ref[i] = mmh(mmh(lroot_ref[i], g), rroot_ref[i])
        if j == PIECE - 1:
            store(4 * part, own_ref, own_hbm, part * PIECE, PIECE)
            store(4 * part + 1, ggt_ref, ggt_hbm, part * PIECE, PIECE)
            store(4 * part + 2, gtg_ref, gtg_hbm, part * PIECE, PIECE)
            store(4 * part + 3, lgr_ref, lgr_hbm, part * PIECE, PIECE)

    def small_root():
        first = tail[me * 2]
        data = tail[me * 2 + 1, 0 : ROWS - HALF, :]
        return jnp.sum(first * first, keepdims=True) + jnp.sum(data * data, keepdims=True)

    spread = gather_steps(
        place,
        TAIL,
        [step[1:] for step in REDUCE_PLAN if step[0] == 1],
        lambda i: tail.at[i],
        lambda n: tail.at[pl.ds(0, n)],
        t_recv,
        t_send,
        t_sib.at[pl.ds(0, 1)],
        t_sib.at[pl.ds(1, 1)],
    )
    def send_norm(squares):
        norms[place.s] = jnp.broadcast_to(
            jnp.sum(squares, keepdims=True) + small_root(), (8, BLOCK)
        )
        lax.fori_loop(1, NSEQ, lambda o, _: (norm_copy(o).start(), 0)[1], 0)

    def norm_copy(o):
        peer = lax.rem(place.s + o, NSEQ)
        return pltpu.make_async_remote_copy(
            norms.at[place.s],
            norms.at[place.s],
            n_send.at[o],
            n_recv.at[o],
            (peer, place.y),
            MESH_ID,
        )

    squares = jnp.zeros((BLOCK, BLOCK), F32)
    roots = 0
    turned = 0
    small_roots = 0
    swapped = False
    for kind, part, dx, dy, rank in REDUCE_PLAN:
        root = dx == 0 and dy == 0 and rank == 3
        if kind == 1:
            next(spread)
        elif kind == 2:
            product(part, dx)
        elif kind == 3:
            if turned == 0:
                for c in later:
                    c.wait()
            turned_ref[turned] = mmh(mmh(lroot_ref[turned], mom_ref[turned]), rroot_ref[turned])
            turned += 1
            if turned == SHARE:
                store(16, turned_ref, turned_hbm, 0, SHARE)
        elif part >= 4:
            if not swapped:
                swapped = True
                swap.wait()
                mine[...] += theirs[...]
            small_step((part - 4, dx, dy, rank))
            small_roots += root
        else:
            main_step((part, dx, dy, rank))
            if root:
                for i in range(part * PIECE, (part + 1) * PIECE):
                    squares = squares + own_ref[i] * own_ref[i]
                roots += 1
        if kind == 0 and root and roots == 4 and small_roots == 2:
            send_norm(squares)

    for _ in spread:
        pass
    for d in range(32):
        all_ref[d, 0:HALF, :] = tail[2 * d]
        all_ref[d, HALF:ROWS, :] = tail[2 * d + 1, 0 : ROWS - HALF, :]
    lax.fori_loop(1, NSEQ, lambda o, _: (norm_copy(o).wait(), 0)[1], 0)
    total = norms[0]
    for k in range(1, NSEQ):
        total = total + norms[k]
    across[0] = total
    over = pltpu.make_async_remote_copy(
        across.at[0], across.at[1], n_send.at[0], n_recv.at[0], (place.s, 1 - place.y), MESH_ID
    )
    over.start()
    drain(place, MAIN, lambda n: out.at[pl.ds(0, n)], send, REDUCE_HOPS)
    drain(place, SMALL, lambda n: out_small.at[pl.ds(0, n)], send_small, REDUCE_HOPS)
    for copy in stores:
        copy.wait()
    over.wait()
    sum_ref[0] = across[0] + across[1]
    sum_ref[1] = tail[1, ROWS - HALF : HALF, :]


def run_reduce(order, left, right, small, lroots, momentum, rroots):
    vmem = pl.BlockSpec(memory_space=VM)
    smem = pl.BlockSpec(memory_space=pltpu.SMEM)
    anyspace = pl.BlockSpec(memory_space=pl.ANY)
    dma = pltpu.SemaphoreType.DMA
    _, count = landing_base(MAIN)
    _, count_small = landing_base(SMALL)
    stack = jax.ShapeDtypeStruct((SHARE, BLOCK, BLOCK), F32)
    return pl.pallas_call(
        reduce_kernel,
        name="reduce",
        out_shape=(stack,) * 5
        + (
            jax.ShapeDtypeStruct((32, ROWS, BLOCK), F32),
            jax.ShapeDtypeStruct((2, 8, BLOCK), F32),
        ),
        in_specs=[smem] + [anyspace] * 6,
        out_specs=(anyspace,) * 5 + (vmem, vmem),
        scratch_shapes=[VM((SHARE, BLOCK, BLOCK), F32)] * 8
        + [
            VM((N_LEFT, BLOCK, 2 * TOK), BF),
            VM((N_RIGHT, 2 * TOK, BLOCK), BF),
            VM((8, 2, 2 * HALF, BLOCK), F32),
            VM((8, 2, 2 * HALF, BLOCK), F32),
            VM((PIECE, BLOCK, BLOCK), F32),
            VM((HALF, BLOCK), F32),
            VM((count, PIECE, BLOCK, BLOCK), BF),
            VM((count_small, HALF, BLOCK), F32),
            VM((64, PIECE, BLOCK, BLOCK), BF),
            VM((32, HALF, BLOCK), F32),
            VM((64, HALF, BLOCK), F32),
            dma((5,)),
            dma((2,)),
            dma((count,)),
            dma((4,)),
            dma((count_small,)),
            dma((4,)),
            VM((NSEQ, 8, BLOCK), F32),
            VM((2, 8, BLOCK), F32),
            dma((2, 16)),
            dma((4,)),
            dma((2,)),
            dma((NSEQ,)),
            dma((NSEQ,)),
            dma((3,)),
            dma((17,)),
        ],
        compiler_params=pltpu.CompilerParams(
            collective_id=3, has_side_effects=True, vmem_limit_bytes=60 * 1024 * 1024
        ),
    )(order, left, right, small, lroots, momentum, rroots)


def final_kernel(
    sums_ref, own, ggt, gtg, lgr, turned, mom, stat_l, stat_r, blk,
    ge, gv, gh, e, e1, e2, v, v1, v2, h, h1, h2,
    loss_o, norm_o, blk_o, mom_o, l_o, r_o,
    e1_o, e2_o, e_o, v1_o, v2_o, v_o, h1_o, h2_o, h_o,
):
    norm = jnp.sqrt(sums_ref[0, 0:1, 0:1])
    loss_o[...] = sums_ref[1, 4:5, 0:1]
    norm_o[...] = norm
    clip = CLIP_NORM / jnp.maximum(norm, CLIP_NORM)
    for i in range(6):
        mom_o[i] = BETA_ONE * mom[i] + (1.0 - BETA_ONE) * (own[i] * clip)
        l_o[i] = BETA_TWO * stat_l[i] + (1.0 - BETA_TWO) * ((ggt[i] * clip) * clip)
        r_o[i] = BETA_TWO * stat_r[i] + (1.0 - BETA_TWO) * ((gtg[i] * clip) * clip)
        direction = BETA_ONE * turned[i] + (1.0 - BETA_ONE) * (lgr[i] * clip)
        blk_o[i] = blk[i] - SHAMPOO_RATE * (direction + DECAY * blk[i])
    e1_o[...], e2_o[...], e_o[...] = adam(e[...], e1[...], e2[...], jnp.concatenate([ge[0:EROWS], ge[EROWS:]], 1) * clip, EMBED_RATE)
    v1_o[...], v2_o[...], v_o[...] = adam(
        v[...], v1[...], v2[...], jnp.concatenate([gv[0:15, :], gv[16:31, :]], 1) * clip, VECTOR_RATE
    )
    h1_o[...], h2_o[...], h_o[...] = adam(h[...], h1[...], h2[...], jnp.concatenate([gh[0:HOUT], gh[HOUT:]], 1) * clip, HEAD_RATE)


def run_final(sums, stacks, flat, embed, vec, head):
    slots = pl.BlockSpec((6, BLOCK, BLOCK), lambda k: (k, 0, 0))
    table = pl.BlockSpec((EROWS, 2 * BLOCK), lambda k: (0, k))
    rows = pl.BlockSpec((15, 2 * BLOCK), lambda k: (0, k))
    wide = pl.BlockSpec((HOUT, 2 * BLOCK), lambda k: (0, k))
    one = pl.BlockSpec((1, 1), lambda k: (0, 0))
    stack = jax.ShapeDtypeStruct((SHARE, BLOCK, BLOCK), F32)
    shapes = (
        (jax.ShapeDtypeStruct((1, 1), F32),) * 2
        + (stack,) * 4
        + (jax.ShapeDtypeStruct((EROWS, D), F32),) * 3
        + (jax.ShapeDtypeStruct((15, D), F32),) * 3
        + (jax.ShapeDtypeStruct((HOUT, D), F32),) * 3
    )
    return pl.pallas_call(
        final_kernel,
        name="final",
        grid=(4,),
        out_shape=shapes,
        in_specs=[pl.BlockSpec((2, 8, BLOCK), lambda k: (0, 0, 0))]
        + [slots] * 9
        + [
            pl.BlockSpec((2 * EROWS, BLOCK), lambda k: (k, 0)),
            pl.BlockSpec((32, BLOCK), lambda k: (VEC_AT // 32 + k, 0)),
            pl.BlockSpec((2 * HOUT, BLOCK), lambda k: (HEAD_AT // HOUT // 2 + k, 0)),
        ]
        + [table] * 3
        + [rows] * 3
        + [wide] * 3,
        out_specs=(one,) * 2 + (slots,) * 4 + (table,) * 3 + (rows,) * 3 + (wide,) * 3,
        compiler_params=pltpu.CompilerParams(vmem_limit_bytes=60 * 1024 * 1024),
    )(sums, *stacks, flat, flat, flat, *embed, *vec, *head)


def fast_shards(
    inputs,
    targets,
    var_ids,
    lead_ids,
    block_order,
    blocks,
    block_momentum,
    left_stats,
    right_stats,
    left_roots,
    right_roots,
    embed_params,
    embed_first,
    embed_second,
    vectors,
    vector_first,
    vector_second,
    head_weight,
    head_first,
    head_second,
):
    slots = jnp.arange(SLOTS, dtype=jnp.int32)
    hit = block_order[None, :] == slots[:, None]
    place = jnp.sum(jnp.where(hit, slots[None, :], 0), 1)
    lat = ((np.arange(2 * LAT_P, dtype=np.float64) + 0.5) / (2 * LAT_P) - 0.5) * math.pi
    wlat = np.cos(lat)
    wlat = (wlat / np.mean(wlat)).reshape(1, LAT_P, 1, 2, 1)
    wlat = np.broadcast_to(wlat, (TOK // LAT_P, LAT_P, VARS, 2, 2)).reshape(TOK, HOUT)
    left, right, small = run_layer(
        place, lead_ids, blocks, var_ids, jnp.swapaxes(inputs, 1, 2), jnp.swapaxes(targets, 1, 2),
        embed_params, vectors, head_weight.T,
        jnp.asarray(wlat, F32),
    )
    owned, ggt, gtg, lgr, turned, every, sums = run_reduce(
        block_order, left, right, small.reshape(8, 2, 2, 2 * HALF, BLOCK),
        left_roots, block_momentum, right_roots,
    )
    loss, norm, *rest = run_final(
        sums,
        (owned, ggt, gtg, lgr, turned, block_momentum, left_stats, right_stats, blocks),
        every.reshape(32 * ROWS, BLOCK),
        (embed_params, embed_first, embed_second),
        (vectors, vector_first, vector_second),
        (head_weight.T, head_first.T, head_second.T),
    )
    return (loss.reshape(()), norm.reshape(()), *rest[:-3], *(a.T for a in rest[-3:]))


def solution(mesh):
    in_specs = (
        P("batch", "seq", None),
        P("batch", "seq", None),
        P("batch", None),
        P("batch"),
        P(),
        P(("seq", "batch"), None, None),
        P(("seq", "batch"), None, None),
        P(("seq", "batch"), None, None),
        P(("seq", "batch"), None, None),
        P(("seq", "batch"), None, None),
        P(("seq", "batch"), None, None),
        P(),
        P(),
        P(),
        P(),
        P(),
        P(),
        P(),
        P(),
        P(),
    )
    out_specs = (
        P(),
        P(),
        P(("seq", "batch"), None, None),
        P(("seq", "batch"), None, None),
        P(("seq", "batch"), None, None),
        P(("seq", "batch"), None, None),
        P(),
        P(),
        P(),
        P(),
        P(),
        P(),
        P(),
        P(),
        P(),
    )
    sizes = dict(mesh.shape)
    fast = sizes == {"seq": NSEQ, "batch": 2}
    return jax.shard_map(fast_shards if fast else shards, mesh=mesh, in_specs=in_specs, out_specs=out_specs, check_vma=False)
```

```python
import math

import jax
import jax.numpy as jnp
import numpy as np
from jax import lax
from jax.experimental import pallas as pl
from jax.experimental.pallas import tpu as pltpu
from jax.sharding import PartitionSpec as P

D = 1024
HEADS = 16
HD = 64
FF = 4096
VARS = 48
LEADS = 32
LAT_P = 64
KMODES = 32
STEP = 10


HIGH = lax.Precision.HIGHEST
EPS = 1e-05
CLIP_NORM = 0.001
SPECTRAL = 0.5
BETA_ONE = 0.9
BETA_TWO = 0.95
SHAMPOO_RATE = 0.1
DECAY = 0.01
ADAM_EPS = 1e-08
EMBED_RATE = 0.2
VECTOR_RATE = 0.5
HEAD_RATE = 0.05
FLOOR = -1e30
EROWS = VARS * 5 + LEADS
HOUT = VARS * 4
MSE_COUNT = 786432.0
DFT_COUNT = 25165824.0


def layer_norm(rows, gain, shift):
    mean = jnp.mean(rows, -1, keepdims=True)
    centred = rows - mean
    return centred * lax.rsqrt(jnp.mean(centred * centred, -1, keepdims=True) + EPS) * gain + shift


def to_blocks(matrix, size):
    rows, cols = matrix.shape
    return (
        matrix.reshape(rows // size, size, cols // size, size)
        .transpose(0, 2, 1, 3)
        .reshape(-1, size, size)
    )


def from_blocks(stack, rows, cols):
    size = stack.shape[-1]
    return (
        stack.reshape(rows // size, cols // size, size, size)
        .transpose(0, 2, 1, 3)
        .reshape(rows, cols)
    )


def split_matrices(stack):
    size = stack.shape[-1]
    found = []
    begin = 0
    for rows, cols in ((D, 3 * D), (D, D), (D, FF), (FF, D)):
        count = rows * cols // (size * size)
        found.append(from_blocks(stack[begin : begin + count], rows, cols))
        begin += count
    return found


def embed_patches(pixels, tok_sel, emb_sel, query, lead_rows):
    tokens = jnp.einsum("spvc,svcd->spvd", pixels, tok_sel, precision=HIGH) + emb_sel[:, None]
    logits = jnp.einsum("spvd,d->spv", tokens, query, precision=HIGH) * (1.0 / math.sqrt(D))
    weights = jax.nn.softmax(logits, -1)
    return jnp.einsum("spv,spvd->spd", weights, tokens, precision=HIGH) + lead_rows[:, None]


def split_heads(rows):
    return rows.reshape(rows.shape[0], rows.shape[1], HEADS, HD)


def attention_forward(query, keys, values):
    seqs, length, _ = query.shape
    scale = 1.0 / math.sqrt(HD)
    heads_q = split_heads(query)
    start_state = (
        jnp.zeros((seqs, HEADS, length, HD), jnp.float32),
        jnp.full((seqs, HEADS, length), FLOOR, jnp.float32),
        jnp.zeros((seqs, HEADS, length), jnp.float32),
    )
    key_rows = lax.all_gather(keys, "seq", axis=1, tiled=True)
    value_rows = lax.all_gather(values, "seq", axis=1, tiled=True)
    count = key_rows.shape[1] // length
    key_blocks = key_rows.reshape(seqs, count, length, HEADS, HD)
    value_blocks = value_rows.reshape(seqs, count, length, HEADS, HD)

    def visit(inner, index):
        acc, top, total = inner
        scores = (
            jnp.einsum(
                "sphd,snhd->shpn", heads_q, key_blocks[:, index], preferred_element_type=jnp.float32
            )
            * scale
        )
        new_top = jnp.maximum(top, jnp.max(scores, -1))
        fade = jnp.exp(top - new_top)
        probs = jnp.exp(scores - new_top[..., None])
        total = total * fade + jnp.sum(probs, -1)
        acc = acc * fade[..., None] + jnp.einsum(
            "shpn,snhd->shpd",
            probs.astype(jnp.bfloat16),
            value_blocks[:, index],
            preferred_element_type=jnp.float32,
        )
        return ((acc, new_top, total), None)

    inner, _ = lax.scan(visit, start_state, jnp.arange(count))
    acc, top, total = inner
    attended = (acc / total[..., None]).transpose(0, 2, 1, 3).reshape(seqs, length, HEADS * HD)
    return (attended, (top + jnp.log(total)).transpose(0, 2, 1))


def attention_backward(query, keys, values, attended, lse, d_att):
    seqs, length, _ = query.shape
    scale = 1.0 / math.sqrt(HD)
    heads_q = split_heads(query)
    heads_k = split_heads(keys)
    heads_v = split_heads(values)
    heads_d = split_heads(d_att)
    delta = jnp.sum(heads_d.astype(jnp.float32) * split_heads(attended), -1)
    lse_h = lse.transpose(0, 2, 1)
    delta_h = delta.transpose(0, 2, 1)
    key_rows = lax.all_gather(keys, "seq", axis=1, tiled=True)
    value_rows = lax.all_gather(values, "seq", axis=1, tiled=True)
    count = key_rows.shape[1] // length
    key_blocks = key_rows.reshape(seqs, count, length, HEADS, HD)
    value_blocks = value_rows.reshape(seqs, count, length, HEADS, HD)

    def visit(inner, index):
        k_part = key_blocks[:, index]
        scores = (
            jnp.einsum("sphd,snhd->shpn", heads_q, k_part, preferred_element_type=jnp.float32)
            * scale
        )
        probs = jnp.exp(scores - lse_h[..., None])
        d_prob = jnp.einsum(
            "sphd,snhd->shpn", heads_d, value_blocks[:, index], preferred_element_type=jnp.float32
        )
        d_score = (probs * (d_prob - delta_h[..., None])).astype(jnp.bfloat16)
        return (
            inner
            + jnp.einsum("shpn,snhd->sphd", d_score, k_part, preferred_element_type=jnp.float32)
            * scale,
            None,
        )

    inner, _ = lax.scan(visit, jnp.zeros((seqs, length, HEADS, HD), jnp.float32), jnp.arange(count))
    d_query = inner
    all_lse, all_delta = (
        lax.all_gather(lse, "seq", axis=1, tiled=True),
        lax.all_gather(delta, "seq", axis=1, tiled=True),
    )
    empty = jnp.zeros((seqs, length, HEADS, HD), jnp.float32)
    q_rows = lax.all_gather(query, "seq", axis=1, tiled=True)
    g_rows = lax.all_gather(d_att, "seq", axis=1, tiled=True)
    count = q_rows.shape[1] // length
    q_blocks = q_rows.reshape(seqs, count, length, HEADS, HD)
    g_blocks = g_rows.reshape(seqs, count, length, HEADS, HD)
    lse_rows = all_lse.reshape(seqs, count, length, HEADS)
    delta_rows = all_delta.reshape(seqs, count, length, HEADS)

    def visit(inner, index):
        d_key, d_value = inner
        q_part = q_blocks[:, index]
        g_part = g_blocks[:, index]
        scores = (
            jnp.einsum("snhd,sphd->shnp", q_part, heads_k, preferred_element_type=jnp.float32)
            * scale
        )
        probs = jnp.exp(scores - lse_rows[:, index].transpose(0, 2, 1)[..., None])
        d_value = d_value + jnp.einsum(
            "shnp,snhd->sphd",
            probs.astype(jnp.bfloat16),
            g_part,
            preferred_element_type=jnp.float32,
        )
        d_prob = jnp.einsum("snhd,sphd->shnp", g_part, heads_v, preferred_element_type=jnp.float32)
        d_score = (probs * (d_prob - delta_rows[:, index].transpose(0, 2, 1)[..., None])).astype(
            jnp.bfloat16
        )
        d_key = (
            d_key
            + jnp.einsum("shnp,snhd->sphd", d_score, q_part, preferred_element_type=jnp.float32)
            * scale
        )
        return ((d_key, d_value), None)

    inner, _ = lax.scan(visit, (empty, empty), jnp.arange(count))
    d_key, d_value = inner
    return (d_query, d_key, d_value)


def feed_inner(normed_two, w_up, vectors):
    upper = jnp.dot(normed_two, w_up, preferred_element_type=jnp.float32) + vectors[11:].reshape(-1)
    return (upper, jax.nn.gelu(upper).astype(jnp.bfloat16))


def layer_forward(rows, seqs, mats, vectors):
    w_qkv, w_out, w_up, w_down = mats
    normed = layer_norm(rows, vectors[1], vectors[2]).astype(jnp.bfloat16)
    bias = jnp.concatenate([vectors[9], jnp.zeros_like(vectors[9]), vectors[10]])
    qkv = (jnp.dot(normed, w_qkv, preferred_element_type=jnp.float32) + bias).astype(jnp.bfloat16)
    query = qkv[:, :D].reshape(seqs, -1, D)
    keys = qkv[:, D : 2 * D].reshape(seqs, -1, D)
    values = qkv[:, 2 * D :].reshape(seqs, -1, D)
    attended, lse = attention_forward(query, keys, values)
    att_low = attended.reshape(-1, D).astype(jnp.bfloat16)
    mid = rows + jnp.dot(att_low, w_out, preferred_element_type=jnp.float32) + vectors[7]
    normed_two = layer_norm(mid, vectors[3], vectors[4]).astype(jnp.bfloat16)
    upper, active = feed_inner(normed_two, w_up, vectors)
    out = mid + jnp.dot(active, w_down, preferred_element_type=jnp.float32) + vectors[8]
    saved = (upper, active)
    return (out, (rows, normed, query, keys, values, attended, lse, mid, normed_two, saved))


def layer_backward(d_out, kept, mats, vectors):
    rows, normed, query, keys, values, attended, lse, mid, normed_two, saved = kept
    w_qkv, w_out, w_up, w_down = mats
    upper, active = saved
    d_branch = d_out.astype(jnp.bfloat16)
    g_down = jnp.einsum("rf,rd->fd", active, d_branch, preferred_element_type=jnp.float32)
    d_active = jnp.einsum("rd,fd->rf", d_branch, w_down, preferred_element_type=jnp.float32)
    d_upper = jax.vjp(jax.nn.gelu, upper)[1](d_active)[0].astype(jnp.bfloat16)
    g_up = jnp.einsum("rd,rf->df", normed_two, d_upper, preferred_element_type=jnp.float32)
    d_normed_two = jnp.einsum("rf,df->rd", d_upper, w_up, preferred_element_type=jnp.float32)
    d_mid_norm, g_gain_two, g_shift_two = jax.vjp(layer_norm, mid, vectors[3], vectors[4])[1](
        d_normed_two
    )
    d_mid = d_out + d_mid_norm
    d_mid_low = d_mid.astype(jnp.bfloat16)
    att_low = attended.reshape(-1, D).astype(jnp.bfloat16)
    g_out = jnp.einsum("ra,rd->ad", att_low, d_mid_low, preferred_element_type=jnp.float32)
    d_att = jnp.einsum("rd,ad->ra", d_mid_low, w_out, preferred_element_type=jnp.float32).astype(
        jnp.bfloat16
    )
    seqs = query.shape[0]
    d_query, d_key, d_value = attention_backward(
        query, keys, values, attended, lse, d_att.reshape(seqs, -1, D)
    )
    d_qkv = jnp.concatenate(
        [d_query.reshape(-1, D), d_key.reshape(-1, D), d_value.reshape(-1, D)], 1
    ).astype(jnp.bfloat16)
    g_qkv = jnp.einsum("rd,re->de", normed, d_qkv, preferred_element_type=jnp.float32)
    d_normed = jnp.einsum("re,de->rd", d_qkv, w_qkv, preferred_element_type=jnp.float32)
    d_rows_norm, g_gain_one, g_shift_one = jax.vjp(layer_norm, rows, vectors[1], vectors[2])[1](
        d_normed
    )
    qkv_sums = jnp.sum(d_qkv.astype(jnp.float32), 0)
    small = (
        g_gain_one,
        g_shift_one,
        g_gain_two,
        g_shift_two,
        jnp.sum(d_mid_low.astype(jnp.float32), 0),
        jnp.sum(d_branch.astype(jnp.float32), 0),
        qkv_sums[:D],
        qkv_sums[2 * D :],
        jnp.sum(d_upper.astype(jnp.float32), 0),
    )
    return (d_mid + d_rows_norm, (g_qkv, g_out, g_up, g_down), small)


def loss_terms(pred, targets, seqs, length):
    strips = lax.axis_size("seq")
    cols = length // LAT_P
    nlat = 2 * LAT_P
    nlon = 2 * cols * strips
    all_seqs = seqs * lax.axis_size("batch")
    diff = pred.reshape(seqs, length, -1) - targets.astype(jnp.float32)
    grid = (
        diff.reshape(seqs, cols, LAT_P, VARS, 2, 2)
        .transpose(0, 3, 2, 4, 1, 5)
        .reshape(seqs, VARS, nlat, 2 * cols)
    )
    lat = ((jnp.arange(nlat, dtype=jnp.float32) + 0.5) / nlat - 0.5) * math.pi
    weight = jnp.cos(lat)
    weight = (weight / jnp.mean(weight))[None, None, :, None]
    column = lax.axis_index("seq") * (2 * cols) + jnp.arange(2 * cols, dtype=jnp.int32)
    modes = jnp.arange(KMODES, dtype=jnp.int32)
    angle = (column[:, None] * modes[None] % nlon).astype(jnp.float32) * (2.0 * math.pi / nlon)
    cosine = jnp.cos(angle)
    sine = jnp.sin(angle)
    part_c = jnp.einsum("svrc,ck->svrk", grid, cosine, precision=HIGH)
    part_s = jnp.einsum("svrc,ck->svrk", grid, sine, precision=HIGH)
    full_c, full_s = lax.psum((part_c, part_s), "seq")
    mse_count = all_seqs * VARS * nlat * nlon
    dft_count = nlon * all_seqs * VARS * nlat * KMODES
    mse = jnp.sum(weight * grid * grid) / mse_count
    spectral = SPECTRAL * jnp.sum(weight * (full_c * full_c + full_s * full_s)) / dft_count
    first = (lax.axis_index("seq") == 0).astype(jnp.float32)
    back_wave = jnp.einsum("svrk,ck->svrc", full_c, cosine, precision=HIGH) + jnp.einsum(
        "svrk,ck->svrc", full_s, sine, precision=HIGH
    )
    d_grid = 2.0 * weight * grid / mse_count + 2.0 * SPECTRAL / dft_count * weight * back_wave
    d_pred = (
        d_grid.reshape(seqs, VARS, LAT_P, 2, cols, 2)
        .transpose(0, 4, 2, 1, 3, 5)
        .reshape(seqs * length, VARS * 4)
    )
    return (d_pred, mse + first * spectral)


def adam(value, first, second, grad, rate):
    first = BETA_ONE * first + (1.0 - BETA_ONE) * grad
    second = BETA_TWO * second + (1.0 - BETA_TWO) * grad * grad
    step = first / (1.0 - BETA_ONE**STEP) / (jnp.sqrt(second / (1.0 - BETA_TWO**STEP)) + ADAM_EPS)
    return (first, second, value - rate * (step + DECAY * value))


def shards(
    inputs,
    targets,
    var_ids,
    lead_ids,
    block_order,
    blocks,
    block_momentum,
    left_stats,
    right_stats,
    left_roots,
    right_roots,
    embed_params,
    embed_first,
    embed_second,
    vectors,
    vector_first,
    vector_second,
    head_weight,
    head_first,
    head_second,
):
    seqs, length, _ = inputs.shape
    size = blocks.shape[-1]
    low_blocks = blocks.astype(jnp.bfloat16)
    stack = lax.all_gather(low_blocks, ("seq", "batch"), axis=0, tiled=True)
    natural = jnp.zeros_like(stack).at[block_order].set(stack)
    mats = split_matrices(natural)
    head_low = head_weight.astype(jnp.bfloat16)
    pick = (var_ids[..., None] == jnp.arange(VARS, dtype=jnp.int32)[None, None]).astype(jnp.float32)
    lead_pick = (lead_ids[:, None] == jnp.arange(LEADS, dtype=jnp.int32)[None]).astype(jnp.float32)
    tok_sel = jnp.einsum(
        "svw,wcd->svcd", pick, embed_params[: VARS * 4].reshape(VARS, 4, D), precision=HIGH
    )
    emb_sel = jnp.einsum("svw,wd->svd", pick, embed_params[VARS * 4 : VARS * 5], precision=HIGH)
    lead_rows = jnp.dot(lead_pick, embed_params[VARS * 5 :], precision=HIGH)
    pixels = inputs.astype(jnp.float32).reshape(seqs, length, VARS, 4)

    def embed_local(tok_part, emb_part, query, lead_part):
        return embed_patches(pixels, tok_part, emb_part, query, lead_part)

    stream, embed_back = jax.vjp(embed_local, tok_sel, emb_sel, vectors[0], lead_rows)
    out, kept = layer_forward(stream.reshape(-1, D), seqs, mats, vectors)
    final_rows, final_back = jax.vjp(layer_norm, out, vectors[5], vectors[6])
    final = final_rows.astype(jnp.bfloat16)
    pred = jnp.dot(final, head_low, preferred_element_type=jnp.float32)
    d_pred, loss_part = loss_terms(pred, targets, seqs, length)
    d_low = d_pred.astype(jnp.bfloat16)
    g_head = jnp.einsum("rd,ro->do", final, d_low, preferred_element_type=jnp.float32)
    d_final = jnp.einsum("ro,do->rd", d_low, head_low, preferred_element_type=jnp.float32)
    d_out, g_gain_final, g_shift_final = final_back(d_final)
    d_rows, matrix_grads, small = layer_backward(d_out, kept, mats, vectors)
    d_tok, d_emb, d_query, d_lead = embed_back(d_rows.reshape(seqs, length, D))
    g_embed = jnp.concatenate(
        [
            jnp.einsum("svw,svcd->wcd", pick, d_tok, precision=HIGH).reshape(VARS * 4, D),
            jnp.einsum("svw,svd->wd", pick, d_emb, precision=HIGH),
            jnp.einsum("sl,sd->ld", lead_pick, d_lead, precision=HIGH),
        ]
    )
    g_gain_one, g_shift_one, g_gain_two, g_shift_two, b_out, b_down, b_query, b_value, b_up = small
    g_vectors = jnp.concatenate(
        [
            jnp.stack(
                [
                    d_query,
                    g_gain_one,
                    g_shift_one,
                    g_gain_two,
                    g_shift_two,
                    g_gain_final,
                    g_shift_final,
                    b_out,
                    b_down,
                    b_query,
                    b_value,
                ]
            ),
            b_up.reshape(-1, D),
        ]
    )
    slot_grads = jnp.concatenate([to_blocks(grad, size) for grad in matrix_grads])[block_order]
    owned = lax.psum_scatter(slot_grads, ("seq", "batch"), scatter_dimension=0, tiled=True)
    g_embed, g_vectors, g_head, loss_total = lax.psum(
        (g_embed, g_vectors, g_head, loss_part), ("seq", "batch")
    )
    rest_squares = (
        jnp.sum(g_embed * g_embed) + jnp.sum(g_vectors * g_vectors) + jnp.sum(g_head * g_head)
    )
    grad_norm = jnp.sqrt(lax.psum(jnp.sum(owned * owned), ("seq", "batch")) + rest_squares)
    clip = CLIP_NORM / jnp.maximum(grad_norm, CLIP_NORM)
    owned = owned * clip
    new_momentum = BETA_ONE * block_momentum + (1.0 - BETA_ONE) * owned
    new_left = BETA_TWO * left_stats + (1.0 - BETA_TWO) * jnp.einsum(
        "bij,bkj->bik", owned, owned, precision=HIGH
    )
    new_right = BETA_TWO * right_stats + (1.0 - BETA_TWO) * jnp.einsum(
        "bji,bjk->bik", owned, owned, precision=HIGH
    )
    direction = jnp.einsum(
        "bij,bjk->bik",
        jnp.einsum("bij,bjk->bik", left_roots, new_momentum, precision=HIGH),
        right_roots,
        precision=HIGH,
    )
    new_blocks = blocks - SHAMPOO_RATE * (direction + DECAY * blocks)
    e_one, e_two, e_new = adam(embed_params, embed_first, embed_second, g_embed * clip, EMBED_RATE)
    v_one, v_two, v_new = adam(vectors, vector_first, vector_second, g_vectors * clip, VECTOR_RATE)
    h_one, h_two, h_new = adam(head_weight, head_first, head_second, g_head * clip, HEAD_RATE)
    return (
        loss_total,
        grad_norm,
        new_blocks,
        new_momentum,
        new_left,
        new_right,
        e_one,
        e_two,
        e_new,
        v_one,
        v_two,
        v_new,
        h_one,
        h_two,
        h_new,
    )


SHARE = 24
PIECE = 6
MAIN = ("zxy", "zyx", "xzy", "yzx")
SMALL = ("xyz", "yxz")
TAIL = ("zxy", "zyx")
GATHER_SIZES = (5, 5, 7, 7)
GATHER_ORDER = (
    (0, 0, 0, 3), (3, 0, 0, 3), (1, 0, 0, 3), (2, 0, 0, 3), (1, 0, 0, 2), (1, 0, 1, 3), (0, 0, 0, 2), (1, 1, 0, 3),
    (3, 0, 0, 2), (0, 0, 0, 1), (2, 1, 0, 3), (1, 0, 0, 0), (1, 0, 0, 1), (2, 0, 0, 2), (3, 0, 1, 3), (2, 1, 0, 1),
    (2, 1, 0, 2), (0, 0, 1, 3), (0, 0, 0, 0), (3, 0, 1, 2), (2, 0, 1, 3), (1, 0, 1, 2), (0, 1, 0, 1), (2, 0, 0, 0),
    (2, 0, 0, 1), (0, 1, 0, 3), (1, 0, 1, 0), (0, 1, 0, 0), (3, 0, 0, 0), (0, 1, 0, 2), (1, 1, 0, 2), (3, 0, 1, 1),
    (3, 0, 1, 0), (3, 0, 0, 1), (3, 1, 1, 2), (1, 1, 1, 0), (2, 0, 1, 2), (3, 1, 0, 3), (1, 1, 1, 2), (1, 0, 1, 1),
    (3, 1, 0, 2), (2, 1, 0, 0), (1, 1, 0, 0), (0, 0, 1, 2), (0, 0, 1, 0), (2, 1, 1, 1), (3, 1, 1, 0), (0, 1, 1, 3),
    (0, 1, 1, 0), (0, 1, 1, 1), (2, 0, 1, 0), (2, 1, 1, 2), (3, 1, 1, 1), (2, 0, 1, 1), (2, 1, 1, 3), (0, 0, 1, 1),
    (3, 1, 0, 1), (3, 1, 0, 0), (1, 1, 1, 3), (0, 1, 1, 2), (1, 1, 0, 1), (3, 1, 1, 3), (1, 1, 1, 1), (2, 1, 1, 0),
)
REDUCE_PLAN = (
    (0, 4, 1, 1, 1), (0, 4, 0, 0, 0), (0, 3, 1, 0, 1), (0, 4, 1, 1, 0), (0, 0, 1, 1, 1), (0, 4, 0, 1, 0), (0, 5, 0, 0, 1),
    (3, 0, 0, 0, 0), (3, 0, 0, 0, 0), (0, 5, 1, 1, 0), (0, 5, 0, 1, 0), (0, 3, 1, 0, 0), (0, 2, 1, 1, 0), (0, 5, 1, 0, 0),
    (3, 0, 0, 0, 0), (0, 4, 1, 0, 0), (0, 5, 1, 1, 1), (0, 5, 1, 0, 1), (0, 1, 1, 1, 0), (0, 5, 0, 1, 1), (0, 5, 1, 1, 2),
    (0, 4, 1, 1, 2), (0, 2, 0, 1, 0), (0, 2, 1, 1, 2), (3, 0, 0, 0, 0), (0, 4, 0, 1, 1), (0, 3, 1, 1, 2), (0, 1, 1, 1, 1),
    (0, 4, 1, 0, 2), (3, 0, 0, 0, 0), (3, 0, 0, 0, 0), (0, 4, 0, 1, 2), (0, 5, 0, 0, 0), (0, 3, 0, 0, 1), (3, 0, 0, 0, 0),
    (3, 0, 0, 0, 0), (0, 0, 1, 1, 0), (0, 0, 1, 1, 3), (0, 3, 1, 1, 0), (0, 3, 0, 0, 0), (3, 0, 0, 0, 0), (0, 5, 0, 1, 2),
    (0, 3, 1, 1, 1), (0, 0, 1, 0, 1), (3, 0, 0, 0, 0), (3, 0, 0, 0, 0), (0, 4, 1, 1, 3), (3, 0, 0, 0, 0), (3, 0, 0, 0, 0),
    (0, 2, 1, 0, 0), (0, 5, 1, 1, 3), (0, 2, 1, 1, 1), (3, 0, 0, 0, 0), (0, 0, 0, 1, 1), (0, 0, 1, 1, 2), (0, 5, 1, 0, 2),
    (3, 0, 0, 0, 0), (0, 2, 0, 0, 0), (0, 1, 1, 1, 2), (0, 0, 0, 1, 0), (0, 2, 1, 0, 2), (0, 1, 1, 0, 0), (0, 1, 0, 1, 0),
    (0, 2, 1, 1, 3), (3, 0, 0, 0, 0), (3, 0, 0, 0, 0), (0, 4, 1, 0, 1), (0, 1, 1, 1, 3), (0, 0, 1, 0, 0), (0, 1, 1, 0, 1),
    (3, 0, 0, 0, 0), (0, 2, 1, 0, 1), (0, 1, 0, 1, 1), (0, 5, 0, 1, 3), (0, 3, 0, 1, 1), (3, 0, 0, 0, 0), (0, 2, 0, 1, 1),
    (0, 4, 1, 0, 3), (3, 0, 0, 0, 0), (0, 5, 1, 0, 3), (0, 5, 0, 0, 2), (3, 0, 0, 0, 0), (0, 3, 0, 1, 0), (0, 2, 0, 1, 2),
    (0, 0, 0, 1, 2), (0, 3, 1, 0, 2), (0, 1, 0, 1, 2), (0, 3, 1, 1, 3), (3, 0, 0, 0, 0), (0, 0, 0, 0, 1), (0, 4, 0, 1, 3),
    (0, 0, 1, 0, 2), (0, 2, 0, 1, 3), (3, 0, 0, 0, 0), (0, 1, 0, 0, 0), (0, 0, 0, 1, 3), (0, 0, 0, 0, 0), (0, 1, 1, 0, 2),
    (0, 2, 1, 0, 3), (3, 0, 0, 0, 0), (0, 0, 1, 0, 3), (0, 1, 0, 0, 1), (0, 3, 0, 1, 2), (0, 1, 1, 0, 3), (0, 1, 0, 1, 3),
    (0, 3, 1, 0, 3), (0, 5, 0, 0, 3), (0, 2, 0, 0, 1), (0, 4, 0, 0, 1), (1, 1, 0, 0, 3), (0, 4, 0, 0, 2), (0, 2, 0, 0, 2),
    (0, 0, 0, 0, 2), (1, 1, 0, 0, 2), (0, 1, 0, 0, 2), (0, 3, 0, 1, 3), (0, 4, 0, 0, 3), (1, 0, 0, 0, 3), (0, 2, 0, 0, 3),
    (2, 2, 0, 0, 0), (2, 2, 1, 0, 0), (2, 2, 2, 0, 0), (0, 3, 0, 0, 2), (2, 2, 3, 0, 0), (0, 0, 0, 0, 3), (2, 2, 4, 0, 0),
    (2, 2, 5, 0, 0), (2, 0, 0, 0, 0), (1, 0, 0, 0, 2), (2, 0, 1, 0, 0), (2, 0, 2, 0, 0), (0, 1, 0, 0, 3), (2, 1, 0, 0, 0),
    (1, 1, 0, 1, 3), (2, 1, 1, 0, 0), (2, 1, 2, 0, 0), (1, 1, 0, 1, 2), (2, 1, 3, 0, 0), (1, 1, 0, 0, 0), (2, 1, 4, 0, 0),
    (2, 0, 3, 0, 0), (1, 0, 0, 0, 0), (1, 1, 1, 0, 3), (2, 1, 5, 0, 0), (1, 0, 0, 0, 1), (2, 0, 4, 0, 0), (2, 0, 5, 0, 0),
    (1, 1, 0, 0, 1), (1, 1, 0, 1, 0), (1, 0, 1, 0, 3), (1, 0, 1, 0, 2), (0, 3, 0, 0, 3), (1, 0, 1, 0, 1), (2, 3, 0, 0, 0),
    (1, 0, 1, 0, 0), (1, 1, 0, 1, 1), (1, 0, 0, 1, 1), (2, 3, 1, 0, 0), (2, 3, 2, 0, 0), (2, 3, 3, 0, 0), (1, 1, 1, 1, 2),
    (2, 3, 4, 0, 0), (1, 1, 1, 1, 0), (1, 1, 1, 0, 0), (1, 0, 0, 1, 2), (1, 0, 1, 1, 1), (1, 0, 0, 1, 0), (1, 1, 1, 0, 1),
    (2, 3, 5, 0, 0), (1, 0, 1, 1, 2), (1, 0, 1, 1, 0), (1, 0, 0, 1, 3), (1, 1, 1, 0, 2), (1, 1, 1, 1, 1), (1, 0, 1, 1, 3),
    (1, 1, 1, 1, 3),
)

class Place:
    def __init__(self):
        s = lax.axis_index("seq")
        self.y = lax.axis_index("batch")
        self.core = lax.rem(s, 2)
        self.x = lax.rem(s // 2, 2)
        self.z = s // 4
        self.s = s

    def chip(self, z, x, y):
        return (z * 2 + x) * 2 + y

    def linear(self, z, x, y):
        return ((z * 2 + x) * 2 + self.core) * 2 + y

    def device(self, z, x, y):
        return ((z * 2 + x) * 2 + self.core, y)

    def sibling(self):
        return (self.s + 1 - 2 * self.core, self.y)

    def far(self, rank):
        z = self.z
        if rank == 3:
            return z
        if rank == 2:
            return z + 1 - 2 * lax.rem(z, 2)
        low = z // 2
        return (3 - 3 * low) if rank == 0 else (2 - low)

    def flipped(self, dx, dy):
        x = self.x if dx == 0 else 1 - self.x
        y = self.y if dy == 0 else 1 - self.y
        return x, y

    def greet(self):
        barrier = pltpu.get_barrier_semaphore()

        def hail(o, _):
            peer = lax.rem(self.s + o, NSEQ)
            pl.semaphore_signal(barrier, inc=1, device_id=(peer, self.y), device_id_type=MESH_ID)
            return _

        lax.fori_loop(1, NSEQ, hail, 0)
        pl.semaphore_signal(
            barrier, inc=1, device_id=(self.s, 1 - self.y), device_id_type=MESH_ID
        )
        pl.semaphore_wait(barrier, NSEQ)


def last_move(order, dx, dy, rank):
    found = -1
    for i, c in enumerate(order):
        if (c == "x" and dx) or (c == "y" and dy) or (c == "z" and rank != 3):
            found = i
    return found


def sends_before(order, axis):
    count = 1
    for c in order:
        if c == axis:
            return count
        count *= 4 if c == "z" else 2
    return count


def drain(place, orders, total, sem, hops, sizes=None):
    sizes = sizes or (1,) * len(orders)
    count = {
        c: sum(sends_before(order, c) * size for order, size in zip(orders, sizes)) for c in "xyz"
    }

    def finish(i, pieces):
        ref = total(pieces)
        pltpu.make_async_remote_copy(
            ref, ref, sem.at[i], sem.at[i], place.sibling(), MESH_ID
        ).wait_send()

    finish(0, count["x"])
    finish(1, count["y"])
    for z in range(4):
        for i in (2, 3):
            if hops[i - 2][z]:

                @pl.when(place.z == z)
                def _(i=i, z=z):
                    finish(i, count["z"] * hops[i - 2][z])


GATHER_HOPS = ((1, 2, 3, 0), (0, 3, 2, 1))
REDUCE_HOPS = ((3, 2, 1, 0), (0, 1, 2, 3))


def gather_steps(place, orders, sizes, steps, piece, total, recv, send, sib_send, sib_recv):
    z = place.z

    def copy(ref, device, send_sem, recv_sem):
        return pltpu.make_async_remote_copy(ref, ref, send_sem, recv_sem, device, MESH_ID)

    for number, (part, dx, dy, rank) in enumerate(steps):
        order = orders[part]
        tz = place.far(rank)
        sx, sy = place.flipped(dx, dy)
        ref = piece(place.linear(tz, sx, sy), part)
        landed = recv.at[part, place.chip(tz, sx, sy)]
        own = dx == 0 and dy == 0 and rank == 3
        if not own:
            copy(ref, place.sibling(), landed, landed).wait_recv()
        last = last_move(order, dx, dy, rank)
        if last >= 0 and order[last] == "z" and rank != 3:
            up = (z > tz).astype(jnp.int32)
            nz = z + 2 * up - 1

            @pl.when(jnp.logical_and(nz >= 0, nz <= 3))
            def _():
                copy(ref, place.device(nz, place.x, place.y), send.at[3 - up], landed).start()

        for c in order[last + 1 :]:
            if c == "x":
                copy(ref, place.device(z, 1 - place.x, place.y), send.at[0], landed).start()
            elif c == "y":
                copy(ref, place.device(z, place.x, 1 - place.y), send.at[1], landed).start()
            else:

                @pl.when(z < 3)
                def _():
                    copy(ref, place.device(z + 1, place.x, place.y), send.at[2], landed).start()

                @pl.when(z > 0)
                def _():
                    copy(ref, place.device(z - 1, place.x, place.y), send.at[3], landed).start()

        copy(ref, place.sibling(), sib_send.at[0], sib_recv.at[0]).start()
        yield number
    drain(place, orders, total, send, GATHER_HOPS, sizes)
    whole = total(16 * sum(sizes))
    copy(whole, place.sibling(), sib_send.at[0], sib_recv.at[0]).wait()


def radix(order, stop, dx, dy, tz):
    index = 0
    size = 1
    for c in order[: order.index(stop[0])]:
        value, base = {"x": (dx, 2), "y": (dy, 2), "z": (tz, 4)}[c]
        index = index * base + value
        size *= base
    if stop[0] == "z":
        index = index * 3 + (tz if stop == "z+" else tz - 1)
        size *= 3
    return index, size


def landing_base(orders):
    base = {}
    at = 0
    for axis in ("x", "y", "z+", "z-"):
        for part, order in enumerate(orders):
            base[(axis, part)] = at
            at += radix(order, axis, 0, 0, 0)[1]
    return base, at


def reduce_step(place, orders, base, step, own_piece, add_landed, land, recv, out, send, keep, offset):
    part, dx, dy, rank = step
    order = orders[part]
    z = place.z
    tz = place.far(rank)
    tx, ty = place.flipped(dx, dy)
    chip = place.chip(tz, tx, ty)
    root = dx == 0 and dy == 0 and rank == 3
    last = last_move(order, dx, dy, rank)
    out_at = part * 16 + chip
    own_piece(part + offset, place.linear(tz, tx, ty), chip, out_at)

    def slot(axis):
        return base[(axis, part)] + radix(order, axis, dx, dy, tz)[0]

    def take(index):
        ref = land.at[index]
        sem = recv.at[index]
        pltpu.make_async_remote_copy(ref, ref, sem, sem, place.sibling(), MESH_ID).wait_recv()
        add_landed(part + offset, index)

    if last >= 0 and order[last] == "z" and rank != 3:
        up = (z > tz).astype(jnp.int32)
        nz = z + 2 * up - 1
        plus = slot("z+")
        minus = slot("z-")

        @pl.when(jnp.logical_and(nz >= 0, nz <= 3))
        def _():
            take(up * plus + (1 - up) * minus)

    for c in order[last + 1 :]:
        if c == "z":

            @pl.when(z < 3)
            def _():
                take(slot("z+"))

            @pl.when(z > 0)
            def _():
                take(slot("z-"))

        else:
            take(slot(c))
    keep(part + offset, out_at, root)
    if root:
        return
    ref = out.at[out_at]

    def push(device, index, direction):
        pltpu.make_async_remote_copy(
            ref, land.at[index], send.at[direction], recv.at[index], device, MESH_ID
        ).start()

    axis = order[last]
    if axis == "x":
        index = base[("x", part)] + radix(order, "x", 0, dy, tz)[0]
        push(place.device(z, 1 - place.x, place.y), index, 0)
    elif axis == "y":
        index = base[("y", part)] + radix(order, "y", dx, 0, tz)[0]
        push(place.device(z, place.x, 1 - place.y), index, 1)
    else:
        down = (z > tz).astype(jnp.int32)
        index = down * slot("z+") + (1 - down) * slot("z-")
        push(place.device(z + 1 - 2 * down, place.x, place.y), index, 2 + down)


TOK = 128
NSEQ = 16
BLOCK = 128
N_LEFT = 56
N_RIGHT = 72
QCH = 256
LOG2E = math.log2(math.e)
MESH_ID = pl.DeviceIdType.MESH
NT = (((1,), (1,)), ((), ()))
TN = (((0,), (0,)), ((), ()))
NN = (((1,), (0,)), ((), ()))
BF = jnp.bfloat16
F32 = jnp.float32
VM = pltpu.VMEM


def mm(a, b, dims=NN):
    return lax.dot_general(a, b, dims, preferred_element_type=F32)


def mmh(a, b, dims=NN):
    return lax.dot_general(a, b, dims, precision=HIGH, preferred_element_type=F32)


def flip(x):
    return jnp.swapaxes(x.astype(F32), 0, 1).astype(x.dtype)


def normalise(x):
    mean = jnp.mean(x, -1, keepdims=True)
    centred = x - mean
    rstd = lax.rsqrt(jnp.mean(centred * centred, -1, keepdims=True) + EPS)
    return centred * rstd, rstd


def normalise_back(grad, unit, rstd, gain):
    inner = grad * gain
    return rstd * (
        inner
        - jnp.mean(inner, -1, keepdims=True)
        - unit * jnp.mean(inner * unit, -1, keepdims=True)
    )


def column_sum(x):
    return jnp.sum(x, 0, keepdims=True)


GELU_K = math.sqrt(2.0 / math.pi)


def gelu_value(x):
    return 0.5 * x * (1.0 + jnp.tanh(GELU_K * (x + 0.044715 * x * x * x)))


def gelu_slope(x):
    t = jnp.tanh(GELU_K * (x + 0.044715 * x * x * x))
    return 0.5 * (1.0 + t) + 0.5 * x * (1.0 - t * t) * GELU_K * (1.0 + 3.0 * 0.044715 * x * x)


def layer_kernel(
    place_ref,
    lead_ref,
    blocks_ref,
    ids_ref,
    pix_ref,
    goal_ref,
    emb_ref,
    vec_ref,
    head_ref,
    wlat_ref,
    left_hbm,
    right_hbm,
    small_ref,
    stack,
    left,
    right,
    slab,
    qkv_t,
    out_t,
    out_t32,
    lse,
    o_in,
    d_slab,
    do_t,
    dqkv_t,
    dqkv_in,
    k_row,
    v_row,
    q_row,
    do_row,
    s_scr,
    dq_acc,
    h0_s,
    n1_s,
    xp_s,
    a_s,
    mid_s,
    up_s,
    act_s,
    acc,
    wave,
    wave_in,
    wave_tile,
    wave_all,
    pix_s,
    goal_s,
    head_s,
    gvec,
    t_recv,
    t_send,
    t_sib_send,
    t_sib_recv,
    a_send,
    a_recv,
    in_sem,
    g_local,
    g_send,
    g_recv,
):
    s = lax.axis_index("seq")
    b = lax.axis_index("batch")
    place = Place()
    sibling = s + 1 - 2 * place.core

    loads = []
    for i, (src, dst) in enumerate(((pix_ref, pix_s), (goal_ref, goal_s), (head_ref, head_s))):
        c = pltpu.make_async_copy(src, dst, in_sem.at[i])
        c.start()
        loads.append(c)
    mine = place.linear(place.z, place.x, place.y)
    stack[pl.ds(mine * SHARE, SHARE)] = blocks_ref[...].astype(BF)
    place.greet()

    for number in gather_steps(
        place,
        MAIN,
        GATHER_SIZES,
        GATHER_ORDER,
        lambda d, p: stack.at[pl.ds(d * SHARE + sum(GATHER_SIZES[:p]), GATHER_SIZES[p])],
        lambda n: stack.at[pl.ds(0, n)],
        t_recv,
        t_send,
        t_sib_send,
        t_sib_recv,
    ):
        if number == 3:
            loads[0].wait()
            embed_forward(pix_s, ids_ref, lead_ref, emb_ref, vec_ref, h0_s, n1_s, xp_s, a_s)

    def block(begin, across, r, c):
        return stack[place_ref[begin + r * across + c]]

    def two_columns(begin, across, pair):
        return jnp.concatenate(
            [
                jnp.concatenate(
                    [block(begin, across, r, 2 * pair), block(begin, across, r, 2 * pair + 1)], 1
                )
                for r in range(8)
            ],
            0,
        )

    def two_rows(begin, pair):
        return jnp.concatenate(
            [
                jnp.concatenate([block(begin, 8, 2 * pair + r, c) for c in range(8)], 1)
                for r in range(2)
            ],
            0,
        )

    def eight_columns(begin, across, quad):
        return jnp.concatenate(
            [
                jnp.concatenate([block(begin, across, r, 8 * quad + k) for k in range(8)], 1)
                for r in range(8)
            ],
            0,
        )

    def eight_rows(begin, quad):
        return jnp.concatenate(
            [
                jnp.concatenate([block(begin, 8, 8 * quad + r, c) for c in range(8)], 1)
                for r in range(8)
            ],
            0,
        )

    at_qkv, at_o, at_up, at_down = 0, 192, 256, 512
    share = []

    def share_group(index, stage, target, begin, count):
        part = pl.ds(begin, count)
        c = pltpu.make_async_copy(stage.at[part], target.at[0, part], g_local.at[index])
        c.start()
        r = pltpu.make_async_remote_copy(
            src_ref=stage.at[part],
            dst_ref=target.at[1, part],
            send_sem=g_send.at[index],
            recv_sem=g_recv.at[index],
            device_id=(sibling, b),
            device_id_type=MESH_ID,
        )
        r.start()
        share.append((c, r))

    def exchange(which, src_at, dst_at):
        def copy(o):
            peer = lax.rem(s + o, NSEQ)
            return pltpu.make_async_remote_copy(
                src_ref=src_at(peer),
                dst_ref=dst_at(s),
                send_sem=a_send.at[which, o],
                recv_sem=a_recv.at[which, o],
                device_id=(peer, b),
                device_id_type=MESH_ID,
            )

        def begin(o, _):
            copy(o).start()
            return _

        def finish(o, _):
            copy(o).wait()
            return _

        def start():
            lax.fori_loop(1, NSEQ, begin, 0)

        def start_to(peer):
            @pl.when(peer != s)
            def _():
                copy(lax.rem(peer - s + NSEQ, NSEQ)).start()

        def wait():
            lax.fori_loop(1, NSEQ, finish, 0)

        return start, wait, start_to

    def lanes(i, size):
        return pl.ds(pl.multiple_of(i * size, size), size)

    def rows_at(i, size):
        return pl.ds(pl.multiple_of(i * size, size), size)

    n1 = n1_s[...]
    waits = {}
    for which in (1, 0, 2):

        def qkv_tile(t, _, which=which):
            piece = mm(n1, two_columns(at_qkv, 24, 4 * which + t))
            if which != 1:
                piece = piece + vec_ref[9 + which // 2 : 10 + which // 2, lanes(t, 256)]
            piece = piece.astype(BF)
            for k in range(2):
                turned = flip(piece[:, k * BLOCK : (k + 1) * BLOCK])
                for half in range(2):
                    slab[4 * t + 2 * k + half, which * HD : (which + 1) * HD, :] = turned[
                        half * HD : (half + 1) * HD
                    ]
            return _

        lax.fori_loop(0, 4, qkv_tile, 0, unroll=4)
        part = pl.ds(which * HD, HD)
        start, waits[which], _ = exchange(
            which,
            lambda p, part=part: slab.at[p, part],
            lambda p, part=part: qkv_t.at[part, lanes(p, TOK)],
        )
        start()
    qkv_t[:, lanes(s, TOK)] = slab[s]
    for k in range(8):
        left[k] = flip(n1[:, k * BLOCK : (k + 1) * BLOCK])

    scale2 = LOG2E / math.sqrt(HD)

    def turn_rows(source, begin, target):
        def one(t, _):
            target[rows_at(t, TOK), :] = flip(source[begin : begin + HD, lanes(t, TOK)])
            return _

        lax.fori_loop(0, NSEQ, one, 0, unroll=4)

    waits[1]()
    turn_rows(qkv_t, HD, k_row)
    waits[0]()
    tiles = (NSEQ * TOK) // QCH
    start, wait_o, send_o = exchange(
        3, lambda p: out_t.at[:, lanes(p, TOK)], lambda p: o_in.at[p]
    )

    def forward_chunk(i, _):
        c = lax.rem(i + s // 2, tiles)
        part = lanes(c, QCH)
        q_part = qkv_t[0:HD, part]
        top = None
        for t in range(tiles):
            tile = slice(t * QCH, (t + 1) * QCH)
            scores = mm(k_row[tile, :], q_part)
            s_scr[tile, :] = scores
            best = jnp.max(scores, 0, keepdims=True)
            top = best if top is None else jnp.maximum(top, best)
        top = top * scale2

        @pl.when(i == 0)
        def _():
            waits[2]()

        total = jnp.zeros((1, QCH), F32)
        mixed = jnp.zeros((HD, QCH), F32)
        for t in range(2):
            tile = slice(4 * t * QCH, (4 * t + 4) * QCH)
            probs = jnp.exp2(s_scr[tile, :] * scale2 - top)
            total = total + jnp.sum(probs, 0, keepdims=True)
            mixed = mixed + mm(qkv_t[2 * HD : 3 * HD, tile], probs.astype(BF))
        mixed = mixed / total
        lse[c] = top + jnp.log2(total)
        out_t32[:, part] = mixed
        out_t[:, part] = mixed.astype(BF)
        send_o(2 * c)
        send_o(2 * c + 1)
        return 0

    lax.fori_loop(0, tiles, forward_chunk, 0)
    share_group(0, left, left_hbm, 0, 8)
    o_in[s] = out_t[:, lanes(s, TOK)]
    turn_rows(qkv_t, 0, q_row)
    turn_rows(qkv_t, 2 * HD, v_row)
    wait_o()

    parts = []
    for k in range(8):
        pair = jnp.concatenate([o_in[2 * k], o_in[2 * k + 1]], 0)
        left[8 + k] = pair
        parts.append(flip(pair))
    share_group(1, left, left_hbm, 8, 8)
    o_low = jnp.concatenate(parts, 1)

    def out_tile(t, _):
        part = lanes(t, 256)
        mid_s[:, part] = h0_s[:, part] + (
            mm(o_low, two_columns(at_o, 8, t)) + vec_ref[7:8, part]
        )
        return _

    lax.fori_loop(0, 4, out_tile, 0, unroll=4)
    mid = mid_s[...]
    unit, _ = normalise(mid)
    n2 = (unit * vec_ref[3:4, :] + vec_ref[4:5, :]).astype(BF)
    acc[...] = mid + vec_ref[8:9, :]

    def up_tile(t, _):
        part = lanes(t, 1024)
        bias = vec_ref[pl.ds(11 + t, 1), :]
        upper = mm(n2, eight_columns(at_up, 32, t)) + bias
        up_s[:, part] = upper
        active = gelu_value(upper).astype(BF)
        act_s[:, part] = active
        acc[...] += mm(active, eight_rows(at_down, t))
        return _

    lax.fori_loop(0, 4, up_tile, 0)

    unit_f, rstd_f = normalise(acc[...])
    final = (unit_f * vec_ref[5:6, :] + vec_ref[6:7, :]).astype(BF)
    loads[2].wait()
    head = head_s[...].astype(BF)
    loads[1].wait()
    diff = mm(final, head, NT) - jnp.swapaxes(goal_s[0].astype(F32), 0, 1)
    wave[...] = jnp.concatenate(
        [diff[0:64] + diff[64:128], jnp.zeros((64, 2 * BLOCK - HOUT), F32)], 1
    )

    def tile_of(ref, j):
        return ref.at[
            pl.ds(pl.multiple_of(j // 2 * 8, 8), 8),
            pl.ds(pl.multiple_of(lax.rem(j, 2) * BLOCK, BLOCK), BLOCK),
        ]

    start, wait, _ = exchange(7, lambda p: tile_of(wave, p), lambda p: wave_in.at[p])
    start()
    wave_in[s] = tile_of(wave, s)[...]
    for k in range(8):
        left[16 + k] = flip(n2[:, k * BLOCK : (k + 1) * BLOCK])
    share_group(2, left, left_hbm, 16, 8)
    wait()
    tile = wave_in[0]
    for k in range(1, NSEQ):
        tile = tile + wave_in[k]
    wave_tile[...] = tile
    start, wait, _ = exchange(8, lambda p: wave_tile, lambda p: tile_of(wave_all, p))
    start()
    tile_of(wave_all, s)[...] = tile

    def turn_active(k, _):
        left[24 + k] = flip(act_s[:, lanes(k, BLOCK)])
        return _

    lax.fori_loop(0, 12, turn_active, 0)
    wait()
    total_wave = wave_all[:, 0:HOUT]
    one = lax.broadcasted_iota(jnp.int32, (HOUT, HOUT), 0)
    two = lax.broadcasted_iota(jnp.int32, (HOUT, HOUT), 1)
    swap = (one == two + 1 - 2 * (two % 2)).astype(F32)
    other = mmh(total_wave, swap)
    weight = wlat_ref[...]
    square = jnp.sum(weight * diff * diff, keepdims=True)
    cross = jnp.sum(weight[0:64] * total_wave * other, keepdims=True) * (1.0 / NSEQ)
    loss = square * (1.0 / MSE_COUNT) + (SPECTRAL / DFT_COUNT) * (float(KMODES) * square + cross)
    other2 = jnp.concatenate([other, other], 0)
    d_pred = weight * (
        (2.0 / MSE_COUNT) * diff + (2.0 * SPECTRAL / DFT_COUNT) * (float(KMODES) * diff + other2)
    )
    d_low = d_pred.astype(BF)
    put_head(small_ref, mm(d_low, final, TN), loss)
    d_final = mm(d_low, head)
    gvec[5:6, :] = column_sum(d_final * unit_f)
    gvec[6:7, :] = column_sum(d_final)
    d_out = normalise_back(d_final, unit_f, rstd_f, vec_ref[5:6, :])
    d_branch = d_out.astype(BF)
    gvec[8:9, :] = column_sum(d_branch.astype(F32))
    for k in range(8):
        right[64 + k] = d_branch[:, k * BLOCK : (k + 1) * BLOCK]
    share_group(4, right, right_hbm, 64, 8)
    acc[...] = jnp.zeros_like(acc)

    def down_tile(t, _):
        part = lanes(t, 1024)
        d_active = mm(d_branch, eight_rows(at_down, t), NT)
        d_upper = (d_active * gelu_slope(up_s[:, part])).astype(BF)
        gvec[pl.ds(11 + t, 1), :] = column_sum(d_upper.astype(F32))
        for k in range(8):
            right[32 + 8 * t + k] = d_upper[:, k * BLOCK : (k + 1) * BLOCK]
        acc[...] += mm(d_upper, eight_columns(at_up, 32, t), NT)
        return _

    lax.fori_loop(0, 4, down_tile, 0)
    share_group(5, right, right_hbm, 32, 32)
    d_n2 = acc[...]
    unit, rstd = normalise(mid_s[...])
    gvec[3:4, :] = column_sum(d_n2 * unit)
    gvec[4:5, :] = column_sum(d_n2)
    d_mid = d_out + normalise_back(d_n2, unit, rstd, vec_ref[3:4, :])
    mid_s[...] = d_mid
    d_mid_low = d_mid.astype(BF)
    start, wait_d, send_d = exchange(
        4, lambda p: d_slab.at[p], lambda p: do_t.at[:, lanes(p, TOK)]
    )

    def att_tile(t, _):
        piece = mm(d_mid_low, two_rows(at_o, t), NT).astype(BF)
        for k in range(2):
            turned = flip(piece[:, k * BLOCK : (k + 1) * BLOCK])
            for half in range(2):
                d_slab[4 * t + 2 * k + half] = turned[half * HD : (half + 1) * HD]
        for k in range(4):
            send_d(4 * t + k)
        return _

    lax.fori_loop(0, 4, att_tile, 0, unroll=4)
    do_t[:, lanes(s, TOK)] = d_slab[s]
    gvec[7:8, :] = column_sum(d_mid_low.astype(F32))
    for k in range(8):
        right[24 + k] = d_mid_low[:, k * BLOCK : (k + 1) * BLOCK]
    share_group(6, right, right_hbm, 24, 8)
    dq_acc[...] = jnp.zeros_like(dq_acc)
    lax.fori_loop(12, 32, turn_active, 0)
    share_group(3, left, left_hbm, 24, 32)
    wait_d()

    turn_rows(do_t, 0, do_row)
    scale = 1.0 / math.sqrt(HD)

    def deltas(c, _):
        part = lanes(c, QCH)
        s_scr[pl.ds(c, 1), :] = jnp.sum(
            do_t[:, part].astype(F32) * out_t32[:, part], 0, keepdims=True
        )
        return _

    lax.fori_loop(0, tiles, deltas, 0)
    start, wait_kv, send_kv = exchange(
        5,
        lambda p: dqkv_t.at[pl.ds(HD, 2 * HD), lanes(p, TOK)],
        lambda p: dqkv_in.at[p, pl.ds(HD, 2 * HD)],
    )

    def backward_tile(i, _):
        c = lax.rem(i + s // 2, tiles)
        keys = rows_at(c, QCH)
        k_part = k_row[keys, :]
        v_part = v_row[keys, :]
        k_turned = qkv_t[HD : 2 * HD, lanes(c, QCH)]
        d_key = jnp.zeros((QCH, HD), F32)
        d_value = jnp.zeros((QCH, HD), F32)
        for t in range(tiles // 2):
            tile = slice(2 * t * QCH, (2 * t + 2) * QCH)
            base = jnp.concatenate([lse[2 * t], lse[2 * t + 1]], 1)
            delta = jnp.concatenate([s_scr[2 * t : 2 * t + 1, :], s_scr[2 * t + 1 : 2 * t + 2, :]], 1)
            probs = jnp.exp2(mm(k_part, qkv_t[0:HD, tile]) * scale2 - base)
            d_prob = mm(v_part, do_t[:, tile])
            d_score = (probs * (d_prob - delta)).astype(BF)
            d_value = d_value + mm(probs.astype(BF), do_row[tile, :])
            d_key = d_key + mm(d_score, q_row[tile, :])
            dq_acc[:, tile] += mm(k_turned, d_score)
        d_key = d_key * scale
        for k in range(2):
            part = lanes(2 * c + k, TOK)
            half = slice(k * TOK, (k + 1) * TOK)
            dqkv_t[HD : 2 * HD, part] = flip(d_key[half]).astype(BF)
            dqkv_t[2 * HD : 3 * HD, part] = flip(d_value[half]).astype(BF)
            send_kv(2 * c + k)
        return _

    lax.fori_loop(0, tiles, backward_tile, 0)
    dqkv_t[0:HD, :] = (dq_acc[...] * scale).astype(BF)
    start_q, wait_q, _ = exchange(
        6,
        lambda p: dqkv_t.at[pl.ds(0, HD), lanes(p, TOK)],
        lambda p: dqkv_in.at[p, pl.ds(0, HD)],
    )
    start_q()
    dqkv_in[s] = dqkv_t[:, lanes(s, TOK)]
    acc[...] = jnp.zeros_like(acc)

    def finish_part(which):
        def one(t, _):
            parts = []
            for k in range(2):
                j = 2 * t + k
                part = slice(which * HD, (which + 1) * HD)
                pair = jnp.concatenate([dqkv_in[2 * j, part, :], dqkv_in[2 * j + 1, part, :]], 0)
                piece = flip(pair)
                right[8 * which + j] = piece
                parts.append(piece)
            piece = jnp.concatenate(parts, 1)
            if which != 1:
                gvec[9 + which // 2 : 10 + which // 2, lanes(t, 256)] = column_sum(
                    piece.astype(F32)
                )
            acc[...] += mm(piece, two_columns(at_qkv, 24, 4 * which + t), NT)
            return _

        lax.fori_loop(0, 4, one, 0, unroll=4)

    wait_kv()
    finish_part(1)
    finish_part(2)
    wait_q()
    finish_part(0)
    share_group(7, right, right_hbm, 0, 24)
    d_n1 = acc[...]
    unit, rstd = normalise(h0_s[...])
    gvec[1:2, :] = column_sum(d_n1 * unit)
    gvec[2:3, :] = column_sum(d_n1)
    d_rows = mid_s[...] + normalise_back(d_n1, unit, rstd, vec_ref[1:2, :])
    embed_backward(d_rows, xp_s, a_s, lead_ref, emb_ref, vec_ref, gvec, small_ref)
    for c, r in share:
        c.wait()
        r.wait()


def run_layer(place, lead, blocks, ids, pix, goals, embed, vec, head, wlat):
    vmem = pl.BlockSpec(memory_space=VM)
    smem = pl.BlockSpec(memory_space=pltpu.SMEM)
    anyspace = pl.BlockSpec(memory_space=pl.ANY)
    dma = pltpu.SemaphoreType.DMA
    length = NSEQ * TOK
    return pl.pallas_call(
        layer_kernel,
        name="layer",
        out_shape=(
            jax.ShapeDtypeStruct((2, N_LEFT, BLOCK, TOK), BF),
            jax.ShapeDtypeStruct((2, N_RIGHT, TOK, BLOCK), BF),
            jax.ShapeDtypeStruct((32, 2 * HALF, BLOCK), F32),
        ),
        in_specs=[smem, smem, vmem, vmem, anyspace, anyspace, vmem, vmem, anyspace, vmem],
        out_specs=(anyspace, anyspace, vmem),
        scratch_shapes=[
            VM((SLOTS, BLOCK, BLOCK), BF),
            VM((N_LEFT, BLOCK, TOK), BF),
            VM((N_RIGHT, TOK, BLOCK), BF),
            VM((HEADS, 3 * HD, TOK), BF),
            VM((3 * HD, length), BF),
            VM((HD, length), BF),
            VM((HD, length), F32),
            VM((length // QCH, 1, QCH), F32),
            VM((HEADS, HD, TOK), BF),
            VM((HEADS, HD, TOK), BF),
            VM((HD, length), BF),
            VM((3 * HD, length), BF),
            VM((HEADS, 3 * HD, TOK), BF),
            VM((length, HD), BF),
            VM((length, HD), BF),
            VM((length, HD), BF),
            VM((length, HD), BF),
            VM((length, QCH), F32),
            VM((HD, length), F32),
            VM((TOK, D), F32),
            VM((TOK, D), BF),
            VM((TOK, HOUT), F32),
            VM((TOK, VARS), F32),
            VM((TOK, D), F32),
            VM((TOK, FF), F32),
            VM((TOK, FF), BF),
            VM((TOK, D), F32),
            VM((64, 2 * BLOCK), F32),
            VM((NSEQ, 8, BLOCK), F32),
            VM((8, BLOCK), F32),
            VM((64, 2 * BLOCK), F32),
            VM((1, HOUT, TOK), BF),
            VM((1, HOUT, TOK), BF),
            VM((HOUT, D), F32),
            VM((16, D), F32),
            dma((4, 16)),
            dma((4,)),
            dma((1,)),
            dma((1,)),
            dma((9, NSEQ)),
            dma((9, NSEQ)),
            dma((3,)),
            dma((8,)),
            dma((8,)),
            dma((8,)),
        ],
        compiler_params=pltpu.CompilerParams(
            collective_id=1, has_side_effects=True, vmem_limit_bytes=60 * 1024 * 1024
        ),
    )(place, lead, blocks, ids, pix, goals, embed, vec, head, wlat)


def token_maps():
    row = lax.broadcasted_iota(jnp.int32, (VARS, HOUT), 0)
    col = lax.broadcasted_iota(jnp.int32, (VARS, HOUT), 1)
    return (col // 4 == row).astype(F32)


def embed_forward(pix_ref, ids_ref, lead_ref, emb_ref, vec_ref, h0_ref, n1_ref, xp_ref, a_ref):
    spread = token_maps()
    var = lax.broadcasted_iota(jnp.int32, (VARS, VARS), 0)
    chosen = (ids_ref[...] == var).astype(BF)
    low = spread.astype(BF)
    wide_ids = mm(chosen, low)
    routes = mm(wide_ids.astype(BF), low, TN)
    one = lax.broadcasted_iota(jnp.int32, (HOUT, HOUT), 0)
    two = lax.broadcasted_iota(jnp.int32, (HOUT, HOUT), 1)
    routes = jnp.where(one % 4 == two % 4, routes, 0.0).astype(BF)
    pix = mm(pix_ref[0], routes, TN)
    xp_ref[...] = pix
    tok = emb_ref[0:HOUT, :]
    emb = emb_ref[HOUT : HOUT + VARS, :]
    query = vec_ref[0:1, :]
    tok_q = jnp.sum(tok * query, -1, keepdims=True)
    emb_q = mmh(query, emb, NT)
    back = lax.broadcasted_iota(jnp.int32, (HOUT, VARS), 0) // 4
    col = lax.broadcasted_iota(jnp.int32, (HOUT, VARS), 1)
    reduce = jnp.where(back == col, tok_q, 0.0)
    logits = (mmh(pix, reduce) + emb_q) * (1.0 / math.sqrt(D))
    logits = logits - jnp.max(logits, -1, keepdims=True)
    weights = jnp.exp(logits)
    weights = weights / jnp.sum(weights, -1, keepdims=True)
    a_ref[...] = weights
    wide = mmh(weights, spread) * pix
    lead = emb_ref[pl.ds(HOUT + VARS + lead_ref[0], 1), :]
    h0 = mmh(wide, tok) + mmh(weights, emb) + lead
    h0_ref[...] = h0
    unit, _ = normalise(h0)
    n1_ref[...] = (unit * vec_ref[1:2, :] + vec_ref[2:3, :]).astype(BF)


VEC_AT = 8 * EROWS
HEAD_AT = VEC_AT + 128


def put(small_ref, begin, value):
    rows = value.shape[0]
    at = 0
    while at < rows:
        device, inside = divmod(begin + at, ROWS)
        count = min(rows - at, ROWS - inside)
        small_ref[device, inside : inside + count, :] = value[at : at + count]
        at += count


def put_head(small_ref, grad, loss):
    for k in range(8):
        put(small_ref, HEAD_AT + HOUT * k, grad[:, k * BLOCK : (k + 1) * BLOCK])
    tile = jnp.broadcast_to(loss, (8, BLOCK))
    for d in range(32):
        small_ref[d, ROWS : 2 * HALF, :] = tile


def embed_backward(d_rows, xp_ref, a_ref, lead_ref, emb_ref, vec_ref, gvec, small_ref):
    pix = xp_ref[...]
    weights = a_ref[...]
    tok = emb_ref[0:HOUT, :]
    emb = emb_ref[HOUT : HOUT + VARS, :]
    query = vec_ref[0:1, :]
    spread = token_maps()
    d_wide = mmh(d_rows, tok, NT)
    d_weight = mmh(pix * d_wide, spread, NT) + mmh(d_rows, emb, NT)
    d_logit = (
        weights
        * (d_weight - jnp.sum(weights * d_weight, -1, keepdims=True))
        * (1.0 / math.sqrt(D))
    )
    wide = mmh(weights, spread) * pix
    d_wide_l = mmh(d_logit, spread) * pix
    ones = jnp.ones((TOK, 1), F32)
    d_tok_q = mmh(d_wide_l, ones, TN)
    d_emb_q = mmh(d_logit, ones, TN)
    g_tok = mmh(wide, d_rows, TN) + d_tok_q * query
    g_emb = mmh(weights, d_rows, TN) + d_emb_q * query
    row = lax.broadcasted_iota(jnp.int32, (LEADS, D), 0)
    g_lead = jnp.where(row == lead_ref[0], column_sum(d_rows), 0.0)
    gvec[0:1, :] = column_sum(d_tok_q * tok) + column_sum(d_emb_q * emb)
    gvec[15:16, :] = jnp.zeros((1, D), F32)
    for k in range(8):
        part = slice(k * BLOCK, (k + 1) * BLOCK)
        put(small_ref, EROWS * k, g_tok[:, part])
        put(small_ref, EROWS * k + HOUT, g_emb[:, part])
        put(small_ref, EROWS * k + HOUT + VARS, g_lead[:, part])
        put(small_ref, VEC_AT + 16 * k, gvec[:, part])


SLOTS = 768
ROWS = 120
HALF = 64


def sides_of(b):
    li = jnp.where(
        b < 192, b // 24, jnp.where(b < 256, b // 8 - 16, jnp.where(b < 512, b // 32 + 8, b // 8 - 40))
    )
    ri = jnp.where(
        b < 192,
        lax.rem(b, 24),
        jnp.where(
            b < 256,
            24 + lax.rem(b, 8),
            jnp.where(b < 512, 32 + lax.rem(b, 32), 64 + lax.rem(b, 8)),
        ),
    )
    return li, ri


def reduce_kernel(
    order_ref,
    left_hbm,
    right_hbm,
    small_ref,
    lroot_hbm,
    mom_hbm,
    rroot_hbm,
    own_hbm,
    ggt_hbm,
    gtg_hbm,
    lgr_hbm,
    turned_hbm,
    all_ref,
    sum_ref,
    lroot_ref,
    mom_ref,
    rroot_ref,
    own_ref,
    ggt_ref,
    gtg_ref,
    lgr_ref,
    turned_ref,
    lt,
    rt,
    mine,
    theirs,
    acc,
    acc_small,
    land,
    land_small,
    out,
    out_small,
    tail,
    in_sem,
    swap_sem,
    recv,
    send,
    recv_small,
    send_small,
    norms,
    across,
    t_recv,
    t_send,
    t_sib,
    n_send,
    n_recv,
    root_sem,
    out_sem,
):
    place = Place()
    loads = [
        pltpu.make_async_copy(left_hbm.at[0], lt.at[:, :, pl.ds(0, TOK)], in_sem.at[0]),
        pltpu.make_async_copy(left_hbm.at[1], lt.at[:, :, pl.ds(TOK, TOK)], in_sem.at[1]),
        pltpu.make_async_copy(right_hbm.at[0], rt.at[:, pl.ds(0, TOK), :], in_sem.at[2]),
        pltpu.make_async_copy(right_hbm.at[1], rt.at[:, pl.ds(TOK, TOK), :], in_sem.at[3]),
    ]
    loads.append(pltpu.make_async_copy(small_ref.at[:, place.core], mine, in_sem.at[4]))
    for c in loads:
        c.start()
    later = [
        pltpu.make_async_copy(src, dst, root_sem.at[i])
        for i, (src, dst) in enumerate(
            ((lroot_hbm, lroot_ref), (mom_hbm, mom_ref), (rroot_hbm, rroot_ref))
        )
    ]
    place.greet()
    swap = pltpu.make_async_remote_copy(
        small_ref.at[:, 1 - place.core],
        theirs,
        swap_sem.at[0],
        swap_sem.at[1],
        place.sibling(),
        MESH_ID,
    )
    swap.start()
    for c in later:
        c.start()
    for c in loads:
        c.wait()

    def own_piece(part, device, chip, out_at):
        if part < 4:

            def block(j, _):
                slot = device * SHARE + part * PIECE + j
                li, ri = sides_of(order_ref[slot])
                acc[j] = mm(lt[li], rt[ri])
                return 0

            lax.fori_loop(0, PIECE, block, 0, unroll=3)
        else:
            acc_small[...] = mine[chip // 2, lax.rem(chip, 2), pl.ds((part - 4) * HALF, HALF), :]

    def add_landed(part, index):
        if part < 4:
            acc[...] += land[index].astype(F32)
        else:
            acc_small[...] += land_small[index]

    me = place.linear(place.z, place.x, place.y)

    def keep(part, out_at, root):
        if part < 4:
            if root:
                own_ref[pl.ds(part * PIECE, PIECE)] = acc[...]
            else:
                out[out_at] = acc[...].astype(BF)
        elif root:
            tail[me * 2 + part - 4] = acc_small[...]
        else:
            out_small[out_at] = acc_small[...]

    base, _ = landing_base(MAIN)
    base_small, _ = landing_base(SMALL)

    def main_step(step):
        reduce_step(
            place, MAIN, base, step, own_piece, add_landed, land, recv, out, send, keep, 0
        )

    def small_step(step):
        reduce_step(
            place, SMALL, base_small, step, own_piece, add_landed,
            land_small, recv_small, out_small, send_small, keep, 4,
        )

    stores = []

    def store(index, source, target, begin, count):
        part = pl.ds(begin, count)
        copy = pltpu.make_async_copy(source.at[part], target.at[part], out_sem.at[index])
        copy.start()
        stores.append(copy)

    def product(part, j):
        i = part * PIECE + j
        g = own_ref[i]
        ggt_ref[i] = mmh(g, g, NT)
        gtg_ref[i] = mmh(g, g, TN)
        lgr_ref[i] = mmh(mmh(lroot_ref[i], g), rroot_ref[i])
        if j == PIECE - 1:
            store(4 * part, own_ref, own_hbm, part * PIECE, PIECE)
            store(4 * part + 1, ggt_ref, ggt_hbm, part * PIECE, PIECE)
            store(4 * part + 2, gtg_ref, gtg_hbm, part * PIECE, PIECE)
            store(4 * part + 3, lgr_ref, lgr_hbm, part * PIECE, PIECE)

    def small_root():
        first = tail[me * 2]
        data = tail[me * 2 + 1, 0 : ROWS - HALF, :]
        return jnp.sum(first * first, keepdims=True) + jnp.sum(data * data, keepdims=True)

    spread = gather_steps(
        place,
        TAIL,
        (1, 1),
        [step[1:] for step in REDUCE_PLAN if step[0] == 1],
        lambda d, p: tail.at[d * 2 + p],
        lambda n: tail.at[pl.ds(0, n)],
        t_recv,
        t_send,
        t_sib.at[pl.ds(0, 1)],
        t_sib.at[pl.ds(1, 1)],
    )
    def send_norm(squares):
        norms[place.s] = jnp.broadcast_to(
            jnp.sum(squares, keepdims=True) + small_root(), (8, BLOCK)
        )
        lax.fori_loop(1, NSEQ, lambda o, _: (norm_copy(o).start(), 0)[1], 0)

    def norm_copy(o):
        peer = lax.rem(place.s + o, NSEQ)
        return pltpu.make_async_remote_copy(
            norms.at[place.s],
            norms.at[place.s],
            n_send.at[o],
            n_recv.at[o],
            (peer, place.y),
            MESH_ID,
        )

    squares = jnp.zeros((BLOCK, BLOCK), F32)
    roots = 0
    turned = 0
    small_roots = 0
    swapped = False
    for kind, part, dx, dy, rank in REDUCE_PLAN:
        root = dx == 0 and dy == 0 and rank == 3
        if kind == 1:
            next(spread)
        elif kind == 2:
            product(part, dx)
        elif kind == 3:
            if turned == 0:
                for c in later:
                    c.wait()
            turned_ref[turned] = mmh(mmh(lroot_ref[turned], mom_ref[turned]), rroot_ref[turned])
            turned += 1
            if turned == SHARE:
                store(16, turned_ref, turned_hbm, 0, SHARE)
        elif part >= 4:
            if not swapped:
                swapped = True
                swap.wait()
                mine[...] += theirs[...]
            small_step((part - 4, dx, dy, rank))
            small_roots += root
        else:
            main_step((part, dx, dy, rank))
            if root:
                for i in range(part * PIECE, (part + 1) * PIECE):
                    squares = squares + own_ref[i] * own_ref[i]
                roots += 1
        if kind == 0 and root and roots == 4 and small_roots == 2:
            send_norm(squares)

    for _ in spread:
        pass
    for d in range(32):
        all_ref[d, 0:HALF, :] = tail[2 * d]
        all_ref[d, HALF:ROWS, :] = tail[2 * d + 1, 0 : ROWS - HALF, :]
    lax.fori_loop(1, NSEQ, lambda o, _: (norm_copy(o).wait(), 0)[1], 0)
    total = norms[0]
    for k in range(1, NSEQ):
        total = total + norms[k]
    across[0] = total
    over = pltpu.make_async_remote_copy(
        across.at[0], across.at[1], n_send.at[0], n_recv.at[0], (place.s, 1 - place.y), MESH_ID
    )
    over.start()
    drain(place, MAIN, lambda n: out.at[pl.ds(0, n)], send, REDUCE_HOPS)
    drain(place, SMALL, lambda n: out_small.at[pl.ds(0, n)], send_small, REDUCE_HOPS)
    for copy in stores:
        copy.wait()
    over.wait()
    sum_ref[0] = across[0] + across[1]
    sum_ref[1] = tail[1, ROWS - HALF : HALF, :]


def run_reduce(order, left, right, small, lroots, momentum, rroots):
    vmem = pl.BlockSpec(memory_space=VM)
    smem = pl.BlockSpec(memory_space=pltpu.SMEM)
    anyspace = pl.BlockSpec(memory_space=pl.ANY)
    dma = pltpu.SemaphoreType.DMA
    _, count = landing_base(MAIN)
    _, count_small = landing_base(SMALL)
    stack = jax.ShapeDtypeStruct((SHARE, BLOCK, BLOCK), F32)
    return pl.pallas_call(
        reduce_kernel,
        name="reduce",
        out_shape=(stack,) * 5
        + (
            jax.ShapeDtypeStruct((32, ROWS, BLOCK), F32),
            jax.ShapeDtypeStruct((2, 8, BLOCK), F32),
        ),
        in_specs=[smem] + [anyspace] * 6,
        out_specs=(anyspace,) * 5 + (vmem, vmem),
        scratch_shapes=[VM((SHARE, BLOCK, BLOCK), F32)] * 8
        + [
            VM((N_LEFT, BLOCK, 2 * TOK), BF),
            VM((N_RIGHT, 2 * TOK, BLOCK), BF),
            VM((8, 2, 2 * HALF, BLOCK), F32),
            VM((8, 2, 2 * HALF, BLOCK), F32),
            VM((PIECE, BLOCK, BLOCK), F32),
            VM((HALF, BLOCK), F32),
            VM((count, PIECE, BLOCK, BLOCK), BF),
            VM((count_small, HALF, BLOCK), F32),
            VM((64, PIECE, BLOCK, BLOCK), BF),
            VM((32, HALF, BLOCK), F32),
            VM((64, HALF, BLOCK), F32),
            dma((5,)),
            dma((2,)),
            dma((count,)),
            dma((4,)),
            dma((count_small,)),
            dma((4,)),
            VM((NSEQ, 8, BLOCK), F32),
            VM((2, 8, BLOCK), F32),
            dma((2, 16)),
            dma((4,)),
            dma((2,)),
            dma((NSEQ,)),
            dma((NSEQ,)),
            dma((3,)),
            dma((17,)),
        ],
        compiler_params=pltpu.CompilerParams(
            collective_id=3, has_side_effects=True, vmem_limit_bytes=60 * 1024 * 1024
        ),
    )(order, left, right, small, lroots, momentum, rroots)


def final_kernel(
    sums_ref, own, ggt, gtg, lgr, turned, mom, stat_l, stat_r, blk,
    ge, gv, gh, e, e1, e2, v, v1, v2, h, h1, h2,
    loss_o, norm_o, blk_o, mom_o, l_o, r_o,
    e1_o, e2_o, e_o, v1_o, v2_o, v_o, h1_o, h2_o, h_o,
):
    norm = jnp.sqrt(sums_ref[0, 0:1, 0:1])
    loss_o[...] = sums_ref[1, 4:5, 0:1]
    norm_o[...] = norm
    clip = CLIP_NORM / jnp.maximum(norm, CLIP_NORM)
    for i in range(6):
        mom_o[i] = BETA_ONE * mom[i] + (1.0 - BETA_ONE) * (own[i] * clip)
        l_o[i] = BETA_TWO * stat_l[i] + (1.0 - BETA_TWO) * ((ggt[i] * clip) * clip)
        r_o[i] = BETA_TWO * stat_r[i] + (1.0 - BETA_TWO) * ((gtg[i] * clip) * clip)
        direction = BETA_ONE * turned[i] + (1.0 - BETA_ONE) * (lgr[i] * clip)
        blk_o[i] = blk[i] - SHAMPOO_RATE * (direction + DECAY * blk[i])
    e1_o[...], e2_o[...], e_o[...] = adam(e[...], e1[...], e2[...], jnp.concatenate([ge[0:EROWS], ge[EROWS:]], 1) * clip, EMBED_RATE)
    v1_o[...], v2_o[...], v_o[...] = adam(
        v[...], v1[...], v2[...], jnp.concatenate([gv[0:15, :], gv[16:31, :]], 1) * clip, VECTOR_RATE
    )
    h1_o[...], h2_o[...], h_o[...] = adam(h[...], h1[...], h2[...], jnp.concatenate([gh[0:HOUT], gh[HOUT:]], 1) * clip, HEAD_RATE)


def run_final(sums, stacks, flat, embed, vec, head):
    slots = pl.BlockSpec((6, BLOCK, BLOCK), lambda k: (k, 0, 0))
    table = pl.BlockSpec((EROWS, 2 * BLOCK), lambda k: (0, k))
    rows = pl.BlockSpec((15, 2 * BLOCK), lambda k: (0, k))
    wide = pl.BlockSpec((HOUT, 2 * BLOCK), lambda k: (0, k))
    one = pl.BlockSpec((1, 1), lambda k: (0, 0))
    stack = jax.ShapeDtypeStruct((SHARE, BLOCK, BLOCK), F32)
    shapes = (
        (jax.ShapeDtypeStruct((1, 1), F32),) * 2
        + (stack,) * 4
        + (jax.ShapeDtypeStruct((EROWS, D), F32),) * 3
        + (jax.ShapeDtypeStruct((15, D), F32),) * 3
        + (jax.ShapeDtypeStruct((HOUT, D), F32),) * 3
    )
    return pl.pallas_call(
        final_kernel,
        name="final",
        grid=(4,),
        out_shape=shapes,
        in_specs=[pl.BlockSpec((2, 8, BLOCK), lambda k: (0, 0, 0))]
        + [slots] * 9
        + [
            pl.BlockSpec((2 * EROWS, BLOCK), lambda k: (k, 0)),
            pl.BlockSpec((32, BLOCK), lambda k: (VEC_AT // 32 + k, 0)),
            pl.BlockSpec((2 * HOUT, BLOCK), lambda k: (HEAD_AT // HOUT // 2 + k, 0)),
        ]
        + [table] * 3
        + [rows] * 3
        + [wide] * 3,
        out_specs=(one,) * 2 + (slots,) * 4 + (table,) * 3 + (rows,) * 3 + (wide,) * 3,
        compiler_params=pltpu.CompilerParams(vmem_limit_bytes=60 * 1024 * 1024),
    )(sums, *stacks, flat, flat, flat, *embed, *vec, *head)


def fast_shards(
    inputs,
    targets,
    var_ids,
    lead_ids,
    block_order,
    blocks,
    block_momentum,
    left_stats,
    right_stats,
    left_roots,
    right_roots,
    embed_params,
    embed_first,
    embed_second,
    vectors,
    vector_first,
    vector_second,
    head_weight,
    head_first,
    head_second,
):
    slots = jnp.arange(SLOTS, dtype=jnp.int32)
    hit = block_order[None, :] == slots[:, None]
    place = jnp.sum(jnp.where(hit, slots[None, :], 0), 1)
    lat = ((np.arange(2 * LAT_P, dtype=np.float64) + 0.5) / (2 * LAT_P) - 0.5) * math.pi
    wlat = np.cos(lat)
    wlat = (wlat / np.mean(wlat)).reshape(1, LAT_P, 1, 2, 1)
    wlat = np.broadcast_to(wlat, (TOK // LAT_P, LAT_P, VARS, 2, 2)).reshape(TOK, HOUT)
    left, right, small = run_layer(
        place, lead_ids, blocks, var_ids, jnp.swapaxes(inputs, 1, 2), jnp.swapaxes(targets, 1, 2),
        embed_params, vectors, head_weight.T,
        jnp.asarray(wlat, F32),
    )
    owned, ggt, gtg, lgr, turned, every, sums = run_reduce(
        block_order, left, right, small.reshape(8, 2, 2, 2 * HALF, BLOCK),
        left_roots, block_momentum, right_roots,
    )
    loss, norm, *rest = run_final(
        sums,
        (owned, ggt, gtg, lgr, turned, block_momentum, left_stats, right_stats, blocks),
        every.reshape(32 * ROWS, BLOCK),
        (embed_params, embed_first, embed_second),
        (vectors, vector_first, vector_second),
        (head_weight.T, head_first.T, head_second.T),
    )
    return (loss.reshape(()), norm.reshape(()), *rest[:-3], *(a.T for a in rest[-3:]))


def solution(mesh):
    in_specs = (
        P("batch", "seq", None),
        P("batch", "seq", None),
        P("batch", None),
        P("batch"),
        P(),
        P(("seq", "batch"), None, None),
        P(("seq", "batch"), None, None),
        P(("seq", "batch"), None, None),
        P(("seq", "batch"), None, None),
        P(("seq", "batch"), None, None),
        P(("seq", "batch"), None, None),
        P(),
        P(),
        P(),
        P(),
        P(),
        P(),
        P(),
        P(),
        P(),
    )
    out_specs = (
        P(),
        P(),
        P(("seq", "batch"), None, None),
        P(("seq", "batch"), None, None),
        P(("seq", "batch"), None, None),
        P(("seq", "batch"), None, None),
        P(),
        P(),
        P(),
        P(),
        P(),
        P(),
        P(),
        P(),
        P(),
    )
    sizes = dict(mesh.shape)
    fast = sizes == {"seq": NSEQ, "batch": 2}
    return jax.shard_map(fast_shards if fast else shards, mesh=mesh, in_specs=in_specs, out_specs=out_specs, check_vma=False)
```

```python
import math

import jax
import jax.numpy as jnp
import numpy as np
from jax import lax
from jax.experimental import pallas as pl
from jax.experimental.pallas import tpu as pltpu
from jax.sharding import PartitionSpec as P

D = 1024
HEADS = 16
HD = 64
FF = 4096
VARS = 48
LEADS = 32
LAT_P = 64
KMODES = 32
STEP = 10


HIGH = lax.Precision.HIGHEST
EPS = 1e-05
CLIP_NORM = 0.001
SPECTRAL = 0.5
BETA_ONE = 0.9
BETA_TWO = 0.95
SHAMPOO_RATE = 0.1
DECAY = 0.01
ADAM_EPS = 1e-08
EMBED_RATE = 0.2
VECTOR_RATE = 0.5
HEAD_RATE = 0.05
FLOOR = -1e30
EROWS = VARS * 5 + LEADS
HOUT = VARS * 4
MSE_COUNT = 786432.0
DFT_COUNT = 25165824.0


def layer_norm(rows, gain, shift):
    mean = jnp.mean(rows, -1, keepdims=True)
    centred = rows - mean
    return centred * lax.rsqrt(jnp.mean(centred * centred, -1, keepdims=True) + EPS) * gain + shift


def to_blocks(matrix, size):
    rows, cols = matrix.shape
    return (
        matrix.reshape(rows // size, size, cols // size, size)
        .transpose(0, 2, 1, 3)
        .reshape(-1, size, size)
    )


def from_blocks(stack, rows, cols):
    size = stack.shape[-1]
    return (
        stack.reshape(rows // size, cols // size, size, size)
        .transpose(0, 2, 1, 3)
        .reshape(rows, cols)
    )


def split_matrices(stack):
    size = stack.shape[-1]
    found = []
    begin = 0
    for rows, cols in ((D, 3 * D), (D, D), (D, FF), (FF, D)):
        count = rows * cols // (size * size)
        found.append(from_blocks(stack[begin : begin + count], rows, cols))
        begin += count
    return found


def embed_patches(pixels, tok_sel, emb_sel, query, lead_rows):
    tokens = jnp.einsum("spvc,svcd->spvd", pixels, tok_sel, precision=HIGH) + emb_sel[:, None]
    logits = jnp.einsum("spvd,d->spv", tokens, query, precision=HIGH) * (1.0 / math.sqrt(D))
    weights = jax.nn.softmax(logits, -1)
    return jnp.einsum("spv,spvd->spd", weights, tokens, precision=HIGH) + lead_rows[:, None]


def split_heads(rows):
    return rows.reshape(rows.shape[0], rows.shape[1], HEADS, HD)


def attention_forward(query, keys, values):
    seqs, length, _ = query.shape
    scale = 1.0 / math.sqrt(HD)
    heads_q = split_heads(query)
    start_state = (
        jnp.zeros((seqs, HEADS, length, HD), jnp.float32),
        jnp.full((seqs, HEADS, length), FLOOR, jnp.float32),
        jnp.zeros((seqs, HEADS, length), jnp.float32),
    )
    key_rows = lax.all_gather(keys, "seq", axis=1, tiled=True)
    value_rows = lax.all_gather(values, "seq", axis=1, tiled=True)
    count = key_rows.shape[1] // length
    key_blocks = key_rows.reshape(seqs, count, length, HEADS, HD)
    value_blocks = value_rows.reshape(seqs, count, length, HEADS, HD)

    def visit(inner, index):
        acc, top, total = inner
        scores = (
            jnp.einsum(
                "sphd,snhd->shpn", heads_q, key_blocks[:, index], preferred_element_type=jnp.float32
            )
            * scale
        )
        new_top = jnp.maximum(top, jnp.max(scores, -1))
        fade = jnp.exp(top - new_top)
        probs = jnp.exp(scores - new_top[..., None])
        total = total * fade + jnp.sum(probs, -1)
        acc = acc * fade[..., None] + jnp.einsum(
            "shpn,snhd->shpd",
            probs.astype(jnp.bfloat16),
            value_blocks[:, index],
            preferred_element_type=jnp.float32,
        )
        return ((acc, new_top, total), None)

    inner, _ = lax.scan(visit, start_state, jnp.arange(count))
    acc, top, total = inner
    attended = (acc / total[..., None]).transpose(0, 2, 1, 3).reshape(seqs, length, HEADS * HD)
    return (attended, (top + jnp.log(total)).transpose(0, 2, 1))


def attention_backward(query, keys, values, attended, lse, d_att):
    seqs, length, _ = query.shape
    scale = 1.0 / math.sqrt(HD)
    heads_q = split_heads(query)
    heads_k = split_heads(keys)
    heads_v = split_heads(values)
    heads_d = split_heads(d_att)
    delta = jnp.sum(heads_d.astype(jnp.float32) * split_heads(attended), -1)
    lse_h = lse.transpose(0, 2, 1)
    delta_h = delta.transpose(0, 2, 1)
    key_rows = lax.all_gather(keys, "seq", axis=1, tiled=True)
    value_rows = lax.all_gather(values, "seq", axis=1, tiled=True)
    count = key_rows.shape[1] // length
    key_blocks = key_rows.reshape(seqs, count, length, HEADS, HD)
    value_blocks = value_rows.reshape(seqs, count, length, HEADS, HD)

    def visit(inner, index):
        k_part = key_blocks[:, index]
        scores = (
            jnp.einsum("sphd,snhd->shpn", heads_q, k_part, preferred_element_type=jnp.float32)
            * scale
        )
        probs = jnp.exp(scores - lse_h[..., None])
        d_prob = jnp.einsum(
            "sphd,snhd->shpn", heads_d, value_blocks[:, index], preferred_element_type=jnp.float32
        )
        d_score = (probs * (d_prob - delta_h[..., None])).astype(jnp.bfloat16)
        return (
            inner
            + jnp.einsum("shpn,snhd->sphd", d_score, k_part, preferred_element_type=jnp.float32)
            * scale,
            None,
        )

    inner, _ = lax.scan(visit, jnp.zeros((seqs, length, HEADS, HD), jnp.float32), jnp.arange(count))
    d_query = inner
    all_lse, all_delta = (
        lax.all_gather(lse, "seq", axis=1, tiled=True),
        lax.all_gather(delta, "seq", axis=1, tiled=True),
    )
    empty = jnp.zeros((seqs, length, HEADS, HD), jnp.float32)
    q_rows = lax.all_gather(query, "seq", axis=1, tiled=True)
    g_rows = lax.all_gather(d_att, "seq", axis=1, tiled=True)
    count = q_rows.shape[1] // length
    q_blocks = q_rows.reshape(seqs, count, length, HEADS, HD)
    g_blocks = g_rows.reshape(seqs, count, length, HEADS, HD)
    lse_rows = all_lse.reshape(seqs, count, length, HEADS)
    delta_rows = all_delta.reshape(seqs, count, length, HEADS)

    def visit(inner, index):
        d_key, d_value = inner
        q_part = q_blocks[:, index]
        g_part = g_blocks[:, index]
        scores = (
            jnp.einsum("snhd,sphd->shnp", q_part, heads_k, preferred_element_type=jnp.float32)
            * scale
        )
        probs = jnp.exp(scores - lse_rows[:, index].transpose(0, 2, 1)[..., None])
        d_value = d_value + jnp.einsum(
            "shnp,snhd->sphd",
            probs.astype(jnp.bfloat16),
            g_part,
            preferred_element_type=jnp.float32,
        )
        d_prob = jnp.einsum("snhd,sphd->shnp", g_part, heads_v, preferred_element_type=jnp.float32)
        d_score = (probs * (d_prob - delta_rows[:, index].transpose(0, 2, 1)[..., None])).astype(
            jnp.bfloat16
        )
        d_key = (
            d_key
            + jnp.einsum("shnp,snhd->sphd", d_score, q_part, preferred_element_type=jnp.float32)
            * scale
        )
        return ((d_key, d_value), None)

    inner, _ = lax.scan(visit, (empty, empty), jnp.arange(count))
    d_key, d_value = inner
    return (d_query, d_key, d_value)


def feed_inner(normed_two, w_up, vectors):
    upper = jnp.dot(normed_two, w_up, preferred_element_type=jnp.float32) + vectors[11:].reshape(-1)
    return (upper, jax.nn.gelu(upper).astype(jnp.bfloat16))


def layer_forward(rows, seqs, mats, vectors):
    w_qkv, w_out, w_up, w_down = mats
    normed = layer_norm(rows, vectors[1], vectors[2]).astype(jnp.bfloat16)
    bias = jnp.concatenate([vectors[9], jnp.zeros_like(vectors[9]), vectors[10]])
    qkv = (jnp.dot(normed, w_qkv, preferred_element_type=jnp.float32) + bias).astype(jnp.bfloat16)
    query = qkv[:, :D].reshape(seqs, -1, D)
    keys = qkv[:, D : 2 * D].reshape(seqs, -1, D)
    values = qkv[:, 2 * D :].reshape(seqs, -1, D)
    attended, lse = attention_forward(query, keys, values)
    att_low = attended.reshape(-1, D).astype(jnp.bfloat16)
    mid = rows + jnp.dot(att_low, w_out, preferred_element_type=jnp.float32) + vectors[7]
    normed_two = layer_norm(mid, vectors[3], vectors[4]).astype(jnp.bfloat16)
    upper, active = feed_inner(normed_two, w_up, vectors)
    out = mid + jnp.dot(active, w_down, preferred_element_type=jnp.float32) + vectors[8]
    saved = (upper, active)
    return (out, (rows, normed, query, keys, values, attended, lse, mid, normed_two, saved))


def layer_backward(d_out, kept, mats, vectors):
    rows, normed, query, keys, values, attended, lse, mid, normed_two, saved = kept
    w_qkv, w_out, w_up, w_down = mats
    upper, active = saved
    d_branch = d_out.astype(jnp.bfloat16)
    g_down = jnp.einsum("rf,rd->fd", active, d_branch, preferred_element_type=jnp.float32)
    d_active = jnp.einsum("rd,fd->rf", d_branch, w_down, preferred_element_type=jnp.float32)
    d_upper = jax.vjp(jax.nn.gelu, upper)[1](d_active)[0].astype(jnp.bfloat16)
    g_up = jnp.einsum("rd,rf->df", normed_two, d_upper, preferred_element_type=jnp.float32)
    d_normed_two = jnp.einsum("rf,df->rd", d_upper, w_up, preferred_element_type=jnp.float32)
    d_mid_norm, g_gain_two, g_shift_two = jax.vjp(layer_norm, mid, vectors[3], vectors[4])[1](
        d_normed_two
    )
    d_mid = d_out + d_mid_norm
    d_mid_low = d_mid.astype(jnp.bfloat16)
    att_low = attended.reshape(-1, D).astype(jnp.bfloat16)
    g_out = jnp.einsum("ra,rd->ad", att_low, d_mid_low, preferred_element_type=jnp.float32)
    d_att = jnp.einsum("rd,ad->ra", d_mid_low, w_out, preferred_element_type=jnp.float32).astype(
        jnp.bfloat16
    )
    seqs = query.shape[0]
    d_query, d_key, d_value = attention_backward(
        query, keys, values, attended, lse, d_att.reshape(seqs, -1, D)
    )
    d_qkv = jnp.concatenate(
        [d_query.reshape(-1, D), d_key.reshape(-1, D), d_value.reshape(-1, D)], 1
    ).astype(jnp.bfloat16)
    g_qkv = jnp.einsum("rd,re->de", normed, d_qkv, preferred_element_type=jnp.float32)
    d_normed = jnp.einsum("re,de->rd", d_qkv, w_qkv, preferred_element_type=jnp.float32)
    d_rows_norm, g_gain_one, g_shift_one = jax.vjp(layer_norm, rows, vectors[1], vectors[2])[1](
        d_normed
    )
    qkv_sums = jnp.sum(d_qkv.astype(jnp.float32), 0)
    small = (
        g_gain_one,
        g_shift_one,
        g_gain_two,
        g_shift_two,
        jnp.sum(d_mid_low.astype(jnp.float32), 0),
        jnp.sum(d_branch.astype(jnp.float32), 0),
        qkv_sums[:D],
        qkv_sums[2 * D :],
        jnp.sum(d_upper.astype(jnp.float32), 0),
    )
    return (d_mid + d_rows_norm, (g_qkv, g_out, g_up, g_down), small)


def loss_terms(pred, targets, seqs, length):
    strips = lax.axis_size("seq")
    cols = length // LAT_P
    nlat = 2 * LAT_P
    nlon = 2 * cols * strips
    all_seqs = seqs * lax.axis_size("batch")
    diff = pred.reshape(seqs, length, -1) - targets.astype(jnp.float32)
    grid = (
        diff.reshape(seqs, cols, LAT_P, VARS, 2, 2)
        .transpose(0, 3, 2, 4, 1, 5)
        .reshape(seqs, VARS, nlat, 2 * cols)
    )
    lat = ((jnp.arange(nlat, dtype=jnp.float32) + 0.5) / nlat - 0.5) * math.pi
    weight = jnp.cos(lat)
    weight = (weight / jnp.mean(weight))[None, None, :, None]
    column = lax.axis_index("seq") * (2 * cols) + jnp.arange(2 * cols, dtype=jnp.int32)
    modes = jnp.arange(KMODES, dtype=jnp.int32)
    angle = (column[:, None] * modes[None] % nlon).astype(jnp.float32) * (2.0 * math.pi / nlon)
    cosine = jnp.cos(angle)
    sine = jnp.sin(angle)
    part_c = jnp.einsum("svrc,ck->svrk", grid, cosine, precision=HIGH)
    part_s = jnp.einsum("svrc,ck->svrk", grid, sine, precision=HIGH)
    full_c, full_s = lax.psum((part_c, part_s), "seq")
    mse_count = all_seqs * VARS * nlat * nlon
    dft_count = nlon * all_seqs * VARS * nlat * KMODES
    mse = jnp.sum(weight * grid * grid) / mse_count
    spectral = SPECTRAL * jnp.sum(weight * (full_c * full_c + full_s * full_s)) / dft_count
    first = (lax.axis_index("seq") == 0).astype(jnp.float32)
    back_wave = jnp.einsum("svrk,ck->svrc", full_c, cosine, precision=HIGH) + jnp.einsum(
        "svrk,ck->svrc", full_s, sine, precision=HIGH
    )
    d_grid = 2.0 * weight * grid / mse_count + 2.0 * SPECTRAL / dft_count * weight * back_wave
    d_pred = (
        d_grid.reshape(seqs, VARS, LAT_P, 2, cols, 2)
        .transpose(0, 4, 2, 1, 3, 5)
        .reshape(seqs * length, VARS * 4)
    )
    return (d_pred, mse + first * spectral)


def adam(value, first, second, grad, rate):
    first = BETA_ONE * first + (1.0 - BETA_ONE) * grad
    second = BETA_TWO * second + (1.0 - BETA_TWO) * grad * grad
    step = first / (1.0 - BETA_ONE**STEP) / (jnp.sqrt(second / (1.0 - BETA_TWO**STEP)) + ADAM_EPS)
    return (first, second, value - rate * (step + DECAY * value))


def shards(
    inputs,
    targets,
    var_ids,
    lead_ids,
    block_order,
    blocks,
    block_momentum,
    left_stats,
    right_stats,
    left_roots,
    right_roots,
    embed_params,
    embed_first,
    embed_second,
    vectors,
    vector_first,
    vector_second,
    head_weight,
    head_first,
    head_second,
):
    seqs, length, _ = inputs.shape
    size = blocks.shape[-1]
    low_blocks = blocks.astype(jnp.bfloat16)
    stack = lax.all_gather(low_blocks, ("seq", "batch"), axis=0, tiled=True)
    natural = jnp.zeros_like(stack).at[block_order].set(stack)
    mats = split_matrices(natural)
    head_low = head_weight.astype(jnp.bfloat16)
    pick = (var_ids[..., None] == jnp.arange(VARS, dtype=jnp.int32)[None, None]).astype(jnp.float32)
    lead_pick = (lead_ids[:, None] == jnp.arange(LEADS, dtype=jnp.int32)[None]).astype(jnp.float32)
    tok_sel = jnp.einsum(
        "svw,wcd->svcd", pick, embed_params[: VARS * 4].reshape(VARS, 4, D), precision=HIGH
    )
    emb_sel = jnp.einsum("svw,wd->svd", pick, embed_params[VARS * 4 : VARS * 5], precision=HIGH)
    lead_rows = jnp.dot(lead_pick, embed_params[VARS * 5 :], precision=HIGH)
    pixels = inputs.astype(jnp.float32).reshape(seqs, length, VARS, 4)

    def embed_local(tok_part, emb_part, query, lead_part):
        return embed_patches(pixels, tok_part, emb_part, query, lead_part)

    stream, embed_back = jax.vjp(embed_local, tok_sel, emb_sel, vectors[0], lead_rows)
    out, kept = layer_forward(stream.reshape(-1, D), seqs, mats, vectors)
    final_rows, final_back = jax.vjp(layer_norm, out, vectors[5], vectors[6])
    final = final_rows.astype(jnp.bfloat16)
    pred = jnp.dot(final, head_low, preferred_element_type=jnp.float32)
    d_pred, loss_part = loss_terms(pred, targets, seqs, length)
    d_low = d_pred.astype(jnp.bfloat16)
    g_head = jnp.einsum("rd,ro->do", final, d_low, preferred_element_type=jnp.float32)
    d_final = jnp.einsum("ro,do->rd", d_low, head_low, preferred_element_type=jnp.float32)
    d_out, g_gain_final, g_shift_final = final_back(d_final)
    d_rows, matrix_grads, small = layer_backward(d_out, kept, mats, vectors)
    d_tok, d_emb, d_query, d_lead = embed_back(d_rows.reshape(seqs, length, D))
    g_embed = jnp.concatenate(
        [
            jnp.einsum("svw,svcd->wcd", pick, d_tok, precision=HIGH).reshape(VARS * 4, D),
            jnp.einsum("svw,svd->wd", pick, d_emb, precision=HIGH),
            jnp.einsum("sl,sd->ld", lead_pick, d_lead, precision=HIGH),
        ]
    )
    g_gain_one, g_shift_one, g_gain_two, g_shift_two, b_out, b_down, b_query, b_value, b_up = small
    g_vectors = jnp.concatenate(
        [
            jnp.stack(
                [
                    d_query,
                    g_gain_one,
                    g_shift_one,
                    g_gain_two,
                    g_shift_two,
                    g_gain_final,
                    g_shift_final,
                    b_out,
                    b_down,
                    b_query,
                    b_value,
                ]
            ),
            b_up.reshape(-1, D),
        ]
    )
    slot_grads = jnp.concatenate([to_blocks(grad, size) for grad in matrix_grads])[block_order]
    owned = lax.psum_scatter(slot_grads, ("seq", "batch"), scatter_dimension=0, tiled=True)
    g_embed, g_vectors, g_head, loss_total = lax.psum(
        (g_embed, g_vectors, g_head, loss_part), ("seq", "batch")
    )
    rest_squares = (
        jnp.sum(g_embed * g_embed) + jnp.sum(g_vectors * g_vectors) + jnp.sum(g_head * g_head)
    )
    grad_norm = jnp.sqrt(lax.psum(jnp.sum(owned * owned), ("seq", "batch")) + rest_squares)
    clip = CLIP_NORM / jnp.maximum(grad_norm, CLIP_NORM)
    owned = owned * clip
    new_momentum = BETA_ONE * block_momentum + (1.0 - BETA_ONE) * owned
    new_left = BETA_TWO * left_stats + (1.0 - BETA_TWO) * jnp.einsum(
        "bij,bkj->bik", owned, owned, precision=HIGH
    )
    new_right = BETA_TWO * right_stats + (1.0 - BETA_TWO) * jnp.einsum(
        "bji,bjk->bik", owned, owned, precision=HIGH
    )
    direction = jnp.einsum(
        "bij,bjk->bik",
        jnp.einsum("bij,bjk->bik", left_roots, new_momentum, precision=HIGH),
        right_roots,
        precision=HIGH,
    )
    new_blocks = blocks - SHAMPOO_RATE * (direction + DECAY * blocks)
    e_one, e_two, e_new = adam(embed_params, embed_first, embed_second, g_embed * clip, EMBED_RATE)
    v_one, v_two, v_new = adam(vectors, vector_first, vector_second, g_vectors * clip, VECTOR_RATE)
    h_one, h_two, h_new = adam(head_weight, head_first, head_second, g_head * clip, HEAD_RATE)
    return (
        loss_total,
        grad_norm,
        new_blocks,
        new_momentum,
        new_left,
        new_right,
        e_one,
        e_two,
        e_new,
        v_one,
        v_two,
        v_new,
        h_one,
        h_two,
        h_new,
    )


SHARE = 24
PIECE = 6
MAIN = ("zxy", "zyx", "xzy", "yzx")
SMALL = ("xyz", "yxz")
TAIL = ("zxy", "zyx")
GATHER_SIZES = (5, 5, 7, 7)
GATHER_ORDER = (
    (0, 0, 0, 3), (3, 0, 0, 3), (1, 0, 0, 3), (2, 0, 0, 3), (1, 0, 0, 2), (1, 0, 1, 3), (0, 0, 0, 2), (1, 1, 0, 3),
    (3, 0, 0, 2), (0, 0, 0, 1), (2, 1, 0, 3), (1, 0, 0, 0), (1, 0, 0, 1), (2, 0, 0, 2), (3, 0, 1, 3), (2, 1, 0, 1),
    (2, 1, 0, 2), (0, 0, 1, 3), (0, 0, 0, 0), (3, 0, 1, 2), (2, 0, 1, 3), (1, 0, 1, 2), (0, 1, 0, 1), (2, 0, 0, 0),
    (2, 0, 0, 1), (0, 1, 0, 3), (1, 0, 1, 0), (0, 1, 0, 0), (3, 0, 0, 0), (0, 1, 0, 2), (1, 1, 0, 2), (3, 0, 1, 1),
    (3, 0, 1, 0), (3, 0, 0, 1), (3, 1, 1, 2), (1, 1, 1, 0), (2, 0, 1, 2), (3, 1, 0, 3), (1, 1, 1, 2), (1, 0, 1, 1),
    (3, 1, 0, 2), (2, 1, 0, 0), (1, 1, 0, 0), (0, 0, 1, 2), (0, 0, 1, 0), (2, 1, 1, 1), (3, 1, 1, 0), (0, 1, 1, 3),
    (0, 1, 1, 0), (0, 1, 1, 1), (2, 0, 1, 0), (2, 1, 1, 2), (3, 1, 1, 1), (2, 0, 1, 1), (2, 1, 1, 3), (0, 0, 1, 1),
    (3, 1, 0, 1), (3, 1, 0, 0), (1, 1, 1, 3), (0, 1, 1, 2), (1, 1, 0, 1), (3, 1, 1, 3), (1, 1, 1, 1), (2, 1, 1, 0),
)
REDUCE_PLAN = (
    (0, 4, 1, 1, 1), (0, 4, 0, 0, 0), (0, 3, 1, 0, 1), (0, 4, 1, 1, 0), (0, 0, 1, 1, 1), (0, 4, 0, 1, 0), (0, 5, 0, 0, 1),
    (3, 0, 0, 0, 0), (3, 0, 0, 0, 0), (0, 5, 1, 1, 0), (0, 5, 0, 1, 0), (0, 3, 1, 0, 0), (0, 2, 1, 1, 0), (0, 5, 1, 0, 0),
    (3, 0, 0, 0, 0), (0, 4, 1, 0, 0), (0, 5, 1, 1, 1), (0, 5, 1, 0, 1), (0, 1, 1, 1, 0), (0, 5, 0, 1, 1), (0, 5, 1, 1, 2),
    (0, 4, 1, 1, 2), (0, 2, 0, 1, 0), (0, 2, 1, 1, 2), (3, 0, 0, 0, 0), (0, 4, 0, 1, 1), (0, 3, 1, 1, 2), (0, 1, 1, 1, 1),
    (0, 4, 1, 0, 2), (3, 0, 0, 0, 0), (3, 0, 0, 0, 0), (0, 4, 0, 1, 2), (0, 5, 0, 0, 0), (0, 3, 0, 0, 1), (3, 0, 0, 0, 0),
    (3, 0, 0, 0, 0), (0, 0, 1, 1, 0), (0, 0, 1, 1, 3), (0, 3, 1, 1, 0), (0, 3, 0, 0, 0), (3, 0, 0, 0, 0), (0, 5, 0, 1, 2),
    (0, 3, 1, 1, 1), (0, 0, 1, 0, 1), (3, 0, 0, 0, 0), (3, 0, 0, 0, 0), (0, 4, 1, 1, 3), (3, 0, 0, 0, 0), (3, 0, 0, 0, 0),
    (0, 2, 1, 0, 0), (0, 5, 1, 1, 3), (0, 2, 1, 1, 1), (3, 0, 0, 0, 0), (0, 0, 0, 1, 1), (0, 0, 1, 1, 2), (0, 5, 1, 0, 2),
    (3, 0, 0, 0, 0), (0, 2, 0, 0, 0), (0, 1, 1, 1, 2), (0, 0, 0, 1, 0), (0, 2, 1, 0, 2), (0, 1, 1, 0, 0), (0, 1, 0, 1, 0),
    (0, 2, 1, 1, 3), (3, 0, 0, 0, 0), (3, 0, 0, 0, 0), (0, 4, 1, 0, 1), (0, 1, 1, 1, 3), (0, 0, 1, 0, 0), (0, 1, 1, 0, 1),
    (3, 0, 0, 0, 0), (0, 2, 1, 0, 1), (0, 1, 0, 1, 1), (0, 5, 0, 1, 3), (0, 3, 0, 1, 1), (3, 0, 0, 0, 0), (0, 2, 0, 1, 1),
    (0, 4, 1, 0, 3), (3, 0, 0, 0, 0), (0, 5, 1, 0, 3), (0, 5, 0, 0, 2), (3, 0, 0, 0, 0), (0, 3, 0, 1, 0), (0, 2, 0, 1, 2),
    (0, 0, 0, 1, 2), (0, 3, 1, 0, 2), (0, 1, 0, 1, 2), (0, 3, 1, 1, 3), (3, 0, 0, 0, 0), (0, 0, 0, 0, 1), (0, 4, 0, 1, 3),
    (0, 0, 1, 0, 2), (0, 2, 0, 1, 3), (3, 0, 0, 0, 0), (0, 1, 0, 0, 0), (0, 0, 0, 1, 3), (0, 0, 0, 0, 0), (0, 1, 1, 0, 2),
    (0, 2, 1, 0, 3), (3, 0, 0, 0, 0), (0, 0, 1, 0, 3), (0, 1, 0, 0, 1), (0, 3, 0, 1, 2), (0, 1, 1, 0, 3), (0, 1, 0, 1, 3),
    (0, 3, 1, 0, 3), (0, 5, 0, 0, 3), (0, 2, 0, 0, 1), (0, 4, 0, 0, 1), (1, 1, 0, 0, 3), (0, 4, 0, 0, 2), (0, 2, 0, 0, 2),
    (0, 0, 0, 0, 2), (1, 1, 0, 0, 2), (0, 1, 0, 0, 2), (0, 3, 0, 1, 3), (0, 4, 0, 0, 3), (1, 0, 0, 0, 3), (0, 2, 0, 0, 3),
    (2, 2, 0, 0, 0), (2, 2, 1, 0, 0), (2, 2, 2, 0, 0), (0, 3, 0, 0, 2), (2, 2, 3, 0, 0), (0, 0, 0, 0, 3), (2, 2, 4, 0, 0),
    (2, 2, 5, 0, 0), (2, 0, 0, 0, 0), (1, 0, 0, 0, 2), (2, 0, 1, 0, 0), (2, 0, 2, 0, 0), (0, 1, 0, 0, 3), (2, 1, 0, 0, 0),
    (1, 1, 0, 1, 3), (2, 1, 1, 0, 0), (2, 1, 2, 0, 0), (1, 1, 0, 1, 2), (2, 1, 3, 0, 0), (1, 1, 0, 0, 0), (2, 1, 4, 0, 0),
    (2, 0, 3, 0, 0), (1, 0, 0, 0, 0), (1, 1, 1, 0, 3), (2, 1, 5, 0, 0), (1, 0, 0, 0, 1), (2, 0, 4, 0, 0), (2, 0, 5, 0, 0),
    (1, 1, 0, 0, 1), (1, 1, 0, 1, 0), (1, 0, 1, 0, 3), (1, 0, 1, 0, 2), (0, 3, 0, 0, 3), (1, 0, 1, 0, 1), (2, 3, 0, 0, 0),
    (1, 0, 1, 0, 0), (1, 1, 0, 1, 1), (1, 0, 0, 1, 1), (2, 3, 1, 0, 0), (2, 3, 2, 0, 0), (2, 3, 3, 0, 0), (1, 1, 1, 1, 2),
    (2, 3, 4, 0, 0), (1, 1, 1, 1, 0), (1, 1, 1, 0, 0), (1, 0, 0, 1, 2), (1, 0, 1, 1, 1), (1, 0, 0, 1, 0), (1, 1, 1, 0, 1),
    (2, 3, 5, 0, 0), (1, 0, 1, 1, 2), (1, 0, 1, 1, 0), (1, 0, 0, 1, 3), (1, 1, 1, 0, 2), (1, 1, 1, 1, 1), (1, 0, 1, 1, 3),
    (1, 1, 1, 1, 3),
)

class Place:
    def __init__(self):
        s = lax.axis_index("seq")
        self.y = lax.axis_index("batch")
        self.core = lax.rem(s, 2)
        self.x = lax.rem(s // 2, 2)
        self.z = s // 4
        self.s = s

    def chip(self, z, x, y):
        return (z * 2 + x) * 2 + y

    def linear(self, z, x, y):
        return ((z * 2 + x) * 2 + self.core) * 2 + y

    def device(self, z, x, y):
        return ((z * 2 + x) * 2 + self.core, y)

    def sibling(self):
        return (self.s + 1 - 2 * self.core, self.y)

    def far(self, rank):
        z = self.z
        if rank == 3:
            return z
        if rank == 2:
            return z + 1 - 2 * lax.rem(z, 2)
        low = z // 2
        return (3 - 3 * low) if rank == 0 else (2 - low)

    def flipped(self, dx, dy):
        x = self.x if dx == 0 else 1 - self.x
        y = self.y if dy == 0 else 1 - self.y
        return x, y

    def greet(self):
        barrier = pltpu.get_barrier_semaphore()

        def hail(o, _):
            peer = lax.rem(self.s + o, NSEQ)
            pl.semaphore_signal(barrier, inc=1, device_id=(peer, self.y), device_id_type=MESH_ID)
            return _

        lax.fori_loop(1, NSEQ, hail, 0)
        pl.semaphore_signal(
            barrier, inc=1, device_id=(self.s, 1 - self.y), device_id_type=MESH_ID
        )
        pl.semaphore_wait(barrier, NSEQ)


def last_move(order, dx, dy, rank):
    found = -1
    for i, c in enumerate(order):
        if (c == "x" and dx) or (c == "y" and dy) or (c == "z" and rank != 3):
            found = i
    return found


def sends_before(order, axis):
    count = 1
    for c in order:
        if c == axis:
            return count
        count *= 4 if c == "z" else 2
    return count


def drain(place, orders, total, sem, hops, sizes=None):
    sizes = sizes or (1,) * len(orders)
    count = {
        c: sum(sends_before(order, c) * size for order, size in zip(orders, sizes)) for c in "xyz"
    }

    def finish(i, pieces):
        ref = total(pieces)
        pltpu.make_async_remote_copy(
            ref, ref, sem.at[i], sem.at[i], place.sibling(), MESH_ID
        ).wait_send()

    finish(0, count["x"])
    finish(1, count["y"])
    for z in range(4):
        for i in (2, 3):
            if hops[i - 2][z]:

                @pl.when(place.z == z)
                def _(i=i, z=z):
                    finish(i, count["z"] * hops[i - 2][z])


GATHER_HOPS = ((1, 2, 3, 0), (0, 3, 2, 1))
REDUCE_HOPS = ((3, 2, 1, 0), (0, 1, 2, 3))


def gather_steps(place, orders, sizes, steps, piece, total, recv, send, sib_send, sib_recv):
    z = place.z

    def copy(ref, device, send_sem, recv_sem):
        return pltpu.make_async_remote_copy(ref, ref, send_sem, recv_sem, device, MESH_ID)

    for number, (part, dx, dy, rank) in enumerate(steps):
        order = orders[part]
        tz = place.far(rank)
        sx, sy = place.flipped(dx, dy)
        ref = piece(place.linear(tz, sx, sy), part)
        landed = recv.at[part, place.chip(tz, sx, sy)]
        own = dx == 0 and dy == 0 and rank == 3
        if not own:
            copy(ref, place.sibling(), landed, landed).wait_recv()
        last = last_move(order, dx, dy, rank)
        if last >= 0 and order[last] == "z" and rank != 3:
            up = (z > tz).astype(jnp.int32)
            nz = z + 2 * up - 1

            @pl.when(jnp.logical_and(nz >= 0, nz <= 3))
            def _():
                copy(ref, place.device(nz, place.x, place.y), send.at[3 - up], landed).start()

        for c in order[last + 1 :]:
            if c == "x":
                copy(ref, place.device(z, 1 - place.x, place.y), send.at[0], landed).start()
            elif c == "y":
                copy(ref, place.device(z, place.x, 1 - place.y), send.at[1], landed).start()
            else:

                @pl.when(z < 3)
                def _():
                    copy(ref, place.device(z + 1, place.x, place.y), send.at[2], landed).start()

                @pl.when(z > 0)
                def _():
                    copy(ref, place.device(z - 1, place.x, place.y), send.at[3], landed).start()

        copy(ref, place.sibling(), sib_send.at[0], sib_recv.at[0]).start()
        yield number
    drain(place, orders, total, send, GATHER_HOPS, sizes)
    whole = total(16 * sum(sizes))
    copy(whole, place.sibling(), sib_send.at[0], sib_recv.at[0]).wait()


def radix(order, stop, dx, dy, tz):
    index = 0
    size = 1
    for c in order[: order.index(stop[0])]:
        value, base = {"x": (dx, 2), "y": (dy, 2), "z": (tz, 4)}[c]
        index = index * base + value
        size *= base
    if stop[0] == "z":
        index = index * 3 + (tz if stop == "z+" else tz - 1)
        size *= 3
    return index, size


def landing_base(orders):
    base = {}
    at = 0
    for axis in ("x", "y", "z+", "z-"):
        for part, order in enumerate(orders):
            base[(axis, part)] = at
            at += radix(order, axis, 0, 0, 0)[1]
    return base, at


def reduce_step(place, orders, base, step, own_piece, add_landed, land, recv, out, send, keep, offset):
    part, dx, dy, rank = step
    order = orders[part]
    z = place.z
    tz = place.far(rank)
    tx, ty = place.flipped(dx, dy)
    chip = place.chip(tz, tx, ty)
    root = dx == 0 and dy == 0 and rank == 3
    last = last_move(order, dx, dy, rank)
    out_at = part * 16 + chip
    own_piece(part + offset, place.linear(tz, tx, ty), chip, out_at)

    def slot(axis):
        return base[(axis, part)] + radix(order, axis, dx, dy, tz)[0]

    def take(index):
        ref = land.at[index]
        sem = recv.at[index]
        pltpu.make_async_remote_copy(ref, ref, sem, sem, place.sibling(), MESH_ID).wait_recv()
        add_landed(part + offset, index)

    if last >= 0 and order[last] == "z" and rank != 3:
        up = (z > tz).astype(jnp.int32)
        nz = z + 2 * up - 1
        plus = slot("z+")
        minus = slot("z-")

        @pl.when(jnp.logical_and(nz >= 0, nz <= 3))
        def _():
            take(up * plus + (1 - up) * minus)

    for c in order[last + 1 :]:
        if c == "z":

            @pl.when(z < 3)
            def _():
                take(slot("z+"))

            @pl.when(z > 0)
            def _():
                take(slot("z-"))

        else:
            take(slot(c))
    keep(part + offset, out_at, root)
    if root:
        return
    ref = out.at[out_at]

    def push(device, index, direction):
        pltpu.make_async_remote_copy(
            ref, land.at[index], send.at[direction], recv.at[index], device, MESH_ID
        ).start()

    axis = order[last]
    if axis == "x":
        index = base[("x", part)] + radix(order, "x", 0, dy, tz)[0]
        push(place.device(z, 1 - place.x, place.y), index, 0)
    elif axis == "y":
        index = base[("y", part)] + radix(order, "y", dx, 0, tz)[0]
        push(place.device(z, place.x, 1 - place.y), index, 1)
    else:
        down = (z > tz).astype(jnp.int32)
        index = down * slot("z+") + (1 - down) * slot("z-")
        push(place.device(z + 1 - 2 * down, place.x, place.y), index, 2 + down)


TOK = 128
NSEQ = 16
BLOCK = 128
N_LEFT = 56
N_RIGHT = 72
QCH = 256
LOG2E = math.log2(math.e)
MESH_ID = pl.DeviceIdType.MESH
NT = (((1,), (1,)), ((), ()))
TN = (((0,), (0,)), ((), ()))
NN = (((1,), (0,)), ((), ()))
BF = jnp.bfloat16
F32 = jnp.float32
VM = pltpu.VMEM


def mm(a, b, dims=NN):
    return lax.dot_general(a, b, dims, preferred_element_type=F32)


def mmh(a, b, dims=NN):
    return lax.dot_general(a, b, dims, precision=HIGH, preferred_element_type=F32)


def flip(x):
    return jnp.swapaxes(x.astype(F32), 0, 1).astype(x.dtype)


def normalise(x):
    mean = jnp.mean(x, -1, keepdims=True)
    centred = x - mean
    rstd = lax.rsqrt(jnp.mean(centred * centred, -1, keepdims=True) + EPS)
    return centred * rstd, rstd


def normalise_back(grad, unit, rstd, gain):
    inner = grad * gain
    return rstd * (
        inner
        - jnp.mean(inner, -1, keepdims=True)
        - unit * jnp.mean(inner * unit, -1, keepdims=True)
    )


def column_sum(x):
    return jnp.sum(x, 0, keepdims=True)


GELU_K = math.sqrt(2.0 / math.pi)


def gelu_value(x):
    return 0.5 * x * (1.0 + jnp.tanh(GELU_K * (x + 0.044715 * x * x * x)))


def gelu_slope(x):
    t = jnp.tanh(GELU_K * (x + 0.044715 * x * x * x))
    return 0.5 * (1.0 + t) + 0.5 * x * (1.0 - t * t) * GELU_K * (1.0 + 3.0 * 0.044715 * x * x)


def layer_kernel(
    place_ref,
    lead_ref,
    blocks_ref,
    ids_ref,
    pix_ref,
    goal_ref,
    emb_ref,
    vec_ref,
    head_ref,
    wlat_ref,
    left_hbm,
    right_hbm,
    small_ref,
    stack,
    left,
    right,
    slab,
    qkv_t,
    out_t,
    out_t32,
    lse,
    o_in,
    d_slab,
    do_t,
    dqkv_t,
    dqkv_in,
    k_row,
    v_row,
    q_row,
    do_row,
    s_scr,
    dq_acc,
    h0_s,
    n1_s,
    xp_s,
    a_s,
    mid_s,
    up_s,
    act_s,
    acc,
    wave,
    wave_in,
    wave_tile,
    wave_all,
    pix_s,
    goal_s,
    head_s,
    gvec,
    t_recv,
    t_send,
    t_sib_send,
    t_sib_recv,
    a_send,
    a_recv,
    in_sem,
    g_local,
    g_send,
    g_recv,
):
    s = lax.axis_index("seq")
    b = lax.axis_index("batch")
    place = Place()
    sibling = s + 1 - 2 * place.core

    loads = []
    for i, (src, dst) in enumerate(((pix_ref, pix_s), (goal_ref, goal_s), (head_ref, head_s))):
        c = pltpu.make_async_copy(src, dst, in_sem.at[i])
        c.start()
        loads.append(c)
    mine = place.linear(place.z, place.x, place.y)
    stack[pl.ds(mine * SHARE, SHARE)] = blocks_ref[...].astype(BF)
    place.greet()

    for number in gather_steps(
        place,
        MAIN,
        GATHER_SIZES,
        GATHER_ORDER,
        lambda d, p: stack.at[pl.ds(d * SHARE + sum(GATHER_SIZES[:p]), GATHER_SIZES[p])],
        lambda n: stack.at[pl.ds(0, n)],
        t_recv,
        t_send,
        t_sib_send,
        t_sib_recv,
    ):
        if number == 3:
            loads[0].wait()
            embed_forward(pix_s, ids_ref, lead_ref, emb_ref, vec_ref, h0_s, n1_s, xp_s, a_s)

    def block(begin, across, r, c):
        return stack[place_ref[begin + r * across + c]]

    def two_columns(begin, across, pair):
        return jnp.concatenate(
            [
                jnp.concatenate(
                    [block(begin, across, r, 2 * pair), block(begin, across, r, 2 * pair + 1)], 1
                )
                for r in range(8)
            ],
            0,
        )

    def two_rows(begin, pair):
        return jnp.concatenate(
            [
                jnp.concatenate([block(begin, 8, 2 * pair + r, c) for c in range(8)], 1)
                for r in range(2)
            ],
            0,
        )

    def eight_columns(begin, across, quad):
        return jnp.concatenate(
            [
                jnp.concatenate([block(begin, across, r, 8 * quad + k) for k in range(8)], 1)
                for r in range(8)
            ],
            0,
        )

    def eight_rows(begin, quad):
        return jnp.concatenate(
            [
                jnp.concatenate([block(begin, 8, 8 * quad + r, c) for c in range(8)], 1)
                for r in range(8)
            ],
            0,
        )

    at_qkv, at_o, at_up, at_down = 0, 192, 256, 512
    share = []

    def share_group(index, stage, target, begin, count):
        part = pl.ds(begin, count)
        c = pltpu.make_async_copy(stage.at[part], target.at[0, part], g_local.at[index])
        c.start()
        r = pltpu.make_async_remote_copy(
            src_ref=stage.at[part],
            dst_ref=target.at[1, part],
            send_sem=g_send.at[index],
            recv_sem=g_recv.at[index],
            device_id=(sibling, b),
            device_id_type=MESH_ID,
        )
        r.start()
        share.append((c, r))

    def exchange(which, src_at, dst_at):
        def copy(o):
            peer = lax.rem(s + o, NSEQ)
            return pltpu.make_async_remote_copy(
                src_ref=src_at(peer),
                dst_ref=dst_at(s),
                send_sem=a_send.at[which, o],
                recv_sem=a_recv.at[which, o],
                device_id=(peer, b),
                device_id_type=MESH_ID,
            )

        def begin(o, _):
            copy(o).start()
            return _

        def finish(o, _):
            copy(o).wait()
            return _

        def start():
            lax.fori_loop(1, NSEQ, begin, 0)

        def start_to(peer):
            @pl.when(peer != s)
            def _():
                copy(lax.rem(peer - s + NSEQ, NSEQ)).start()

        def wait():
            lax.fori_loop(1, NSEQ, finish, 0)

        return start, wait, start_to

    def lanes(i, size):
        return pl.ds(pl.multiple_of(i * size, size), size)

    def rows_at(i, size):
        return pl.ds(pl.multiple_of(i * size, size), size)

    n1 = n1_s[...]
    waits = {}
    for which in (1, 0, 2):

        def qkv_tile(t, _, which=which):
            piece = mm(n1, two_columns(at_qkv, 24, 4 * which + t))
            if which != 1:
                piece = piece + vec_ref[9 + which // 2 : 10 + which // 2, lanes(t, 256)]
            piece = piece.astype(BF)
            for k in range(2):
                turned = flip(piece[:, k * BLOCK : (k + 1) * BLOCK])
                for half in range(2):
                    slab[4 * t + 2 * k + half, which * HD : (which + 1) * HD, :] = turned[
                        half * HD : (half + 1) * HD
                    ]
            return _

        lax.fori_loop(0, 4, qkv_tile, 0, unroll=4)
        part = pl.ds(which * HD, HD)
        start, waits[which], _ = exchange(
            which,
            lambda p, part=part: slab.at[p, part],
            lambda p, part=part: qkv_t.at[part, lanes(p, TOK)],
        )
        start()
    qkv_t[:, lanes(s, TOK)] = slab[s]
    for k in range(8):
        left[k] = flip(n1[:, k * BLOCK : (k + 1) * BLOCK])

    scale2 = LOG2E / math.sqrt(HD)

    def turn_rows(source, begin, target):
        def one(t, _):
            target[rows_at(t, TOK), :] = flip(source[begin : begin + HD, lanes(t, TOK)])
            return _

        lax.fori_loop(0, NSEQ, one, 0, unroll=4)

    waits[1]()
    turn_rows(qkv_t, HD, k_row)
    waits[0]()
    tiles = (NSEQ * TOK) // QCH
    start, wait_o, send_o = exchange(
        3, lambda p: out_t.at[:, lanes(p, TOK)], lambda p: o_in.at[p]
    )

    def forward_chunk(i, _):
        c = lax.rem(i + s // 2, tiles)
        part = lanes(c, QCH)
        q_part = qkv_t[0:HD, part]
        top = None
        for t in range(tiles):
            tile = slice(t * QCH, (t + 1) * QCH)
            scores = mm(k_row[tile, :], q_part)
            s_scr[tile, :] = scores
            best = jnp.max(scores, 0, keepdims=True)
            top = best if top is None else jnp.maximum(top, best)
        top = top * scale2

        @pl.when(i == 0)
        def _():
            waits[2]()

        total = jnp.zeros((1, QCH), F32)
        mixed = jnp.zeros((HD, QCH), F32)
        for t in range(2):
            tile = slice(4 * t * QCH, (4 * t + 4) * QCH)
            probs = jnp.exp2(s_scr[tile, :] * scale2 - top)
            total = total + jnp.sum(probs, 0, keepdims=True)
            mixed = mixed + mm(qkv_t[2 * HD : 3 * HD, tile], probs.astype(BF))
        mixed = mixed / total
        lse[c] = top + jnp.log2(total)
        out_t32[:, part] = mixed
        out_t[:, part] = mixed.astype(BF)
        send_o(2 * c)
        send_o(2 * c + 1)
        return 0

    lax.fori_loop(0, tiles, forward_chunk, 0)
    share_group(0, left, left_hbm, 0, 8)
    o_in[s] = out_t[:, lanes(s, TOK)]
    turn_rows(qkv_t, 0, q_row)
    turn_rows(qkv_t, 2 * HD, v_row)
    wait_o()

    parts = []
    for k in range(8):
        pair = jnp.concatenate([o_in[2 * k], o_in[2 * k + 1]], 0)
        left[8 + k] = pair
        parts.append(flip(pair))
    share_group(1, left, left_hbm, 8, 8)
    o_low = jnp.concatenate(parts, 1)

    def out_tile(t, _):
        part = lanes(t, 256)
        mid_s[:, part] = h0_s[:, part] + (
            mm(o_low, two_columns(at_o, 8, t)) + vec_ref[7:8, part]
        )
        return _

    lax.fori_loop(0, 4, out_tile, 0, unroll=4)
    mid = mid_s[...]
    unit, _ = normalise(mid)
    n2 = (unit * vec_ref[3:4, :] + vec_ref[4:5, :]).astype(BF)
    acc[...] = mid + vec_ref[8:9, :]

    def up_tile(t, _):
        part = lanes(t, 1024)
        bias = vec_ref[pl.ds(11 + t, 1), :]
        upper = mm(n2, eight_columns(at_up, 32, t)) + bias
        up_s[:, part] = upper
        active = gelu_value(upper).astype(BF)
        act_s[:, part] = active
        acc[...] += mm(active, eight_rows(at_down, t))
        return _

    lax.fori_loop(0, 4, up_tile, 0, unroll=2)

    unit_f, rstd_f = normalise(acc[...])
    final = (unit_f * vec_ref[5:6, :] + vec_ref[6:7, :]).astype(BF)
    loads[2].wait()
    head = head_s[...].astype(BF)
    loads[1].wait()
    diff = mm(final, head, NT) - jnp.swapaxes(goal_s[0].astype(F32), 0, 1)
    wave[...] = jnp.concatenate(
        [diff[0:64] + diff[64:128], jnp.zeros((64, 2 * BLOCK - HOUT), F32)], 1
    )

    def tile_of(ref, j):
        return ref.at[
            pl.ds(pl.multiple_of(j // 2 * 8, 8), 8),
            pl.ds(pl.multiple_of(lax.rem(j, 2) * BLOCK, BLOCK), BLOCK),
        ]

    start, wait, _ = exchange(7, lambda p: tile_of(wave, p), lambda p: wave_in.at[p])
    start()
    wave_in[s] = tile_of(wave, s)[...]
    for k in range(8):
        left[16 + k] = flip(n2[:, k * BLOCK : (k + 1) * BLOCK])
    share_group(2, left, left_hbm, 16, 8)
    wait()
    tile = wave_in[0]
    for k in range(1, NSEQ):
        tile = tile + wave_in[k]
    wave_tile[...] = tile
    start, wait, _ = exchange(8, lambda p: wave_tile, lambda p: tile_of(wave_all, p))
    start()
    tile_of(wave_all, s)[...] = tile

    def turn_active(k, _):
        left[24 + k] = flip(act_s[:, lanes(k, BLOCK)])
        return _

    lax.fori_loop(0, 12, turn_active, 0)
    wait()
    total_wave = wave_all[:, 0:HOUT]
    one = lax.broadcasted_iota(jnp.int32, (HOUT, HOUT), 0)
    two = lax.broadcasted_iota(jnp.int32, (HOUT, HOUT), 1)
    swap = (one == two + 1 - 2 * (two % 2)).astype(F32)
    other = mmh(total_wave, swap)
    weight = wlat_ref[...]
    square = jnp.sum(weight * diff * diff, keepdims=True)
    cross = jnp.sum(weight[0:64] * total_wave * other, keepdims=True) * (1.0 / NSEQ)
    loss = square * (1.0 / MSE_COUNT) + (SPECTRAL / DFT_COUNT) * (float(KMODES) * square + cross)
    other2 = jnp.concatenate([other, other], 0)
    d_pred = weight * (
        (2.0 / MSE_COUNT) * diff + (2.0 * SPECTRAL / DFT_COUNT) * (float(KMODES) * diff + other2)
    )
    d_low = d_pred.astype(BF)
    put_head(small_ref, mm(d_low, final, TN), loss)
    d_final = mm(d_low, head)
    gvec[5:6, :] = column_sum(d_final * unit_f)
    gvec[6:7, :] = column_sum(d_final)
    d_out = normalise_back(d_final, unit_f, rstd_f, vec_ref[5:6, :])
    d_branch = d_out.astype(BF)
    gvec[8:9, :] = column_sum(d_branch.astype(F32))
    for k in range(8):
        right[64 + k] = d_branch[:, k * BLOCK : (k + 1) * BLOCK]
    share_group(4, right, right_hbm, 64, 8)
    acc[...] = jnp.zeros_like(acc)

    def down_tile(t, _):
        part = lanes(t, 1024)
        d_active = mm(d_branch, eight_rows(at_down, t), NT)
        d_upper = (d_active * gelu_slope(up_s[:, part])).astype(BF)
        gvec[pl.ds(11 + t, 1), :] = column_sum(d_upper.astype(F32))
        for k in range(8):
            right[32 + 8 * t + k] = d_upper[:, k * BLOCK : (k + 1) * BLOCK]
        acc[...] += mm(d_upper, eight_columns(at_up, 32, t), NT)
        return _

    lax.fori_loop(0, 4, down_tile, 0, unroll=2)
    share_group(5, right, right_hbm, 32, 32)
    d_n2 = acc[...]
    unit, rstd = normalise(mid_s[...])
    gvec[3:4, :] = column_sum(d_n2 * unit)
    gvec[4:5, :] = column_sum(d_n2)
    d_mid = d_out + normalise_back(d_n2, unit, rstd, vec_ref[3:4, :])
    mid_s[...] = d_mid
    d_mid_low = d_mid.astype(BF)
    start, wait_d, send_d = exchange(
        4, lambda p: d_slab.at[p], lambda p: do_t.at[:, lanes(p, TOK)]
    )

    def att_tile(t, _):
        piece = mm(d_mid_low, two_rows(at_o, t), NT).astype(BF)
        for k in range(2):
            turned = flip(piece[:, k * BLOCK : (k + 1) * BLOCK])
            for half in range(2):
                d_slab[4 * t + 2 * k + half] = turned[half * HD : (half + 1) * HD]
        for k in range(4):
            send_d(4 * t + k)
        return _

    lax.fori_loop(0, 4, att_tile, 0, unroll=4)
    do_t[:, lanes(s, TOK)] = d_slab[s]
    gvec[7:8, :] = column_sum(d_mid_low.astype(F32))
    for k in range(8):
        right[24 + k] = d_mid_low[:, k * BLOCK : (k + 1) * BLOCK]
    share_group(6, right, right_hbm, 24, 8)
    dq_acc[...] = jnp.zeros_like(dq_acc)
    lax.fori_loop(12, 32, turn_active, 0)
    share_group(3, left, left_hbm, 24, 32)
    wait_d()

    turn_rows(do_t, 0, do_row)
    scale = 1.0 / math.sqrt(HD)

    def deltas(c, _):
        part = lanes(c, QCH)
        s_scr[pl.ds(c, 1), :] = jnp.sum(
            do_t[:, part].astype(F32) * out_t32[:, part], 0, keepdims=True
        )
        return _

    lax.fori_loop(0, tiles, deltas, 0)
    start, wait_kv, send_kv = exchange(
        5,
        lambda p: dqkv_t.at[pl.ds(HD, 2 * HD), lanes(p, TOK)],
        lambda p: dqkv_in.at[p, pl.ds(HD, 2 * HD)],
    )

    def backward_tile(i, _):
        c = lax.rem(i + s // 2, tiles)
        keys = rows_at(c, QCH)
        k_part = k_row[keys, :]
        v_part = v_row[keys, :]
        k_turned = qkv_t[HD : 2 * HD, lanes(c, QCH)]
        d_key = jnp.zeros((QCH, HD), F32)
        d_value = jnp.zeros((QCH, HD), F32)
        for t in range(tiles // 2):
            tile = slice(2 * t * QCH, (2 * t + 2) * QCH)
            base = jnp.concatenate([lse[2 * t], lse[2 * t + 1]], 1)
            delta = jnp.concatenate([s_scr[2 * t : 2 * t + 1, :], s_scr[2 * t + 1 : 2 * t + 2, :]], 1)
            probs = jnp.exp2(mm(k_part, qkv_t[0:HD, tile]) * scale2 - base)
            d_prob = mm(v_part, do_t[:, tile])
            d_score = (probs * (d_prob - delta)).astype(BF)
            d_value = d_value + mm(probs.astype(BF), do_row[tile, :])
            d_key = d_key + mm(d_score, q_row[tile, :])
            dq_acc[:, tile] += mm(k_turned, d_score)
        d_key = d_key * scale
        for k in range(2):
            part = lanes(2 * c + k, TOK)
            half = slice(k * TOK, (k + 1) * TOK)
            dqkv_t[HD : 2 * HD, part] = flip(d_key[half]).astype(BF)
            dqkv_t[2 * HD : 3 * HD, part] = flip(d_value[half]).astype(BF)
            send_kv(2 * c + k)
        return _

    lax.fori_loop(0, tiles, backward_tile, 0)
    dqkv_t[0:HD, :] = (dq_acc[...] * scale).astype(BF)
    start_q, wait_q, _ = exchange(
        6,
        lambda p: dqkv_t.at[pl.ds(0, HD), lanes(p, TOK)],
        lambda p: dqkv_in.at[p, pl.ds(0, HD)],
    )
    start_q()
    dqkv_in[s] = dqkv_t[:, lanes(s, TOK)]
    acc[...] = jnp.zeros_like(acc)

    def finish_part(which):
        def one(t, _):
            parts = []
            for k in range(2):
                j = 2 * t + k
                part = slice(which * HD, (which + 1) * HD)
                pair = jnp.concatenate([dqkv_in[2 * j, part, :], dqkv_in[2 * j + 1, part, :]], 0)
                piece = flip(pair)
                right[8 * which + j] = piece
                parts.append(piece)
            piece = jnp.concatenate(parts, 1)
            if which != 1:
                gvec[9 + which // 2 : 10 + which // 2, lanes(t, 256)] = column_sum(
                    piece.astype(F32)
                )
            acc[...] += mm(piece, two_columns(at_qkv, 24, 4 * which + t), NT)
            return _

        lax.fori_loop(0, 4, one, 0, unroll=4)

    wait_kv()
    finish_part(1)
    finish_part(2)
    wait_q()
    finish_part(0)
    share_group(7, right, right_hbm, 0, 24)
    d_n1 = acc[...]
    unit, rstd = normalise(h0_s[...])
    gvec[1:2, :] = column_sum(d_n1 * unit)
    gvec[2:3, :] = column_sum(d_n1)
    d_rows = mid_s[...] + normalise_back(d_n1, unit, rstd, vec_ref[1:2, :])
    embed_backward(d_rows, xp_s, a_s, lead_ref, emb_ref, vec_ref, gvec, small_ref)
    for c, r in share:
        c.wait()
        r.wait()


def run_layer(place, lead, blocks, ids, pix, goals, embed, vec, head, wlat):
    vmem = pl.BlockSpec(memory_space=VM)
    smem = pl.BlockSpec(memory_space=pltpu.SMEM)
    anyspace = pl.BlockSpec(memory_space=pl.ANY)
    dma = pltpu.SemaphoreType.DMA
    length = NSEQ * TOK
    return pl.pallas_call(
        layer_kernel,
        name="layer",
        out_shape=(
            jax.ShapeDtypeStruct((2, N_LEFT, BLOCK, TOK), BF),
            jax.ShapeDtypeStruct((2, N_RIGHT, TOK, BLOCK), BF),
            jax.ShapeDtypeStruct((32, 2 * HALF, BLOCK), F32),
        ),
        in_specs=[smem, smem, vmem, vmem, anyspace, anyspace, vmem, vmem, anyspace, vmem],
        out_specs=(anyspace, anyspace, vmem),
        scratch_shapes=[
            VM((SLOTS, BLOCK, BLOCK), BF),
            VM((N_LEFT, BLOCK, TOK), BF),
            VM((N_RIGHT, TOK, BLOCK), BF),
            VM((HEADS, 3 * HD, TOK), BF),
            VM((3 * HD, length), BF),
            VM((HD, length), BF),
            VM((HD, length), F32),
            VM((length // QCH, 1, QCH), F32),
            VM((HEADS, HD, TOK), BF),
            VM((HEADS, HD, TOK), BF),
            VM((HD, length), BF),
            VM((3 * HD, length), BF),
            VM((HEADS, 3 * HD, TOK), BF),
            VM((length, HD), BF),
            VM((length, HD), BF),
            VM((length, HD), BF),
            VM((length, HD), BF),
            VM((length, QCH), F32),
            VM((HD, length), F32),
            VM((TOK, D), F32),
            VM((TOK, D), BF),
            VM((TOK, HOUT), F32),
            VM((TOK, VARS), F32),
            VM((TOK, D), F32),
            VM((TOK, FF), F32),
            VM((TOK, FF), BF),
            VM((TOK, D), F32),
            VM((64, 2 * BLOCK), F32),
            VM((NSEQ, 8, BLOCK), F32),
            VM((8, BLOCK), F32),
            VM((64, 2 * BLOCK), F32),
            VM((1, HOUT, TOK), BF),
            VM((1, HOUT, TOK), BF),
            VM((HOUT, D), F32),
            VM((16, D), F32),
            dma((4, 16)),
            dma((4,)),
            dma((1,)),
            dma((1,)),
            dma((9, NSEQ)),
            dma((9, NSEQ)),
            dma((3,)),
            dma((8,)),
            dma((8,)),
            dma((8,)),
        ],
        compiler_params=pltpu.CompilerParams(
            collective_id=1, has_side_effects=True, vmem_limit_bytes=60 * 1024 * 1024
        ),
    )(place, lead, blocks, ids, pix, goals, embed, vec, head, wlat)


def token_maps():
    row = lax.broadcasted_iota(jnp.int32, (VARS, HOUT), 0)
    col = lax.broadcasted_iota(jnp.int32, (VARS, HOUT), 1)
    return (col // 4 == row).astype(F32)


def embed_forward(pix_ref, ids_ref, lead_ref, emb_ref, vec_ref, h0_ref, n1_ref, xp_ref, a_ref):
    spread = token_maps()
    var = lax.broadcasted_iota(jnp.int32, (VARS, VARS), 0)
    chosen = (ids_ref[...] == var).astype(BF)
    low = spread.astype(BF)
    wide_ids = mm(chosen, low)
    routes = mm(wide_ids.astype(BF), low, TN)
    one = lax.broadcasted_iota(jnp.int32, (HOUT, HOUT), 0)
    two = lax.broadcasted_iota(jnp.int32, (HOUT, HOUT), 1)
    routes = jnp.where(one % 4 == two % 4, routes, 0.0).astype(BF)
    pix = mm(pix_ref[0], routes, TN)
    xp_ref[...] = pix
    tok = emb_ref[0:HOUT, :]
    emb = emb_ref[HOUT : HOUT + VARS, :]
    query = vec_ref[0:1, :]
    tok_q = jnp.sum(tok * query, -1, keepdims=True)
    emb_q = mmh(query, emb, NT)
    back = lax.broadcasted_iota(jnp.int32, (HOUT, VARS), 0) // 4
    col = lax.broadcasted_iota(jnp.int32, (HOUT, VARS), 1)
    reduce = jnp.where(back == col, tok_q, 0.0)
    logits = (mmh(pix, reduce) + emb_q) * (1.0 / math.sqrt(D))
    logits = logits - jnp.max(logits, -1, keepdims=True)
    weights = jnp.exp(logits)
    weights = weights / jnp.sum(weights, -1, keepdims=True)
    a_ref[...] = weights
    wide = mmh(weights, spread) * pix
    lead = emb_ref[pl.ds(HOUT + VARS + lead_ref[0], 1), :]
    h0 = mmh(wide, tok) + mmh(weights, emb) + lead
    h0_ref[...] = h0
    unit, _ = normalise(h0)
    n1_ref[...] = (unit * vec_ref[1:2, :] + vec_ref[2:3, :]).astype(BF)


VEC_AT = 8 * EROWS
HEAD_AT = VEC_AT + 128


def put(small_ref, begin, value):
    rows = value.shape[0]
    at = 0
    while at < rows:
        device, inside = divmod(begin + at, ROWS)
        count = min(rows - at, ROWS - inside)
        small_ref[device, inside : inside + count, :] = value[at : at + count]
        at += count


def put_head(small_ref, grad, loss):
    for k in range(8):
        put(small_ref, HEAD_AT + HOUT * k, grad[:, k * BLOCK : (k + 1) * BLOCK])
    tile = jnp.broadcast_to(loss, (8, BLOCK))
    for d in range(32):
        small_ref[d, ROWS : 2 * HALF, :] = tile


def embed_backward(d_rows, xp_ref, a_ref, lead_ref, emb_ref, vec_ref, gvec, small_ref):
    pix = xp_ref[...]
    weights = a_ref[...]
    tok = emb_ref[0:HOUT, :]
    emb = emb_ref[HOUT : HOUT + VARS, :]
    query = vec_ref[0:1, :]
    spread = token_maps()
    d_wide = mmh(d_rows, tok, NT)
    d_weight = mmh(pix * d_wide, spread, NT) + mmh(d_rows, emb, NT)
    d_logit = (
        weights
        * (d_weight - jnp.sum(weights * d_weight, -1, keepdims=True))
        * (1.0 / math.sqrt(D))
    )
    wide = mmh(weights, spread) * pix
    d_wide_l = mmh(d_logit, spread) * pix
    ones = jnp.ones((TOK, 1), F32)
    d_tok_q = mmh(d_wide_l, ones, TN)
    d_emb_q = mmh(d_logit, ones, TN)
    g_tok = mmh(wide, d_rows, TN) + d_tok_q * query
    g_emb = mmh(weights, d_rows, TN) + d_emb_q * query
    row = lax.broadcasted_iota(jnp.int32, (LEADS, D), 0)
    g_lead = jnp.where(row == lead_ref[0], column_sum(d_rows), 0.0)
    gvec[0:1, :] = column_sum(d_tok_q * tok) + column_sum(d_emb_q * emb)
    gvec[15:16, :] = jnp.zeros((1, D), F32)
    for k in range(8):
        part = slice(k * BLOCK, (k + 1) * BLOCK)
        put(small_ref, EROWS * k, g_tok[:, part])
        put(small_ref, EROWS * k + HOUT, g_emb[:, part])
        put(small_ref, EROWS * k + HOUT + VARS, g_lead[:, part])
        put(small_ref, VEC_AT + 16 * k, gvec[:, part])


SLOTS = 768
ROWS = 120
HALF = 64


def sides_of(b):
    li = jnp.where(
        b < 192, b // 24, jnp.where(b < 256, b // 8 - 16, jnp.where(b < 512, b // 32 + 8, b // 8 - 40))
    )
    ri = jnp.where(
        b < 192,
        lax.rem(b, 24),
        jnp.where(
            b < 256,
            24 + lax.rem(b, 8),
            jnp.where(b < 512, 32 + lax.rem(b, 32), 64 + lax.rem(b, 8)),
        ),
    )
    return li, ri


def reduce_kernel(
    order_ref,
    left_hbm,
    right_hbm,
    small_ref,
    lroot_hbm,
    mom_hbm,
    rroot_hbm,
    own_hbm,
    ggt_hbm,
    gtg_hbm,
    lgr_hbm,
    turned_hbm,
    all_ref,
    sum_ref,
    lroot_ref,
    mom_ref,
    rroot_ref,
    own_ref,
    ggt_ref,
    gtg_ref,
    lgr_ref,
    turned_ref,
    lt,
    rt,
    mine,
    theirs,
    acc,
    acc_small,
    land,
    land_small,
    out,
    out_small,
    tail,
    in_sem,
    swap_sem,
    recv,
    send,
    recv_small,
    send_small,
    norms,
    across,
    t_recv,
    t_send,
    t_sib,
    n_send,
    n_recv,
    root_sem,
    out_sem,
):
    place = Place()
    loads = [
        pltpu.make_async_copy(left_hbm.at[0], lt.at[:, :, pl.ds(0, TOK)], in_sem.at[0]),
        pltpu.make_async_copy(left_hbm.at[1], lt.at[:, :, pl.ds(TOK, TOK)], in_sem.at[1]),
        pltpu.make_async_copy(right_hbm.at[0], rt.at[:, pl.ds(0, TOK), :], in_sem.at[2]),
        pltpu.make_async_copy(right_hbm.at[1], rt.at[:, pl.ds(TOK, TOK), :], in_sem.at[3]),
    ]
    loads.append(pltpu.make_async_copy(small_ref.at[:, place.core], mine, in_sem.at[4]))
    for c in loads:
        c.start()
    later = [
        pltpu.make_async_copy(src, dst, root_sem.at[i])
        for i, (src, dst) in enumerate(
            ((lroot_hbm, lroot_ref), (mom_hbm, mom_ref), (rroot_hbm, rroot_ref))
        )
    ]
    place.greet()
    swap = pltpu.make_async_remote_copy(
        small_ref.at[:, 1 - place.core],
        theirs,
        swap_sem.at[0],
        swap_sem.at[1],
        place.sibling(),
        MESH_ID,
    )
    swap.start()
    for c in later:
        c.start()
    for c in loads:
        c.wait()

    def own_piece(part, device, chip, out_at):
        if part < 4:

            def block(j, _):
                slot = device * SHARE + part * PIECE + j
                li, ri = sides_of(order_ref[slot])
                acc[j] = mm(lt[li], rt[ri])
                return 0

            lax.fori_loop(0, PIECE, block, 0, unroll=3)
        else:
            acc_small[...] = mine[chip // 2, lax.rem(chip, 2), pl.ds((part - 4) * HALF, HALF), :]

    def add_landed(part, index):
        if part < 4:
            acc[...] += land[index].astype(F32)
        else:
            acc_small[...] += land_small[index]

    me = place.linear(place.z, place.x, place.y)

    def keep(part, out_at, root):
        if part < 4:
            if root:
                own_ref[pl.ds(part * PIECE, PIECE)] = acc[...]
            else:
                out[out_at] = acc[...].astype(BF)
        elif root:
            tail[me * 2 + part - 4] = acc_small[...]
        else:
            out_small[out_at] = acc_small[...]

    base, _ = landing_base(MAIN)
    base_small, _ = landing_base(SMALL)

    def main_step(step):
        reduce_step(
            place, MAIN, base, step, own_piece, add_landed, land, recv, out, send, keep, 0
        )

    def small_step(step):
        reduce_step(
            place, SMALL, base_small, step, own_piece, add_landed,
            land_small, recv_small, out_small, send_small, keep, 4,
        )

    stores = []

    def store(index, source, target, begin, count):
        part = pl.ds(begin, count)
        copy = pltpu.make_async_copy(source.at[part], target.at[part], out_sem.at[index])
        copy.start()
        stores.append(copy)

    def product(part, j):
        i = part * PIECE + j
        g = own_ref[i]
        ggt_ref[i] = mmh(g, g, NT)
        gtg_ref[i] = mmh(g, g, TN)
        lgr_ref[i] = mmh(mmh(lroot_ref[i], g), rroot_ref[i])
        if j == PIECE - 1:
            store(4 * part, own_ref, own_hbm, part * PIECE, PIECE)
            store(4 * part + 1, ggt_ref, ggt_hbm, part * PIECE, PIECE)
            store(4 * part + 2, gtg_ref, gtg_hbm, part * PIECE, PIECE)
            store(4 * part + 3, lgr_ref, lgr_hbm, part * PIECE, PIECE)

    def small_root():
        first = tail[me * 2]
        data = tail[me * 2 + 1, 0 : ROWS - HALF, :]
        return jnp.sum(first * first, keepdims=True) + jnp.sum(data * data, keepdims=True)

    spread = gather_steps(
        place,
        TAIL,
        (1, 1),
        [step[1:] for step in REDUCE_PLAN if step[0] == 1],
        lambda d, p: tail.at[d * 2 + p],
        lambda n: tail.at[pl.ds(0, n)],
        t_recv,
        t_send,
        t_sib.at[pl.ds(0, 1)],
        t_sib.at[pl.ds(1, 1)],
    )
    def send_norm(squares):
        norms[place.s] = jnp.broadcast_to(
            jnp.sum(squares, keepdims=True) + small_root(), (8, BLOCK)
        )
        lax.fori_loop(1, NSEQ, lambda o, _: (norm_copy(o).start(), 0)[1], 0)

    def norm_copy(o):
        peer = lax.rem(place.s + o, NSEQ)
        return pltpu.make_async_remote_copy(
            norms.at[place.s],
            norms.at[place.s],
            n_send.at[o],
            n_recv.at[o],
            (peer, place.y),
            MESH_ID,
        )

    squares = jnp.zeros((BLOCK, BLOCK), F32)
    roots = 0
    turned = 0
    small_roots = 0
    swapped = False
    for kind, part, dx, dy, rank in REDUCE_PLAN:
        root = dx == 0 and dy == 0 and rank == 3
        if kind == 1:
            next(spread)
        elif kind == 2:
            product(part, dx)
        elif kind == 3:
            if turned == 0:
                for c in later:
                    c.wait()
            turned_ref[turned] = mmh(mmh(lroot_ref[turned], mom_ref[turned]), rroot_ref[turned])
            turned += 1
            if turned == SHARE:
                store(16, turned_ref, turned_hbm, 0, SHARE)
        elif part >= 4:
            if not swapped:
                swapped = True
                swap.wait()
                mine[...] += theirs[...]
            small_step((part - 4, dx, dy, rank))
            small_roots += root
        else:
            main_step((part, dx, dy, rank))
            if root:
                for i in range(part * PIECE, (part + 1) * PIECE):
                    squares = squares + own_ref[i] * own_ref[i]
                roots += 1
        if kind == 0 and root and roots == 4 and small_roots == 2:
            send_norm(squares)

    for _ in spread:
        pass
    for d in range(32):
        all_ref[d, 0:HALF, :] = tail[2 * d]
        all_ref[d, HALF:ROWS, :] = tail[2 * d + 1, 0 : ROWS - HALF, :]
    lax.fori_loop(1, NSEQ, lambda o, _: (norm_copy(o).wait(), 0)[1], 0)
    total = norms[0]
    for k in range(1, NSEQ):
        total = total + norms[k]
    across[0] = total
    over = pltpu.make_async_remote_copy(
        across.at[0], across.at[1], n_send.at[0], n_recv.at[0], (place.s, 1 - place.y), MESH_ID
    )
    over.start()
    drain(place, MAIN, lambda n: out.at[pl.ds(0, n)], send, REDUCE_HOPS)
    drain(place, SMALL, lambda n: out_small.at[pl.ds(0, n)], send_small, REDUCE_HOPS)
    for copy in stores:
        copy.wait()
    over.wait()
    sum_ref[0] = across[0] + across[1]
    sum_ref[1] = tail[1, ROWS - HALF : HALF, :]


def run_reduce(order, left, right, small, lroots, momentum, rroots):
    vmem = pl.BlockSpec(memory_space=VM)
    smem = pl.BlockSpec(memory_space=pltpu.SMEM)
    anyspace = pl.BlockSpec(memory_space=pl.ANY)
    dma = pltpu.SemaphoreType.DMA
    _, count = landing_base(MAIN)
    _, count_small = landing_base(SMALL)
    stack = jax.ShapeDtypeStruct((SHARE, BLOCK, BLOCK), F32)
    return pl.pallas_call(
        reduce_kernel,
        name="reduce",
        out_shape=(stack,) * 5
        + (
            jax.ShapeDtypeStruct((32, ROWS, BLOCK), F32),
            jax.ShapeDtypeStruct((2, 8, BLOCK), F32),
        ),
        in_specs=[smem] + [anyspace] * 6,
        out_specs=(anyspace,) * 5 + (vmem, vmem),
        scratch_shapes=[VM((SHARE, BLOCK, BLOCK), F32)] * 8
        + [
            VM((N_LEFT, BLOCK, 2 * TOK), BF),
            VM((N_RIGHT, 2 * TOK, BLOCK), BF),
            VM((8, 2, 2 * HALF, BLOCK), F32),
            VM((8, 2, 2 * HALF, BLOCK), F32),
            VM((PIECE, BLOCK, BLOCK), F32),
            VM((HALF, BLOCK), F32),
            VM((count, PIECE, BLOCK, BLOCK), BF),
            VM((count_small, HALF, BLOCK), F32),
            VM((64, PIECE, BLOCK, BLOCK), BF),
            VM((32, HALF, BLOCK), F32),
            VM((64, HALF, BLOCK), F32),
            dma((5,)),
            dma((2,)),
            dma((count,)),
            dma((4,)),
            dma((count_small,)),
            dma((4,)),
            VM((NSEQ, 8, BLOCK), F32),
            VM((2, 8, BLOCK), F32),
            dma((2, 16)),
            dma((4,)),
            dma((2,)),
            dma((NSEQ,)),
            dma((NSEQ,)),
            dma((3,)),
            dma((17,)),
        ],
        compiler_params=pltpu.CompilerParams(
            collective_id=3, has_side_effects=True, vmem_limit_bytes=60 * 1024 * 1024
        ),
    )(order, left, right, small, lroots, momentum, rroots)


def final_kernel(
    sums_ref, own, ggt, gtg, lgr, turned, mom, stat_l, stat_r, blk,
    ge, gv, gh, e, e1, e2, v, v1, v2, h, h1, h2,
    loss_o, norm_o, blk_o, mom_o, l_o, r_o,
    e1_o, e2_o, e_o, v1_o, v2_o, v_o, h1_o, h2_o, h_o,
):
    norm = jnp.sqrt(sums_ref[0, 0:1, 0:1])
    loss_o[...] = sums_ref[1, 4:5, 0:1]
    norm_o[...] = norm
    clip = CLIP_NORM / jnp.maximum(norm, CLIP_NORM)
    for i in range(6):
        mom_o[i] = BETA_ONE * mom[i] + (1.0 - BETA_ONE) * (own[i] * clip)
        l_o[i] = BETA_TWO * stat_l[i] + (1.0 - BETA_TWO) * ((ggt[i] * clip) * clip)
        r_o[i] = BETA_TWO * stat_r[i] + (1.0 - BETA_TWO) * ((gtg[i] * clip) * clip)
        direction = BETA_ONE * turned[i] + (1.0 - BETA_ONE) * (lgr[i] * clip)
        blk_o[i] = blk[i] - SHAMPOO_RATE * (direction + DECAY * blk[i])
    e1_o[...], e2_o[...], e_o[...] = adam(e[...], e1[...], e2[...], jnp.concatenate([ge[0:EROWS], ge[EROWS:]], 1) * clip, EMBED_RATE)
    v1_o[...], v2_o[...], v_o[...] = adam(
        v[...], v1[...], v2[...], jnp.concatenate([gv[0:15, :], gv[16:31, :]], 1) * clip, VECTOR_RATE
    )
    h1_o[...], h2_o[...], h_o[...] = adam(h[...], h1[...], h2[...], jnp.concatenate([gh[0:HOUT], gh[HOUT:]], 1) * clip, HEAD_RATE)


def run_final(sums, stacks, flat, embed, vec, head):
    slots = pl.BlockSpec((6, BLOCK, BLOCK), lambda k: (k, 0, 0))
    table = pl.BlockSpec((EROWS, 2 * BLOCK), lambda k: (0, k))
    rows = pl.BlockSpec((15, 2 * BLOCK), lambda k: (0, k))
    wide = pl.BlockSpec((HOUT, 2 * BLOCK), lambda k: (0, k))
    one = pl.BlockSpec((1, 1), lambda k: (0, 0))
    stack = jax.ShapeDtypeStruct((SHARE, BLOCK, BLOCK), F32)
    shapes = (
        (jax.ShapeDtypeStruct((1, 1), F32),) * 2
        + (stack,) * 4
        + (jax.ShapeDtypeStruct((EROWS, D), F32),) * 3
        + (jax.ShapeDtypeStruct((15, D), F32),) * 3
        + (jax.ShapeDtypeStruct((HOUT, D), F32),) * 3
    )
    return pl.pallas_call(
        final_kernel,
        name="final",
        grid=(4,),
        out_shape=shapes,
        in_specs=[pl.BlockSpec((2, 8, BLOCK), lambda k: (0, 0, 0))]
        + [slots] * 9
        + [
            pl.BlockSpec((2 * EROWS, BLOCK), lambda k: (k, 0)),
            pl.BlockSpec((32, BLOCK), lambda k: (VEC_AT // 32 + k, 0)),
            pl.BlockSpec((2 * HOUT, BLOCK), lambda k: (HEAD_AT // HOUT // 2 + k, 0)),
        ]
        + [table] * 3
        + [rows] * 3
        + [wide] * 3,
        out_specs=(one,) * 2 + (slots,) * 4 + (table,) * 3 + (rows,) * 3 + (wide,) * 3,
        compiler_params=pltpu.CompilerParams(vmem_limit_bytes=60 * 1024 * 1024),
    )(sums, *stacks, flat, flat, flat, *embed, *vec, *head)


def fast_shards(
    inputs,
    targets,
    var_ids,
    lead_ids,
    block_order,
    blocks,
    block_momentum,
    left_stats,
    right_stats,
    left_roots,
    right_roots,
    embed_params,
    embed_first,
    embed_second,
    vectors,
    vector_first,
    vector_second,
    head_weight,
    head_first,
    head_second,
):
    slots = jnp.arange(SLOTS, dtype=jnp.int32)
    hit = block_order[None, :] == slots[:, None]
    place = jnp.sum(jnp.where(hit, slots[None, :], 0), 1)
    lat = ((np.arange(2 * LAT_P, dtype=np.float64) + 0.5) / (2 * LAT_P) - 0.5) * math.pi
    wlat = np.cos(lat)
    wlat = (wlat / np.mean(wlat)).reshape(1, LAT_P, 1, 2, 1)
    wlat = np.broadcast_to(wlat, (TOK // LAT_P, LAT_P, VARS, 2, 2)).reshape(TOK, HOUT)
    left, right, small = run_layer(
        place, lead_ids, blocks, var_ids, jnp.swapaxes(inputs, 1, 2), jnp.swapaxes(targets, 1, 2),
        embed_params, vectors, head_weight.T,
        jnp.asarray(wlat, F32),
    )
    owned, ggt, gtg, lgr, turned, every, sums = run_reduce(
        block_order, left, right, small.reshape(8, 2, 2, 2 * HALF, BLOCK),
        left_roots, block_momentum, right_roots,
    )
    loss, norm, *rest = run_final(
        sums,
        (owned, ggt, gtg, lgr, turned, block_momentum, left_stats, right_stats, blocks),
        every.reshape(32 * ROWS, BLOCK),
        (embed_params, embed_first, embed_second),
        (vectors, vector_first, vector_second),
        (head_weight.T, head_first.T, head_second.T),
    )
    return (loss.reshape(()), norm.reshape(()), *rest[:-3], *(a.T for a in rest[-3:]))


def solution(mesh):
    in_specs = (
        P("batch", "seq", None),
        P("batch", "seq", None),
        P("batch", None),
        P("batch"),
        P(),
        P(("seq", "batch"), None, None),
        P(("seq", "batch"), None, None),
        P(("seq", "batch"), None, None),
        P(("seq", "batch"), None, None),
        P(("seq", "batch"), None, None),
        P(("seq", "batch"), None, None),
        P(),
        P(),
        P(),
        P(),
        P(),
        P(),
        P(),
        P(),
        P(),
    )
    out_specs = (
        P(),
        P(),
        P(("seq", "batch"), None, None),
        P(("seq", "batch"), None, None),
        P(("seq", "batch"), None, None),
        P(("seq", "batch"), None, None),
        P(),
        P(),
        P(),
        P(),
        P(),
        P(),
        P(),
        P(),
        P(),
    )
    sizes = dict(mesh.shape)
    fast = sizes == {"seq": NSEQ, "batch": 2}
    return jax.shard_map(fast_shards if fast else shards, mesh=mesh, in_specs=in_specs, out_specs=out_specs, check_vma=False)
```
